32 devices in a mesh: dp: 8 (over z, y), fsdp: 4 (over x, core).
Axes of the slice: x: 2, y: 2, z: 4, core: 2. Of those that a mesh axis runs over, the one named last changes fastest.
Arguments:
- tokens: bfloat16 [8192, 2048], P(('dp', 'fsdp')), may hold values from -6 to 6
- widths: int32 [8], P('dp'), may hold values from 0 to 3, as said below
- cotangent: bfloat16 [8192, 2048], P(('dp', 'fsdp')), may hold values from -6 to 6
- in_weight: float32 [2048, 8512], P(('dp', 'fsdp')), may hold values from -0.125 to 0.125
- in_first: float32 [2048, 8512], P(('dp', 'fsdp')), may hold values from -0.0029296875 to 0.0029296875
- in_second: float32 [2048, 8512], P(('dp', 'fsdp')), may hold values from 3.8685798e-08 to 1.5474319e-07
- out_weight: float32 [4096, 2048], P(('dp', 'fsdp')), may hold values from -0.09375 to 0.09375
- out_first: float32 [4096, 2048], P(('dp', 'fsdp')), may hold values from -0.0029296875 to 0.0029296875
- out_second: float32 [4096, 2048], P(('dp', 'fsdp')), may hold values from 3.8685798e-08 to 1.5474319e-07
- vectors: float32 [28096], replicated, may hold values from -8 to 3
- vector_first: float32 [28096], replicated, may hold values from -0.0078125 to 0.0078125
- vector_second: float32 [28096], replicated, may hold values from 1.5474319e-07 to 6.1897276e-07
Outputs:
- layer_out: bfloat16 [8192, 2048], P(('dp', 'fsdp'))
- token_grad: bfloat16 [8192, 2048], P(('dp', 'fsdp'))
- in_grad: float32 [2048, 8512], P(('dp', 'fsdp'))
- out_grad: float32 [4096, 2048], P(('dp', 'fsdp'))
- vector_grad: float32 [28096], replicated
- grad_norm: float32 [], replicated
- in_moment: float32 [2048, 8512], P(('dp', 'fsdp'))
- in_square: float32 [2048, 8512], P(('dp', 'fsdp'))
- in_master: float32 [2048, 8512], P(('dp', 'fsdp'))
- in_rounded: bfloat16 [2048, 8512], P(('dp', 'fsdp'))
- out_moment: float32 [4096, 2048], P(('dp', 'fsdp'))
- out_square: float32 [4096, 2048], P(('dp', 'fsdp'))
- out_master: float32 [4096, 2048], P(('dp', 'fsdp'))
- out_rounded: bfloat16 [4096, 2048], P(('dp', 'fsdp'))
- vector_moment: float32 [28096], replicated
- vector_square: float32 [28096], replicated
- vector_master: float32 [28096], replicated
The draws below stay inside these ranges and needn't reach their ends.
Inputs may be any that keep to these rules, and one draw needn't show every extreme that they name: `widths`: every width index 0, 1, 2 and 3 occurs in every draw.
All inputs are finite; a program needn't handle non-finite values.
Results may differ from the reference program's by a relative error of at most 0.0087.
The reference program's roundings to bfloat16 on the way count: a program that leaves them out, or rounds other values in their place, can miss the bound.
Values may be sent and summed in bfloat16 or wider, within the bound.
A program may use at most 232 MiB of HBM per device.

```python
import math
import jax
import jax.numpy as jnp
from jax import lax

D = 2048
HEADS = 64
HEAD_DIM = 64
STATE = 128
CONV = 4
SPAN = 256
STEP = 10
INNER = 4096
XBC = 4352
PIN = 8512
SMALL = 28096
SEQ_LEN = 1024
SEQS = 8
TOKENS = 8192


def draw_widths(key, part):
    key = jax.random.fold_in(key, 11)
    first_key, second_key = jax.random.split(key)
    random_widths = jax.random.randint(first_key, (SEQS,), 0, 4, dtype=jnp.int32)
    shuffled = jax.random.permutation(second_key, SEQS)
    positions = jnp.argsort(shuffled).astype(jnp.int32)
    return jnp.where(positions < 4, positions, random_widths)


def draw_vectors(key, part):
    key = jax.random.fold_in(key, 23)
    split_keys = jax.random.split(key, 7)
    norm_ramp = jnp.arange(D, dtype=jnp.float32) / D
    gate_ramp = jnp.arange(INNER, dtype=jnp.float32) / INNER
    lowest = 0.5
    norm_wobble = jnp.clip(0.05 * jax.random.normal(split_keys[0], (D,), jnp.float32), -0.1, 0.1)
    gate_wobble = jnp.clip(0.05 * jax.random.normal(split_keys[1], (INNER,), jnp.float32), -0.1, 0.1)
    tap_values = jnp.clip(0.5 * jax.random.normal(split_keys[2], (CONV * XBC,), jnp.float32), -2.0, 2.0)
    norm_gain = (lowest + norm_ramp) * (1.0 + norm_wobble)
    gate_gain = (lowest + gate_ramp) * (1.0 + gate_wobble)
    filter_bias = jnp.clip(0.2 * jax.random.normal(split_keys[3], (XBC,), jnp.float32), -1.0, 1.0)
    step_sizes = jnp.exp(jax.random.uniform(split_keys[4], (HEADS,), jnp.float32, math.log(0.0005), math.log(0.05)))
    step_bias = jnp.log(jnp.expm1(step_sizes))
    decay_log = jax.random.uniform(split_keys[5], (HEADS,), jnp.float32, math.log(0.5), math.log(8.0))
    skip_gain = jax.random.uniform(split_keys[6], (HEADS,), jnp.float32, 0.5, 1.5)
    return jnp.concatenate([norm_gain, gate_gain, tap_values, filter_bias, step_bias, decay_log, skip_gain]).astype(jnp.float32)


def block_scale(rng, shape, cuts, smallest, largest):
    def one(axis_at, parts):
        steps = jax.random.uniform(jax.random.fold_in(jax.random.fold_in(rng, 6), axis_at), (parts,), jnp.float32, smallest / len(cuts), largest / len(cuts))
        return jnp.repeat(jnp.exp(steps), shape[axis_at] // parts).reshape((-1,) + (1,) * (len(shape) - axis_at - 1))

    gain = one(*cuts[0])
    for cut in cuts[1:]:
        gain = gain * one(*cut)
    return gain


def bell_draw(stream_key, extent, deviation, reach, shards=(), kind=jnp.bfloat16):
    drawn = deviation * jax.random.normal(stream_key, extent, jnp.float32)
    if shards:
        drawn = drawn * block_scale(stream_key, extent, shards, -0.22, 0.18)
    return jnp.clip(drawn, -reach, reach).astype(kind)


def setup_inputs(seed: int = 0) -> dict:
    key_of = jax.random.split(jax.random.key(seed), 13)
    return {
        "tokens": bell_draw(key_of[0], (TOKENS, D), 1.0, 6.0, ((0, 32),)),
        "widths": draw_widths(jax.random.fold_in(key_of[12], 71), 0),
        "cotangent": bell_draw(key_of[2], (TOKENS, D), 1.0, 6.0, ((0, 32),)),
        "in_weight": bell_draw(key_of[3], (D, PIN), D ** -0.5, 0.125, ((0, 32),), jnp.float32),
        "in_first": bell_draw(key_of[4], (D, PIN), (1.0 / (D * PIN + INNER * D + SMALL) ** 0.5), 0.0029296875, ((0, 32),), jnp.float32),
        "in_second": jnp.clip(jnp.exp(math.log(1.547431907056307e-07) - 1.3862944 * jax.random.uniform(key_of[5], (D, PIN), jnp.float32) ** block_scale(key_of[5], (D, PIN), ((0, 32),), -0.2, 0.2)), 3.8685797676407674e-08, 1.547431907056307e-07),
        "out_weight": bell_draw(key_of[6], (INNER, D), INNER ** -0.5, 0.09375, ((0, 32),), jnp.float32),
        "out_first": bell_draw(key_of[7], (INNER, D), (1.0 / (D * PIN + INNER * D + SMALL) ** 0.5), 0.0029296875, ((0, 32),), jnp.float32),
        "out_second": jnp.clip(jnp.exp(math.log(1.547431907056307e-07) - 1.3862944 * jax.random.uniform(key_of[8], (INNER, D), jnp.float32) ** block_scale(key_of[8], (INNER, D), ((0, 32),), -0.2, 0.2)), 3.8685797676407674e-08, 1.547431907056307e-07),
        "vectors": draw_vectors(jax.random.fold_in(key_of[12], 71), 0),
        "vector_first": bell_draw(key_of[10], (SMALL,), (3.0 / (D * PIN + INNER * D + SMALL) ** 0.5), 0.0078125, (), jnp.float32),
        "vector_second": jnp.clip(jnp.exp(jax.random.uniform(key_of[11], (SMALL,), jnp.float32, math.log(1.547431907056307e-07), math.log(6.189727628225228e-07))), 1.547431907056307e-07, 6.189727628225228e-07),
    }


@jax.custom_vjp
def low(v):
    return lax.optimization_barrier(v.astype(jnp.bfloat16)).astype(jnp.float32)

@jax.custom_vjp
def low_back(v):
    return v

def low_keep(v):
    return (low(v), None)

def low_pass(kept, grad):
    return (grad,)

def back_keep(v):
    return (v, None)

def back_low(kept, grad):
    return (low(grad),)
low.defvjp(low_keep, low_pass)
low_back.defvjp(back_keep, back_low)
norm_eps = 1e-05
clip_norm = 1.0
beta_first = 0.5
beta_second = 0.5
adam_eps = 1e-08
weight_decay = 0.1
rate_in_proj = 0.03
rate_out_proj = 0.02
rate_vectors = 0.5
highest = lax.Precision.HIGHEST

def unpack(vectors):
    offset = D + INNER
    taps_end = offset + CONV * XBC
    heads_start = taps_end + XBC
    norm_gain = vectors[:D]
    gate_gain = vectors[D:offset]
    filter_taps = vectors[offset:taps_end].reshape(CONV, XBC)
    filter_bias = vectors[taps_end:heads_start]
    step_bias = vectors[heads_start:heads_start + HEADS]
    decay_log = vectors[heads_start + HEADS:heads_start + 2 * HEADS]
    skip_gain = vectors[heads_start + 2 * HEADS:heads_start + 3 * HEADS]
    return (norm_gain, gate_gain, filter_taps, filter_bias, step_bias, decay_log, skip_gain)

def rms_scale(values, gain_vector):
    return values * lax.rsqrt(lax.optimization_barrier(jnp.mean(values * values, axis=-1, keepdims=True)) + norm_eps) * gain_vector[None, :]

def causal_filter(signal, previous, filter_taps, filter_bias):
    padded = jnp.concatenate([previous, signal], axis=0)
    length = signal.shape[0]
    summed = filter_bias[None, :] + filter_taps[0][None, :] * padded[0:length]
    for offset in range(1, CONV):
        summed = summed + filter_taps[offset][None, :] * padded[offset:offset + length]
    return summed

def span_apply(carry_state, values, step_sizes, key_rows, query_rows, decay_rates):
    block_rows = values.shape[0]
    log_sums = jnp.cumsum(step_sizes * decay_rates[None, :], axis=0)
    weighted = values * step_sizes[:, :, None]
    causal = jnp.arange(block_rows)[:, None] >= jnp.arange(block_rows)[None, :]
    log_heads = log_sums.T
    differences = log_heads[:, :, None] - log_heads[:, None, :]
    decays = jnp.exp(jnp.where(causal[None], differences, 0.0)) * causal[None].astype(jnp.float32)
    intersection = jnp.dot(query_rows, key_rows.T, precision=highest)
    mixing = decays * intersection[None]
    within = jnp.einsum('hij,jhp->ihp', mixing, weighted, precision=highest)
    carried = jnp.einsum('in,hpn->ihp', query_rows, carry_state, precision=highest) * jnp.exp(log_sums)[:, :, None]
    tail_decay = jnp.exp(log_sums[-1][None, :] - log_sums)
    renewed = carry_state * jnp.exp(log_sums[-1])[:, None, None] + jnp.einsum('jhp,jn->hpn', weighted * tail_decay[:, :, None], key_rows, precision=highest)
    return (renewed, within + carried)

def sequence_forward(inputs, width_index, in_low, out_low, vectors):
    norm_gain, gate_gain, filter_taps, filter_bias, step_bias, decay_log, skip_gain = unpack(vectors)
    length = inputs.shape[0]
    active = HEADS // 8 * jnp.left_shift(jnp.int32(1), width_index)
    head_mask = (jnp.arange(HEADS, dtype=jnp.int32) < active).astype(jnp.float32)
    channel_mask = jnp.repeat(head_mask, HEAD_DIM)
    column_mask = jnp.concatenate([channel_mask, channel_mask, jnp.ones((2 * STATE,), jnp.float32), head_mask])
    normed = low(rms_scale(inputs, norm_gain))
    projected = low_back(jnp.dot(normed, in_low, precision=highest) * column_mask[None, :])
    gate_part = projected[:, :INNER]
    mixed_part = projected[:, INNER:INNER + XBC]
    step_raw = projected[:, INNER + XBC:]
    activated = jax.nn.silu(causal_filter(mixed_part, jnp.zeros((CONV - 1, XBC), jnp.float32), filter_taps, filter_bias))
    values = activated[:, :INNER].reshape(length, HEADS, HEAD_DIM) * head_mask[None, :, None]
    key_rows = activated[:, INNER:INNER + STATE]
    query_rows = activated[:, INNER + STATE:]
    step_sizes = jax.nn.softplus(step_raw + step_bias[None, :])
    decay_rates = -jnp.exp(decay_log)
    blocks = length // SPAN

    def advance(carry_state, pieces):
        return span_apply(carry_state, pieces[0], pieces[1], pieces[2], pieces[3], decay_rates)
    last_state, outputs = lax.scan(advance, jnp.zeros((HEADS, HEAD_DIM, STATE), jnp.float32), (values.reshape(blocks, SPAN, HEADS, HEAD_DIM), step_sizes.reshape(blocks, SPAN, HEADS), key_rows.reshape(blocks, SPAN, STATE), query_rows.reshape(blocks, SPAN, STATE)))
    scanned = outputs.reshape(length, HEADS, HEAD_DIM) + skip_gain[None, :, None] * values
    gated = scanned.reshape(length, INNER) * jax.nn.silu(gate_part)
    channel_count = (active * HEAD_DIM).astype(jnp.float32)
    inverse_rms = lax.rsqrt(lax.optimization_barrier(jnp.sum(gated * gated, axis=-1, keepdims=True)) / channel_count + norm_eps)
    gated_out = low(gated * inverse_rms * gate_gain[None, :])
    added = low_back(jnp.dot(gated_out, out_low, precision=highest))
    return inputs + added

def adamw(weight, moment, square, gradient, step_rate):
    moment_new = beta_first * moment + (1.0 - beta_first) * gradient
    square_new = beta_second * square + (1.0 - beta_second) * gradient * gradient
    moment_hat = moment_new / (1.0 - beta_first ** STEP)
    square_hat = square_new / (1.0 - beta_second ** STEP)
    weight_new = weight - step_rate * (moment_hat / (jnp.sqrt(square_hat) + adam_eps) + weight_decay * weight)
    return (moment_new, square_new, weight_new)

def reference(tokens, widths, cotangent, in_weight, in_first, in_second, out_weight, out_first, out_second, vectors, vector_first, vector_second):
    inputs = tokens.astype(jnp.float32).reshape(SEQS, SEQ_LEN, D)

    def all_sequences(inputs, in_weight, out_weight, vectors):
        in_low = low(in_weight)
        out_low = low(out_weight)

        def one_sequence(sequence_pair):
            return sequence_forward(sequence_pair[0], sequence_pair[1], in_low, out_low, vectors)
        return lax.map(jax.checkpoint(one_sequence), (inputs, widths))
    outputs, pullback = jax.vjp(all_sequences, inputs, in_weight, out_weight, vectors)
    token_back, in_raw, out_raw, vector_raw = pullback(cotangent.astype(jnp.float32).reshape(SEQS, SEQ_LEN, D))
    squares = jnp.sum(in_raw * in_raw) + jnp.sum(out_raw * out_raw) + jnp.sum(vector_raw * vector_raw)
    grad_norm = jnp.sqrt(squares)
    factor = jnp.minimum(1.0, clip_norm / (grad_norm + 1e-06))
    in_grad = in_raw * factor
    out_grad = out_raw * factor
    vector_grad = vector_raw * factor
    in_moment, in_square, in_master = adamw(in_weight, in_first, in_second, in_grad, rate_in_proj)
    out_moment, out_square, out_master = adamw(out_weight, out_first, out_second, out_grad, rate_out_proj)
    vector_moment, vector_square, vector_master = adamw(vectors, vector_first, vector_second, vector_grad, rate_vectors)
    return (outputs.reshape(TOKENS, D).astype(jnp.bfloat16), token_back.reshape(TOKENS, D).astype(jnp.bfloat16), in_grad, out_grad, vector_grad, grad_norm, in_moment, in_square, in_master, in_master.astype(jnp.bfloat16), out_moment, out_square, out_master, out_master.astype(jnp.bfloat16), vector_moment, vector_square, vector_master)
```

```python
from functools import partial

import jax
import jax.numpy as jnp
from jax import lax
from jax.experimental import pallas as pl
from jax.experimental.pallas import tpu as pltpu
from jax.sharding import PartitionSpec as P

D = 2048
HEADS = 64
HEAD_DIM = 64
STATE = 128
CONV = 4
SPAN = 128
STEP = 10
INNER = 4096
XBC = 4352
PAIR = 2 * HEAD_DIM
GROUP = 4
LANES = GROUP * HEAD_DIM
ROW_TILE = 256
RING_LIMIT = 16

norm_eps = 1e-05
clip_norm = 1.0
beta_first = 0.5
beta_second = 0.5
adam_eps = 1e-08
weight_decay = 0.1
rate_in_proj = 0.03
rate_out_proj = 0.02
rate_vectors = 0.5
highest = lax.Precision.HIGHEST
f32 = jnp.float32
bf16 = jnp.bfloat16
VMEM_BYTES = 56 * 1024 * 1024


def ring_order(count):
    return list(range(0, count, 2)) + list(range(count - 1, 0, -2))


def ring_links(count):
    order = ring_order(count)
    right = [(order[i], order[(i + 1) % count]) for i in range(count)]
    return right, [(b, a) for a, b in right]


def ring_place(axis):
    count = lax.axis_size(axis)
    order = ring_order(count)
    places = [0] * count
    for place, member in enumerate(order):
        places[member] = place
    place = jnp.asarray(places, jnp.int32)[lax.axis_index(axis)]

    def member_at(distance):
        return jnp.asarray(order, jnp.int32)[lax.rem(place + distance + count, count)]

    return member_at


def uses_ring(axis):
    count = lax.axis_size(axis)
    return count % 2 == 0 and 4 <= count <= RING_LIMIT


def gather_rows(block, axis):
    count = lax.axis_size(axis)
    if not uses_ring(axis):
        return lax.all_gather(block, axis, axis=0, tiled=True)
    right, left = ring_links(count)
    member_at = ring_place(axis)
    rows, half = block.shape[0], block.shape[0] // 2
    whole = jnp.zeros((count * rows,) + block.shape[1:], block.dtype)
    columns = (0,) * (block.ndim - 1)

    def put(whole, piece, distance, shift=0):
        return lax.dynamic_update_slice(
            whole, piece, (member_at(distance) * rows + shift,) + columns
        )

    whole = put(whole, block, 0)
    going_right = going_left = block
    for hop in range(1, count // 2):
        going_right = lax.ppermute(going_right, axis, right)
        going_left = lax.ppermute(going_left, axis, left)
        whole = put(whole, going_right, -hop)
        whole = put(whole, going_left, hop)
    first = lax.ppermute(going_right[:half], axis, right)
    second = lax.ppermute(going_left[half:], axis, left)
    whole = put(whole, first, count // 2)
    return put(whole, second, count // 2, half)


def scatter_rows(terms, axis):
    count = lax.axis_size(axis)
    if not uses_ring(axis):
        return lax.psum_scatter(terms.astype(f32), axis, scatter_dimension=0, tiled=True)
    right, left = ring_links(count)
    member_at = ring_place(axis)
    rows = terms.shape[0] // count
    half = rows // 2

    def term(distance):
        return lax.dynamic_slice_in_dim(terms, member_at(distance) * rows, rows, 0).astype(f32)

    far = term(count // 2).astype(bf16)
    going_right = lax.ppermute(far[:half], axis, right)
    going_left = lax.ppermute(far[half:], axis, left)
    for distance in range(count // 2 - 1, 0, -1):
        to_right, to_left = term(distance), term(-distance)
        if distance == count // 2 - 1:
            to_right = jnp.concatenate([to_right[:half] + going_right, to_right[half:]])
            to_left = jnp.concatenate([to_left[:half], to_left[half:] + going_left])
        else:
            to_right, to_left = to_right + going_right, to_left + going_left
        going_right = lax.ppermute(to_right.astype(bf16), axis, right)
        going_left = lax.ppermute(to_left.astype(bf16), axis, left)
    return term(0) + going_right + going_left


def swapped(value, axis, flip):
    count = lax.axis_size(axis)
    return lax.ppermute(value, axis, [(i, i ^ flip) for i in range(count)])


def summed(value, axis):
    count = lax.axis_size(axis)
    if count <= 8:
        parts = [value] + [swapped(value, axis, flip) for flip in range(1, count)]
        while len(parts) > 1:
            parts = [parts[i] + parts[i + 1] for i in range(0, len(parts), 2)]
        return parts[0]
    return summed_in_steps(value, axis)


def summed_in_steps(value, axis):
    flip = 1
    while flip < lax.axis_size(axis):
        value = value + swapped(value, axis, flip)
        flip *= 2
    return value


def placed(parts, axis):
    count = lax.axis_size(axis)
    me = lax.axis_index(axis)
    whole = jnp.zeros((count,) + parts[0].shape, parts[0].dtype)
    for flip, part in enumerate(parts):
        whole = lax.dynamic_update_index_in_dim(whole, part, lax.bitwise_xor(me, flip), 0)
    return whole


def spread(value, axis):
    count = lax.axis_size(axis)
    parts = [value]
    flip = count // 2
    known = {0: value}
    while flip:
        fresh = {k ^ flip: swapped(v, axis, flip) for k, v in known.items()}
        known.update(fresh)
        flip //= 2
    parts = [known[k] for k in range(count)]
    return placed(parts, axis)


def spread_small(value, axis):
    count = lax.axis_size(axis)
    return placed([value] + [swapped(value, axis, k) for k in range(1, count)], axis)


def exchanged(blocks, axis):
    count = lax.axis_size(axis)
    me = lax.axis_index(axis)

    def block_for(flip):
        return lax.dynamic_index_in_dim(blocks, lax.bitwise_xor(me, flip), 0, False)

    return placed(
        [block_for(0)] + [swapped(block_for(k), axis, k) for k in range(1, count)], axis
    )


def halved(blocks, axis):
    count = lax.axis_size(axis)
    me = lax.axis_index(axis)
    held = {
        k: lax.dynamic_index_in_dim(blocks, lax.bitwise_xor(me, k), 0, False)
        for k in range(count)
    }
    flip = 1
    while flip < count:
        kept = {}
        for k in sorted(held):
            if k & flip:
                continue
            arrived = swapped(held[k ^ flip].astype(bf16), axis, flip)
            kept[k] = held[k].astype(f32) + arrived
        held = kept
        flip *= 2
    return held[0]


def dot_rows(a, b):
    return lax.dot_general(a, b, (((1,), (0,)), ((), ())), preferred_element_type=f32)


def dot_lanes(a, b):
    return lax.dot_general(a, b, (((1,), (1,)), ((), ())), preferred_element_type=f32)


def head_lanes(columns, base):
    rows = columns.shape[0]
    full = [
        jnp.broadcast_to(columns[:, base + j : base + j + 1], (rows, PAIR)) for j in range(GROUP)
    ]
    first = lax.broadcasted_iota(jnp.int32, (rows, PAIR), 1) < HEAD_DIM
    lanes = jnp.concatenate(
        [jnp.where(first, full[i], full[i + 1]) for i in range(0, GROUP, 2)], axis=1
    )
    return full, lanes


def stacked_heads(values, block_mask):
    return jnp.concatenate([values] * GROUP, axis=0) * block_mask


def filtered(window, taps, bias, rows):
    pre = bias + taps[CONV - 1 : CONV] * window[8 : 8 + rows]
    for k in range(CONV - 1):
        pre = pre + taps[k : k + 1] * window[5 + k : 5 + k + rows]
    return pre


def scan_forward_kernel(
    x_ref, taps_ref, bias_ref, mask_ref, skip_ref, column_ref, row_ref, key_ref, query_ref,
    key_t_ref, block_ref, y_ref, states_ref, padded, state,
):
    length = x_ref.shape[0]
    rows = SPAN
    mask = mask_ref[...]
    padded[0:8, :] = jnp.zeros((8, LANES), f32)
    padded[8 : 8 + length, :] = x_ref[...] * mask
    state[...] = jnp.zeros_like(state)
    taps, bias, skip = taps_ref[...], bias_ref[...], skip_ref[...]
    causal = lax.broadcasted_iota(jnp.int32, (rows, rows), 0) >= lax.broadcasted_iota(
        jnp.int32, (rows, rows), 1
    )

    def chunk(c, carry):
        start = pl.multiple_of(c * rows, rows)
        here = pl.ds(start, rows)
        pre = filtered(padded[pl.ds(start, rows + 8), :], taps, bias, rows)
        values = pre * jax.nn.sigmoid(pre) * mask
        columns = column_ref[here, :]
        log_full, log_lanes = head_lanes(columns, 0)
        step_lanes = head_lanes(columns, GROUP)[1]
        weighted = step_lanes * values
        weighted_low = weighted.astype(bf16)
        keys, queries, keys_t = key_ref[here, :], query_ref[here, :], key_t_ref[:, here]
        inner = dot_lanes(queries, keys)
        mixing = jnp.concatenate(
            [
                (
                    jnp.where(causal, jnp.exp(log_full[j] - row_ref[j : j + 1, here]), 0.0)
                    * inner
                ).astype(bf16)
                for j in range(GROUP)
            ],
            axis=1,
        )
        state_now = state[...]
        state_low = state_now.astype(bf16)
        states_ref[pl.ds(c, 1)] = state_low[None]
        y = dot_rows(mixing, stacked_heads(weighted_low, block_ref[...]))
        y = y + jnp.exp(log_lanes) * dot_rows(queries, state_low)
        y_ref[here, :] = y + skip * values
        log_last = log_lanes[rows - 1 : rows, :]
        tail = (weighted * jnp.exp(log_last - log_lanes)).astype(bf16)
        state[...] = jnp.exp(log_last) * state_now + dot_rows(keys_t, tail)
        return carry

    lax.fori_loop(0, length // rows, chunk, 0)


def scan_backward_kernel(
    x_ref, taps_ref, bias_ref, mask_ref, skip_ref, column_ref, row_ref, key_ref, query_ref,
    query_t_ref, block_ref, pick_ref, grad_ref, states_ref,
    x_grad_ref, key_grad_ref, query_grad_ref, sums_ref, rest_ref, channel_ref,
    padded, following, state_back, inner_grad,
):
    length = x_ref.shape[0]
    rows = SPAN
    chunks = length // rows
    group = pl.program_id(0)
    mask = mask_ref[...]
    padded[0:8, :] = jnp.zeros((8, LANES), f32)
    padded[8 : 8 + length, :] = x_ref[...] * mask
    following[...] = jnp.zeros_like(following)
    state_back[...] = jnp.zeros_like(state_back)
    channel_ref[...] = jnp.zeros_like(channel_ref)

    @pl.when(group == 0)
    def _():
        key_grad_ref[...] = jnp.zeros_like(key_grad_ref)
        query_grad_ref[...] = jnp.zeros_like(query_grad_ref)
        inner_grad[...] = jnp.zeros_like(inner_grad)

    taps, bias, skip = taps_ref[...], bias_ref[...], skip_ref[...]
    row_at = lax.broadcasted_iota(jnp.int32, (rows, rows), 0)
    lane_at = lax.broadcasted_iota(jnp.int32, (rows, rows), 1)
    causal, causal_t = row_at >= lane_at, lane_at >= row_at

    def chunk(lap, carry):
        c = chunks - 1 - lap
        start = pl.multiple_of(c * rows, rows)
        here = pl.ds(start, rows)
        window = padded[pl.ds(start, rows + 8), :]
        pre = filtered(window, taps, bias, rows)
        gate = jax.nn.sigmoid(pre)
        values = pre * gate * mask
        columns = column_ref[here, :]
        log_full, log_lanes = head_lanes(columns, 0)
        step_lanes = head_lanes(columns, GROUP)[1]
        weighted = step_lanes * values
        weighted_low = weighted.astype(bf16)
        keys, queries, queries_t = key_ref[here, :], query_ref[here, :], query_t_ref[:, here]
        grad_low = grad_ref[here, :]
        grad = grad_low.astype(f32)
        inner, inner_t = dot_lanes(queries, keys), dot_lanes(keys, queries)
        blocks = block_ref[...]
        weighted_blocks = stacked_heads(weighted_low, blocks)
        grad_blocks = stacked_heads(grad_low, blocks)
        mixing_grad = dot_lanes(grad_low, weighted_blocks)
        mixing, mixing_t, inner_sum = [], [], jnp.zeros((rows, rows), f32)
        for j in range(GROUP):
            log_row = row_ref[j : j + 1, here]
            decay = jnp.where(causal, jnp.exp(log_full[j] - log_row), 0.0)
            decay_t = jnp.where(causal_t, jnp.exp(log_row - log_full[j]), 0.0)
            mixing.append((decay * inner).astype(bf16))
            mixing_t.append((decay_t * inner_t).astype(bf16))
            inner_sum = inner_sum + decay * mixing_grad[:, j * rows : (j + 1) * rows]
        inner_grad[pl.ds(c, 1)] = inner_grad[pl.ds(c, 1)] + inner_sum[None]
        y = dot_rows(jnp.concatenate(mixing, axis=1), weighted_blocks)
        state_low = states_ref[pl.ds(c, 1)][0]
        entry = jnp.exp(log_lanes)
        y = y + entry * dot_rows(queries, state_low)
        inside = dot_rows(jnp.concatenate(mixing_t, axis=1), grad_blocks)
        back = state_back[...]
        back_low = back.astype(bf16)
        log_last = log_lanes[rows - 1 : rows, :]
        tail = jnp.exp(log_last - log_lanes)
        outside = tail * dot_rows(keys, back_low)
        entry_grad = (grad * entry).astype(bf16)
        tail_low = (weighted * tail).astype(bf16)
        query_grad_ref[here, :] = query_grad_ref[here, :] + dot_lanes(entry_grad, state_low)
        key_grad_ref[here, :] = key_grad_ref[here, :] + dot_lanes(tail_low, back_low)
        last = jnp.exp(log_last)
        rest_ref[pl.ds(c, 1)] = (
            last * jnp.sum(state_low.astype(f32) * back, axis=0, keepdims=True)
        )[None]
        state_back[...] = last * back + dot_rows(queries_t, entry_grad)
        weighted_grad = inside + outside
        first = grad * y - weighted_low.astype(f32) * inside
        first_high = first.astype(bf16)
        first_rest = (first - first_high.astype(f32)).astype(bf16)
        sums_ref[here, :] = (
            dot_rows(first_high, pick_ref[0])
            + dot_rows(first_rest, pick_ref[0])
            + dot_rows((weighted * outside).astype(bf16), pick_ref[1])
            + dot_rows((values * weighted_grad).astype(bf16), pick_ref[2])
        )
        values_grad = step_lanes * weighted_grad + skip * grad
        pre_grad = values_grad * mask * (gate * (1.0 + pre * (1.0 - gate)))
        channel_ref[CONV : CONV + 1, :] += jnp.sum(pre_grad, axis=0, keepdims=True)
        channel_ref[CONV + 1 : CONV + 2, :] += jnp.sum(grad * values, axis=0, keepdims=True)
        for k in range(CONV):
            channel_ref[k : k + 1, :] += jnp.sum(
                pre_grad * window[5 + k : 5 + k + rows], axis=0, keepdims=True
            )
        ahead = jnp.concatenate([pre_grad, following[...]], axis=0)
        following[...] = pre_grad[0:8]
        x_grad = taps[CONV - 1 : CONV] * ahead[0:rows]
        for k in range(CONV - 1):
            x_grad = x_grad + taps[k : k + 1] * ahead[CONV - 1 - k : CONV - 1 - k + rows]
        x_grad_ref[here, :] = (x_grad * mask).astype(bf16)
        return carry

    lax.fori_loop(0, chunks, chunk, 0)

    @pl.when(group == pl.num_programs(0) - 1)
    def _():
        def finish(c, carry):
            here = pl.ds(pl.multiple_of(c * rows, rows), rows)
            inner_low = inner_grad[pl.ds(c, 1)][0].astype(bf16)
            query_grad_ref[here, :] = query_grad_ref[here, :] + dot_rows(
                inner_low, key_ref[here, :]
            )
            key_grad_ref[here, :] = key_grad_ref[here, :] + lax.dot_general(
                inner_low, query_ref[here, :], (((0,), (0,)), ((), ())),
                preferred_element_type=f32,
            )
            return carry

        lax.fori_loop(0, chunks, finish, 0)


def block_mask():
    row = jnp.arange(GROUP * SPAN)[:, None] // SPAN
    lane = jnp.arange(LANES)[None, :] // HEAD_DIM
    return (row == lane).astype(bf16)


def pick_masks():
    lane = jnp.arange(LANES)[:, None] // HEAD_DIM
    target = jnp.arange(PAIR)[None, :]
    return jnp.stack([(target == lane + GROUP * kind).astype(bf16) for kind in range(3)])


def whole_spec():
    return pl.BlockSpec(memory_space=pltpu.VMEM)


def lane_spec(rows):
    return pl.BlockSpec((rows, LANES), lambda g: (0, g))


def head_specs(length):
    return [
        lane_spec(length),
        lane_spec(CONV),
        lane_spec(1),
        lane_spec(1),
        lane_spec(1),
        pl.BlockSpec((length, PAIR), lambda g: (0, g)),
        pl.BlockSpec((8, length), lambda g: (g, 0)),
        whole_spec(),
        whole_spec(),
        whole_spec(),
        whole_spec(),
    ]


def scan_forward(x, taps, bias, mask, skip, columns, rows, keys, queries, keys_t):
    length, width = x.shape
    chunks = length // SPAN
    return pl.pallas_call(
        scan_forward_kernel,
        grid=(width // LANES,),
        in_specs=head_specs(length),
        out_specs=[
            lane_spec(length),
            pl.BlockSpec((chunks, STATE, LANES), lambda g: (0, 0, g)),
        ],
        out_shape=[
            jax.ShapeDtypeStruct((length, width), f32),
            jax.ShapeDtypeStruct((chunks, STATE, width), bf16),
        ],
        scratch_shapes=[pltpu.VMEM((length + 8, LANES), f32), pltpu.VMEM((STATE, LANES), f32)],
        compiler_params=pltpu.CompilerParams(vmem_limit_bytes=VMEM_BYTES),
        cost_estimate=pl.CostEstimate(
            flops=10_000_000_000, bytes_accessed=12_000_000, transcendentals=4_000_000
        ),
        name="scan_forward",
    )(x, taps, bias, mask, skip, columns, rows, keys, queries, keys_t, block_mask())


def scan_backward(
    x, taps, bias, mask, skip, columns, rows, keys, queries, queries_t, grad, states
):
    length, width = x.shape
    chunks = length // SPAN
    groups = width // LANES
    same = lambda g: (0, 0)
    return pl.pallas_call(
        scan_backward_kernel,
        grid=(groups,),
        in_specs=head_specs(length)
        + [
            whole_spec(),
            lane_spec(length),
            pl.BlockSpec((chunks, STATE, LANES), lambda g: (0, 0, g)),
        ],
        out_specs=[
            lane_spec(length),
            pl.BlockSpec((length, STATE), same),
            pl.BlockSpec((length, STATE), same),
            pl.BlockSpec((length, PAIR), lambda g: (0, g)),
            pl.BlockSpec((chunks, 1, LANES), lambda g: (0, 0, g)),
            lane_spec(8),
        ],
        out_shape=[
            jax.ShapeDtypeStruct((length, width), bf16),
            jax.ShapeDtypeStruct((length, STATE), f32),
            jax.ShapeDtypeStruct((length, STATE), f32),
            jax.ShapeDtypeStruct((length, PAIR * groups), f32),
            jax.ShapeDtypeStruct((chunks, 1, width), f32),
            jax.ShapeDtypeStruct((8, width), f32),
        ],
        scratch_shapes=[
            pltpu.VMEM((length + 8, LANES), f32),
            pltpu.VMEM((8, LANES), f32),
            pltpu.VMEM((STATE, LANES), f32),
            pltpu.VMEM((chunks, SPAN, SPAN), f32),
        ],
        compiler_params=pltpu.CompilerParams(vmem_limit_bytes=VMEM_BYTES),
        cost_estimate=pl.CostEstimate(
            flops=30_000_000_000, bytes_accessed=16_000_000, transcendentals=8_000_000
        ),
        name="scan_backward",
    )(
        x, taps, bias, mask, skip, columns, rows, keys, queries, queries_t, block_mask(),
        pick_masks(), grad, states,
    )


def gate_kernel(
    normed_ref, weight_ref, cotangent_ref, out_ref, y_ref, gain_ref, mask_ref,
    gate_part_ref, gated_grad_ref, stats_ref,
):
    gate_part = dot_rows(normed_ref[...], weight_ref[...]) * mask_ref[...]
    gated_grad = dot_lanes(cotangent_ref[...], out_ref[...])
    gate_part_ref[...] = gate_part
    gated_grad_ref[...] = gated_grad
    gated = y_ref[...] * (gate_part * jax.nn.sigmoid(gate_part))
    squares = jnp.sum(gated * gated, axis=1, keepdims=True)
    products = jnp.sum(gated * gated_grad * gain_ref[...], axis=1, keepdims=True)
    lane = lax.broadcasted_iota(jnp.int32, stats_ref.shape, 1)
    stats_ref[...] = jnp.where(lane == 0, squares, products)


def gate_forward(normed, weight, cotangent, out_weight, y, gain, mask):
    length, width = y.shape
    rows = lambda lanes: pl.BlockSpec((ROW_TILE, lanes), lambda i: (i, 0))
    return pl.pallas_call(
        gate_kernel,
        grid=(length // ROW_TILE,),
        in_specs=[
            rows(D), whole_spec(), rows(D), whole_spec(), rows(width), whole_spec(), whole_spec(),
        ],
        out_specs=[rows(width), rows(width), rows(PAIR)],
        out_shape=[
            jax.ShapeDtypeStruct((length, width), f32),
            jax.ShapeDtypeStruct((length, width), f32),
            jax.ShapeDtypeStruct((length, PAIR), f32),
        ],
        compiler_params=pltpu.CompilerParams(vmem_limit_bytes=VMEM_BYTES),
        cost_estimate=pl.CostEstimate(
            flops=9_000_000_000, bytes_accessed=28_000_000, transcendentals=1_000_000
        ),
        name="gate_forward",
    )(normed, weight, cotangent, out_weight, y, gain, mask)


def norm_back_kernel(
    y_ref, gate_part_ref, gated_grad_ref, scale_ref, gain_ref, mask_ref,
    gated_ref, y_grad_ref, gate_grad_ref, gain_grad_ref,
):
    @pl.when(pl.program_id(0) == 0)
    def _():
        gain_grad_ref[...] = jnp.zeros_like(gain_grad_ref)

    y, gate_part, gated_grad = y_ref[...], gate_part_ref[...], gated_grad_ref[...]
    inverse, pull = scale_ref[:, 0:1], scale_ref[:, 1:2]
    gate = jax.nn.sigmoid(gate_part)
    silu = gate_part * gate
    gated = y * silu
    scaled = gated * inverse
    gain = gain_ref[...]
    gated_ref[...] = (scaled * gain).astype(bf16)
    gain_grad_ref[0:1, :] += jnp.sum(gated_grad * scaled, axis=0, keepdims=True)
    back = inverse * (gated_grad * gain) - gated * pull
    y_grad_ref[...] = (back * silu).astype(bf16)
    gate_grad_ref[...] = (
        back * y * (gate * (1.0 + gate_part * (1.0 - gate))) * mask_ref[...]
    ).astype(bf16)


def norm_back(y, gate_part, gated_grad, scales, gain, mask):
    length, width = y.shape
    rows = lambda lanes: pl.BlockSpec((ROW_TILE, lanes), lambda i: (i, 0))
    return pl.pallas_call(
        norm_back_kernel,
        grid=(length // ROW_TILE,),
        in_specs=[rows(width), rows(width), rows(width), rows(2), whole_spec(), whole_spec()],
        out_specs=[
            rows(width), rows(width), rows(width), pl.BlockSpec((8, width), lambda i: (0, 0)),
        ],
        out_shape=[
            jax.ShapeDtypeStruct((length, width), bf16),
            jax.ShapeDtypeStruct((length, width), bf16),
            jax.ShapeDtypeStruct((length, width), bf16),
            jax.ShapeDtypeStruct((8, width), f32),
        ],
        compiler_params=pltpu.CompilerParams(vmem_limit_bytes=VMEM_BYTES),
        cost_estimate=pl.CostEstimate(
            flops=30_000_000, bytes_accessed=18_000_000, transcendentals=1_000_000
        ),
        name="norm_back",
    )(y, gate_part, gated_grad, scales, gain, mask)


def unpack(vectors):
    offset = D + INNER
    taps_end = offset + CONV * XBC
    heads_start = taps_end + XBC
    norm_gain = vectors[:D]
    gate_gain = vectors[D:offset]
    filter_taps = vectors[offset:taps_end].reshape(CONV, XBC)
    filter_bias = vectors[taps_end:heads_start]
    step_bias = vectors[heads_start : heads_start + HEADS]
    decay_log = vectors[heads_start + HEADS : heads_start + 2 * HEADS]
    skip_gain = vectors[heads_start + 2 * HEADS : heads_start + 3 * HEADS]
    return (norm_gain, gate_gain, filter_taps, filter_bias, step_bias, decay_log, skip_gain)


def adamw(weight, moment, square, gradient, step_rate):
    moment_new = beta_first * moment + (1.0 - beta_first) * gradient
    square_new = beta_second * square + (1.0 - beta_second) * gradient * gradient
    moment_hat = moment_new / (1.0 - beta_first**STEP)
    square_hat = square_new / (1.0 - beta_second**STEP)
    weight_new = weight - step_rate * (
        moment_hat / (jnp.sqrt(square_hat) + adam_eps) + weight_decay * weight
    )
    return (moment_new, square_new, weight_new)


def on_device(
    tokens,
    widths,
    cotangent,
    in_weight,
    in_first,
    in_second,
    out_weight,
    out_first,
    out_second,
    vectors,
    vector_first,
    vector_second,
):
    fsdp = lax.axis_size("fsdp")
    me = lax.axis_index("fsdp")
    heads = HEADS // fsdp
    inner = INNER // fsdp
    shared = 2 * STATE // fsdp
    pairs = HEADS // 2 // fsdp
    rows_in, rows_out = in_weight.shape[0], out_weight.shape[0]
    length = tokens.shape[0] * fsdp
    chunks = length // SPAN
    out_aligned = rows_out == PAIR

    def own_channels(v):
        lead = v.shape[:-1]
        cut = v.reshape(lead + (pairs, fsdp, PAIR))
        return lax.dynamic_index_in_dim(cut, me, len(lead) + 1, False).reshape(lead + (inner,))

    def own_heads(v):
        return lax.dynamic_index_in_dim(v.reshape(pairs, fsdp, 2), me, 1, False).reshape(heads)

    def own_shared(v):
        return lax.dynamic_slice_in_dim(v, me * shared, shared, v.ndim - 1)

    norm_gain, gate_gain, filter_taps, filter_bias, step_bias, decay_log, skip_gain = unpack(
        vectors
    )
    gain_own = own_channels(gate_gain)[None]
    taps_own = own_channels(filter_taps[:, :INNER])
    bias_own = own_channels(filter_bias[:INNER])[None]
    taps_shared = own_shared(filter_taps[:, INNER:])
    bias_shared = own_shared(filter_bias[INNER:])
    step_bias_own, decay_own = own_heads(step_bias), -jnp.exp(own_heads(decay_log))
    skip_own = jnp.repeat(own_heads(skip_gain), HEAD_DIM)[None]

    width_index = widths[0]
    active = HEADS // 8 * jnp.left_shift(jnp.int32(1), width_index)
    head_mask = (jnp.arange(heads, dtype=jnp.int32) < active // fsdp).astype(f32)
    mask = jnp.repeat(head_mask, HEAD_DIM)[None]
    channel_count = (active * HEAD_DIM).astype(f32)

    in_low = in_weight.astype(bf16)
    shared_cut = jnp.concatenate(
        [
            in_low[:, 2 * INNER : 2 * INNER + 2 * STATE]
            .reshape(rows_in, fsdp, shared)
            .transpose(1, 0, 2),
            in_low[:, 2 * INNER + 2 * STATE :]
            .reshape(rows_in, pairs, fsdp, 2)
            .transpose(2, 0, 1, 3)
            .reshape(fsdp, rows_in, heads),
        ],
        axis=2,
    )

    def channel_cut(part):
        return (
            part.reshape(rows_in, pairs, fsdp, PAIR)
            .transpose(2, 0, 1, 3)
            .reshape(fsdp, rows_in, inner)
        )

    def gathered(cut):
        block = exchanged(cut, "fsdp")
        return gather_rows(block.reshape(fsdp * rows_in, cut.shape[2]), "dp")

    weight_shared = gathered(shared_cut)
    weight_x = gathered(channel_cut(in_low[:, INNER : 2 * INNER]))
    weight_gate = gathered(channel_cut(in_low[:, :INNER]))
    out_low = out_weight.astype(bf16)
    if out_aligned:
        weight_out = gather_rows(out_low, "dp")
    else:
        weight_out = lax.dynamic_index_in_dim(
            lax.all_gather(out_low, ("dp", "fsdp"), axis=0, tiled=True).reshape(
                pairs, fsdp, PAIR, D
            ),
            me,
            1,
            False,
        ).reshape(inner, D)

    inputs = tokens.astype(f32)
    inverse_in = lax.rsqrt(jnp.mean(inputs * inputs, axis=-1, keepdims=True) + norm_eps)
    normed_own = (inputs * inverse_in * norm_gain[None, :]).astype(bf16)
    normed = spread(normed_own, "fsdp").reshape(length, D)
    cotangents = spread(cotangent, "fsdp").reshape(length, D)

    small = lax.dot_general(
        weight_shared, normed, (((0,), (1,)), ((), ())), preferred_element_type=f32
    )
    shared_part = small[:shared]
    step_raw = small[shared:] * head_mask[:, None]
    shared_padded = jnp.pad(shared_part, ((0, 0), (CONV - 1, 0)))
    shared_pre = bias_shared[:, None] + sum(
        taps_shared[k][:, None] * shared_padded[:, k : k + length] for k in range(CONV)
    )
    shared_gate = jax.nn.sigmoid(shared_pre)
    shared_all = spread_small((shared_pre * shared_gate).astype(bf16), "fsdp").reshape(
        2 * STATE, length
    )
    keys_t, queries_t = shared_all[:STATE], shared_all[STATE:]
    keys, queries = keys_t.T, queries_t.T
    step_logits = step_raw + step_bias_own[:, None]
    step_sizes = jax.nn.softplus(step_logits)
    upto = (jnp.arange(SPAN)[:, None] <= jnp.arange(SPAN)[None, :]).astype(f32)
    log_sums = jnp.dot(
        (step_sizes * decay_own[:, None]).reshape(heads, chunks, SPAN), upto, precision=highest
    ).reshape(heads, length)
    groups = heads // GROUP
    head_rows = jnp.concatenate(
        [log_sums.reshape(groups, GROUP, length), step_sizes.reshape(groups, GROUP, length)],
        axis=1,
    )
    head_columns = jnp.pad(
        head_rows.transpose(2, 0, 1), ((0, 0), (0, 0), (0, PAIR - 2 * GROUP))
    ).reshape(length, groups * PAIR)
    head_rows = head_rows.reshape(groups * 2 * GROUP, length)

    x_part = jnp.dot(normed, weight_x, preferred_element_type=f32)
    y, states = scan_forward(
        x_part, taps_own, bias_own, mask, skip_own, head_columns, head_rows, keys, queries, keys_t
    )
    gate_part, gated_grad, stats = gate_forward(
        normed, weight_gate, cotangents, weight_out, y, gain_own, mask
    )
    stats = summed(stats[:, :2].T, "fsdp")
    inverse_out = lax.rsqrt(stats[0] / channel_count + norm_eps)
    pull = inverse_out**3 / channel_count * stats[1]
    gated_low, y_grad, gate_grad, gain_grad = norm_back(
        y, gate_part, gated_grad, jnp.stack([inverse_out, pull], axis=1), gain_own, mask
    )

    out_term = lax.dot_general(
        gated_low, cotangents, (((0,), (0,)), ((), ())), preferred_element_type=f32
    ).astype(bf16)
    if out_aligned:
        out_raw = scatter_rows(out_term, "dp")
    else:
        whole_term = jnp.zeros((pairs, fsdp, PAIR, D), f32)
        whole_term = lax.dynamic_update_slice(
            whole_term, out_term.astype(f32).reshape(pairs, 1, PAIR, D), (0, me, 0, 0)
        )
        out_raw = lax.psum_scatter(
            whole_term.reshape(INNER, D), ("dp", "fsdp"), scatter_dimension=0, tiled=True
        )
    added = halved(
        jnp.dot(gated_low, weight_out, preferred_element_type=f32)
        .astype(bf16)
        .reshape(fsdp, tokens.shape[0], D),
        "fsdp",
    )
    layer_out = (inputs + added).astype(bf16)

    def in_term(grad):
        return lax.dot_general(
            normed, grad, (((0,), (0,)), ((), ())), preferred_element_type=f32
        ).astype(bf16)

    gate_raw = scatter_rows(in_term(gate_grad), "dp")

    x_grad, key_grad, query_grad, sums, rest, channel_grad = scan_backward(
        x_part, taps_own, bias_own, mask, skip_own, head_columns, head_rows, keys, queries,
        queries_t, y_grad, states,
    )
    x_raw = scatter_rows(in_term(x_grad), "dp")

    shared_grads = jnp.concatenate([key_grad, query_grad], axis=1).T.astype(bf16)
    arrived = exchanged(shared_grads.reshape(fsdp, shared, length), "fsdp").astype(f32)
    activated_grad = jnp.sum(arrived, axis=0)
    shared_pre_grad = activated_grad * shared_gate * (1.0 + shared_pre * (1.0 - shared_gate))
    shared_ahead = jnp.pad(shared_pre_grad, ((0, 0), (0, CONV - 1)))
    shared_grad = sum(
        taps_shared[k][:, None] * shared_ahead[:, CONV - 1 - k : CONV - 1 - k + length]
        for k in range(CONV)
    )
    taps_shared_grad = jnp.stack(
        [
            jnp.sum(shared_pre_grad * shared_padded[:, k : k + length], axis=1)
            for k in range(CONV)
        ]
    )
    bias_shared_grad = jnp.sum(shared_pre_grad, axis=1)

    sums = (
        sums.reshape(length, groups, PAIR)[:, :, : 3 * GROUP]
        .reshape(length, groups, 3, GROUP)
        .transpose(2, 1, 3, 0)
        .reshape(3, heads, chunks, SPAN)
    )
    before = (jnp.arange(SPAN)[:, None] < jnp.arange(SPAN)[None, :]).astype(f32)
    rest = rest.reshape(chunks, heads, HEAD_DIM).sum(axis=2).T
    log_grad = (
        jnp.dot(sums[0], 1.0 - before, precision=highest)
        + jnp.dot(sums[1], before, precision=highest)
        + rest[:, :, None]
    ).reshape(heads, length)
    step_grad = decay_own[:, None] * log_grad + sums[2].reshape(heads, length)
    raw_grad = step_grad * jax.nn.sigmoid(step_logits)
    step_bias_grad = jnp.sum(raw_grad, axis=1)
    decay_grad = jnp.sum(step_sizes * log_grad, axis=1) * decay_own
    small_grad = jnp.concatenate([shared_grad, raw_grad * head_mask[:, None]], axis=0).astype(bf16)
    small_raw = scatter_rows(
        lax.dot_general(
            normed, small_grad, (((0,), (1,)), ((), ())), preferred_element_type=f32
        ).astype(bf16),
        "dp",
    )

    def in_back(grad, weight, grad_dim=1):
        return lax.dot_general(
            grad, weight, (((grad_dim,), (1,)), ((), ())), preferred_element_type=f32
        )

    normed_grad = halved(
        (
            in_back(gate_grad, weight_gate)
            + in_back(x_grad, weight_x)
            + in_back(small_grad, weight_shared, 0)
        )
        .astype(bf16)
        .reshape(fsdp, tokens.shape[0], D),
        "fsdp",
    )
    pulled = normed_grad * norm_gain[None, :]
    input_grad = inverse_in * pulled - inputs * (
        inverse_in**3 * jnp.mean(pulled * inputs, axis=-1, keepdims=True)
    )
    token_grad = (cotangent.astype(f32) + input_grad).astype(bf16)
    norm_gain_grad = jnp.sum(normed_grad * inputs * inverse_in, axis=0)

    skip_grad = channel_grad[CONV + 1].reshape(heads, HEAD_DIM).sum(axis=1)
    head_row = jnp.concatenate(
        [
            step_bias_grad, decay_grad, skip_grad, bias_shared_grad, taps_shared_grad.reshape(-1),
        ]
    )
    head_row = jnp.pad(head_row, (0, inner - head_row.shape[0]))
    vector_rows = jnp.concatenate(
        [
            gain_grad[0:1],
            channel_grad[: CONV + 1],
            head_row[None],
            norm_gain_grad.reshape(-1, inner),
        ]
    )
    vector_rows = spread_small(summed_in_steps(vector_rows, "dp"), "fsdp")

    def joined_channels(v):
        return v.reshape(fsdp, pairs, PAIR).transpose(1, 0, 2).reshape(INNER)

    def joined_heads(v):
        return v.reshape(fsdp, pairs, 2).transpose(1, 0, 2).reshape(HEADS)

    head_all = vector_rows[:, CONV + 2]
    taps_shared_all = (
        head_all[:, 3 * heads + shared : 3 * heads + 5 * shared]
        .reshape(fsdp, CONV, shared)
        .transpose(1, 0, 2)
        .reshape(CONV, 2 * STATE)
    )
    taps_all = [
        jnp.concatenate([joined_channels(vector_rows[:, 1 + k]), taps_shared_all[k]])
        for k in range(CONV)
    ]
    bias_all = jnp.concatenate(
        [
            joined_channels(vector_rows[:, CONV + 1]),
            head_all[:, 3 * heads : 3 * heads + shared].reshape(-1),
        ]
    )
    norm_rows = vector_rows[:, CONV + 3 :].reshape(fsdp, D)
    norm_all = norm_rows[0]
    for member in range(1, fsdp):
        norm_all = norm_all + norm_rows[member]
    vector_raw = jnp.concatenate(
        [norm_all, joined_channels(vector_rows[:, 0])]
        + taps_all
        + [bias_all]
        + [joined_heads(head_all[:, i * heads : (i + 1) * heads]) for i in range(3)]
    )

    squares = (
        jnp.sum(gate_raw * gate_raw)
        + jnp.sum(x_raw * x_raw)
        + jnp.sum(small_raw * small_raw)
        + jnp.sum(out_raw * out_raw)
    )
    squares = summed(summed(jnp.broadcast_to(squares, (8, 128)), "fsdp"), "dp")[0, 0]
    grad_norm = jnp.sqrt(squares + jnp.sum(vector_raw * vector_raw))
    factor = jnp.minimum(1.0, clip_norm / (grad_norm + 1e-06))

    def returned(raw):
        return exchanged(raw.astype(bf16).reshape(fsdp, rows_in, raw.shape[1]), "fsdp")

    def joined_columns(part):
        return (
            part.reshape(fsdp, rows_in, pairs, PAIR).transpose(1, 2, 0, 3).reshape(rows_in, INNER)
        )

    small_back = returned(small_raw)
    in_raw = jnp.concatenate(
        [
            joined_columns(returned(gate_raw)),
            joined_columns(returned(x_raw)),
            small_back[:, :, :shared].transpose(1, 0, 2).reshape(rows_in, 2 * STATE),
            small_back[:, :, shared:]
            .reshape(fsdp, rows_in, pairs, 2)
            .transpose(1, 2, 0, 3)
            .reshape(rows_in, HEADS),
        ],
        axis=1,
    ).astype(f32)
    in_grad = in_raw * factor
    out_grad = out_raw * factor
    vector_grad = vector_raw * factor
    in_moment, in_square, in_master = adamw(in_weight, in_first, in_second, in_grad, rate_in_proj)
    out_moment, out_square, out_master = adamw(
        out_weight, out_first, out_second, out_grad, rate_out_proj
    )
    vector_moment, vector_square, vector_master = adamw(
        vectors, vector_first, vector_second, vector_grad, rate_vectors
    )
    return (
        layer_out,
        token_grad,
        in_grad,
        out_grad,
        vector_grad,
        grad_norm,
        in_moment,
        in_square,
        in_master,
        in_master.astype(bf16),
        out_moment,
        out_square,
        out_master,
        out_master.astype(bf16),
        vector_moment,
        vector_square,
        vector_master,
    )


def solution(mesh):
    rows = P(("dp", "fsdp"), None)
    return jax.shard_map(
        on_device,
        mesh=mesh,
        in_specs=(rows, P("dp")) + (rows,) * 7 + (P(),) * 3,
        out_specs=(rows,) * 4 + (P(),) * 2 + (rows,) * 8 + (P(),) * 3,
        check_vma=False,
    )
```

```python
from functools import partial

import jax
import jax.numpy as jnp
from jax import lax
from jax.experimental import pallas as pl
from jax.experimental.pallas import tpu as pltpu
from jax.sharding import PartitionSpec as P

D = 2048
HEADS = 64
HEAD_DIM = 64
STATE = 128
CONV = 4
SPAN = 128
STEP = 10
INNER = 4096
XBC = 4352
PAIR = 2 * HEAD_DIM
GROUP = 4
LANES = GROUP * HEAD_DIM
ROW_TILE = 256
RING_LIMIT = 16

norm_eps = 1e-05
clip_norm = 1.0
beta_first = 0.5
beta_second = 0.5
adam_eps = 1e-08
weight_decay = 0.1
rate_in_proj = 0.03
rate_out_proj = 0.02
rate_vectors = 0.5
highest = lax.Precision.HIGHEST
f32 = jnp.float32
bf16 = jnp.bfloat16
VMEM_BYTES = 60 * 1024 * 1024


def ring_order(count):
    return list(range(0, count, 2)) + list(range(count - 1, 0, -2))


def ring_links(count):
    order = ring_order(count)
    right = [(order[i], order[(i + 1) % count]) for i in range(count)]
    return right, [(b, a) for a, b in right]


def ring_place(axis):
    count = lax.axis_size(axis)
    order = ring_order(count)
    places = [0] * count
    for place, member in enumerate(order):
        places[member] = place
    place = jnp.asarray(places, jnp.int32)[lax.axis_index(axis)]

    def member_at(distance):
        return jnp.asarray(order, jnp.int32)[lax.rem(place + distance + count, count)]

    return member_at


def uses_ring(axis):
    count = lax.axis_size(axis)
    return count % 2 == 0 and 4 <= count <= RING_LIMIT


def gather_rows(block, axis):
    count = lax.axis_size(axis)
    if not uses_ring(axis):
        return lax.all_gather(block, axis, axis=0, tiled=True)
    right, left = ring_links(count)
    member_at = ring_place(axis)
    rows, half = block.shape[0], block.shape[0] // 2
    whole = jnp.zeros((count * rows,) + block.shape[1:], block.dtype)
    columns = (0,) * (block.ndim - 1)

    def put(whole, piece, distance, shift=0):
        return lax.dynamic_update_slice(
            whole, piece, (member_at(distance) * rows + shift,) + columns
        )

    whole = put(whole, block, 0)
    going_right = going_left = block
    for hop in range(1, count // 2):
        going_right = lax.ppermute(going_right, axis, right)
        going_left = lax.ppermute(going_left, axis, left)
        whole = put(whole, going_right, -hop)
        whole = put(whole, going_left, hop)
    first = lax.ppermute(going_right[:half], axis, right)
    second = lax.ppermute(going_left[half:], axis, left)
    whole = put(whole, first, count // 2)
    return put(whole, second, count // 2, half)


def scatter_rows(terms, axis):
    count = lax.axis_size(axis)
    if not uses_ring(axis):
        return lax.psum_scatter(terms.astype(f32), axis, scatter_dimension=0, tiled=True)
    right, left = ring_links(count)
    member_at = ring_place(axis)
    rows = terms.shape[0] // count
    half = rows // 2

    def term(distance):
        return lax.dynamic_slice_in_dim(terms, member_at(distance) * rows, rows, 0).astype(f32)

    far = term(count // 2).astype(bf16)
    going_right = lax.ppermute(far[:half], axis, right)
    going_left = lax.ppermute(far[half:], axis, left)
    for distance in range(count // 2 - 1, 0, -1):
        to_right, to_left = term(distance), term(-distance)
        if distance == count // 2 - 1:
            to_right = jnp.concatenate([to_right[:half] + going_right, to_right[half:]])
            to_left = jnp.concatenate([to_left[:half], to_left[half:] + going_left])
        else:
            to_right, to_left = to_right + going_right, to_left + going_left
        going_right = lax.ppermute(to_right.astype(bf16), axis, right)
        going_left = lax.ppermute(to_left.astype(bf16), axis, left)
    return term(0) + going_right + going_left


def swapped(value, axis, flip):
    count = lax.axis_size(axis)
    return lax.ppermute(value, axis, [(i, i ^ flip) for i in range(count)])


def summed(value, axis):
    count = lax.axis_size(axis)
    if count <= 8:
        parts = [value] + [swapped(value, axis, flip) for flip in range(1, count)]
        while len(parts) > 1:
            parts = [parts[i] + parts[i + 1] for i in range(0, len(parts), 2)]
        return parts[0]
    return summed_in_steps(value, axis)


def summed_in_steps(value, axis):
    flip = 1
    while flip < lax.axis_size(axis):
        value = value + swapped(value, axis, flip)
        flip *= 2
    return value


def placed(parts, axis):
    count = lax.axis_size(axis)
    me = lax.axis_index(axis)
    whole = jnp.zeros((count,) + parts[0].shape, parts[0].dtype)
    for flip, part in enumerate(parts):
        whole = lax.dynamic_update_index_in_dim(whole, part, lax.bitwise_xor(me, flip), 0)
    return whole


def spread(value, axis):
    count = lax.axis_size(axis)
    parts = [value]
    flip = count // 2
    known = {0: value}
    while flip:
        fresh = {k ^ flip: swapped(v, axis, flip) for k, v in known.items()}
        known.update(fresh)
        flip //= 2
    parts = [known[k] for k in range(count)]
    return placed(parts, axis)


def spread_small(value, axis):
    count = lax.axis_size(axis)
    return placed([value] + [swapped(value, axis, k) for k in range(1, count)], axis)


def exchanged(blocks, axis):
    count = lax.axis_size(axis)
    me = lax.axis_index(axis)

    def block_for(flip):
        return lax.dynamic_index_in_dim(blocks, lax.bitwise_xor(me, flip), 0, False)

    return placed(
        [block_for(0)] + [swapped(block_for(k), axis, k) for k in range(1, count)], axis
    )


def halved(blocks, axis):
    count = lax.axis_size(axis)
    me = lax.axis_index(axis)
    held = {
        k: lax.dynamic_index_in_dim(blocks, lax.bitwise_xor(me, k), 0, False)
        for k in range(count)
    }
    flip = 1
    while flip < count:
        kept = {}
        for k in sorted(held):
            if k & flip:
                continue
            arrived = swapped(held[k ^ flip].astype(bf16), axis, flip)
            kept[k] = held[k].astype(f32) + arrived
        held = kept
        flip *= 2
    return held[0]


def dot_rows(a, b):
    return lax.dot_general(a, b, (((1,), (0,)), ((), ())), preferred_element_type=f32)


def dot_lanes(a, b):
    return lax.dot_general(a, b, (((1,), (1,)), ((), ())), preferred_element_type=f32)


def head_lanes(columns, base):
    rows = columns.shape[0]
    full = [
        jnp.broadcast_to(columns[:, base + j : base + j + 1], (rows, PAIR)) for j in range(GROUP)
    ]
    first = lax.broadcasted_iota(jnp.int32, (rows, PAIR), 1) < HEAD_DIM
    lanes = jnp.concatenate(
        [jnp.where(first, full[i], full[i + 1]) for i in range(0, GROUP, 2)], axis=1
    )
    return full, lanes


def stacked_heads(values, block_mask):
    return jnp.concatenate([values] * GROUP, axis=0) * block_mask


def filtered(window, taps, bias, rows):
    pre = bias + taps[CONV - 1 : CONV] * window[8 : 8 + rows]
    for k in range(CONV - 1):
        pre = pre + taps[k : k + 1] * window[5 + k : 5 + k + rows]
    return pre


def scan_forward_kernel(
    x_ref, taps_ref, bias_ref, mask_ref, skip_ref, column_ref, row_ref, key_ref, query_ref,
    key_t_ref, block_ref, y_ref, states_ref, padded, state,
):
    length = x_ref.shape[0]
    rows = SPAN
    mask = mask_ref[...]
    padded[0:8, :] = jnp.zeros((8, LANES), f32)
    padded[8 : 8 + length, :] = x_ref[...] * mask
    state[...] = jnp.zeros_like(state)
    taps, bias, skip = taps_ref[...], bias_ref[...], skip_ref[...]
    causal = lax.broadcasted_iota(jnp.int32, (rows, rows), 0) >= lax.broadcasted_iota(
        jnp.int32, (rows, rows), 1
    )

    def chunk(c, carry):
        start = pl.multiple_of(c * rows, rows)
        here = pl.ds(start, rows)
        pre = filtered(padded[pl.ds(start, rows + 8), :], taps, bias, rows)
        values = pre * jax.nn.sigmoid(pre) * mask
        columns = column_ref[here, :]
        log_full, log_lanes = head_lanes(columns, 0)
        step_lanes = head_lanes(columns, GROUP)[1]
        weighted = step_lanes * values
        weighted_low = weighted.astype(bf16)
        keys, queries, keys_t = key_ref[here, :], query_ref[here, :], key_t_ref[:, here]
        inner = dot_lanes(queries, keys)
        mixing = jnp.concatenate(
            [
                (
                    jnp.where(causal, jnp.exp(log_full[j] - row_ref[j : j + 1, here]), 0.0)
                    * inner
                ).astype(bf16)
                for j in range(GROUP)
            ],
            axis=1,
        )
        state_now = state[...]
        state_low = state_now.astype(bf16)
        states_ref[pl.ds(c, 1)] = state_low[None]
        y = dot_rows(mixing, stacked_heads(weighted_low, block_ref[...]))
        y = y + jnp.exp(log_lanes) * dot_rows(queries, state_low)
        y_ref[here, :] = y + skip * values
        log_last = log_lanes[rows - 1 : rows, :]
        tail = (weighted * jnp.exp(log_last - log_lanes)).astype(bf16)
        state[...] = jnp.exp(log_last) * state_now + dot_rows(keys_t, tail)
        return carry

    lax.fori_loop(0, length // rows, chunk, 0)


def scan_backward_kernel(
    x_ref, taps_ref, bias_ref, mask_ref, skip_ref, column_ref, row_ref, key_ref, query_ref,
    query_t_ref, block_ref, pick_ref, grad_ref, states_ref,
    x_grad_ref, key_grad_ref, query_grad_ref, sums_ref, rest_ref, channel_ref,
    padded, following, state_back, inner_grad,
):
    length = x_ref.shape[0]
    rows = SPAN
    chunks = length // rows
    group = pl.program_id(0)
    mask = mask_ref[...]
    padded[0:8, :] = jnp.zeros((8, LANES), f32)
    padded[8 : 8 + length, :] = x_ref[...] * mask
    following[...] = jnp.zeros_like(following)
    state_back[...] = jnp.zeros_like(state_back)
    channel_ref[...] = jnp.zeros_like(channel_ref)

    @pl.when(group == 0)
    def _():
        key_grad_ref[...] = jnp.zeros_like(key_grad_ref)
        query_grad_ref[...] = jnp.zeros_like(query_grad_ref)
        inner_grad[...] = jnp.zeros_like(inner_grad)

    taps, bias, skip = taps_ref[...], bias_ref[...], skip_ref[...]
    row_at = lax.broadcasted_iota(jnp.int32, (rows, rows), 0)
    lane_at = lax.broadcasted_iota(jnp.int32, (rows, rows), 1)
    causal, causal_t = row_at >= lane_at, lane_at >= row_at

    def chunk(lap, carry):
        c = chunks - 1 - lap
        start = pl.multiple_of(c * rows, rows)
        here = pl.ds(start, rows)
        window = padded[pl.ds(start, rows + 8), :]
        pre = filtered(window, taps, bias, rows)
        gate = jax.nn.sigmoid(pre)
        values = pre * gate * mask
        columns = column_ref[here, :]
        log_full, log_lanes = head_lanes(columns, 0)
        step_lanes = head_lanes(columns, GROUP)[1]
        weighted = step_lanes * values
        weighted_low = weighted.astype(bf16)
        keys, queries, queries_t = key_ref[here, :], query_ref[here, :], query_t_ref[:, here]
        grad_low = grad_ref[here, :]
        grad = grad_low.astype(f32)
        inner, inner_t = dot_lanes(queries, keys), dot_lanes(keys, queries)
        blocks = block_ref[...]
        weighted_blocks = stacked_heads(weighted_low, blocks)
        grad_blocks = stacked_heads(grad_low, blocks)
        mixing_grad = dot_lanes(grad_low, weighted_blocks)
        mixing, mixing_t, inner_sum = [], [], jnp.zeros((rows, rows), f32)
        for j in range(GROUP):
            log_row = row_ref[j : j + 1, here]
            decay = jnp.where(causal, jnp.exp(log_full[j] - log_row), 0.0)
            decay_t = jnp.where(causal_t, jnp.exp(log_row - log_full[j]), 0.0)
            mixing.append((decay * inner).astype(bf16))
            mixing_t.append((decay_t * inner_t).astype(bf16))
            inner_sum = inner_sum + decay * mixing_grad[:, j * rows : (j + 1) * rows]
        inner_grad[pl.ds(c, 1)] = inner_grad[pl.ds(c, 1)] + inner_sum[None]
        y = dot_rows(jnp.concatenate(mixing, axis=1), weighted_blocks)
        state_low = states_ref[pl.ds(c, 1)][0]
        entry = jnp.exp(log_lanes)
        y = y + entry * dot_rows(queries, state_low)
        inside = dot_rows(jnp.concatenate(mixing_t, axis=1), grad_blocks)
        back = state_back[...]
        back_low = back.astype(bf16)
        log_last = log_lanes[rows - 1 : rows, :]
        tail = jnp.exp(log_last - log_lanes)
        outside = tail * dot_rows(keys, back_low)
        entry_grad = (grad * entry).astype(bf16)
        tail_low = (weighted * tail).astype(bf16)
        query_grad_ref[here, :] = query_grad_ref[here, :] + dot_lanes(entry_grad, state_low)
        key_grad_ref[here, :] = key_grad_ref[here, :] + dot_lanes(tail_low, back_low)
        last = jnp.exp(log_last)
        rest_ref[pl.ds(c, 1)] = (
            last * jnp.sum(state_low.astype(f32) * back, axis=0, keepdims=True)
        )[None]
        state_back[...] = last * back + dot_rows(queries_t, entry_grad)
        weighted_grad = inside + outside
        first = grad * y - weighted_low.astype(f32) * inside
        first_high = first.astype(bf16)
        first_rest = (first - first_high.astype(f32)).astype(bf16)
        sums_ref[here, :] = (
            dot_rows(first_high, pick_ref[0])
            + dot_rows(first_rest, pick_ref[0])
            + dot_rows((weighted * outside).astype(bf16), pick_ref[1])
            + dot_rows((values * weighted_grad).astype(bf16), pick_ref[2])
        )
        values_grad = step_lanes * weighted_grad + skip * grad
        pre_grad = values_grad * mask * (gate * (1.0 + pre * (1.0 - gate)))
        channel_ref[CONV : CONV + 1, :] += jnp.sum(pre_grad, axis=0, keepdims=True)
        channel_ref[CONV + 1 : CONV + 2, :] += jnp.sum(grad * values, axis=0, keepdims=True)
        for k in range(CONV):
            channel_ref[k : k + 1, :] += jnp.sum(
                pre_grad * window[5 + k : 5 + k + rows], axis=0, keepdims=True
            )
        ahead = jnp.concatenate([pre_grad, following[...]], axis=0)
        following[...] = pre_grad[0:8]
        x_grad = taps[CONV - 1 : CONV] * ahead[0:rows]
        for k in range(CONV - 1):
            x_grad = x_grad + taps[k : k + 1] * ahead[CONV - 1 - k : CONV - 1 - k + rows]
        x_grad_ref[here, :] = (x_grad * mask).astype(bf16)
        return carry

    lax.fori_loop(0, chunks, chunk, 0)

    @pl.when(group == pl.num_programs(0) - 1)
    def _():
        def finish(c, carry):
            here = pl.ds(pl.multiple_of(c * rows, rows), rows)
            inner_low = inner_grad[pl.ds(c, 1)][0].astype(bf16)
            query_grad_ref[here, :] = query_grad_ref[here, :] + dot_rows(
                inner_low, key_ref[here, :]
            )
            key_grad_ref[here, :] = key_grad_ref[here, :] + lax.dot_general(
                inner_low, query_ref[here, :], (((0,), (0,)), ((), ())),
                preferred_element_type=f32,
            )
            return carry

        lax.fori_loop(0, chunks, finish, 0)


def block_mask():
    row = jnp.arange(GROUP * SPAN)[:, None] // SPAN
    lane = jnp.arange(LANES)[None, :] // HEAD_DIM
    return (row == lane).astype(bf16)


def pick_masks():
    lane = jnp.arange(LANES)[:, None] // HEAD_DIM
    target = jnp.arange(PAIR)[None, :]
    return jnp.stack([(target == lane + GROUP * kind).astype(bf16) for kind in range(3)])


def whole_spec():
    return pl.BlockSpec(memory_space=pltpu.VMEM)


def lane_spec(rows):
    return pl.BlockSpec((rows, LANES), lambda g: (0, g))


def head_specs(length):
    return [
        lane_spec(length),
        lane_spec(CONV),
        lane_spec(1),
        lane_spec(1),
        lane_spec(1),
        pl.BlockSpec((length, PAIR), lambda g: (0, g)),
        pl.BlockSpec((8, length), lambda g: (g, 0)),
        whole_spec(),
        whole_spec(),
        whole_spec(),
        whole_spec(),
    ]


def scan_forward(x, taps, bias, mask, skip, columns, rows, keys, queries, keys_t):
    length, width = x.shape
    chunks = length // SPAN
    return pl.pallas_call(
        scan_forward_kernel,
        grid=(width // LANES,),
        in_specs=head_specs(length),
        out_specs=[
            lane_spec(length),
            pl.BlockSpec((chunks, STATE, LANES), lambda g: (0, 0, g)),
        ],
        out_shape=[
            jax.ShapeDtypeStruct((length, width), f32),
            jax.ShapeDtypeStruct((chunks, STATE, width), bf16),
        ],
        scratch_shapes=[pltpu.VMEM((length + 8, LANES), f32), pltpu.VMEM((STATE, LANES), f32)],
        compiler_params=pltpu.CompilerParams(vmem_limit_bytes=VMEM_BYTES),
        cost_estimate=pl.CostEstimate(
            flops=10_000_000_000, bytes_accessed=12_000_000, transcendentals=4_000_000
        ),
        name="scan_forward",
    )(x, taps, bias, mask, skip, columns, rows, keys, queries, keys_t, block_mask())


def scan_backward(
    x, taps, bias, mask, skip, columns, rows, keys, queries, queries_t, grad, states
):
    length, width = x.shape
    chunks = length // SPAN
    groups = width // LANES
    same = lambda g: (0, 0)
    return pl.pallas_call(
        scan_backward_kernel,
        grid=(groups,),
        in_specs=head_specs(length)
        + [
            whole_spec(),
            lane_spec(length),
            pl.BlockSpec((chunks, STATE, LANES), lambda g: (0, 0, g)),
        ],
        out_specs=[
            lane_spec(length),
            pl.BlockSpec((length, STATE), same),
            pl.BlockSpec((length, STATE), same),
            pl.BlockSpec((length, PAIR), lambda g: (0, g)),
            pl.BlockSpec((chunks, 1, LANES), lambda g: (0, 0, g)),
            lane_spec(8),
        ],
        out_shape=[
            jax.ShapeDtypeStruct((length, width), bf16),
            jax.ShapeDtypeStruct((length, STATE), f32),
            jax.ShapeDtypeStruct((length, STATE), f32),
            jax.ShapeDtypeStruct((length, PAIR * groups), f32),
            jax.ShapeDtypeStruct((chunks, 1, width), f32),
            jax.ShapeDtypeStruct((8, width), f32),
        ],
        scratch_shapes=[
            pltpu.VMEM((length + 8, LANES), f32),
            pltpu.VMEM((8, LANES), f32),
            pltpu.VMEM((STATE, LANES), f32),
            pltpu.VMEM((chunks, SPAN, SPAN), f32),
        ],
        compiler_params=pltpu.CompilerParams(vmem_limit_bytes=VMEM_BYTES),
        cost_estimate=pl.CostEstimate(
            flops=30_000_000_000, bytes_accessed=16_000_000, transcendentals=8_000_000
        ),
        name="scan_backward",
    )(
        x, taps, bias, mask, skip, columns, rows, keys, queries, queries_t, block_mask(),
        pick_masks(), grad, states,
    )


def gate_kernel(
    normed_ref, weight_ref, cotangent_ref, out_ref, y_ref, gain_ref, mask_ref,
    gate_part_ref, gated_grad_ref, stats_ref,
):
    gate_part = dot_rows(normed_ref[...], weight_ref[...]) * mask_ref[...]
    gated_grad = dot_lanes(cotangent_ref[...], out_ref[...])
    gate_part_ref[...] = gate_part
    gated_grad_ref[...] = gated_grad
    gated = y_ref[...] * (gate_part * jax.nn.sigmoid(gate_part))
    squares = jnp.sum(gated * gated, axis=1, keepdims=True)
    products = jnp.sum(gated * gated_grad * gain_ref[...], axis=1, keepdims=True)
    lane = lax.broadcasted_iota(jnp.int32, stats_ref.shape, 1)
    stats_ref[...] = jnp.where(lane == 0, squares, products)


def gate_forward(normed, weight, cotangent, out_weight, y, gain, mask):
    length, width = y.shape
    rows = lambda lanes: pl.BlockSpec((ROW_TILE, lanes), lambda i: (i, 0))
    return pl.pallas_call(
        gate_kernel,
        grid=(length // ROW_TILE,),
        in_specs=[
            rows(D), whole_spec(), rows(D), whole_spec(), rows(width), whole_spec(), whole_spec(),
        ],
        out_specs=[rows(width), rows(width), rows(PAIR)],
        out_shape=[
            jax.ShapeDtypeStruct((length, width), f32),
            jax.ShapeDtypeStruct((length, width), f32),
            jax.ShapeDtypeStruct((length, PAIR), f32),
        ],
        compiler_params=pltpu.CompilerParams(vmem_limit_bytes=VMEM_BYTES),
        cost_estimate=pl.CostEstimate(
            flops=9_000_000_000, bytes_accessed=28_000_000, transcendentals=1_000_000
        ),
        name="gate_forward",
    )(normed, weight, cotangent, out_weight, y, gain, mask)


def norm_back_kernel(
    y_ref, gate_part_ref, gated_grad_ref, scale_ref, gain_ref, mask_ref,
    gated_ref, y_grad_ref, gate_grad_ref, gain_grad_ref,
):
    @pl.when(pl.program_id(0) == 0)
    def _():
        gain_grad_ref[...] = jnp.zeros_like(gain_grad_ref)

    y, gate_part, gated_grad = y_ref[...], gate_part_ref[...], gated_grad_ref[...]
    inverse, pull = scale_ref[:, 0:1], scale_ref[:, 1:2]
    gate = jax.nn.sigmoid(gate_part)
    silu = gate_part * gate
    gated = y * silu
    scaled = gated * inverse
    gain = gain_ref[...]
    gated_ref[...] = (scaled * gain).astype(bf16)
    gain_grad_ref[0:1, :] += jnp.sum(gated_grad * scaled, axis=0, keepdims=True)
    back = inverse * (gated_grad * gain) - gated * pull
    y_grad_ref[...] = (back * silu).astype(bf16)
    gate_grad_ref[...] = (
        back * y * (gate * (1.0 + gate_part * (1.0 - gate))) * mask_ref[...]
    ).astype(bf16)


def norm_back(y, gate_part, gated_grad, scales, gain, mask):
    length, width = y.shape
    rows = lambda lanes: pl.BlockSpec((ROW_TILE, lanes), lambda i: (i, 0))
    return pl.pallas_call(
        norm_back_kernel,
        grid=(length // ROW_TILE,),
        in_specs=[rows(width), rows(width), rows(width), rows(2), whole_spec(), whole_spec()],
        out_specs=[
            rows(width), rows(width), rows(width), pl.BlockSpec((8, width), lambda i: (0, 0)),
        ],
        out_shape=[
            jax.ShapeDtypeStruct((length, width), bf16),
            jax.ShapeDtypeStruct((length, width), bf16),
            jax.ShapeDtypeStruct((length, width), bf16),
            jax.ShapeDtypeStruct((8, width), f32),
        ],
        compiler_params=pltpu.CompilerParams(vmem_limit_bytes=VMEM_BYTES),
        cost_estimate=pl.CostEstimate(
            flops=30_000_000, bytes_accessed=18_000_000, transcendentals=1_000_000
        ),
        name="norm_back",
    )(y, gate_part, gated_grad, scales, gain, mask)


MESH = pl.DeviceIdType.MESH


class Ring:
    def __init__(self):
        self.count = lax.axis_size("dp")
        self.far = self.count // 2
        me = lax.axis_index("dp")
        odd = lax.rem(me, 2)
        self.me = me
        self.place = (1 - odd) * lax.div(me, 2) + odd * lax.div(2 * self.count - 1 - me, 2)

    def member(self, distance):
        n = self.count
        place = lax.rem(self.place + distance + n, n)
        back = lax.div(place, n // 2)
        return (1 - back) * 2 * place + back * (2 * n - 1 - 2 * place)

    def target(self, way):
        return {"dp": self.member(1 if way == 0 else -1)}


def partner(flip):
    f = lax.axis_index("fsdp")
    return (f, f + 1 - 2 * lax.rem(f, 2), lax.rem(f + 2, 4), 3 - f)[flip]


def greet(targets):
    barrier = pltpu.get_barrier_semaphore()
    for target in targets:
        pl.semaphore_signal(barrier, inc=1, device_id=target, device_id_type=MESH)
    pl.semaphore_wait(barrier, len(targets))


def row_slice(ref, start, size):
    return ref.at[pl.ds(pl.multiple_of(start, 16), size)]


class RingGather:
    def __init__(self, ring, wholes, send, recv):
        self.ring, self.wholes, self.send, self.recv = ring, wholes, send, recv

    @staticmethod
    def semaphores(parts, count):
        return pltpu.SemaphoreType.DMA((parts * 4 * (count // 2),))

    def copy(self, part, way, half, hop):
        whole = self.wholes[part]
        rows = whole.shape[0] // self.ring.count
        size = rows // 2
        owner = self.ring.member(-hop if way == 0 else hop)
        place = row_slice(whole, owner * rows + half * size, size)
        at = ((part * 2 + way) * 2 + half) * self.ring.far + hop
        return pltpu.make_async_remote_copy(
            place, place, self.send.at[at], self.recv.at[at],
            device_id=self.ring.target(way), device_id_type=MESH,
        )

    def pieces(self, hop):
        return [
            (way, half)
            for half in (0, 1)
            for way in (0, 1)
            if hop < self.ring.far - 1 or half == way
        ]

    def start(self, part, hop):
        for way, half in self.pieces(hop):
            if hop:
                self.copy(part, way, half, hop - 1).wait_recv()
            self.copy(part, way, half, hop).start()

    def finish(self, part):
        last = self.ring.far - 1
        for way, half in self.pieces(last):
            self.copy(part, way, half, last).wait_recv()
            if last:
                self.copy(part, way, 1 - half, last - 1).wait_recv()
        for hop in range(last + 1):
            for way, half in self.pieces(hop):
                self.copy(part, way, half, hop).wait_send()


class RingScatter:
    def __init__(self, ring, held, arrived, send, recv):
        self.ring, self.held, self.arrived = ring, held, arrived
        self.send, self.recv = send, recv

    @staticmethod
    def scratch(count, rows, columns):
        hops = count // 2
        return [
            pltpu.VMEM((2, 2, rows, columns), bf16),
            pltpu.VMEM((2, hops, rows, columns), bf16),
            pltpu.SemaphoreType.DMA((2 * hops,)),
            pltpu.SemaphoreType.DMA((2 * hops,)),
        ]

    def copy(self, way, hop):
        rows = self.held.shape[2]
        size = rows // 2 if hop == 0 else rows
        at = way * self.ring.far + hop
        return pltpu.make_async_remote_copy(
            self.held.at[way, hop % 2, pl.ds(0, size)],
            self.arrived.at[way, hop, pl.ds(0, size)],
            self.send.at[at], self.recv.at[at],
            device_id=self.ring.target(way), device_id_type=MESH,
        )

    def owner(self, way, hop):
        distance = self.ring.far - hop
        return self.ring.member(distance if way == 0 else -distance)

    def start(self, hop, term):
        rows = self.held.shape[2]
        half = rows // 2
        if hop == 0:
            value = term(self.owner(0, 0)).astype(bf16)
            self.held[0, 0, 0:half] = value[:half]
            self.copy(0, 0).start()
            self.held[1, 0, 0:half] = value[half:]
            self.copy(1, 0).start()
            return
        for way in (0, 1):
            value = term(self.owner(way, hop))
            self.copy(way, hop - 1).wait_recv()
            slot = hop % 2
            if hop >= 2:
                self.copy(way, hop - 2).wait_send()
            if hop == 1:
                low = slice(way * half, (way + 1) * half)
                rest = slice((1 - way) * half, (2 - way) * half)
                self.held[way, slot, low] = (
                    value[low] + self.arrived[way, 0, 0:half].astype(f32)
                ).astype(bf16)
                self.held[way, slot, rest] = value[rest].astype(bf16)
            else:
                self.held[way, slot] = (
                    value + self.arrived[way, hop - 1].astype(f32)
                ).astype(bf16)
            self.copy(way, hop).start()

    def finish(self, term):
        last = self.ring.far - 1
        value = term(self.ring.me)
        for way in (0, 1):
            self.copy(way, last).wait_recv()
            value = value + self.arrived[way, last].astype(f32)
        for hop in range(last - 1, last + 1):
            for way in (0, 1):
                self.copy(way, hop).wait_send()
        return value


def gather_first_kernel(
    small_cut, x_cut, normed_own, cotangent_own, small, x, normed, cotangent,
    local_sem, swap_send, swap_recv, token_send, token_recv, ring_send, ring_recv,
):
    ring = Ring()
    d, f = ring.me, lax.axis_index("fsdp")
    greet([{"fsdp": partner(k)} for k in (1, 2, 3)] + [ring.target(0), ring.target(1)])
    cuts, wholes = [small_cut, x_cut], [small, x]
    sub = small_cut.shape[1]
    tokens = normed_own.shape[0]
    local = [
        pltpu.make_async_copy(
            cut.at[f], row_slice(whole, (4 * d + f) * sub, sub), local_sem.at[i]
        )
        for i, (cut, whole) in enumerate(zip(cuts, wholes))
    ] + [
        pltpu.make_async_copy(own, row_slice(whole, f * tokens, tokens), local_sem.at[2 + i])
        for i, (own, whole) in enumerate([(normed_own, normed), (cotangent_own, cotangent)])
    ]
    swaps = [
        [
            pltpu.make_async_remote_copy(
                cut.at[partner(k)], row_slice(whole, (4 * d + f) * sub, sub),
                swap_send.at[3 * i + k - 1], swap_recv.at[3 * i + k - 1],
                device_id={"fsdp": partner(k)}, device_id_type=MESH,
            )
            for k in (2, 3, 1)
        ]
        for i, (cut, whole) in enumerate(zip(cuts, wholes))
    ]

    def token_copies(i, own, whole):
        def one(at, source, owner, k):
            return pltpu.make_async_remote_copy(
                source, row_slice(whole, owner * tokens, tokens),
                token_send.at[3 * i + at], token_recv.at[3 * i + at],
                device_id={"fsdp": partner(k)}, device_id_type=MESH,
            )

        far = partner(2)
        return (
            one(0, own, f, 2), one(1, own, f, 1),
            one(2, row_slice(whole, far * tokens, tokens), far, 1),
        )

    normed_copies = token_copies(0, normed_own, normed)
    cotangent_copies = token_copies(1, cotangent_own, cotangent)
    for copy in local:
        copy.start()
    for row in swaps:
        for copy in row:
            copy.start()
    for copy in normed_copies[:2]:
        copy.start()
    rings = RingGather(ring, wholes, ring_send, ring_recv)
    for part in (0, 1):
        local[part].wait()
        for copy in swaps[part]:
            copy.wait_recv()
        rings.start(part, 0)
    for hop in range(1, ring.far):
        rings.start(0, hop)
        rings.start(1, hop)
        if hop == 1:
            normed_copies[0].wait_recv()
            normed_copies[2].start()
            for copy in cotangent_copies[:2]:
                copy.start()
        if hop == ring.far - 1:
            cotangent_copies[0].wait_recv()
            cotangent_copies[2].start()
    rings.finish(0)
    rings.finish(1)
    for copy in local[2:]:
        copy.wait()
    for copies in (normed_copies, cotangent_copies):
        for copy in copies[1:]:
            copy.wait_recv()
        for copy in copies:
            copy.wait_send()
    for row in swaps:
        for copy in row:
            copy.wait_send()


def any_specs(count):
    return [pl.BlockSpec(memory_space=pl.ANY)] * count


def gather_first(small_cut, x_cut, normed_own, cotangent_own):
    count, members = lax.axis_size("dp"), lax.axis_size("fsdp")
    rows = count * members * small_cut.shape[1]
    tokens = members * normed_own.shape[0]
    return pl.pallas_call(
        gather_first_kernel,
        in_specs=any_specs(4),
        out_specs=any_specs(4),
        out_shape=[
            jax.ShapeDtypeStruct((rows, small_cut.shape[2]), bf16),
            jax.ShapeDtypeStruct((rows, x_cut.shape[2]), bf16),
            jax.ShapeDtypeStruct((tokens, D), bf16),
            jax.ShapeDtypeStruct((tokens, D), bf16),
        ],
        scratch_shapes=[
            pltpu.SemaphoreType.DMA((4,)),
            pltpu.SemaphoreType.DMA((6,)),
            pltpu.SemaphoreType.DMA((6,)),
            pltpu.SemaphoreType.DMA((6,)),
            pltpu.SemaphoreType.DMA((6,)),
            RingGather.semaphores(2, count),
            RingGather.semaphores(2, count),
        ],
        compiler_params=pltpu.CompilerParams(collective_id=0, has_side_effects=True),
        name="gather_first",
    )(small_cut, x_cut, normed_own, cotangent_own)


def scan_gather_kernel(
    normed_ref, weight_ref, taps_ref, bias_ref, mask_ref, skip_ref, column_ref, row_ref, key_ref,
    query_ref, key_t_ref, block_ref, gate_cut, out_own,
    x_ref, y_ref, states_ref, gate_all, out_all,
    padded, state, local_sem, swap_send, swap_recv, ring_send, ring_recv,
):
    ring = Ring()
    d, f = ring.me, lax.axis_index("fsdp")
    step = pl.program_id(0)
    rings = RingGather(ring, [gate_all, out_all], ring_send, ring_recv)
    sub, rows = gate_cut.shape[1], out_own.shape[0]
    local = [
        pltpu.make_async_copy(
            gate_cut.at[f], row_slice(gate_all, (4 * d + f) * sub, sub), local_sem.at[0]
        ),
        pltpu.make_async_copy(out_own, row_slice(out_all, d * rows, rows), local_sem.at[1]),
    ]
    swaps = [
        pltpu.make_async_remote_copy(
            gate_cut.at[partner(k)], row_slice(gate_all, (4 * d + f) * sub, sub),
            swap_send.at[k - 1], swap_recv.at[k - 1],
            device_id={"fsdp": partner(k)}, device_id_type=MESH,
        )
        for k in (2, 3, 1)
    ]

    @pl.when(step == 0)
    def _():
        greet([{"fsdp": partner(k)} for k in (1, 2, 3)] + [ring.target(0), ring.target(1)])
        for copy in local + swaps:
            copy.start()
        local[1].wait()
        rings.start(1, 0)
        local[0].wait()
        for copy in swaps:
            copy.wait_recv()
        rings.start(0, 0)

    for hop in range(1, ring.far):
        @pl.when(step == hop)
        def _(hop=hop):
            rings.start(1, hop)
            rings.start(0, hop)

    x_ref[...] = dot_rows(normed_ref[...], weight_ref[...])
    scan_forward_kernel(
        x_ref, taps_ref, bias_ref, mask_ref, skip_ref, column_ref, row_ref, key_ref, query_ref,
        key_t_ref, block_ref, y_ref, states_ref, padded, state,
    )

    @pl.when(step == pl.num_programs(0) - 1)
    def _():
        rings.finish(1)
        rings.finish(0)
        for copy in swaps:
            copy.wait_send()


def scan_gather(
    normed, weight, taps, bias, mask, skip, columns, rows, keys, queries, keys_t, gate_cut, out_own
):
    length = normed.shape[0]
    width = weight.shape[1]
    chunks = length // SPAN
    count = lax.axis_size("dp")
    assert width // LANES == count // 2
    return pl.pallas_call(
        scan_gather_kernel,
        grid=(width // LANES,),
        in_specs=[whole_spec(), lane_spec(D)] + head_specs(length)[1:] + any_specs(2),
        out_specs=[
            lane_spec(length),
            lane_spec(length),
            pl.BlockSpec((chunks, STATE, LANES), lambda g: (0, 0, g)),
        ]
        + any_specs(2),
        out_shape=[
            jax.ShapeDtypeStruct((length, width), f32),
            jax.ShapeDtypeStruct((length, width), f32),
            jax.ShapeDtypeStruct((chunks, STATE, width), bf16),
            jax.ShapeDtypeStruct((D, width), bf16),
            jax.ShapeDtypeStruct((count * out_own.shape[0], D), bf16),
        ],
        scratch_shapes=[
            pltpu.VMEM((length + 8, LANES), f32),
            pltpu.VMEM((STATE, LANES), f32),
            pltpu.SemaphoreType.DMA((2,)),
            pltpu.SemaphoreType.DMA((3,)),
            pltpu.SemaphoreType.DMA((3,)),
            RingGather.semaphores(2, count),
            RingGather.semaphores(2, count),
        ],
        compiler_params=pltpu.CompilerParams(
            collective_id=1, has_side_effects=True, vmem_limit_bytes=VMEM_BYTES
        ),
        name="scan_gather",
    )(
        normed, weight, taps, bias, mask, skip, columns, rows, keys, queries, keys_t, block_mask(),
        gate_cut, out_own,
    )


def scan_scatter_kernel(
    x_ref, taps_ref, bias_ref, mask_ref, skip_ref, column_ref, row_ref, key_ref, query_ref,
    query_t_ref, block_ref, pick_ref, grad_ref, states_ref,
    normed_t_ref, gate_grad_ref, gated_ref, gated_t_ref, cotangent_ref, weight_ref, tokens_ref,
    x_grad_ref, key_grad_ref, query_grad_ref, sums_ref, rest_ref, channel_ref,
    gate_raw_ref, out_raw_ref, layer_out_ref,
    padded, following, state_back, inner_grad, added, added_out, added_in, added_send, added_recv,
    *ring_scratch,
):
    ring = Ring()
    step = pl.program_id(0)
    steps = pl.num_programs(0)
    gate_ring = RingScatter(ring, *ring_scratch[:4])
    out_ring = RingScatter(ring, *ring_scratch[4:])
    rows_in, rows_out = gate_raw_ref.shape[0], out_raw_ref.shape[0]
    tokens = tokens_ref.shape[0]

    def gate_term(owner):
        here = pl.ds(pl.multiple_of(owner * rows_in, rows_in), rows_in)
        return dot_rows(normed_t_ref[here, :], gate_grad_ref[...])

    def out_term(owner):
        here = pl.ds(pl.multiple_of(owner * rows_out, rows_out), rows_out)
        return dot_rows(gated_t_ref[here, :], cotangent_ref[...])

    def added_block(flip):
        here = pl.ds(pl.multiple_of(partner(flip) * tokens, tokens), tokens)
        return dot_rows(gated_ref[here, :], weight_ref[...])

    def added_copy(i):
        return pltpu.make_async_remote_copy(
            added_out.at[i], added_in.at[i], added_send.at[i], added_recv.at[i],
            device_id={"fsdp": partner(2 if i == 2 else 1)}, device_id_type=MESH,
        )

    @pl.when(step == 0)
    def _():
        greet([{"fsdp": partner(k)} for k in (1, 2)] + [ring.target(0), ring.target(1)])

    for hop in range(ring.far):
        @pl.when(step == hop)
        def _(hop=hop):
            out_ring.start(hop, out_term)
            gate_ring.start(hop, gate_term)

    @pl.when(step == 0)
    def _():
        for i, flip in ((1, 3), (0, 1)):
            added_out[i] = added_block(flip).astype(bf16)
            added_copy(i).start()

    @pl.when(step == 1)
    def _():
        value = added_block(2)
        added_copy(1).wait_recv()
        added_out[2] = (value + added_in[1].astype(f32)).astype(bf16)
        added_copy(2).start()

    @pl.when(step == 2)
    def _():
        added[...] = added_block(0)

    scan_backward_kernel(
        x_ref, taps_ref, bias_ref, mask_ref, skip_ref, column_ref, row_ref, key_ref, query_ref,
        query_t_ref, block_ref, pick_ref, grad_ref, states_ref,
        x_grad_ref, key_grad_ref, query_grad_ref, sums_ref, rest_ref, channel_ref,
        padded, following, state_back, inner_grad,
    )

    @pl.when(step == steps - 1)
    def _():
        added_copy(0).wait_recv()
        added_copy(2).wait_recv()
        layer_out_ref[...] = (
            tokens_ref[...].astype(f32)
            + ((added[...] + added_in[0].astype(f32)) + added_in[2].astype(f32))
        ).astype(bf16)
        for i in range(3):
            added_copy(i).wait_send()
        out_raw_ref[...] = out_ring.finish(out_term)
        gate_raw_ref[...] = gate_ring.finish(gate_term)


def scan_scatter(
    x, taps, bias, mask, skip, columns, rows, keys, queries, queries_t, grad, states,
    normed_t, gate_grad, gated, gated_t, cotangent, weight, tokens,
):
    length, width = x.shape
    chunks = length // SPAN
    groups = width // LANES
    count = lax.axis_size("dp")
    assert groups == count // 2
    rows_in, rows_out, own = D // count, width // count, tokens.shape[0]
    same = lambda g: (0, 0)
    return pl.pallas_call(
        scan_scatter_kernel,
        grid=(groups,),
        in_specs=head_specs(length)
        + [
            whole_spec(),
            lane_spec(length),
            pl.BlockSpec((chunks, STATE, LANES), lambda g: (0, 0, g)),
        ]
        + [whole_spec()] * 7,
        out_specs=[
            lane_spec(length),
            pl.BlockSpec((length, STATE), same),
            pl.BlockSpec((length, STATE), same),
            pl.BlockSpec((length, PAIR), lambda g: (0, g)),
            pl.BlockSpec((chunks, 1, LANES), lambda g: (0, 0, g)),
            lane_spec(8),
        ]
        + [whole_spec()] * 3,
        out_shape=[
            jax.ShapeDtypeStruct((length, width), bf16),
            jax.ShapeDtypeStruct((length, STATE), f32),
            jax.ShapeDtypeStruct((length, STATE), f32),
            jax.ShapeDtypeStruct((length, PAIR * groups), f32),
            jax.ShapeDtypeStruct((chunks, 1, width), f32),
            jax.ShapeDtypeStruct((8, width), f32),
            jax.ShapeDtypeStruct((rows_in, width), f32),
            jax.ShapeDtypeStruct((rows_out, D), f32),
            jax.ShapeDtypeStruct((own, D), bf16),
        ],
        scratch_shapes=[
            pltpu.VMEM((length + 8, LANES), f32),
            pltpu.VMEM((8, LANES), f32),
            pltpu.VMEM((STATE, LANES), f32),
            pltpu.VMEM((chunks, SPAN, SPAN), f32),
            pltpu.VMEM((own, D), f32),
            pltpu.VMEM((3, own, D), bf16),
            pltpu.VMEM((3, own, D), bf16),
            pltpu.SemaphoreType.DMA((3,)),
            pltpu.SemaphoreType.DMA((3,)),
        ]
        + RingScatter.scratch(count, rows_in, width)
        + RingScatter.scratch(count, rows_out, D),
        compiler_params=pltpu.CompilerParams(
            collective_id=2, has_side_effects=True, vmem_limit_bytes=VMEM_BYTES
        ),
        name="scan_scatter",
    )(
        x, taps, bias, mask, skip, columns, rows, keys, queries, queries_t, block_mask(),
        pick_masks(), grad, states,
        normed_t, gate_grad, gated, gated_t, cotangent, weight, tokens,
    )


def unpack(vectors):
    offset = D + INNER
    taps_end = offset + CONV * XBC
    heads_start = taps_end + XBC
    norm_gain = vectors[:D]
    gate_gain = vectors[D:offset]
    filter_taps = vectors[offset:taps_end].reshape(CONV, XBC)
    filter_bias = vectors[taps_end:heads_start]
    step_bias = vectors[heads_start : heads_start + HEADS]
    decay_log = vectors[heads_start + HEADS : heads_start + 2 * HEADS]
    skip_gain = vectors[heads_start + 2 * HEADS : heads_start + 3 * HEADS]
    return (norm_gain, gate_gain, filter_taps, filter_bias, step_bias, decay_log, skip_gain)


def adamw(weight, moment, square, gradient, step_rate):
    moment_new = beta_first * moment + (1.0 - beta_first) * gradient
    square_new = beta_second * square + (1.0 - beta_second) * gradient * gradient
    moment_hat = moment_new / (1.0 - beta_first**STEP)
    square_hat = square_new / (1.0 - beta_second**STEP)
    weight_new = weight - step_rate * (
        moment_hat / (jnp.sqrt(square_hat) + adam_eps) + weight_decay * weight
    )
    return (moment_new, square_new, weight_new)


def on_device(
    tokens,
    widths,
    cotangent,
    in_weight,
    in_first,
    in_second,
    out_weight,
    out_first,
    out_second,
    vectors,
    vector_first,
    vector_second,
):
    fsdp = lax.axis_size("fsdp")
    me = lax.axis_index("fsdp")
    heads = HEADS // fsdp
    inner = INNER // fsdp
    shared = 2 * STATE // fsdp
    pairs = HEADS // 2 // fsdp
    rows_in, rows_out = in_weight.shape[0], out_weight.shape[0]
    length = tokens.shape[0] * fsdp
    chunks = length // SPAN
    in_kernels = uses_ring("dp") and rows_out == PAIR and rows_in % 16 == 0

    def own_channels(v):
        lead = v.shape[:-1]
        cut = v.reshape(lead + (pairs, fsdp, PAIR))
        return lax.dynamic_index_in_dim(cut, me, len(lead) + 1, False).reshape(lead + (inner,))

    def own_heads(v):
        return lax.dynamic_index_in_dim(v.reshape(pairs, fsdp, 2), me, 1, False).reshape(heads)

    def own_shared(v):
        return lax.dynamic_slice_in_dim(v, me * shared, shared, v.ndim - 1)

    norm_gain, gate_gain, filter_taps, filter_bias, step_bias, decay_log, skip_gain = unpack(
        vectors
    )
    gain_own = own_channels(gate_gain)[None]
    taps_own = own_channels(filter_taps[:, :INNER])
    bias_own = own_channels(filter_bias[:INNER])[None]
    taps_shared = own_shared(filter_taps[:, INNER:])
    bias_shared = own_shared(filter_bias[INNER:])
    step_bias_own, decay_own = own_heads(step_bias), -jnp.exp(own_heads(decay_log))
    skip_own = jnp.repeat(own_heads(skip_gain), HEAD_DIM)[None]

    width_index = widths[0]
    active = HEADS // 8 * jnp.left_shift(jnp.int32(1), width_index)
    head_mask = (jnp.arange(heads, dtype=jnp.int32) < active // fsdp).astype(f32)
    mask = jnp.repeat(head_mask, HEAD_DIM)[None]
    channel_count = (active * HEAD_DIM).astype(f32)

    in_low = in_weight.astype(bf16)
    shared_cut = jnp.concatenate(
        [
            in_low[:, 2 * INNER : 2 * INNER + 2 * STATE]
            .reshape(rows_in, fsdp, shared)
            .transpose(1, 0, 2),
            in_low[:, 2 * INNER + 2 * STATE :]
            .reshape(rows_in, pairs, fsdp, 2)
            .transpose(2, 0, 1, 3)
            .reshape(fsdp, rows_in, heads),
        ],
        axis=2,
    )

    def channel_cut(part):
        return (
            part.reshape(rows_in, pairs, fsdp, PAIR)
            .transpose(2, 0, 1, 3)
            .reshape(fsdp, rows_in, inner)
        )

    def gathered(cut):
        block = exchanged(cut, "fsdp")
        return gather_rows(block.reshape(fsdp * rows_in, cut.shape[2]), "dp")

    inputs = tokens.astype(f32)
    inverse_in = lax.rsqrt(jnp.mean(inputs * inputs, axis=-1, keepdims=True) + norm_eps)
    normed_own = (inputs * inverse_in * norm_gain[None, :]).astype(bf16)
    x_cut = channel_cut(in_low[:, INNER : 2 * INNER])
    gate_cut = channel_cut(in_low[:, :INNER])
    out_low = out_weight.astype(bf16)

    if in_kernels:
        shared_cut = jnp.pad(shared_cut, ((0, 0), (0, 0), (0, PAIR - shared - heads)))
        weight_shared, weight_x, normed, cotangents = gather_first(
            shared_cut, x_cut, normed_own, cotangent
        )
        weight_shared = weight_shared[:, : shared + heads]
    else:
        weight_shared = gathered(shared_cut)
        weight_x = gathered(x_cut)
        weight_gate = gathered(gate_cut)
        weight_out = lax.dynamic_index_in_dim(
            lax.all_gather(out_low, ("dp", "fsdp"), axis=0, tiled=True).reshape(
                pairs, fsdp, PAIR, D
            ),
            me,
            1,
            False,
        ).reshape(inner, D)
        normed = spread(normed_own, "fsdp").reshape(length, D)
        cotangents = spread(cotangent, "fsdp").reshape(length, D)

    small = lax.dot_general(
        weight_shared, normed, (((0,), (1,)), ((), ())), preferred_element_type=f32
    )
    shared_part = small[:shared]
    step_raw = small[shared:] * head_mask[:, None]
    shared_padded = jnp.pad(shared_part, ((0, 0), (CONV - 1, 0)))
    shared_pre = bias_shared[:, None] + sum(
        taps_shared[k][:, None] * shared_padded[:, k : k + length] for k in range(CONV)
    )
    shared_gate = jax.nn.sigmoid(shared_pre)
    shared_all = spread_small((shared_pre * shared_gate).astype(bf16), "fsdp").reshape(
        2 * STATE, length
    )
    keys_t, queries_t = shared_all[:STATE], shared_all[STATE:]
    keys, queries = keys_t.T, queries_t.T
    step_logits = step_raw + step_bias_own[:, None]
    step_sizes = jax.nn.softplus(step_logits)
    upto = (jnp.arange(SPAN)[:, None] <= jnp.arange(SPAN)[None, :]).astype(f32)
    log_sums = jnp.dot(
        (step_sizes * decay_own[:, None]).reshape(heads, chunks, SPAN), upto, precision=highest
    ).reshape(heads, length)
    groups = heads // GROUP
    head_rows = jnp.concatenate(
        [log_sums.reshape(groups, GROUP, length), step_sizes.reshape(groups, GROUP, length)],
        axis=1,
    )
    head_columns = jnp.pad(
        head_rows.transpose(2, 0, 1), ((0, 0), (0, 0), (0, PAIR - 2 * GROUP))
    ).reshape(length, groups * PAIR)
    head_rows = head_rows.reshape(groups * 2 * GROUP, length)

    scan_inputs = (taps_own, bias_own, mask, skip_own, head_columns, head_rows, keys, queries)
    if in_kernels:
        x_part, y, states, weight_gate, weight_out = scan_gather(
            normed, weight_x, *scan_inputs, keys_t, gate_cut, out_low
        )
    else:
        x_part = jnp.dot(normed, weight_x, preferred_element_type=f32)
        y, states = scan_forward(x_part, *scan_inputs, keys_t)
    gate_part, gated_grad, stats = gate_forward(
        normed, weight_gate, cotangents, weight_out, y, gain_own, mask
    )
    stats = summed(stats[:, :2].T, "fsdp")
    inverse_out = lax.rsqrt(stats[0] / channel_count + norm_eps)
    pull = inverse_out**3 / channel_count * stats[1]
    gated_low, y_grad, gate_grad, gain_grad = norm_back(
        y, gate_part, gated_grad, jnp.stack([inverse_out, pull], axis=1), gain_own, mask
    )

    def in_term(grad):
        return lax.dot_general(
            normed, grad, (((0,), (0,)), ((), ())), preferred_element_type=f32
        ).astype(bf16)

    if in_kernels:
        (
            x_grad, key_grad, query_grad, sums, rest, channel_grad, gate_raw, out_raw, layer_out,
        ) = scan_scatter(
            x_part, *scan_inputs, queries_t, y_grad, states,
            normed.T, gate_grad, gated_low, gated_low.T, cotangents, weight_out, tokens,
        )
    else:
        out_term = lax.dot_general(
            gated_low, cotangents, (((0,), (0,)), ((), ())), preferred_element_type=f32
        )
        whole_term = jnp.zeros((pairs, fsdp, PAIR, D), f32)
        whole_term = lax.dynamic_update_slice(
            whole_term, out_term.reshape(pairs, 1, PAIR, D), (0, me, 0, 0)
        )
        out_raw = lax.psum_scatter(
            whole_term.reshape(INNER, D), ("dp", "fsdp"), scatter_dimension=0, tiled=True
        )
        added = halved(
            jnp.dot(gated_low, weight_out, preferred_element_type=f32)
            .astype(bf16)
            .reshape(fsdp, tokens.shape[0], D),
            "fsdp",
        )
        layer_out = (inputs + added).astype(bf16)
        gate_raw = scatter_rows(in_term(gate_grad), "dp")
        x_grad, key_grad, query_grad, sums, rest, channel_grad = scan_backward(
            x_part, *scan_inputs, queries_t, y_grad, states
        )
    x_raw = scatter_rows(in_term(x_grad), "dp")

    shared_grads = jnp.concatenate([key_grad, query_grad], axis=1).T.astype(bf16)
    arrived = exchanged(shared_grads.reshape(fsdp, shared, length), "fsdp").astype(f32)
    activated_grad = jnp.sum(arrived, axis=0)
    shared_pre_grad = activated_grad * shared_gate * (1.0 + shared_pre * (1.0 - shared_gate))
    shared_ahead = jnp.pad(shared_pre_grad, ((0, 0), (0, CONV - 1)))
    shared_grad = sum(
        taps_shared[k][:, None] * shared_ahead[:, CONV - 1 - k : CONV - 1 - k + length]
        for k in range(CONV)
    )
    taps_shared_grad = jnp.stack(
        [
            jnp.sum(shared_pre_grad * shared_padded[:, k : k + length], axis=1)
            for k in range(CONV)
        ]
    )
    bias_shared_grad = jnp.sum(shared_pre_grad, axis=1)

    sums = (
        sums.reshape(length, groups, PAIR)[:, :, : 3 * GROUP]
        .reshape(length, groups, 3, GROUP)
        .transpose(2, 1, 3, 0)
        .reshape(3, heads, chunks, SPAN)
    )
    before = (jnp.arange(SPAN)[:, None] < jnp.arange(SPAN)[None, :]).astype(f32)
    rest = rest.reshape(chunks, heads, HEAD_DIM).sum(axis=2).T
    log_grad = (
        jnp.dot(sums[0], 1.0 - before, precision=highest)
        + jnp.dot(sums[1], before, precision=highest)
        + rest[:, :, None]
    ).reshape(heads, length)
    step_grad = decay_own[:, None] * log_grad + sums[2].reshape(heads, length)
    raw_grad = step_grad * jax.nn.sigmoid(step_logits)
    step_bias_grad = jnp.sum(raw_grad, axis=1)
    decay_grad = jnp.sum(step_sizes * log_grad, axis=1) * decay_own
    small_grad = jnp.concatenate([shared_grad, raw_grad * head_mask[:, None]], axis=0).astype(bf16)
    small_raw = scatter_rows(
        lax.dot_general(
            normed, small_grad, (((0,), (1,)), ((), ())), preferred_element_type=f32
        ).astype(bf16),
        "dp",
    )

    def in_back(grad, weight, grad_dim=1):
        return lax.dot_general(
            grad, weight, (((grad_dim,), (1,)), ((), ())), preferred_element_type=f32
        )

    normed_grad = halved(
        (
            in_back(gate_grad, weight_gate)
            + in_back(x_grad, weight_x)
            + in_back(small_grad, weight_shared, 0)
        )
        .astype(bf16)
        .reshape(fsdp, tokens.shape[0], D),
        "fsdp",
    )
    pulled = normed_grad * norm_gain[None, :]
    input_grad = inverse_in * pulled - inputs * (
        inverse_in**3 * jnp.mean(pulled * inputs, axis=-1, keepdims=True)
    )
    token_grad = (cotangent.astype(f32) + input_grad).astype(bf16)
    norm_gain_grad = jnp.sum(normed_grad * inputs * inverse_in, axis=0)

    skip_grad = channel_grad[CONV + 1].reshape(heads, HEAD_DIM).sum(axis=1)
    head_row = jnp.concatenate(
        [
            step_bias_grad, decay_grad, skip_grad, bias_shared_grad, taps_shared_grad.reshape(-1),
        ]
    )
    head_row = jnp.pad(head_row, (0, inner - head_row.shape[0]))
    vector_rows = jnp.concatenate(
        [
            gain_grad[0:1],
            channel_grad[: CONV + 1],
            head_row[None],
            norm_gain_grad.reshape(-1, inner),
        ]
    )
    vector_rows = jnp.pad(vector_rows, ((0, -vector_rows.shape[0] % 8), (0, 0)))
    vector_rows = spread_small(summed_in_steps(vector_rows, "dp"), "fsdp")

    def joined_channels(v):
        return v.reshape(fsdp, pairs, PAIR).transpose(1, 0, 2).reshape(INNER)

    def joined_heads(v):
        return v.reshape(fsdp, pairs, 2).transpose(1, 0, 2).reshape(HEADS)

    head_all = vector_rows[:, CONV + 2]
    taps_shared_all = (
        head_all[:, 3 * heads + shared : 3 * heads + 5 * shared]
        .reshape(fsdp, CONV, shared)
        .transpose(1, 0, 2)
        .reshape(CONV, 2 * STATE)
    )
    taps_all = [
        jnp.concatenate([joined_channels(vector_rows[:, 1 + k]), taps_shared_all[k]])
        for k in range(CONV)
    ]
    bias_all = jnp.concatenate(
        [
            joined_channels(vector_rows[:, CONV + 1]),
            head_all[:, 3 * heads : 3 * heads + shared].reshape(-1),
        ]
    )
    norm_rows = vector_rows[:, CONV + 3 : CONV + 3 + D // inner].reshape(fsdp, D)
    norm_all = norm_rows[0]
    for member in range(1, fsdp):
        norm_all = norm_all + norm_rows[member]
    vector_raw = jnp.concatenate(
        [norm_all, joined_channels(vector_rows[:, 0])]
        + taps_all
        + [bias_all]
        + [joined_heads(head_all[:, i * heads : (i + 1) * heads]) for i in range(3)]
    )

    squares = (
        jnp.sum(gate_raw * gate_raw)
        + jnp.sum(x_raw * x_raw)
        + jnp.sum(small_raw * small_raw)
        + jnp.sum(out_raw * out_raw)
    )
    squares = summed(summed(jnp.broadcast_to(squares, (8, 128)), "fsdp"), "dp")[0, 0]
    grad_norm = jnp.sqrt(squares + jnp.sum(vector_raw * vector_raw))
    factor = jnp.minimum(1.0, clip_norm / (grad_norm + 1e-06))

    def returned(raw):
        return exchanged(raw.astype(bf16).reshape(fsdp, rows_in, raw.shape[1]), "fsdp")

    def joined_columns(part):
        return (
            part.reshape(fsdp, rows_in, pairs, PAIR).transpose(1, 2, 0, 3).reshape(rows_in, INNER)
        )

    small_back = returned(small_raw)
    in_raw = jnp.concatenate(
        [
            joined_columns(returned(gate_raw)),
            joined_columns(returned(x_raw)),
            small_back[:, :, :shared].transpose(1, 0, 2).reshape(rows_in, 2 * STATE),
            small_back[:, :, shared:]
            .reshape(fsdp, rows_in, pairs, 2)
            .transpose(1, 2, 0, 3)
            .reshape(rows_in, HEADS),
        ],
        axis=1,
    ).astype(f32)
    in_grad = in_raw * factor
    out_grad = out_raw * factor
    vector_grad = vector_raw * factor
    in_moment, in_square, in_master = adamw(in_weight, in_first, in_second, in_grad, rate_in_proj)
    out_moment, out_square, out_master = adamw(
        out_weight, out_first, out_second, out_grad, rate_out_proj
    )
    vector_moment, vector_square, vector_master = adamw(
        vectors, vector_first, vector_second, vector_grad, rate_vectors
    )
    return (
        layer_out,
        token_grad,
        in_grad,
        out_grad,
        vector_grad,
        grad_norm,
        in_moment,
        in_square,
        in_master,
        in_master.astype(bf16),
        out_moment,
        out_square,
        out_master,
        out_master.astype(bf16),
        vector_moment,
        vector_square,
        vector_master,
    )


def solution(mesh):
    rows = P(("dp", "fsdp"), None)
    return jax.shard_map(
        on_device,
        mesh=mesh,
        in_specs=(rows, P("dp")) + (rows,) * 7 + (P(),) * 3,
        out_specs=(rows,) * 4 + (P(),) * 2 + (rows,) * 8 + (P(),) * 3,
        check_vma=False,
    )
```

```python
from functools import partial

import jax
import jax.numpy as jnp
from jax import lax
from jax.experimental import pallas as pl
from jax.experimental.pallas import tpu as pltpu
from jax.sharding import PartitionSpec as P

D = 2048
HEADS = 64
HEAD_DIM = 64
STATE = 128
CONV = 4
SPAN = 128
STEP = 10
INNER = 4096
XBC = 4352
PAIR = 2 * HEAD_DIM
GROUP = 4
LANES = GROUP * HEAD_DIM
ROW_TILE = 256
RING_LIMIT = 16

norm_eps = 1e-05
clip_norm = 1.0
beta_first = 0.5
beta_second = 0.5
adam_eps = 1e-08
weight_decay = 0.1
rate_in_proj = 0.03
rate_out_proj = 0.02
rate_vectors = 0.5
highest = lax.Precision.HIGHEST
f32 = jnp.float32
bf16 = jnp.bfloat16
VMEM_BYTES = 60 * 1024 * 1024


def ring_order(count):
    return list(range(0, count, 2)) + list(range(count - 1, 0, -2))


def ring_links(count):
    order = ring_order(count)
    right = [(order[i], order[(i + 1) % count]) for i in range(count)]
    return right, [(b, a) for a, b in right]


def ring_place(axis):
    count = lax.axis_size(axis)
    order = ring_order(count)
    places = [0] * count
    for place, member in enumerate(order):
        places[member] = place
    place = jnp.asarray(places, jnp.int32)[lax.axis_index(axis)]

    def member_at(distance):
        return jnp.asarray(order, jnp.int32)[lax.rem(place + distance + count, count)]

    return member_at


def uses_ring(axis):
    count = lax.axis_size(axis)
    return count % 2 == 0 and 4 <= count <= RING_LIMIT


def gather_rows(block, axis):
    count = lax.axis_size(axis)
    if not uses_ring(axis):
        return lax.all_gather(block, axis, axis=0, tiled=True)
    right, left = ring_links(count)
    member_at = ring_place(axis)
    rows, half = block.shape[0], block.shape[0] // 2
    whole = jnp.zeros((count * rows,) + block.shape[1:], block.dtype)
    columns = (0,) * (block.ndim - 1)

    def put(whole, piece, distance, shift=0):
        return lax.dynamic_update_slice(
            whole, piece, (member_at(distance) * rows + shift,) + columns
        )

    whole = put(whole, block, 0)
    going_right = going_left = block
    for hop in range(1, count // 2):
        going_right = lax.ppermute(going_right, axis, right)
        going_left = lax.ppermute(going_left, axis, left)
        whole = put(whole, going_right, -hop)
        whole = put(whole, going_left, hop)
    first = lax.ppermute(going_right[:half], axis, right)
    second = lax.ppermute(going_left[half:], axis, left)
    whole = put(whole, first, count // 2)
    return put(whole, second, count // 2, half)


def scatter_rows(terms, axis):
    count = lax.axis_size(axis)
    if not uses_ring(axis):
        return lax.psum_scatter(terms.astype(f32), axis, scatter_dimension=0, tiled=True)
    right, left = ring_links(count)
    member_at = ring_place(axis)
    rows = terms.shape[0] // count
    half = rows // 2

    def term(distance):
        return lax.dynamic_slice_in_dim(terms, member_at(distance) * rows, rows, 0).astype(f32)

    far = term(count // 2).astype(bf16)
    going_right = lax.ppermute(far[:half], axis, right)
    going_left = lax.ppermute(far[half:], axis, left)
    for distance in range(count // 2 - 1, 0, -1):
        to_right, to_left = term(distance), term(-distance)
        if distance == count // 2 - 1:
            to_right = jnp.concatenate([to_right[:half] + going_right, to_right[half:]])
            to_left = jnp.concatenate([to_left[:half], to_left[half:] + going_left])
        else:
            to_right, to_left = to_right + going_right, to_left + going_left
        going_right = lax.ppermute(to_right.astype(bf16), axis, right)
        going_left = lax.ppermute(to_left.astype(bf16), axis, left)
    return term(0) + going_right + going_left


def swapped(value, axis, flip):
    count = lax.axis_size(axis)
    return lax.ppermute(value, axis, [(i, i ^ flip) for i in range(count)])


def summed(value, axis):
    count = lax.axis_size(axis)
    if count <= 8:
        parts = [value] + [swapped(value, axis, flip) for flip in range(1, count)]
        while len(parts) > 1:
            parts = [parts[i] + parts[i + 1] for i in range(0, len(parts), 2)]
        return parts[0]
    return summed_in_steps(value, axis)


def summed_in_steps(value, axis):
    flip = 1
    while flip < lax.axis_size(axis):
        value = value + swapped(value, axis, flip)
        flip *= 2
    return value


def placed(parts, axis):
    count = lax.axis_size(axis)
    me = lax.axis_index(axis)
    whole = jnp.zeros((count,) + parts[0].shape, parts[0].dtype)
    for flip, part in enumerate(parts):
        whole = lax.dynamic_update_index_in_dim(whole, part, lax.bitwise_xor(me, flip), 0)
    return whole


def spread(value, axis):
    count = lax.axis_size(axis)
    parts = [value]
    flip = count // 2
    known = {0: value}
    while flip:
        fresh = {k ^ flip: swapped(v, axis, flip) for k, v in known.items()}
        known.update(fresh)
        flip //= 2
    parts = [known[k] for k in range(count)]
    return placed(parts, axis)


def spread_small(value, axis):
    count = lax.axis_size(axis)
    return placed([value] + [swapped(value, axis, k) for k in range(1, count)], axis)


def exchanged(blocks, axis):
    count = lax.axis_size(axis)
    me = lax.axis_index(axis)

    def block_for(flip):
        return lax.dynamic_index_in_dim(blocks, lax.bitwise_xor(me, flip), 0, False)

    return placed(
        [block_for(0)] + [swapped(block_for(k), axis, k) for k in range(1, count)], axis
    )


def halved(blocks, axis):
    count = lax.axis_size(axis)
    me = lax.axis_index(axis)
    held = {
        k: lax.dynamic_index_in_dim(blocks, lax.bitwise_xor(me, k), 0, False)
        for k in range(count)
    }
    flip = 1
    while flip < count:
        kept = {}
        for k in sorted(held):
            if k & flip:
                continue
            arrived = swapped(held[k ^ flip].astype(bf16), axis, flip)
            kept[k] = held[k].astype(f32) + arrived
        held = kept
        flip *= 2
    return held[0]


def dot_rows(a, b):
    return lax.dot_general(a, b, (((1,), (0,)), ((), ())), preferred_element_type=f32)


def dot_lanes(a, b):
    return lax.dot_general(a, b, (((1,), (1,)), ((), ())), preferred_element_type=f32)


def head_lanes(columns, base):
    rows = columns.shape[0]
    full = [
        jnp.broadcast_to(columns[:, base + j : base + j + 1], (rows, PAIR)) for j in range(GROUP)
    ]
    first = lax.broadcasted_iota(jnp.int32, (rows, PAIR), 1) < HEAD_DIM
    lanes = jnp.concatenate(
        [jnp.where(first, full[i], full[i + 1]) for i in range(0, GROUP, 2)], axis=1
    )
    return full, lanes


def stacked_heads(values, block_mask):
    return jnp.concatenate([values] * GROUP, axis=0) * block_mask


def filtered(window, taps, bias, rows):
    pre = bias + taps[CONV - 1 : CONV] * window[8 : 8 + rows]
    for k in range(CONV - 1):
        pre = pre + taps[k : k + 1] * window[5 + k : 5 + k + rows]
    return pre


def scan_forward_kernel(
    x_ref, taps_ref, bias_ref, mask_ref, skip_ref, column_ref, row_ref, key_ref, query_ref,
    key_t_ref, block_ref, y_ref, states_ref, padded, state,
):
    length = x_ref.shape[0]
    rows = SPAN
    mask = mask_ref[...]
    padded[0:8, :] = jnp.zeros((8, LANES), f32)
    padded[8 : 8 + length, :] = x_ref[...] * mask
    state[...] = jnp.zeros_like(state)
    taps, bias, skip = taps_ref[...], bias_ref[...], skip_ref[...]
    causal = lax.broadcasted_iota(jnp.int32, (rows, rows), 0) >= lax.broadcasted_iota(
        jnp.int32, (rows, rows), 1
    )

    def chunk(c, carry):
        start = pl.multiple_of(c * rows, rows)
        here = pl.ds(start, rows)
        pre = filtered(padded[pl.ds(start, rows + 8), :], taps, bias, rows)
        values = pre * jax.nn.sigmoid(pre) * mask
        columns = column_ref[here, :]
        log_full, log_lanes = head_lanes(columns, 0)
        step_lanes = head_lanes(columns, GROUP)[1]
        weighted = step_lanes * values
        weighted_low = weighted.astype(bf16)
        keys, queries, keys_t = key_ref[here, :], query_ref[here, :], key_t_ref[:, here]
        inner = dot_lanes(queries, keys)
        mixing = jnp.concatenate(
            [
                (
                    jnp.where(causal, jnp.exp(log_full[j] - row_ref[j : j + 1, here]), 0.0)
                    * inner
                ).astype(bf16)
                for j in range(GROUP)
            ],
            axis=1,
        )
        state_now = state[...]
        state_low = state_now.astype(bf16)
        states_ref[pl.ds(c, 1)] = state_low[None]
        y = dot_rows(mixing, stacked_heads(weighted_low, block_ref[...]))
        y = y + jnp.exp(log_lanes) * dot_rows(queries, state_low)
        y_ref[here, :] = y + skip * values
        log_last = log_lanes[rows - 1 : rows, :]
        tail = (weighted * jnp.exp(log_last - log_lanes)).astype(bf16)
        state[...] = jnp.exp(log_last) * state_now + dot_rows(keys_t, tail)
        return carry

    lax.fori_loop(0, length // rows, chunk, 0)


def scan_backward_kernel(
    x_ref, taps_ref, bias_ref, mask_ref, skip_ref, column_ref, row_ref, key_ref, query_ref,
    query_t_ref, block_ref, pick_ref, grad_ref, states_ref,
    x_grad_ref, key_grad_ref, query_grad_ref, sums_ref, rest_ref, channel_ref,
    padded, following, state_back, inner_grad,
):
    length = x_ref.shape[0]
    rows = SPAN
    chunks = length // rows
    group = pl.program_id(0)
    mask = mask_ref[...]
    padded[0:8, :] = jnp.zeros((8, LANES), f32)
    padded[8 : 8 + length, :] = x_ref[...] * mask
    following[...] = jnp.zeros_like(following)
    state_back[...] = jnp.zeros_like(state_back)
    channel_ref[...] = jnp.zeros_like(channel_ref)

    @pl.when(group == 0)
    def _():
        key_grad_ref[...] = jnp.zeros_like(key_grad_ref)
        query_grad_ref[...] = jnp.zeros_like(query_grad_ref)
        inner_grad[...] = jnp.zeros_like(inner_grad)
        sums_ref[...] = jnp.zeros_like(sums_ref)

    taps, bias, skip = taps_ref[...], bias_ref[...], skip_ref[...]
    row_at = lax.broadcasted_iota(jnp.int32, (rows, rows), 0)
    lane_at = lax.broadcasted_iota(jnp.int32, (rows, rows), 1)
    causal, causal_t = row_at >= lane_at, lane_at >= row_at

    def chunk(lap, carry):
        c = chunks - 1 - lap
        start = pl.multiple_of(c * rows, rows)
        here = pl.ds(start, rows)
        window = padded[pl.ds(start, rows + 8), :]
        pre = filtered(window, taps, bias, rows)
        gate = jax.nn.sigmoid(pre)
        values = pre * gate * mask
        columns = column_ref[here, :]
        log_full, log_lanes = head_lanes(columns, 0)
        step_lanes = head_lanes(columns, GROUP)[1]
        weighted = step_lanes * values
        weighted_low = weighted.astype(bf16)
        keys, queries, queries_t = key_ref[here, :], query_ref[here, :], query_t_ref[:, here]
        grad_low = grad_ref[here, :]
        grad = grad_low.astype(f32)
        inner, inner_t = dot_lanes(queries, keys), dot_lanes(keys, queries)
        blocks = block_ref[...]
        weighted_blocks = stacked_heads(weighted_low, blocks)
        grad_blocks = stacked_heads(grad_low, blocks)
        mixing_grad = dot_lanes(grad_low, weighted_blocks)
        mixing, mixing_t, inner_sum = [], [], jnp.zeros((rows, rows), f32)
        for j in range(GROUP):
            log_row = row_ref[j : j + 1, here]
            decay = jnp.where(causal, jnp.exp(log_full[j] - log_row), 0.0)
            decay_t = jnp.where(causal_t, jnp.exp(log_row - log_full[j]), 0.0)
            mixing.append((decay * inner).astype(bf16))
            mixing_t.append((decay_t * inner_t).astype(bf16))
            inner_sum = inner_sum + decay * mixing_grad[:, j * rows : (j + 1) * rows]
        inner_grad[pl.ds(c, 1)] = inner_grad[pl.ds(c, 1)] + inner_sum[None]
        y = dot_rows(jnp.concatenate(mixing, axis=1), weighted_blocks)
        state_low = states_ref[pl.ds(c, 1)][0]
        entry = jnp.exp(log_lanes)
        y = y + entry * dot_rows(queries, state_low)
        inside = dot_rows(jnp.concatenate(mixing_t, axis=1), grad_blocks)
        back = state_back[...]
        back_low = back.astype(bf16)
        log_last = log_lanes[rows - 1 : rows, :]
        tail = jnp.exp(log_last - log_lanes)
        outside = tail * dot_rows(keys, back_low)
        entry_grad = (grad * entry).astype(bf16)
        tail_low = (weighted * tail).astype(bf16)
        query_grad_ref[here, :] = query_grad_ref[here, :] + dot_lanes(entry_grad, state_low)
        key_grad_ref[here, :] = key_grad_ref[here, :] + dot_lanes(tail_low, back_low)
        last = jnp.exp(log_last)
        rest_ref[pl.ds(c, 1)] = (
            last * jnp.sum(state_low.astype(f32) * back, axis=0, keepdims=True)
        )[None]
        state_back[...] = last * back + dot_rows(queries_t, entry_grad)
        weighted_grad = inside + outside
        first = grad * y - weighted_low.astype(f32) * inside
        first_high = first.astype(bf16)
        first_rest = (first - first_high.astype(f32)).astype(bf16)
        sums_ref[here, :] = sums_ref[here, :] + (
            dot_rows(first_high, pick_ref[0])
            + dot_rows(first_rest, pick_ref[0])
            + dot_rows((weighted * outside).astype(bf16), pick_ref[1])
            + dot_rows((values * weighted_grad).astype(bf16), pick_ref[2])
        )
        values_grad = step_lanes * weighted_grad + skip * grad
        pre_grad = values_grad * mask * (gate * (1.0 + pre * (1.0 - gate)))
        channel_ref[CONV : CONV + 1, :] += jnp.sum(pre_grad, axis=0, keepdims=True)
        channel_ref[CONV + 1 : CONV + 2, :] += jnp.sum(grad * values, axis=0, keepdims=True)
        for k in range(CONV):
            channel_ref[k : k + 1, :] += jnp.sum(
                pre_grad * window[5 + k : 5 + k + rows], axis=0, keepdims=True
            )
        ahead = jnp.concatenate([pre_grad, following[...]], axis=0)
        following[...] = pre_grad[0:8]
        x_grad = taps[CONV - 1 : CONV] * ahead[0:rows]
        for k in range(CONV - 1):
            x_grad = x_grad + taps[k : k + 1] * ahead[CONV - 1 - k : CONV - 1 - k + rows]
        x_grad_ref[here, :] = (x_grad * mask).astype(bf16)
        return carry

    lax.fori_loop(0, chunks, chunk, 0)

    @pl.when(group == pl.num_programs(0) - 1)
    def _():
        def finish(c, carry):
            here = pl.ds(pl.multiple_of(c * rows, rows), rows)
            inner_low = inner_grad[pl.ds(c, 1)][0].astype(bf16)
            query_grad_ref[here, :] = query_grad_ref[here, :] + dot_rows(
                inner_low, key_ref[here, :]
            )
            key_grad_ref[here, :] = key_grad_ref[here, :] + lax.dot_general(
                inner_low, query_ref[here, :], (((0,), (0,)), ((), ())),
                preferred_element_type=f32,
            )
            return carry

        lax.fori_loop(0, chunks, finish, 0)


def block_mask():
    row = jnp.arange(GROUP * SPAN)[:, None] // SPAN
    lane = jnp.arange(LANES)[None, :] // HEAD_DIM
    return (row == lane).astype(bf16)


def pick_masks(groups):
    lane = jnp.arange(LANES)[:, None] // HEAD_DIM
    target = jnp.arange(PAIR)[None, :]
    return jnp.stack(
        [
            (target == (kind * groups + group) * GROUP + lane).astype(bf16)
            for group in range(groups)
            for kind in range(3)
        ]
    )


def whole_spec():
    return pl.BlockSpec(memory_space=pltpu.VMEM)


def lane_spec(rows):
    return pl.BlockSpec((rows, LANES), lambda g: (0, g))


def head_specs(length):
    return [
        lane_spec(length),
        lane_spec(CONV),
        lane_spec(1),
        lane_spec(1),
        lane_spec(1),
        pl.BlockSpec((length, PAIR), lambda g: (0, g)),
        pl.BlockSpec((8, length), lambda g: (g, 0)),
        whole_spec(),
        whole_spec(),
        whole_spec(),
        whole_spec(),
    ]


def scan_forward(x, taps, bias, mask, skip, columns, rows, keys, queries, keys_t):
    length, width = x.shape
    chunks = length // SPAN
    return pl.pallas_call(
        scan_forward_kernel,
        grid=(width // LANES,),
        in_specs=head_specs(length),
        out_specs=[
            lane_spec(length),
            pl.BlockSpec((chunks, STATE, LANES), lambda g: (0, 0, g)),
        ],
        out_shape=[
            jax.ShapeDtypeStruct((length, width), f32),
            jax.ShapeDtypeStruct((chunks, STATE, width), bf16),
        ],
        scratch_shapes=[pltpu.VMEM((length + 8, LANES), f32), pltpu.VMEM((STATE, LANES), f32)],
        compiler_params=pltpu.CompilerParams(vmem_limit_bytes=VMEM_BYTES),
        cost_estimate=pl.CostEstimate(
            flops=10_000_000_000, bytes_accessed=12_000_000, transcendentals=4_000_000
        ),
        name="scan_forward",
    )(x, taps, bias, mask, skip, columns, rows, keys, queries, keys_t, block_mask())


def scan_backward(
    x, taps, bias, mask, skip, columns, rows, keys, queries, queries_t, grad, states
):
    length, width = x.shape
    chunks = length // SPAN
    groups = width // LANES
    same = lambda g: (0, 0)
    return pl.pallas_call(
        scan_backward_kernel,
        grid=(groups,),
        in_specs=head_specs(length)
        + [
            pl.BlockSpec((3, LANES, PAIR), lambda g: (g, 0, 0)),
            lane_spec(length),
            pl.BlockSpec((chunks, STATE, LANES), lambda g: (0, 0, g)),
        ],
        out_specs=[
            lane_spec(length),
            pl.BlockSpec((length, STATE), same),
            pl.BlockSpec((length, STATE), same),
            pl.BlockSpec((length, PAIR), same),
            pl.BlockSpec((chunks, 1, LANES), lambda g: (0, 0, g)),
            lane_spec(8),
        ],
        out_shape=[
            jax.ShapeDtypeStruct((length, width), bf16),
            jax.ShapeDtypeStruct((length, STATE), f32),
            jax.ShapeDtypeStruct((length, STATE), f32),
            jax.ShapeDtypeStruct((length, PAIR), f32),
            jax.ShapeDtypeStruct((chunks, 1, width), f32),
            jax.ShapeDtypeStruct((8, width), f32),
        ],
        scratch_shapes=[
            pltpu.VMEM((length + 8, LANES), f32),
            pltpu.VMEM((8, LANES), f32),
            pltpu.VMEM((STATE, LANES), f32),
            pltpu.VMEM((chunks, SPAN, SPAN), f32),
        ],
        compiler_params=pltpu.CompilerParams(vmem_limit_bytes=VMEM_BYTES),
        cost_estimate=pl.CostEstimate(
            flops=30_000_000_000, bytes_accessed=16_000_000, transcendentals=8_000_000
        ),
        name="scan_backward",
    )(
        x, taps, bias, mask, skip, columns, rows, keys, queries, queries_t, block_mask(),
        pick_masks(groups), grad, states,
    )


def gate_kernel(
    normed_ref, weight_ref, cotangent_ref, out_ref, y_ref, gain_ref, mask_ref,
    gate_part_ref, gated_grad_ref, stats_ref,
):
    gate_part = dot_rows(normed_ref[...], weight_ref[...]) * mask_ref[...]
    gated_grad = dot_lanes(cotangent_ref[...], out_ref[...])
    gate_part_ref[...] = gate_part
    gated_grad_ref[...] = gated_grad
    gated = y_ref[...] * (gate_part * jax.nn.sigmoid(gate_part))
    squares = jnp.sum(gated * gated, axis=1, keepdims=True)
    products = jnp.sum(gated * gated_grad * gain_ref[...], axis=1, keepdims=True)
    lane = lax.broadcasted_iota(jnp.int32, stats_ref.shape, 1)
    stats_ref[...] = jnp.where(lane == 0, squares, products)


def gate_forward(normed, weight, cotangent, out_weight, y, gain, mask):
    length, width = y.shape
    rows = lambda lanes: pl.BlockSpec((ROW_TILE, lanes), lambda i: (i, 0))
    return pl.pallas_call(
        gate_kernel,
        grid=(length // ROW_TILE,),
        in_specs=[
            rows(D), whole_spec(), rows(D), whole_spec(), rows(width), whole_spec(), whole_spec(),
        ],
        out_specs=[rows(width), rows(width), rows(PAIR)],
        out_shape=[
            jax.ShapeDtypeStruct((length, width), f32),
            jax.ShapeDtypeStruct((length, width), f32),
            jax.ShapeDtypeStruct((length, PAIR), f32),
        ],
        compiler_params=pltpu.CompilerParams(vmem_limit_bytes=VMEM_BYTES),
        cost_estimate=pl.CostEstimate(
            flops=9_000_000_000, bytes_accessed=28_000_000, transcendentals=1_000_000
        ),
        name="gate_forward",
    )(normed, weight, cotangent, out_weight, y, gain, mask)


def norm_back_kernel(
    y_ref, gate_part_ref, gated_grad_ref, scale_ref, gain_ref, mask_ref,
    gated_ref, y_grad_ref, gate_grad_ref, gain_grad_ref,
):
    @pl.when(pl.program_id(0) == 0)
    def _():
        gain_grad_ref[...] = jnp.zeros_like(gain_grad_ref)

    y, gate_part, gated_grad = y_ref[...], gate_part_ref[...], gated_grad_ref[...]
    inverse, pull = scale_ref[:, 0:1], scale_ref[:, 1:2]
    gate = jax.nn.sigmoid(gate_part)
    silu = gate_part * gate
    gated = y * silu
    scaled = gated * inverse
    gain = gain_ref[...]
    gated_ref[...] = (scaled * gain).astype(bf16)
    gain_grad_ref[0:1, :] += jnp.sum(gated_grad * scaled, axis=0, keepdims=True)
    back = inverse * (gated_grad * gain) - gated * pull
    y_grad_ref[...] = (back * silu).astype(bf16)
    gate_grad_ref[...] = (
        back * y * (gate * (1.0 + gate_part * (1.0 - gate))) * mask_ref[...]
    ).astype(bf16)


def norm_back(y, gate_part, gated_grad, scales, gain, mask):
    length, width = y.shape
    rows = lambda lanes: pl.BlockSpec((ROW_TILE, lanes), lambda i: (i, 0))
    return pl.pallas_call(
        norm_back_kernel,
        grid=(length // ROW_TILE,),
        in_specs=[rows(width), rows(width), rows(width), rows(2), whole_spec(), whole_spec()],
        out_specs=[
            rows(width), rows(width), rows(width), pl.BlockSpec((8, width), lambda i: (0, 0)),
        ],
        out_shape=[
            jax.ShapeDtypeStruct((length, width), bf16),
            jax.ShapeDtypeStruct((length, width), bf16),
            jax.ShapeDtypeStruct((length, width), bf16),
            jax.ShapeDtypeStruct((8, width), f32),
        ],
        compiler_params=pltpu.CompilerParams(vmem_limit_bytes=VMEM_BYTES),
        cost_estimate=pl.CostEstimate(
            flops=30_000_000, bytes_accessed=18_000_000, transcendentals=1_000_000
        ),
        name="norm_back",
    )(y, gate_part, gated_grad, scales, gain, mask)


MESH = pl.DeviceIdType.MESH


class Ring:
    def __init__(self):
        self.count = lax.axis_size("dp")
        self.far = self.count // 2
        me = lax.axis_index("dp")
        odd = lax.rem(me, 2)
        self.me = me
        self.place = (1 - odd) * lax.div(me, 2) + odd * lax.div(2 * self.count - 1 - me, 2)

    def member(self, distance):
        n = self.count
        place = lax.rem(self.place + distance + n, n)
        back = lax.div(place, n // 2)
        return (1 - back) * 2 * place + back * (2 * n - 1 - 2 * place)

    def target(self, way):
        return {"dp": self.member(1 if way == 0 else -1)}


def partner(flip):
    f = lax.axis_index("fsdp")
    return (f, f + 1 - 2 * lax.rem(f, 2), lax.rem(f + 2, 4), 3 - f)[flip]


def greet(targets):
    barrier = pltpu.get_barrier_semaphore()
    for target in targets:
        pl.semaphore_signal(barrier, inc=1, device_id=target, device_id_type=MESH)
    pl.semaphore_wait(barrier, len(targets))


def row_slice(ref, start, size):
    return ref.at[pl.ds(pl.multiple_of(start, 16), size)]


class RingGather:
    def __init__(self, ring, wholes, send, recv):
        self.ring, self.wholes, self.send, self.recv = ring, wholes, send, recv

    @staticmethod
    def semaphores(parts, count):
        return pltpu.SemaphoreType.DMA((parts * 4 * (count // 2),))

    def copy(self, part, way, half, hop):
        whole = self.wholes[part]
        rows = whole.shape[0] // self.ring.count
        size = rows // 2
        owner = self.ring.member(-hop if way == 0 else hop)
        place = row_slice(whole, owner * rows + half * size, size)
        at = ((part * 2 + way) * 2 + half) * self.ring.far + hop
        return pltpu.make_async_remote_copy(
            place, place, self.send.at[at], self.recv.at[at],
            device_id=self.ring.target(way), device_id_type=MESH,
        )

    def pieces(self, hop):
        return [
            (way, half)
            for half in (0, 1)
            for way in (0, 1)
            if hop < self.ring.far - 1 or half == way
        ]

    def start(self, part, hop):
        for way, half in self.pieces(hop):
            if hop:
                self.copy(part, way, half, hop - 1).wait_recv()
            self.copy(part, way, half, hop).start()

    def finish(self, part):
        last = self.ring.far - 1
        for way, half in self.pieces(last):
            self.copy(part, way, half, last).wait_recv()
            if last:
                self.copy(part, way, 1 - half, last - 1).wait_recv()
        for hop in range(last + 1):
            for way, half in self.pieces(hop):
                self.copy(part, way, half, hop).wait_send()


class RingScatter:
    def __init__(self, ring, held, arrived, send, recv):
        self.ring, self.held, self.arrived = ring, held, arrived
        self.send, self.recv = send, recv

    @staticmethod
    def scratch(count, rows, columns):
        hops = count // 2
        return [
            pltpu.VMEM((2, 2, rows, columns), bf16),
            pltpu.VMEM((2, hops, rows, columns), bf16),
            pltpu.SemaphoreType.DMA((2 * hops,)),
            pltpu.SemaphoreType.DMA((2 * hops,)),
        ]

    def copy(self, way, hop):
        rows = self.held.shape[2]
        size = rows // 2 if hop == 0 else rows
        at = way * self.ring.far + hop
        return pltpu.make_async_remote_copy(
            self.held.at[way, hop % 2, pl.ds(0, size)],
            self.arrived.at[way, hop, pl.ds(0, size)],
            self.send.at[at], self.recv.at[at],
            device_id=self.ring.target(way), device_id_type=MESH,
        )

    def owner(self, way, hop):
        distance = self.ring.far - hop
        return self.ring.member(distance if way == 0 else -distance)

    def start(self, hop, term):
        rows = self.held.shape[2]
        half = rows // 2
        if hop == 0:
            value = term(self.owner(0, 0)).astype(bf16)
            self.held[0, 0, 0:half] = value[:half]
            self.copy(0, 0).start()
            self.held[1, 0, 0:half] = value[half:]
            self.copy(1, 0).start()
            return
        for way in (0, 1):
            value = term(self.owner(way, hop))
            self.copy(way, hop - 1).wait_recv()
            slot = hop % 2
            if hop >= 2:
                self.copy(way, hop - 2).wait_send()
            if hop == 1:
                low = slice(way * half, (way + 1) * half)
                rest = slice((1 - way) * half, (2 - way) * half)
                self.held[way, slot, low] = (
                    value[low] + self.arrived[way, 0, 0:half].astype(f32)
                ).astype(bf16)
                self.held[way, slot, rest] = value[rest].astype(bf16)
            else:
                self.held[way, slot] = (
                    value + self.arrived[way, hop - 1].astype(f32)
                ).astype(bf16)
            self.copy(way, hop).start()

    def finish(self, term):
        last = self.ring.far - 1
        value = term(self.ring.me)
        for way in (0, 1):
            self.copy(way, last).wait_recv()
            value = value + self.arrived[way, last].astype(f32)
        for hop in range(last - 1, last + 1):
            for way in (0, 1):
                self.copy(way, hop).wait_send()
        return value


def gather_first_kernel(
    small_cut, x_cut, normed_own, cotangent_own, small, x, normed, cotangent,
    local_sem, swap_send, swap_recv, token_send, token_recv, ring_send, ring_recv,
):
    ring = Ring()
    d, f = ring.me, lax.axis_index("fsdp")
    greet([{"fsdp": partner(k)} for k in (1, 2, 3)] + [ring.target(0), ring.target(1)])
    cuts, wholes = [small_cut, x_cut], [small, x]
    sub = small_cut.shape[1]
    tokens = normed_own.shape[0]
    local = [
        pltpu.make_async_copy(
            cut.at[f], row_slice(whole, (4 * d + f) * sub, sub), local_sem.at[i]
        )
        for i, (cut, whole) in enumerate(zip(cuts, wholes))
    ] + [
        pltpu.make_async_copy(own, row_slice(whole, f * tokens, tokens), local_sem.at[2 + i])
        for i, (own, whole) in enumerate([(normed_own, normed), (cotangent_own, cotangent)])
    ]
    swaps = [
        [
            pltpu.make_async_remote_copy(
                cut.at[partner(k)], row_slice(whole, (4 * d + f) * sub, sub),
                swap_send.at[3 * i + k - 1], swap_recv.at[3 * i + k - 1],
                device_id={"fsdp": partner(k)}, device_id_type=MESH,
            )
            for k in (2, 3, 1)
        ]
        for i, (cut, whole) in enumerate(zip(cuts, wholes))
    ]

    def token_copies(i, own, whole):
        def one(at, source, owner, k):
            return pltpu.make_async_remote_copy(
                source, row_slice(whole, owner * tokens, tokens),
                token_send.at[3 * i + at], token_recv.at[3 * i + at],
                device_id={"fsdp": partner(k)}, device_id_type=MESH,
            )

        far = partner(2)
        return (
            one(0, own, f, 2), one(1, own, f, 1),
            one(2, row_slice(whole, far * tokens, tokens), far, 1),
        )

    normed_copies = token_copies(0, normed_own, normed)
    cotangent_copies = token_copies(1, cotangent_own, cotangent)
    for copy in local:
        copy.start()
    for row in swaps:
        for copy in row:
            copy.start()
    for copy in normed_copies[:2]:
        copy.start()
    rings = RingGather(ring, wholes, ring_send, ring_recv)
    for part in (0, 1):
        local[part].wait()
        for copy in swaps[part]:
            copy.wait_recv()
        rings.start(part, 0)
    for hop in range(1, ring.far):
        rings.start(0, hop)
        rings.start(1, hop)
        if hop == 1:
            normed_copies[0].wait_recv()
            normed_copies[2].start()
            for copy in cotangent_copies[:2]:
                copy.start()
        if hop == ring.far - 1:
            cotangent_copies[0].wait_recv()
            cotangent_copies[2].start()
    rings.finish(0)
    rings.finish(1)
    for copy in local[2:]:
        copy.wait()
    for copies in (normed_copies, cotangent_copies):
        for copy in copies[1:]:
            copy.wait_recv()
        for copy in copies:
            copy.wait_send()
    for row in swaps:
        for copy in row:
            copy.wait_send()


def any_specs(count):
    return [pl.BlockSpec(memory_space=pl.ANY)] * count


def gather_first(small_cut, x_cut, normed_own, cotangent_own):
    count, members = lax.axis_size("dp"), lax.axis_size("fsdp")
    rows = count * members * small_cut.shape[1]
    tokens = members * normed_own.shape[0]
    return pl.pallas_call(
        gather_first_kernel,
        in_specs=any_specs(4),
        out_specs=any_specs(4),
        out_shape=[
            jax.ShapeDtypeStruct((rows, small_cut.shape[2]), bf16),
            jax.ShapeDtypeStruct((rows, x_cut.shape[2]), bf16),
            jax.ShapeDtypeStruct((tokens, D), bf16),
            jax.ShapeDtypeStruct((tokens, D), bf16),
        ],
        scratch_shapes=[
            pltpu.SemaphoreType.DMA((4,)),
            pltpu.SemaphoreType.DMA((6,)),
            pltpu.SemaphoreType.DMA((6,)),
            pltpu.SemaphoreType.DMA((6,)),
            pltpu.SemaphoreType.DMA((6,)),
            RingGather.semaphores(2, count),
            RingGather.semaphores(2, count),
        ],
        compiler_params=pltpu.CompilerParams(collective_id=0, has_side_effects=True),
        name="gather_first",
    )(small_cut, x_cut, normed_own, cotangent_own)


def scan_gather_kernel(
    normed_ref, weight_ref, taps_ref, bias_ref, mask_ref, skip_ref, column_ref, row_ref, key_ref,
    query_ref, key_t_ref, block_ref, gate_cut, out_own,
    x_ref, y_ref, states_ref, gate_all, out_all,
    padded, state, local_sem, swap_send, swap_recv, ring_send, ring_recv,
):
    ring = Ring()
    d, f = ring.me, lax.axis_index("fsdp")
    step = pl.program_id(0)
    rings = RingGather(ring, [gate_all, out_all], ring_send, ring_recv)
    sub, rows = gate_cut.shape[1], out_own.shape[0]
    local = [
        pltpu.make_async_copy(
            gate_cut.at[f], row_slice(gate_all, (4 * d + f) * sub, sub), local_sem.at[0]
        ),
        pltpu.make_async_copy(out_own, row_slice(out_all, d * rows, rows), local_sem.at[1]),
    ]
    swaps = [
        pltpu.make_async_remote_copy(
            gate_cut.at[partner(k)], row_slice(gate_all, (4 * d + f) * sub, sub),
            swap_send.at[k - 1], swap_recv.at[k - 1],
            device_id={"fsdp": partner(k)}, device_id_type=MESH,
        )
        for k in (2, 3, 1)
    ]

    @pl.when(step == 0)
    def _():
        greet([{"fsdp": partner(k)} for k in (1, 2, 3)] + [ring.target(0), ring.target(1)])
        for copy in local + swaps:
            copy.start()
        local[1].wait()
        rings.start(1, 0)
        local[0].wait()
        for copy in swaps:
            copy.wait_recv()
        rings.start(0, 0)

    for hop in range(1, ring.far):
        @pl.when(step == hop)
        def _(hop=hop):
            rings.start(1, hop)
            rings.start(0, hop)

    x_ref[...] = dot_rows(normed_ref[...], weight_ref[...])
    scan_forward_kernel(
        x_ref, taps_ref, bias_ref, mask_ref, skip_ref, column_ref, row_ref, key_ref, query_ref,
        key_t_ref, block_ref, y_ref, states_ref, padded, state,
    )

    @pl.when(step == pl.num_programs(0) - 1)
    def _():
        rings.finish(1)
        rings.finish(0)
        for copy in swaps:
            copy.wait_send()


def scan_gather(
    normed, weight, taps, bias, mask, skip, columns, rows, keys, queries, keys_t, gate_cut, out_own
):
    length = normed.shape[0]
    width = weight.shape[1]
    chunks = length // SPAN
    count = lax.axis_size("dp")
    assert width // LANES == count // 2
    return pl.pallas_call(
        scan_gather_kernel,
        grid=(width // LANES,),
        in_specs=[whole_spec(), lane_spec(D)] + head_specs(length)[1:] + any_specs(2),
        out_specs=[
            lane_spec(length),
            lane_spec(length),
            pl.BlockSpec((chunks, STATE, LANES), lambda g: (0, 0, g)),
        ]
        + any_specs(2),
        out_shape=[
            jax.ShapeDtypeStruct((length, width), f32),
            jax.ShapeDtypeStruct((length, width), f32),
            jax.ShapeDtypeStruct((chunks, STATE, width), bf16),
            jax.ShapeDtypeStruct((D, width), bf16),
            jax.ShapeDtypeStruct((count * out_own.shape[0], D), bf16),
        ],
        scratch_shapes=[
            pltpu.VMEM((length + 8, LANES), f32),
            pltpu.VMEM((STATE, LANES), f32),
            pltpu.SemaphoreType.DMA((2,)),
            pltpu.SemaphoreType.DMA((3,)),
            pltpu.SemaphoreType.DMA((3,)),
            RingGather.semaphores(2, count),
            RingGather.semaphores(2, count),
        ],
        compiler_params=pltpu.CompilerParams(
            collective_id=1, has_side_effects=True, vmem_limit_bytes=VMEM_BYTES
        ),
        name="scan_gather",
    )(
        normed, weight, taps, bias, mask, skip, columns, rows, keys, queries, keys_t, block_mask(),
        gate_cut, out_own,
    )


def total_squares(value):
    return jnp.sum(jnp.sum(value * value, axis=0, keepdims=True), axis=1, keepdims=True)


def scan_scatter_kernel(
    x_ref, taps_ref, bias_ref, mask_ref, skip_ref, column_ref, row_ref, key_ref, query_ref,
    query_t_ref, block_ref, pick_ref, grad_ref, states_ref,
    normed_t_ref, gate_grad_ref, gated_ref, gated_t_ref, cotangent_ref, weight_ref, tokens_ref,
    x_grad_ref, key_grad_ref, query_grad_ref, sums_ref, rest_ref, channel_ref,
    gate_raw_ref, out_raw_ref, layer_out_ref, squares_ref,
    padded, following, state_back, inner_grad, added, added_out, added_in, added_send, added_recv,
    *ring_scratch,
):
    ring = Ring()
    step = pl.program_id(0)
    steps = pl.num_programs(0)
    gate_ring = RingScatter(ring, *ring_scratch[:4])
    out_ring = RingScatter(ring, *ring_scratch[4:])
    rows_in, rows_out = gate_raw_ref.shape[0], out_raw_ref.shape[0]
    tokens = tokens_ref.shape[0]

    def gate_term(owner):
        here = pl.ds(pl.multiple_of(owner * rows_in, rows_in), rows_in)
        return dot_rows(normed_t_ref[here, :], gate_grad_ref[...])

    def out_term(owner):
        here = pl.ds(pl.multiple_of(owner * rows_out, rows_out), rows_out)
        return dot_rows(gated_t_ref[here, :], cotangent_ref[...])

    def added_block(flip):
        here = pl.ds(pl.multiple_of(partner(flip) * tokens, tokens), tokens)
        return dot_rows(gated_ref[here, :], weight_ref[...])

    def added_copy(i):
        return pltpu.make_async_remote_copy(
            added_out.at[i], added_in.at[i], added_send.at[i], added_recv.at[i],
            device_id={"fsdp": partner(2 if i == 2 else 1)}, device_id_type=MESH,
        )

    @pl.when(step == 0)
    def _():
        greet([{"fsdp": partner(k)} for k in (1, 2)] + [ring.target(0), ring.target(1)])

    for hop in range(ring.far):
        @pl.when(step == hop)
        def _(hop=hop):
            out_ring.start(hop, out_term)
            gate_ring.start(hop, gate_term)

    @pl.when(step == 0)
    def _():
        for i, flip in ((1, 3), (0, 1)):
            added_out[i] = added_block(flip).astype(bf16)
            added_copy(i).start()

    @pl.when(step == 1)
    def _():
        value = added_block(2)
        added_copy(1).wait_recv()
        added_out[2] = (value + added_in[1].astype(f32)).astype(bf16)
        added_copy(2).start()

    @pl.when(step == 2)
    def _():
        added[...] = added_block(0)

    scan_backward_kernel(
        x_ref, taps_ref, bias_ref, mask_ref, skip_ref, column_ref, row_ref, key_ref, query_ref,
        query_t_ref, block_ref, pick_ref, grad_ref, states_ref,
        x_grad_ref, key_grad_ref, query_grad_ref, sums_ref, rest_ref, channel_ref,
        padded, following, state_back, inner_grad,
    )

    @pl.when(step == steps - 1)
    def _():
        added_copy(0).wait_recv()
        added_copy(2).wait_recv()
        layer_out_ref[...] = (
            tokens_ref[...].astype(f32)
            + ((added[...] + added_in[0].astype(f32)) + added_in[2].astype(f32))
        ).astype(bf16)
        for i in range(3):
            added_copy(i).wait_send()
        out_raw = out_ring.finish(out_term)
        out_raw_ref[...] = out_raw
        gate_raw = gate_ring.finish(gate_term)
        gate_raw_ref[...] = gate_raw.astype(bf16)
        squares_ref[...] = jnp.broadcast_to(
            total_squares(out_raw) + total_squares(gate_raw), squares_ref.shape
        )


def scan_scatter(
    x, taps, bias, mask, skip, columns, rows, keys, queries, queries_t, grad, states,
    normed_t, gate_grad, gated, gated_t, cotangent, weight, tokens,
):
    length, width = x.shape
    chunks = length // SPAN
    groups = width // LANES
    count = lax.axis_size("dp")
    assert groups == count // 2
    rows_in, rows_out, own = D // count, width // count, tokens.shape[0]
    same = lambda g: (0, 0)
    return pl.pallas_call(
        scan_scatter_kernel,
        grid=(groups,),
        in_specs=head_specs(length)
        + [
            pl.BlockSpec((3, LANES, PAIR), lambda g: (g, 0, 0)),
            lane_spec(length),
            pl.BlockSpec((chunks, STATE, LANES), lambda g: (0, 0, g)),
        ]
        + [whole_spec()] * 7,
        out_specs=[
            lane_spec(length),
            pl.BlockSpec((length, STATE), same),
            pl.BlockSpec((length, STATE), same),
            pl.BlockSpec((length, PAIR), same),
            pl.BlockSpec((chunks, 1, LANES), lambda g: (0, 0, g)),
            lane_spec(8),
        ]
        + [whole_spec()] * 4,
        out_shape=[
            jax.ShapeDtypeStruct((length, width), bf16),
            jax.ShapeDtypeStruct((length, STATE), f32),
            jax.ShapeDtypeStruct((length, STATE), f32),
            jax.ShapeDtypeStruct((length, PAIR), f32),
            jax.ShapeDtypeStruct((chunks, 1, width), f32),
            jax.ShapeDtypeStruct((8, width), f32),
            jax.ShapeDtypeStruct((rows_in, width), bf16),
            jax.ShapeDtypeStruct((rows_out, D), f32),
            jax.ShapeDtypeStruct((own, D), bf16),
            jax.ShapeDtypeStruct((8, PAIR), f32),
        ],
        scratch_shapes=[
            pltpu.VMEM((length + 8, LANES), f32),
            pltpu.VMEM((8, LANES), f32),
            pltpu.VMEM((STATE, LANES), f32),
            pltpu.VMEM((chunks, SPAN, SPAN), f32),
            pltpu.VMEM((own, D), f32),
            pltpu.VMEM((3, own, D), bf16),
            pltpu.VMEM((3, own, D), bf16),
            pltpu.SemaphoreType.DMA((3,)),
            pltpu.SemaphoreType.DMA((3,)),
        ]
        + RingScatter.scratch(count, rows_in, width)
        + RingScatter.scratch(count, rows_out, D),
        compiler_params=pltpu.CompilerParams(
            collective_id=2, has_side_effects=True, vmem_limit_bytes=VMEM_BYTES
        ),
        name="scan_scatter",
    )(
        x, taps, bias, mask, skip, columns, rows, keys, queries, queries_t, block_mask(),
        pick_masks(groups), grad, states,
        normed_t, gate_grad, gated, gated_t, cotangent, weight, tokens,
    )


def flipped(member, flip):
    return member + flip - 2 * flip * lax.rem(lax.div(member, flip), 2)


def shifted(value, by):
    length = value.shape[1]
    lane = lax.broadcasted_iota(jnp.int32, value.shape, 1)
    if by == 0:
        return value
    if by > 0:
        return jnp.where(lane >= by, pltpu.roll(value, by, 1), 0.0)
    return jnp.where(lane < length + by, pltpu.roll(value, length + by, 1), 0.0)


def last_scatter_kernel(
    x_grad_ref, normed_t_ref, gate_grad_hbm, weight_gate_hbm, weight_x_hbm, weight_small_ref,
    key_grad_ref, query_grad_ref, sums_ref, rest_ref, head_pick_ref, steps_ref, heads_ref,
    shared_part_ref, shared_pre_ref, taps_ref, tokens_ref, cotangent_ref, inverse_ref, gain_ref,
    gate_raw_ref, channel_ref, gate_gain_ref, squares_ref,
    gate_back_ref, x_back_ref, small_back_ref, token_grad_ref, vectors_ref, total_ref,
    gate_grad, weight_gate, weight_x, load_sem,
    shared_own, shared_out, shared_in, swap_send, swap_recv, raw, small_t, small_n,
    kept, back_out, back_in, back_send, back_recv,
    vector_sum, vector_in, vector_send, vector_recv,
    x_out, small_out, return_send, return_recv, local_sem,
    scalar_out, scalar_in, scalar_send, scalar_recv,
    *ring_scratch,
):
    ring = Ring()
    d, f = ring.me, lax.axis_index("fsdp")
    count = ring.count
    x_ring = RingScatter(ring, *ring_scratch[:4])
    small_ring = RingScatter(ring, *ring_scratch[4:])
    loads = [
        pltpu.make_async_copy(source, target, load_sem.at[i])
        for i, (source, target) in enumerate(
            [(gate_grad_hbm, gate_grad), (weight_gate_hbm, weight_gate), (weight_x_hbm, weight_x)]
        )
    ]
    for load in loads:
        load.start()
    near = [{"fsdp": partner(k)} for k in (1, 2, 3)]
    over = [{"dp": lax.rem(d + k, count)} for k in range(1, count)]
    greet(near + over)
    length, shared = x_grad_ref.shape[0], shared_own.shape[1]
    rows, sub = x_out.shape[0], x_back_ref.shape[1]
    tokens = tokens_ref.shape[0]

    def rows_of(owner):
        return pl.ds(pl.multiple_of(owner * rows, rows), rows)

    def x_term(owner):
        return dot_rows(normed_t_ref[rows_of(owner), :], x_grad_ref[...])

    def small_term(owner):
        return dot_lanes(normed_t_ref[rows_of(owner), :], small_t[...])

    def to_partner(k, source, target, send, recv, at):
        return pltpu.make_async_remote_copy(
            source, target, send.at[at], recv.at[at],
            device_id={"fsdp": partner(k)}, device_id_type=MESH,
        )

    def return_copy(part, k):
        source = (gate_raw_ref, x_out, small_out)[part]
        target = (gate_back_ref, x_back_ref, small_back_ref)[part]
        return to_partner(
            k, row_slice(source, partner(k) * sub, sub), target.at[f],
            return_send, return_recv, part * 3 + k - 1,
        )

    def own_copy(part):
        source = (gate_raw_ref, x_out, small_out)[part]
        target = (gate_back_ref, x_back_ref, small_back_ref)[part]
        return pltpu.make_async_copy(
            row_slice(source, f * sub, sub), target.at[f], local_sem.at[part]
        )

    x_ring.start(0, x_term)

    for i, ref in ((0, key_grad_ref), (2, query_grad_ref)):
        turned = ref[...].T
        for j in (0, 1):
            shared_own[i + j] = turned[j * shared : (j + 1) * shared]
            shared_out[i + j] = turned[j * shared : (j + 1) * shared].astype(bf16)

    def shared_copy(k):
        return to_partner(
            k, shared_out.at[partner(k)], shared_in.at[k - 1], swap_send, swap_recv, k - 1
        )

    for k in (2, 3, 1):
        shared_copy(k).start()
    for k in (2, 3, 1):
        return_copy(0, k).start()
    own_copy(0).start()

    at_row = lax.broadcasted_iota(jnp.int32, (SPAN, SPAN), 0)
    at_lane = lax.broadcasted_iota(jnp.int32, (SPAN, SPAN), 1)
    later = (at_lane >= at_row).astype(f32)
    earlier = (at_lane < at_row).astype(f32)
    precise = partial(jnp.dot, precision=highest, preferred_element_type=f32)
    heads = HEADS // 4
    rest = precise(rest_ref[...], head_pick_ref[...])
    decay, head_mask = heads_ref[0:1, :], heads_ref[1:2, :]
    step_bias_grad = jnp.zeros((1, PAIR), f32)
    decay_grad = jnp.zeros((1, PAIR), f32)
    for c in range(length // SPAN):
        here = slice(c * SPAN, (c + 1) * SPAN)
        sums = sums_ref[here, :]
        log_grad = (
            precise(later, sums)
            + pltpu.roll(precise(earlier, sums), PAIR - heads, 1)
            + rest[c : c + 1]
        )
        steps = steps_ref[here, :]
        logits = pltpu.roll(steps, PAIR - heads, 1)
        raw_grad = (decay * log_grad + pltpu.roll(sums, PAIR - 2 * heads, 1)) * jax.nn.sigmoid(
            logits
        )
        step_bias_grad = step_bias_grad + jnp.sum(raw_grad, axis=0, keepdims=True)
        decay_grad = decay_grad + jnp.sum(steps * log_grad, axis=0, keepdims=True)
        raw[here, :] = raw_grad * head_mask
    decay_grad = decay_grad * decay

    x_ring.start(1, x_term)

    for k in (2, 3, 1):
        shared_copy(k).wait_recv()
    part, pre = shared_part_ref[...], shared_pre_ref[...]
    gate = jax.nn.sigmoid(pre)
    pre_grad = shared_own[f]
    for k in (1, 2, 3):
        pre_grad = pre_grad + shared_in[k - 1].astype(f32)
    pre_grad = pre_grad * (gate * (1.0 + pre * (1.0 - gate)))
    shared_grad = jnp.zeros_like(pre_grad)
    lane = lax.broadcasted_iota(jnp.int32, (shared, PAIR), 1)
    shared_sums = jnp.where(lane == CONV, jnp.sum(pre_grad, axis=1, keepdims=True), 0.0)
    for k in range(CONV):
        shift = CONV - 1 - k
        shared_grad = shared_grad + taps_ref[:, k : k + 1] * shifted(pre_grad, -shift)
        shared_sums = shared_sums + jnp.where(
            lane == k, jnp.sum(pre_grad * shifted(part, shift), axis=1, keepdims=True), 0.0
        )
    small_t[0:shared, :] = shared_grad.astype(bf16)
    small_t[shared:, :] = raw[...].T[0 : PAIR - shared].astype(bf16)
    small_n[...] = small_t[...].T
    small_ring.start(0, small_term)

    for load in loads:
        load.wait()

    def back_block(flip):
        here = pl.ds(pl.multiple_of(partner(flip) * tokens, tokens), tokens)
        return (
            dot_lanes(gate_grad[here, :], weight_gate[...])
            + dot_lanes(x_grad_ref[here, :], weight_x[...])
            + dot_lanes(small_n[here, :], weight_small_ref[...])
        )

    def back_copy(i):
        return to_partner(
            2 if i == 2 else 1, back_out.at[i], back_in.at[i], back_send, back_recv, i
        )

    for i, flip in ((1, 3), (0, 1)):
        back_out[i] = back_block(flip).astype(bf16)
        back_copy(i).start()
    value = back_block(2)
    back_copy(1).wait_recv()
    back_out[2] = (value + back_in[1].astype(f32)).astype(bf16)
    back_copy(2).start()
    x_ring.start(2, x_term)
    small_ring.start(1, small_term)
    kept[...] = back_block(0)
    for hop in range(3, ring.far):
        x_ring.start(hop, x_term)
        small_ring.start(hop - 1, small_term)
    back_copy(0).wait_recv()
    back_copy(2).wait_recv()
    inputs, inverse = tokens_ref[...].astype(f32), inverse_ref[...]
    normed_grad = (kept[...] + back_in[0].astype(f32)) + back_in[2].astype(f32)
    pulled = normed_grad * gain_ref[...]
    scaled = inputs * inverse
    input_grad = inverse * (
        pulled - scaled * (jnp.sum(pulled * scaled, axis=1, keepdims=True) / D)
    )
    token_grad_ref[...] = (cotangent_ref[...].astype(f32) + input_grad).astype(bf16)
    gain_grad = jnp.sum(normed_grad * scaled, axis=0, keepdims=True)

    width = vector_sum.shape[1]
    vector_sum[...] = jnp.zeros_like(vector_sum)
    vector_sum[0:1, :] = gate_gain_ref[0:1, :]
    vector_sum[1 : CONV + 3, :] = channel_ref[0 : CONV + 2, :]
    for i in range(D // width):
        vector_sum[CONV + 3 + i : CONV + 4 + i, :] = gain_grad[:, i * width : (i + 1) * width]
    vector_sum[15:16, 0:PAIR] = step_bias_grad
    vector_sum[15:16, PAIR : 2 * PAIR] = decay_grad
    wide = jnp.concatenate([shared_sums, jnp.zeros((PAIR - shared, PAIR), f32)], axis=0)
    vector_sum[16:24, 0:PAIR] = wide.T[0:8]

    def vector_copy(step, flip):
        return pltpu.make_async_remote_copy(
            vector_in.at[step, 0], vector_in.at[step, 1], vector_send.at[step],
            vector_recv.at[step],
            device_id={"dp": flipped(d, flip)}, device_id_type=MESH,
        )

    flips = []
    while 1 << len(flips) < count:
        flips.append(1 << len(flips))
    for step, flip in enumerate(flips):
        vector_in[step, 0] = vector_sum[...]
        vector_copy(step, flip).start()
        if step == 0:
            small_ring.start(ring.far - 1, small_term)
        vector_copy(step, flip).wait_recv()
        vector_sum[...] = vector_sum[...] + vector_in[step, 1]

    def vector_spread(k):
        return to_partner(
            k, vector_sum, vectors_ref.at[f], vector_send, vector_recv, len(flips) + k - 1
        )

    for k in (2, 3, 1):
        vector_spread(k).start()
    vectors_ref[f] = vector_sum[...]

    x_raw = x_ring.finish(x_term)
    x_out[...] = x_raw.astype(bf16)
    for k in (2, 3, 1):
        return_copy(1, k).start()
    own_copy(1).start()
    small_raw = small_ring.finish(small_term)
    small_out[...] = small_raw.astype(bf16)
    for k in (2, 3, 1):
        return_copy(2, k).start()
    own_copy(2).start()

    total = squares_ref[...] + jnp.broadcast_to(
        total_squares(x_raw) + total_squares(small_raw), squares_ref.shape
    )
    scalar_out[0] = total

    def near_scalar(k):
        return to_partner(
            k, scalar_out.at[0], scalar_in.at[k], scalar_send, scalar_recv, k
        )

    for k in (2, 3, 1):
        near_scalar(k).start()
    for k in (2, 3, 1):
        near_scalar(k).wait_recv()
    total = (total + scalar_in[1]) + (scalar_in[2] + scalar_in[3])
    scalar_out[1] = total

    def far_scalar(k):
        member = d
        for bit in flips:
            if k & bit:
                member = flipped(member, bit)
        return pltpu.make_async_remote_copy(
            scalar_out.at[1], scalar_in.at[3 + k], scalar_send.at[3 + k], scalar_recv.at[3 + k],
            device_id={"dp": member}, device_id_type=MESH,
        )

    for k in range(count - 1, 0, -1):
        far_scalar(k).start()
    parts = [total]
    for k in range(1, count):
        far_scalar(k).wait_recv()
        parts.append(scalar_in[3 + k])
    while len(parts) > 1:
        parts = [parts[i] + parts[i + 1] for i in range(0, len(parts), 2)]
    total_ref[...] = parts[0]

    for k in (1, 2, 3):
        vector_spread(k).wait_recv()
        vector_spread(k).wait_send()
        shared_copy(k).wait_send()
        near_scalar(k).wait_send()
        for i in range(3):
            return_copy(i, k).wait_recv()
            return_copy(i, k).wait_send()
    for k in range(1, count):
        far_scalar(k).wait_send()
    for i in range(3):
        back_copy(i).wait_send()
        own_copy(i).wait()
    for step, flip in enumerate(flips):
        vector_copy(step, flip).wait_send()


def last_scatter(
    x_grad, normed_t, gate_grad, weight_gate, weight_x, weight_small, key_grad, query_grad, sums,
    rest, steps, head_rows, shared_part, shared_pre, taps, tokens, cotangent, inverse, gain,
    gate_raw, channel, gate_gain, squares,
):
    length, width = x_grad.shape
    count, members = lax.axis_size("dp"), lax.axis_size("fsdp")
    rows = D // count
    sub, own, shared = rows // members, tokens.shape[0], shared_part.shape[0]
    hops = max(count - 1, 1).bit_length()
    head_pick = (
        jnp.arange(width)[:, None] // HEAD_DIM == jnp.arange(PAIR)[None, :]
    ).astype(f32)
    dma = pltpu.SemaphoreType.DMA
    sd = jax.ShapeDtypeStruct
    return pl.pallas_call(
        last_scatter_kernel,
        in_specs=[whole_spec()] * 2 + any_specs(3) + [whole_spec()] * 19,
        out_specs=[whole_spec()] * 6,
        out_shape=[
            sd((members, sub, width), bf16),
            sd((members, sub, width), bf16),
            sd((members, sub, PAIR), bf16),
            sd((own, D), bf16),
            sd((members, 24, width), f32),
            sd((8, PAIR), f32),
        ],
        scratch_shapes=[
            pltpu.VMEM((length, width), bf16),
            pltpu.VMEM((D, width), bf16),
            pltpu.VMEM((D, width), bf16),
            dma((3,)),
            pltpu.VMEM((members, shared, length), f32),
            pltpu.VMEM((members, shared, length), bf16),
            pltpu.VMEM((members - 1, shared, length), bf16),
            dma((3,)),
            dma((3,)),
            pltpu.VMEM((length, PAIR), f32),
            pltpu.VMEM((PAIR, length), bf16),
            pltpu.VMEM((length, PAIR), bf16),
            pltpu.VMEM((own, D), f32),
            pltpu.VMEM((3, own, D), bf16),
            pltpu.VMEM((3, own, D), bf16),
            dma((3,)),
            dma((3,)),
            pltpu.VMEM((24, width), f32),
            pltpu.VMEM((hops, 2, 24, width), f32),
            dma((hops + 3,)),
            dma((hops + 3,)),
            pltpu.VMEM((rows, width), bf16),
            pltpu.VMEM((rows, PAIR), bf16),
            dma((9,)),
            dma((9,)),
            dma((3,)),
            pltpu.VMEM((2, 8, PAIR), f32),
            pltpu.VMEM((3 + count, 8, PAIR), f32),
            dma((3 + count,)),
            dma((3 + count,)),
        ]
        + RingScatter.scratch(count, rows, width)
        + RingScatter.scratch(count, rows, PAIR),
        compiler_params=pltpu.CompilerParams(
            collective_id=3, has_side_effects=True, vmem_limit_bytes=VMEM_BYTES
        ),
        name="last_scatter",
    )(
        x_grad, normed_t, gate_grad, weight_gate, weight_x, weight_small, key_grad, query_grad,
        sums, rest, head_pick, steps, head_rows, shared_part, shared_pre, taps, tokens, cotangent,
        inverse, gain, gate_raw, channel, gate_gain, squares,
    )


COLUMN_TILE = 512


def step_in_kernel(
    factor_ref, gate_ref, x_ref, small_ref, turn_ref, weight_ref, first_ref, second_ref,
    grad_ref, moment_ref, square_ref, master_ref, rounded_ref, raw,
):
    step = pl.program_id(0)
    tiles = INNER // COLUMN_TILE

    def joined(ref):
        return jnp.concatenate([ref[i] for i in range(ref.shape[0])], axis=1)

    @pl.when(step < tiles)
    def _():
        raw[...] = joined(gate_ref).astype(f32)

    @pl.when((step >= tiles) & (step < 2 * tiles))
    def _():
        raw[...] = joined(x_ref).astype(f32)

    @pl.when(step == 2 * tiles)
    def _():
        raw[...] = dot_rows(joined(small_ref), turn_ref[...])

    grad = raw[...] * factor_ref[0:1, 0:1]
    moment, square, master = adamw(
        weight_ref[...], first_ref[...], second_ref[...], grad, rate_in_proj
    )
    grad_ref[...] = grad
    moment_ref[...] = moment
    square_ref[...] = square
    master_ref[...] = master
    rounded_ref[...] = master.astype(bf16)


def step_in(factor, gate, x, small, weight, first, second):
    members, rows, width = x.shape
    tiles = INNER // COLUMN_TILE
    shared, heads = 2 * STATE // members, HEADS // members
    target = jnp.arange(COLUMN_TILE)
    head = target - 2 * STATE
    source = jnp.where(
        target < 2 * STATE,
        target // shared * PAIR + target % shared,
        head // 2 % members * PAIR + shared + head // (2 * members) * 2 + head % 2,
    )
    turn = (
        (jnp.arange(members * PAIR)[:, None] == source[None, :])
        & (target < 2 * STATE + HEADS)[None, :]
    ).astype(bf16)
    piece = lambda low: pl.BlockSpec(
        (members, rows, PAIR), lambda j: (0, 0, jnp.clip(j - low, 0, tiles - 1))
    )
    flat = pl.BlockSpec((rows, COLUMN_TILE), lambda j: (0, j))
    shape = jax.ShapeDtypeStruct(weight.shape, f32)
    return pl.pallas_call(
        step_in_kernel,
        grid=(2 * tiles + 1,),
        in_specs=[whole_spec(), piece(0), piece(tiles), whole_spec(), whole_spec()] + [flat] * 3,
        out_specs=[flat] * 5,
        out_shape=[shape] * 4 + [jax.ShapeDtypeStruct(weight.shape, bf16)],
        scratch_shapes=[pltpu.VMEM((rows, COLUMN_TILE), f32)],
        compiler_params=pltpu.CompilerParams(vmem_limit_bytes=VMEM_BYTES),
        name="step_in",
    )(factor, gate, x, small, turn, weight, first, second)


def unpack(vectors):
    offset = D + INNER
    taps_end = offset + CONV * XBC
    heads_start = taps_end + XBC
    norm_gain = vectors[:D]
    gate_gain = vectors[D:offset]
    filter_taps = vectors[offset:taps_end].reshape(CONV, XBC)
    filter_bias = vectors[taps_end:heads_start]
    step_bias = vectors[heads_start : heads_start + HEADS]
    decay_log = vectors[heads_start + HEADS : heads_start + 2 * HEADS]
    skip_gain = vectors[heads_start + 2 * HEADS : heads_start + 3 * HEADS]
    return (norm_gain, gate_gain, filter_taps, filter_bias, step_bias, decay_log, skip_gain)


def adamw(weight, moment, square, gradient, step_rate):
    moment_new = beta_first * moment + (1.0 - beta_first) * gradient
    square_new = beta_second * square + (1.0 - beta_second) * gradient * gradient
    moment_hat = moment_new / (1.0 - beta_first**STEP)
    square_hat = square_new / (1.0 - beta_second**STEP)
    weight_new = weight - step_rate * (
        moment_hat / (jnp.sqrt(square_hat) + adam_eps) + weight_decay * weight
    )
    return (moment_new, square_new, weight_new)


def on_device(
    tokens,
    widths,
    cotangent,
    in_weight,
    in_first,
    in_second,
    out_weight,
    out_first,
    out_second,
    vectors,
    vector_first,
    vector_second,
):
    fsdp = lax.axis_size("fsdp")
    me = lax.axis_index("fsdp")
    heads = HEADS // fsdp
    inner = INNER // fsdp
    shared = 2 * STATE // fsdp
    pairs = HEADS // 2 // fsdp
    rows_in, rows_out = in_weight.shape[0], out_weight.shape[0]
    length = tokens.shape[0] * fsdp
    chunks = length // SPAN
    in_kernels = uses_ring("dp") and rows_out == PAIR and rows_in % 16 == 0

    def own_channels(v):
        lead = v.shape[:-1]
        cut = v.reshape(lead + (pairs, fsdp, PAIR))
        return lax.dynamic_index_in_dim(cut, me, len(lead) + 1, False).reshape(lead + (inner,))

    def own_heads(v):
        return lax.dynamic_index_in_dim(v.reshape(pairs, fsdp, 2), me, 1, False).reshape(heads)

    def own_shared(v):
        return lax.dynamic_slice_in_dim(v, me * shared, shared, v.ndim - 1)

    norm_gain, gate_gain, filter_taps, filter_bias, step_bias, decay_log, skip_gain = unpack(
        vectors
    )
    gain_own = own_channels(gate_gain)[None]
    taps_own = own_channels(filter_taps[:, :INNER])
    bias_own = own_channels(filter_bias[:INNER])[None]
    taps_shared = own_shared(filter_taps[:, INNER:])
    bias_shared = own_shared(filter_bias[INNER:])
    step_bias_own, decay_own = own_heads(step_bias), -jnp.exp(own_heads(decay_log))
    skip_own = jnp.repeat(own_heads(skip_gain), HEAD_DIM)[None]

    width_index = widths[0]
    active = HEADS // 8 * jnp.left_shift(jnp.int32(1), width_index)
    head_mask = (jnp.arange(heads, dtype=jnp.int32) < active // fsdp).astype(f32)
    mask = jnp.repeat(head_mask, HEAD_DIM)[None]
    channel_count = (active * HEAD_DIM).astype(f32)

    in_low = in_weight.astype(bf16)
    shared_cut = jnp.concatenate(
        [
            in_low[:, 2 * INNER : 2 * INNER + 2 * STATE]
            .reshape(rows_in, fsdp, shared)
            .transpose(1, 0, 2),
            in_low[:, 2 * INNER + 2 * STATE :]
            .reshape(rows_in, pairs, fsdp, 2)
            .transpose(2, 0, 1, 3)
            .reshape(fsdp, rows_in, heads),
        ],
        axis=2,
    )

    def channel_cut(part):
        return (
            part.reshape(rows_in, pairs, fsdp, PAIR)
            .transpose(2, 0, 1, 3)
            .reshape(fsdp, rows_in, inner)
        )

    def gathered(cut):
        block = exchanged(cut, "fsdp")
        return gather_rows(block.reshape(fsdp * rows_in, cut.shape[2]), "dp")

    inputs = tokens.astype(f32)
    inverse_in = lax.rsqrt(jnp.mean(inputs * inputs, axis=-1, keepdims=True) + norm_eps)
    normed_own = (inputs * inverse_in * norm_gain[None, :]).astype(bf16)
    x_cut = channel_cut(in_low[:, INNER : 2 * INNER])
    gate_cut = channel_cut(in_low[:, :INNER])
    out_low = out_weight.astype(bf16)

    if in_kernels:
        shared_cut = jnp.pad(shared_cut, ((0, 0), (0, 0), (0, PAIR - shared - heads)))
        weight_shared, weight_x, normed, cotangents = gather_first(
            shared_cut, x_cut, normed_own, cotangent
        )
        normed_t = normed.T
    else:
        weight_shared = gathered(shared_cut)
        weight_x = gathered(x_cut)
        weight_gate = gathered(gate_cut)
        weight_out = lax.dynamic_index_in_dim(
            lax.all_gather(out_low, ("dp", "fsdp"), axis=0, tiled=True).reshape(
                pairs, fsdp, PAIR, D
            ),
            me,
            1,
            False,
        ).reshape(inner, D)
        normed = spread(normed_own, "fsdp").reshape(length, D)
        cotangents = spread(cotangent, "fsdp").reshape(length, D)

    small = lax.dot_general(
        weight_shared, normed, (((0,), (1,)), ((), ())), preferred_element_type=f32
    )
    shared_part = small[:shared]
    step_raw = small[shared : shared + heads] * head_mask[:, None]
    shared_padded = jnp.pad(shared_part, ((0, 0), (CONV - 1, 0)))
    shared_pre = bias_shared[:, None] + sum(
        taps_shared[k][:, None] * shared_padded[:, k : k + length] for k in range(CONV)
    )
    shared_gate = jax.nn.sigmoid(shared_pre)
    shared_all = spread_small((shared_pre * shared_gate).astype(bf16), "fsdp").reshape(
        2 * STATE, length
    )
    keys_t, queries_t = shared_all[:STATE], shared_all[STATE:]
    keys, queries = keys_t.T, queries_t.T
    step_logits = step_raw + step_bias_own[:, None]
    step_sizes = jax.nn.softplus(step_logits)
    upto = (jnp.arange(SPAN)[:, None] <= jnp.arange(SPAN)[None, :]).astype(f32)
    log_sums = jnp.dot(
        (step_sizes * decay_own[:, None]).reshape(heads, chunks, SPAN), upto, precision=highest
    ).reshape(heads, length)
    groups = heads // GROUP
    head_rows = jnp.concatenate(
        [log_sums.reshape(groups, GROUP, length), step_sizes.reshape(groups, GROUP, length)],
        axis=1,
    )
    head_columns = jnp.pad(
        head_rows.transpose(2, 0, 1), ((0, 0), (0, 0), (0, PAIR - 2 * GROUP))
    ).reshape(length, groups * PAIR)
    head_rows = head_rows.reshape(groups * 2 * GROUP, length)

    scan_inputs = (taps_own, bias_own, mask, skip_own, head_columns, head_rows, keys, queries)
    if in_kernels:
        x_part, y, states, weight_gate, weight_out = scan_gather(
            normed, weight_x, *scan_inputs, keys_t, gate_cut, out_low
        )
    else:
        x_part = jnp.dot(normed, weight_x, preferred_element_type=f32)
        y, states = scan_forward(x_part, *scan_inputs, keys_t)
    gate_part, gated_grad, stats = gate_forward(
        normed, weight_gate, cotangents, weight_out, y, gain_own, mask
    )
    stats = summed(stats[:, :2].T, "fsdp")
    inverse_out = lax.rsqrt(stats[0] / channel_count + norm_eps)
    pull = inverse_out**3 / channel_count * stats[1]
    gated_low, y_grad, gate_grad, gain_grad = norm_back(
        y, gate_part, gated_grad, jnp.stack([inverse_out, pull], axis=1), gain_own, mask
    )

    def in_term(grad):
        return lax.dot_general(
            normed, grad, (((0,), (0,)), ((), ())), preferred_element_type=f32
        ).astype(bf16)

    if in_kernels:
        (
            x_grad, key_grad, query_grad, sums, rest, channel_grad, gate_raw, out_raw, layer_out,
            squares,
        ) = scan_scatter(
            x_part, *scan_inputs, queries_t, y_grad, states,
            normed_t, gate_grad, gated_low, gated_low.T, cotangents, weight_out, tokens,
        )
    else:
        out_term = lax.dot_general(
            gated_low, cotangents, (((0,), (0,)), ((), ())), preferred_element_type=f32
        )
        whole_term = jnp.zeros((pairs, fsdp, PAIR, D), f32)
        whole_term = lax.dynamic_update_slice(
            whole_term, out_term.reshape(pairs, 1, PAIR, D), (0, me, 0, 0)
        )
        out_raw = lax.psum_scatter(
            whole_term.reshape(INNER, D), ("dp", "fsdp"), scatter_dimension=0, tiled=True
        )
        added = halved(
            jnp.dot(gated_low, weight_out, preferred_element_type=f32)
            .astype(bf16)
            .reshape(fsdp, tokens.shape[0], D),
            "fsdp",
        )
        layer_out = (inputs + added).astype(bf16)
        gate_raw = scatter_rows(in_term(gate_grad), "dp")
        x_grad, key_grad, query_grad, sums, rest, channel_grad = scan_backward(
            x_part, *scan_inputs, queries_t, y_grad, states
        )
    if in_kernels:
        steps = jnp.concatenate(
            [step_sizes, step_logits, jnp.zeros((PAIR - 2 * heads, length), f32)]
        ).T
        head_consts = jnp.pad(jnp.stack([decay_own, head_mask]), ((0, 6), (0, PAIR - heads)))
        gate_back, x_back, small_back, token_grad, vector_rows, squares = last_scatter(
            x_grad, normed_t, gate_grad, weight_gate, weight_x, weight_shared, key_grad,
            query_grad, sums, rest.reshape(chunks, inner), steps, head_consts, shared_part,
            shared_pre, jnp.pad(taps_shared.T, ((0, 0), (0, PAIR - CONV))), tokens, cotangent,
            inverse_in, norm_gain[None], gate_raw, channel_grad, gain_grad, squares,
        )
        squares = squares[0, 0]
    else:
        x_raw = scatter_rows(in_term(x_grad), "dp")

        shared_grads = jnp.concatenate([key_grad, query_grad], axis=1).T.astype(bf16)
        arrived = exchanged(shared_grads.reshape(fsdp, shared, length), "fsdp").astype(f32)
        activated_grad = jnp.sum(arrived, axis=0)
        shared_pre_grad = activated_grad * shared_gate * (1.0 + shared_pre * (1.0 - shared_gate))
        shared_ahead = jnp.pad(shared_pre_grad, ((0, 0), (0, CONV - 1)))
        shared_grad = sum(
            taps_shared[k][:, None] * shared_ahead[:, CONV - 1 - k : CONV - 1 - k + length]
            for k in range(CONV)
        )
        taps_shared_grad = jnp.stack(
            [
                jnp.sum(shared_pre_grad * shared_padded[:, k : k + length], axis=1)
                for k in range(CONV)
            ]
        )
        bias_shared_grad = jnp.sum(shared_pre_grad, axis=1)

        sums = sums.T[: 3 * heads].reshape(3, heads, chunks, SPAN)
        before = (jnp.arange(SPAN)[:, None] < jnp.arange(SPAN)[None, :]).astype(f32)
        rest = rest.reshape(chunks, heads, HEAD_DIM).sum(axis=2).T
        log_grad = (
            jnp.dot(sums[0], 1.0 - before, precision=highest)
            + jnp.dot(sums[1], before, precision=highest)
            + rest[:, :, None]
        ).reshape(heads, length)
        step_grad = decay_own[:, None] * log_grad + sums[2].reshape(heads, length)
        raw_grad = step_grad * jax.nn.sigmoid(step_logits)
        step_bias_grad = jnp.sum(raw_grad, axis=1)
        decay_grad = jnp.sum(step_sizes * log_grad, axis=1) * decay_own
        small_grad = jnp.concatenate([shared_grad, raw_grad * head_mask[:, None]], axis=0).astype(bf16)
        small_raw = scatter_rows(
            lax.dot_general(
                normed, small_grad, (((0,), (1,)), ((), ())), preferred_element_type=f32
            ).astype(bf16),
            "dp",
        )

        def in_back(grad, weight, grad_dim=1):
            return lax.dot_general(
                grad, weight, (((grad_dim,), (1,)), ((), ())), preferred_element_type=f32
            )

        normed_grad = halved(
            (
                in_back(gate_grad, weight_gate)
                + in_back(x_grad, weight_x)
                + in_back(small_grad, weight_shared, 0)
            )
            .astype(bf16)
            .reshape(fsdp, tokens.shape[0], D),
            "fsdp",
        )
        pulled = normed_grad * norm_gain[None, :]
        input_grad = inverse_in * pulled - inputs * (
            inverse_in**3 * jnp.mean(pulled * inputs, axis=-1, keepdims=True)
        )
        token_grad = (cotangent.astype(f32) + input_grad).astype(bf16)
        norm_gain_grad = jnp.sum(normed_grad * inputs * inverse_in, axis=0)

        head_row = jnp.concatenate(
            [jnp.pad(step_bias_grad, (0, PAIR - heads)), jnp.pad(decay_grad, (0, PAIR - heads))]
        )
        shared_rows = jnp.concatenate([taps_shared_grad, bias_shared_grad[None]])
        vector_rows = jnp.concatenate(
            [
                gain_grad[0:1],
                channel_grad[: CONV + 2],
                norm_gain_grad.reshape(-1, inner),
                jnp.zeros((15 - CONV - 3 - D // inner, inner), f32),
                jnp.pad(head_row, (0, inner - 2 * PAIR))[None],
                jnp.pad(shared_rows, ((0, 7 - CONV), (0, inner - shared))),
            ]
        )
        vector_rows = spread_small(summed_in_steps(vector_rows, "dp"), "fsdp")
        squares = (
            jnp.sum(gate_raw * gate_raw)
            + jnp.sum(x_raw * x_raw)
            + jnp.sum(small_raw * small_raw)
            + jnp.sum(out_raw * out_raw)
        )
        squares = summed(summed(jnp.broadcast_to(squares, (8, 128)), "fsdp"), "dp")[0, 0]

    def joined_channels(v):
        return v.reshape(fsdp, pairs, PAIR).transpose(1, 0, 2).reshape(INNER)

    def joined_heads(v):
        return v.reshape(fsdp, pairs, 2).transpose(1, 0, 2).reshape(HEADS)

    shared_all = vector_rows[:, 16 : 17 + CONV, :shared]
    bias_shared_all = shared_all[:, CONV].reshape(-1)
    taps_all = [
        jnp.concatenate([joined_channels(vector_rows[:, 1 + k]), shared_all[:, k].reshape(-1)])
        for k in range(CONV)
    ]
    bias_all = jnp.concatenate([joined_channels(vector_rows[:, CONV + 1]), bias_shared_all])
    norm_rows = vector_rows[:, CONV + 3 : CONV + 3 + D // inner].reshape(fsdp, D)
    norm_all = norm_rows[0]
    for member in range(1, fsdp):
        norm_all = norm_all + norm_rows[member]
    skip_all = vector_rows[:, CONV + 2].reshape(fsdp * heads, HEAD_DIM).sum(axis=1)
    vector_raw = jnp.concatenate(
        [norm_all, joined_channels(vector_rows[:, 0])]
        + taps_all
        + [
            bias_all,
            joined_heads(vector_rows[:, 15, :heads]),
            joined_heads(vector_rows[:, 15, PAIR : PAIR + heads]),
            joined_heads(skip_all),
        ]
    )

    grad_norm = jnp.sqrt(squares + jnp.sum(vector_raw * vector_raw))
    factor = jnp.minimum(1.0, clip_norm / (grad_norm + 1e-06))
    if in_kernels:
        in_grad, in_moment, in_square, in_master, in_rounded = step_in(
            jnp.broadcast_to(factor, (8, PAIR)), gate_back, x_back, small_back,
            in_weight, in_first, in_second,
        )
    else:

        def returned(raw):
            return exchanged(raw.astype(bf16).reshape(fsdp, rows_in, raw.shape[1]), "fsdp")

        def joined_columns(part):
            return (
                part.reshape(fsdp, rows_in, pairs, PAIR)
                .transpose(1, 2, 0, 3)
                .reshape(rows_in, INNER)
            )

        small_back = returned(small_raw)
        in_raw = jnp.concatenate(
            [
                joined_columns(returned(gate_raw)),
                joined_columns(returned(x_raw)),
                small_back[:, :, :shared].transpose(1, 0, 2).reshape(rows_in, 2 * STATE),
                small_back[:, :, shared:]
                .reshape(fsdp, rows_in, pairs, 2)
                .transpose(1, 2, 0, 3)
                .reshape(rows_in, HEADS),
            ],
            axis=1,
        ).astype(f32)
        in_grad = in_raw * factor
        in_moment, in_square, in_master = adamw(
            in_weight, in_first, in_second, in_grad, rate_in_proj
        )
        in_rounded = in_master.astype(bf16)
    out_grad = out_raw * factor
    vector_grad = vector_raw * factor
    out_moment, out_square, out_master = adamw(
        out_weight, out_first, out_second, out_grad, rate_out_proj
    )
    vector_moment, vector_square, vector_master = adamw(
        vectors, vector_first, vector_second, vector_grad, rate_vectors
    )
    return (
        layer_out,
        token_grad,
        in_grad,
        out_grad,
        vector_grad,
        grad_norm,
        in_moment,
        in_square,
        in_master,
        in_rounded,
        out_moment,
        out_square,
        out_master,
        out_master.astype(bf16),
        vector_moment,
        vector_square,
        vector_master,
    )


def solution(mesh):
    rows = P(("dp", "fsdp"), None)
    return jax.shard_map(
        on_device,
        mesh=mesh,
        in_specs=(rows, P("dp")) + (rows,) * 7 + (P(),) * 3,
        out_specs=(rows,) * 4 + (P(),) * 2 + (rows,) * 8 + (P(),) * 3,
        check_vma=False,
    )
```

```python
from functools import partial

import jax
import jax.numpy as jnp
from jax import lax
from jax.experimental import pallas as pl
from jax.experimental.pallas import tpu as pltpu
from jax.sharding import PartitionSpec as P

D = 2048
HEADS = 64
HEAD_DIM = 64
STATE = 128
CONV = 4
SPAN = 128
STEP = 10
INNER = 4096
XBC = 4352
PAIR = 2 * HEAD_DIM
GROUP = 4
STEP_LANE = 16
LANES = GROUP * HEAD_DIM
ROW_TILE = 256
RING_LIMIT = 16

norm_eps = 1e-05
clip_norm = 1.0
beta_first = 0.5
beta_second = 0.5
adam_eps = 1e-08
weight_decay = 0.1
rate_in_proj = 0.03
rate_out_proj = 0.02
rate_vectors = 0.5
highest = lax.Precision.HIGHEST
f32 = jnp.float32
bf16 = jnp.bfloat16
VMEM_BYTES = 60 * 1024 * 1024


def ring_order(count):
    return list(range(0, count, 2)) + list(range(count - 1, 0, -2))


def ring_links(count):
    order = ring_order(count)
    right = [(order[i], order[(i + 1) % count]) for i in range(count)]
    return right, [(b, a) for a, b in right]


def ring_place(axis):
    count = lax.axis_size(axis)
    order = ring_order(count)
    places = [0] * count
    for place, member in enumerate(order):
        places[member] = place
    place = jnp.asarray(places, jnp.int32)[lax.axis_index(axis)]

    def member_at(distance):
        return jnp.asarray(order, jnp.int32)[lax.rem(place + distance + count, count)]

    return member_at


def uses_ring(axis):
    count = lax.axis_size(axis)
    return count % 2 == 0 and 4 <= count <= RING_LIMIT


def gather_rows(block, axis):
    count = lax.axis_size(axis)
    if not uses_ring(axis):
        return lax.all_gather(block, axis, axis=0, tiled=True)
    right, left = ring_links(count)
    member_at = ring_place(axis)
    rows, half = block.shape[0], block.shape[0] // 2
    whole = jnp.zeros((count * rows,) + block.shape[1:], block.dtype)
    columns = (0,) * (block.ndim - 1)

    def put(whole, piece, distance, shift=0):
        return lax.dynamic_update_slice(
            whole, piece, (member_at(distance) * rows + shift,) + columns
        )

    whole = put(whole, block, 0)
    going_right = going_left = block
    for hop in range(1, count // 2):
        going_right = lax.ppermute(going_right, axis, right)
        going_left = lax.ppermute(going_left, axis, left)
        whole = put(whole, going_right, -hop)
        whole = put(whole, going_left, hop)
    first = lax.ppermute(going_right[:half], axis, right)
    second = lax.ppermute(going_left[half:], axis, left)
    whole = put(whole, first, count // 2)
    return put(whole, second, count // 2, half)


def scatter_rows(terms, axis):
    count = lax.axis_size(axis)
    if not uses_ring(axis):
        return lax.psum_scatter(terms.astype(f32), axis, scatter_dimension=0, tiled=True)
    right, left = ring_links(count)
    member_at = ring_place(axis)
    rows = terms.shape[0] // count
    half = rows // 2

    def term(distance):
        return lax.dynamic_slice_in_dim(terms, member_at(distance) * rows, rows, 0).astype(f32)

    far = term(count // 2).astype(bf16)
    going_right = lax.ppermute(far[:half], axis, right)
    going_left = lax.ppermute(far[half:], axis, left)
    for distance in range(count // 2 - 1, 0, -1):
        to_right, to_left = term(distance), term(-distance)
        if distance == count // 2 - 1:
            to_right = jnp.concatenate([to_right[:half] + going_right, to_right[half:]])
            to_left = jnp.concatenate([to_left[:half], to_left[half:] + going_left])
        else:
            to_right, to_left = to_right + going_right, to_left + going_left
        going_right = lax.ppermute(to_right.astype(bf16), axis, right)
        going_left = lax.ppermute(to_left.astype(bf16), axis, left)
    return term(0) + going_right + going_left


def swapped(value, axis, flip):
    count = lax.axis_size(axis)
    return lax.ppermute(value, axis, [(i, i ^ flip) for i in range(count)])


def summed(value, axis):
    count = lax.axis_size(axis)
    if count <= 8:
        parts = [value] + [swapped(value, axis, flip) for flip in range(1, count)]
        while len(parts) > 1:
            parts = [parts[i] + parts[i + 1] for i in range(0, len(parts), 2)]
        return parts[0]
    return summed_in_steps(value, axis)


def summed_in_steps(value, axis):
    flip = 1
    while flip < lax.axis_size(axis):
        value = value + swapped(value, axis, flip)
        flip *= 2
    return value


def placed(parts, axis):
    count = lax.axis_size(axis)
    me = lax.axis_index(axis)
    whole = jnp.zeros((count,) + parts[0].shape, parts[0].dtype)
    for flip, part in enumerate(parts):
        whole = lax.dynamic_update_index_in_dim(whole, part, lax.bitwise_xor(me, flip), 0)
    return whole


def spread(value, axis):
    count = lax.axis_size(axis)
    parts = [value]
    flip = count // 2
    known = {0: value}
    while flip:
        fresh = {k ^ flip: swapped(v, axis, flip) for k, v in known.items()}
        known.update(fresh)
        flip //= 2
    parts = [known[k] for k in range(count)]
    return placed(parts, axis)


def spread_small(value, axis):
    count = lax.axis_size(axis)
    return placed([value] + [swapped(value, axis, k) for k in range(1, count)], axis)


def exchanged(blocks, axis):
    count = lax.axis_size(axis)
    me = lax.axis_index(axis)

    def block_for(flip):
        return lax.dynamic_index_in_dim(blocks, lax.bitwise_xor(me, flip), 0, False)

    return placed(
        [block_for(0)] + [swapped(block_for(k), axis, k) for k in range(1, count)], axis
    )


def halved(blocks, axis):
    count = lax.axis_size(axis)
    me = lax.axis_index(axis)
    held = {
        k: lax.dynamic_index_in_dim(blocks, lax.bitwise_xor(me, k), 0, False)
        for k in range(count)
    }
    flip = 1
    while flip < count:
        kept = {}
        for k in sorted(held):
            if k & flip:
                continue
            arrived = swapped(held[k ^ flip].astype(bf16), axis, flip)
            kept[k] = held[k].astype(f32) + arrived
        held = kept
        flip *= 2
    return held[0]


def dot_rows(a, b):
    return lax.dot_general(a, b, (((1,), (0,)), ((), ())), preferred_element_type=f32)


def dot_lanes(a, b):
    return lax.dot_general(a, b, (((1,), (1,)), ((), ())), preferred_element_type=f32)


def head_lanes(columns, base):
    rows = columns.shape[0]
    full = [
        jnp.broadcast_to(columns[:, base + j : base + j + 1], (rows, PAIR)) for j in range(GROUP)
    ]
    first = lax.broadcasted_iota(jnp.int32, (rows, PAIR), 1) < HEAD_DIM
    lanes = jnp.concatenate(
        [jnp.where(first, full[i], full[i + 1]) for i in range(0, GROUP, 2)], axis=1
    )
    return full, lanes


def stacked_heads(values, block_mask):
    return jnp.concatenate([values] * GROUP, axis=0) * block_mask


def filtered(window, taps, bias, rows):
    pre = bias + taps[CONV - 1 : CONV] * window[8 : 8 + rows]
    for k in range(CONV - 1):
        pre = pre + taps[k : k + 1] * window[5 + k : 5 + k + rows]
    return pre


def scan_forward_kernel(
    x_ref, taps_ref, bias_ref, mask_ref, skip_ref, column_ref, row_ref, key_ref, query_ref,
    key_t_ref, block_ref, y_ref, states_ref, padded, state,
):
    length = x_ref.shape[0]
    rows = SPAN
    mask = mask_ref[...]
    padded[0:8, :] = jnp.zeros((8, LANES), f32)
    padded[8 : 8 + length, :] = x_ref[...] * mask
    state[...] = jnp.zeros_like(state)
    taps, bias, skip = taps_ref[...], bias_ref[...], skip_ref[...]
    causal = lax.broadcasted_iota(jnp.int32, (rows, rows), 0) >= lax.broadcasted_iota(
        jnp.int32, (rows, rows), 1
    )

    def chunk(c, carry):
        start = pl.multiple_of(c * rows, rows)
        here = pl.ds(start, rows)
        pre = filtered(padded[pl.ds(start, rows + 8), :], taps, bias, rows)
        values = pre * jax.nn.sigmoid(pre) * mask
        columns = column_ref[here, :]
        log_full, log_lanes = head_lanes(columns, 0)
        step_lanes = head_lanes(columns, STEP_LANE)[1]
        weighted = step_lanes * values
        weighted_low = weighted.astype(bf16)
        keys, queries, keys_t = key_ref[here, :], query_ref[here, :], key_t_ref[:, here]
        inner = dot_lanes(queries, keys)
        mixing = jnp.concatenate(
            [
                (
                    jnp.where(causal, jnp.exp(log_full[j] - row_ref[j : j + 1, here]), 0.0)
                    * inner
                ).astype(bf16)
                for j in range(GROUP)
            ],
            axis=1,
        )
        state_now = state[...]
        state_low = state_now.astype(bf16)
        states_ref[pl.ds(c, 1)] = state_low[None]
        y = dot_rows(mixing, stacked_heads(weighted_low, block_ref[...]))
        y = y + jnp.exp(log_lanes) * dot_rows(queries, state_low)
        y_ref[here, :] = y + skip * values
        log_last = log_lanes[rows - 1 : rows, :]
        tail = (weighted * jnp.exp(log_last - log_lanes)).astype(bf16)
        state[...] = jnp.exp(log_last) * state_now + dot_rows(keys_t, tail)
        return carry

    lax.fori_loop(0, length // rows, chunk, 0)


def scan_backward_kernel(
    x_ref, taps_ref, bias_ref, mask_ref, skip_ref, column_ref, row_ref, key_ref, query_ref,
    query_t_ref, block_ref, pick_ref, grad_ref, states_ref,
    x_grad_ref, key_grad_ref, query_grad_ref, sums_ref, rest_ref, channel_ref,
    padded, following, state_back, inner_grad,
):
    length = x_ref.shape[0]
    rows = SPAN
    chunks = length // rows
    group = pl.program_id(0)
    mask = mask_ref[...]
    padded[0:8, :] = jnp.zeros((8, LANES), f32)
    padded[8 : 8 + length, :] = x_ref[...] * mask
    following[...] = jnp.zeros_like(following)
    state_back[...] = jnp.zeros_like(state_back)
    channel_ref[...] = jnp.zeros_like(channel_ref)

    @pl.when(group == 0)
    def _():
        key_grad_ref[...] = jnp.zeros_like(key_grad_ref)
        query_grad_ref[...] = jnp.zeros_like(query_grad_ref)
        inner_grad[...] = jnp.zeros_like(inner_grad)
        sums_ref[...] = jnp.zeros_like(sums_ref)

    taps, bias, skip = taps_ref[...], bias_ref[...], skip_ref[...]
    row_at = lax.broadcasted_iota(jnp.int32, (rows, rows), 0)
    lane_at = lax.broadcasted_iota(jnp.int32, (rows, rows), 1)
    causal, causal_t = row_at >= lane_at, lane_at >= row_at

    def chunk(lap, carry):
        c = chunks - 1 - lap
        start = pl.multiple_of(c * rows, rows)
        here = pl.ds(start, rows)
        window = padded[pl.ds(start, rows + 8), :]
        pre = filtered(window, taps, bias, rows)
        gate = jax.nn.sigmoid(pre)
        values = pre * gate * mask
        columns = column_ref[here, :]
        log_full, log_lanes = head_lanes(columns, 0)
        step_lanes = head_lanes(columns, STEP_LANE)[1]
        weighted = step_lanes * values
        weighted_low = weighted.astype(bf16)
        keys, queries, queries_t = key_ref[here, :], query_ref[here, :], query_t_ref[:, here]
        grad_low = grad_ref[here, :]
        grad = grad_low.astype(f32)
        inner, inner_t = dot_lanes(queries, keys), dot_lanes(keys, queries)
        blocks = block_ref[...]
        weighted_blocks = stacked_heads(weighted_low, blocks)
        grad_blocks = stacked_heads(grad_low, blocks)
        mixing_grad = dot_lanes(grad_low, weighted_blocks)
        mixing, mixing_t, inner_sum = [], [], jnp.zeros((rows, rows), f32)
        for j in range(GROUP):
            log_row = row_ref[j : j + 1, here]
            decay = jnp.where(causal, jnp.exp(log_full[j] - log_row), 0.0)
            decay_t = jnp.where(causal_t, jnp.exp(log_row - log_full[j]), 0.0)
            mixing.append((decay * inner).astype(bf16))
            mixing_t.append((decay_t * inner_t).astype(bf16))
            inner_sum = inner_sum + decay * mixing_grad[:, j * rows : (j + 1) * rows]
        inner_grad[pl.ds(c, 1)] = inner_grad[pl.ds(c, 1)] + inner_sum[None]
        y = dot_rows(jnp.concatenate(mixing, axis=1), weighted_blocks)
        state_low = states_ref[pl.ds(c, 1)][0]
        entry = jnp.exp(log_lanes)
        y = y + entry * dot_rows(queries, state_low)
        inside = dot_rows(jnp.concatenate(mixing_t, axis=1), grad_blocks)
        back = state_back[...]
        back_low = back.astype(bf16)
        log_last = log_lanes[rows - 1 : rows, :]
        tail = jnp.exp(log_last - log_lanes)
        outside = tail * dot_rows(keys, back_low)
        entry_grad = (grad * entry).astype(bf16)
        tail_low = (weighted * tail).astype(bf16)
        query_grad_ref[here, :] = query_grad_ref[here, :] + dot_lanes(entry_grad, state_low)
        key_grad_ref[here, :] = key_grad_ref[here, :] + dot_lanes(tail_low, back_low)
        last = jnp.exp(log_last)
        rest_ref[pl.ds(c, 1)] = (
            last * jnp.sum(state_low.astype(f32) * back, axis=0, keepdims=True)
        )[None]
        state_back[...] = last * back + dot_rows(queries_t, entry_grad)
        weighted_grad = inside + outside
        first = grad * y - weighted_low.astype(f32) * inside
        first_high = first.astype(bf16)
        first_rest = (first - first_high.astype(f32)).astype(bf16)
        sums_ref[here, :] = sums_ref[here, :] + (
            dot_rows(first_high, pick_ref[0])
            + dot_rows(first_rest, pick_ref[0])
            + dot_rows((weighted * outside).astype(bf16), pick_ref[1])
            + dot_rows((values * weighted_grad).astype(bf16), pick_ref[2])
        )
        values_grad = step_lanes * weighted_grad + skip * grad
        pre_grad = values_grad * mask * (gate * (1.0 + pre * (1.0 - gate)))
        channel_ref[CONV : CONV + 1, :] += jnp.sum(pre_grad, axis=0, keepdims=True)
        channel_ref[CONV + 1 : CONV + 2, :] += jnp.sum(grad * values, axis=0, keepdims=True)
        for k in range(CONV):
            channel_ref[k : k + 1, :] += jnp.sum(
                pre_grad * window[5 + k : 5 + k + rows], axis=0, keepdims=True
            )
        ahead = jnp.concatenate([pre_grad, following[...]], axis=0)
        following[...] = pre_grad[0:8]
        x_grad = taps[CONV - 1 : CONV] * ahead[0:rows]
        for k in range(CONV - 1):
            x_grad = x_grad + taps[k : k + 1] * ahead[CONV - 1 - k : CONV - 1 - k + rows]
        x_grad_ref[here, :] = (x_grad * mask).astype(bf16)
        return carry

    lax.fori_loop(0, chunks, chunk, 0)

    @pl.when(group == pl.num_programs(0) - 1)
    def _():
        def finish(c, carry):
            here = pl.ds(pl.multiple_of(c * rows, rows), rows)
            inner_low = inner_grad[pl.ds(c, 1)][0].astype(bf16)
            query_grad_ref[here, :] = query_grad_ref[here, :] + dot_rows(
                inner_low, key_ref[here, :]
            )
            key_grad_ref[here, :] = key_grad_ref[here, :] + lax.dot_general(
                inner_low, query_ref[here, :], (((0,), (0,)), ((), ())),
                preferred_element_type=f32,
            )
            return carry

        lax.fori_loop(0, chunks, finish, 0)


def block_mask():
    row = jnp.arange(GROUP * SPAN)[:, None] // SPAN
    lane = jnp.arange(LANES)[None, :] // HEAD_DIM
    return (row == lane).astype(bf16)


def pick_masks(groups):
    lane = jnp.arange(LANES)[:, None] // HEAD_DIM
    target = jnp.arange(PAIR)[None, :]
    return jnp.stack(
        [
            (target == (kind * groups + group) * GROUP + lane).astype(bf16)
            for group in range(groups)
            for kind in range(3)
        ]
    )


def whole_spec():
    return pl.BlockSpec(memory_space=pltpu.VMEM)


def lane_spec(rows):
    return pl.BlockSpec((rows, LANES), lambda g: (0, g))


def head_specs(length):
    return [
        lane_spec(length),
        lane_spec(CONV),
        lane_spec(1),
        lane_spec(1),
        lane_spec(1),
        pl.BlockSpec((length, PAIR), lambda g: (0, g)),
        pl.BlockSpec((8, length), lambda g: (g, 0)),
        whole_spec(),
        whole_spec(),
        whole_spec(),
        whole_spec(),
    ]


def scan_forward(x, taps, bias, mask, skip, columns, rows, keys, queries, keys_t):
    length, width = x.shape
    chunks = length // SPAN
    return pl.pallas_call(
        scan_forward_kernel,
        grid=(width // LANES,),
        in_specs=head_specs(length),
        out_specs=[
            lane_spec(length),
            pl.BlockSpec((chunks, STATE, LANES), lambda g: (0, 0, g)),
        ],
        out_shape=[
            jax.ShapeDtypeStruct((length, width), f32),
            jax.ShapeDtypeStruct((chunks, STATE, width), bf16),
        ],
        scratch_shapes=[pltpu.VMEM((length + 8, LANES), f32), pltpu.VMEM((STATE, LANES), f32)],
        compiler_params=pltpu.CompilerParams(vmem_limit_bytes=VMEM_BYTES),
        cost_estimate=pl.CostEstimate(
            flops=10_000_000_000, bytes_accessed=12_000_000, transcendentals=4_000_000
        ),
        name="scan_forward",
    )(x, taps, bias, mask, skip, columns, rows, keys, queries, keys_t, block_mask())


def scan_backward(
    x, taps, bias, mask, skip, columns, rows, keys, queries, queries_t, grad, states
):
    length, width = x.shape
    chunks = length // SPAN
    groups = width // LANES
    same = lambda g: (0, 0)
    return pl.pallas_call(
        scan_backward_kernel,
        grid=(groups,),
        in_specs=head_specs(length)
        + [
            pl.BlockSpec((3, LANES, PAIR), lambda g: (g, 0, 0)),
            lane_spec(length),
            pl.BlockSpec((chunks, STATE, LANES), lambda g: (0, 0, g)),
        ],
        out_specs=[
            lane_spec(length),
            pl.BlockSpec((length, STATE), same),
            pl.BlockSpec((length, STATE), same),
            pl.BlockSpec((length, PAIR), same),
            pl.BlockSpec((chunks, 1, LANES), lambda g: (0, 0, g)),
            lane_spec(8),
        ],
        out_shape=[
            jax.ShapeDtypeStruct((length, width), bf16),
            jax.ShapeDtypeStruct((length, STATE), f32),
            jax.ShapeDtypeStruct((length, STATE), f32),
            jax.ShapeDtypeStruct((length, PAIR), f32),
            jax.ShapeDtypeStruct((chunks, 1, width), f32),
            jax.ShapeDtypeStruct((8, width), f32),
        ],
        scratch_shapes=[
            pltpu.VMEM((length + 8, LANES), f32),
            pltpu.VMEM((8, LANES), f32),
            pltpu.VMEM((STATE, LANES), f32),
            pltpu.VMEM((chunks, SPAN, SPAN), f32),
        ],
        compiler_params=pltpu.CompilerParams(vmem_limit_bytes=VMEM_BYTES),
        cost_estimate=pl.CostEstimate(
            flops=30_000_000_000, bytes_accessed=16_000_000, transcendentals=8_000_000
        ),
        name="scan_backward",
    )(
        x, taps, bias, mask, skip, columns, rows, keys, queries, queries_t, block_mask(),
        pick_masks(groups), grad, states,
    )


def gate_kernel(
    normed_ref, weight_ref, cotangent_ref, out_ref, y_ref, gain_ref, mask_ref,
    gate_part_ref, gated_grad_ref, stats_ref,
):
    gate_part = dot_rows(normed_ref[...], weight_ref[...]) * mask_ref[...]
    gated_grad = dot_lanes(cotangent_ref[...], out_ref[...])
    gate_part_ref[...] = gate_part
    gated_grad_ref[...] = gated_grad
    gated = y_ref[...] * (gate_part * jax.nn.sigmoid(gate_part))
    squares = jnp.sum(gated * gated, axis=1, keepdims=True)
    products = jnp.sum(gated * gated_grad * gain_ref[...], axis=1, keepdims=True)
    lane = lax.broadcasted_iota(jnp.int32, stats_ref.shape, 1)
    stats_ref[...] = jnp.where(lane == 0, squares, products)


def gate_forward(normed, weight, cotangent, out_weight, y, gain, mask):
    length, width = y.shape
    rows = lambda lanes: pl.BlockSpec((ROW_TILE, lanes), lambda i: (i, 0))
    return pl.pallas_call(
        gate_kernel,
        grid=(length // ROW_TILE,),
        in_specs=[
            rows(D), whole_spec(), rows(D), whole_spec(), rows(width), whole_spec(), whole_spec(),
        ],
        out_specs=[rows(width), rows(width), rows(PAIR)],
        out_shape=[
            jax.ShapeDtypeStruct((length, width), f32),
            jax.ShapeDtypeStruct((length, width), f32),
            jax.ShapeDtypeStruct((length, PAIR), f32),
        ],
        compiler_params=pltpu.CompilerParams(vmem_limit_bytes=VMEM_BYTES),
        cost_estimate=pl.CostEstimate(
            flops=9_000_000_000, bytes_accessed=28_000_000, transcendentals=1_000_000
        ),
        name="gate_forward",
    )(normed, weight, cotangent, out_weight, y, gain, mask)


def norm_back_kernel(
    y_ref, gate_part_ref, gated_grad_ref, scale_ref, gain_ref, mask_ref,
    gated_ref, y_grad_ref, gate_grad_ref, gain_grad_ref,
):
    @pl.when(pl.program_id(0) == 0)
    def _():
        gain_grad_ref[...] = jnp.zeros_like(gain_grad_ref)

    y, gate_part, gated_grad = y_ref[...], gate_part_ref[...], gated_grad_ref[...]
    inverse, pull = scale_ref[:, 0:1], scale_ref[:, 1:2]
    gate = jax.nn.sigmoid(gate_part)
    silu = gate_part * gate
    gated = y * silu
    scaled = gated * inverse
    gain = gain_ref[...]
    gated_ref[...] = (scaled * gain).astype(bf16)
    gain_grad_ref[0:1, :] += jnp.sum(gated_grad * scaled, axis=0, keepdims=True)
    back = inverse * (gated_grad * gain) - gated * pull
    y_grad_ref[...] = (back * silu).astype(bf16)
    gate_grad_ref[...] = (
        back * y * (gate * (1.0 + gate_part * (1.0 - gate))) * mask_ref[...]
    ).astype(bf16)


def norm_back(y, gate_part, gated_grad, scales, gain, mask):
    length, width = y.shape
    rows = lambda lanes: pl.BlockSpec((ROW_TILE, lanes), lambda i: (i, 0))
    return pl.pallas_call(
        norm_back_kernel,
        grid=(length // ROW_TILE,),
        in_specs=[rows(width), rows(width), rows(width), rows(2), whole_spec(), whole_spec()],
        out_specs=[
            rows(width), rows(width), rows(width), pl.BlockSpec((8, width), lambda i: (0, 0)),
        ],
        out_shape=[
            jax.ShapeDtypeStruct((length, width), bf16),
            jax.ShapeDtypeStruct((length, width), bf16),
            jax.ShapeDtypeStruct((length, width), bf16),
            jax.ShapeDtypeStruct((8, width), f32),
        ],
        compiler_params=pltpu.CompilerParams(vmem_limit_bytes=VMEM_BYTES),
        cost_estimate=pl.CostEstimate(
            flops=30_000_000, bytes_accessed=18_000_000, transcendentals=1_000_000
        ),
        name="norm_back",
    )(y, gate_part, gated_grad, scales, gain, mask)


MESH = pl.DeviceIdType.MESH


class Ring:
    def __init__(self):
        self.count = lax.axis_size("dp")
        self.far = self.count // 2
        me = lax.axis_index("dp")
        odd = lax.rem(me, 2)
        self.me = me
        self.place = (1 - odd) * lax.div(me, 2) + odd * lax.div(2 * self.count - 1 - me, 2)

    def member(self, distance):
        n = self.count
        place = lax.rem(self.place + distance + n, n)
        back = lax.div(place, n // 2)
        return (1 - back) * 2 * place + back * (2 * n - 1 - 2 * place)

    def target(self, way):
        return {"dp": self.member(1 if way == 0 else -1)}


def partner(flip):
    f = lax.axis_index("fsdp")
    return (f, f + 1 - 2 * lax.rem(f, 2), lax.rem(f + 2, 4), 3 - f)[flip]


def greet(targets):
    barrier = pltpu.get_barrier_semaphore()
    for target in targets:
        pl.semaphore_signal(barrier, inc=1, device_id=target, device_id_type=MESH)
    pl.semaphore_wait(barrier, len(targets))


def row_slice(ref, start, size):
    return ref.at[pl.ds(pl.multiple_of(start, 16), size)]


class RingGather:
    def __init__(self, ring, wholes, send, recv):
        self.ring, self.wholes, self.send, self.recv = ring, wholes, send, recv

    @staticmethod
    def semaphores(parts, count):
        return pltpu.SemaphoreType.DMA((parts * 4 * (count // 2),))

    def copy(self, part, way, half, hop):
        whole = self.wholes[part]
        rows = whole.shape[0] // self.ring.count
        size = rows // 2
        owner = self.ring.member(-hop if way == 0 else hop)
        place = row_slice(whole, owner * rows + half * size, size)
        at = ((part * 2 + way) * 2 + half) * self.ring.far + hop
        return pltpu.make_async_remote_copy(
            place, place, self.send.at[at], self.recv.at[at],
            device_id=self.ring.target(way), device_id_type=MESH,
        )

    def pieces(self, hop):
        return [
            (way, half)
            for half in (0, 1)
            for way in (0, 1)
            if hop < self.ring.far - 1 or half == way
        ]

    def start(self, part, hop):
        for way, half in self.pieces(hop):
            if hop:
                self.copy(part, way, half, hop - 1).wait_recv()
            self.copy(part, way, half, hop).start()

    def finish(self, part):
        last = self.ring.far - 1
        for way, half in self.pieces(last):
            self.copy(part, way, half, last).wait_recv()
            if last:
                self.copy(part, way, 1 - half, last - 1).wait_recv()
        for hop in range(last + 1):
            for way, half in self.pieces(hop):
                self.copy(part, way, half, hop).wait_send()


class RingScatter:
    def __init__(self, ring, held, arrived, send, recv):
        self.ring, self.held, self.arrived = ring, held, arrived
        self.send, self.recv = send, recv

    @staticmethod
    def scratch(count, rows, columns):
        hops = count // 2
        return [
            pltpu.VMEM((2, 2, rows, columns), bf16),
            pltpu.VMEM((2, hops, rows, columns), bf16),
            pltpu.SemaphoreType.DMA((2 * hops,)),
            pltpu.SemaphoreType.DMA((2 * hops,)),
        ]

    def copy(self, way, hop):
        rows = self.held.shape[2]
        size = rows // 2 if hop == 0 else rows
        at = way * self.ring.far + hop
        return pltpu.make_async_remote_copy(
            self.held.at[way, hop % 2, pl.ds(0, size)],
            self.arrived.at[way, hop, pl.ds(0, size)],
            self.send.at[at], self.recv.at[at],
            device_id=self.ring.target(way), device_id_type=MESH,
        )

    def owner(self, way, hop):
        distance = self.ring.far - hop
        return self.ring.member(distance if way == 0 else -distance)

    def start(self, hop, term):
        rows = self.held.shape[2]
        half = rows // 2
        if hop == 0:
            value = term(self.owner(0, 0)).astype(bf16)
            self.held[0, 0, 0:half] = value[:half]
            self.copy(0, 0).start()
            self.held[1, 0, 0:half] = value[half:]
            self.copy(1, 0).start()
            return
        for way in (0, 1):
            value = term(self.owner(way, hop))
            self.copy(way, hop - 1).wait_recv()
            slot = hop % 2
            if hop >= 2:
                self.copy(way, hop - 2).wait_send()
            if hop == 1:
                low = slice(way * half, (way + 1) * half)
                rest = slice((1 - way) * half, (2 - way) * half)
                self.held[way, slot, low] = (
                    value[low] + self.arrived[way, 0, 0:half].astype(f32)
                ).astype(bf16)
                self.held[way, slot, rest] = value[rest].astype(bf16)
            else:
                self.held[way, slot] = (
                    value + self.arrived[way, hop - 1].astype(f32)
                ).astype(bf16)
            self.copy(way, hop).start()

    def finish(self, term):
        last = self.ring.far - 1
        value = term(self.ring.me)
        for way in (0, 1):
            self.copy(way, last).wait_recv()
            value = value + self.arrived[way, last].astype(f32)
        for hop in range(last - 1, last + 1):
            for way in (0, 1):
                self.copy(way, hop).wait_send()
        return value


def any_specs(count):
    return [pl.BlockSpec(memory_space=pl.ANY)] * count


def tokens_exchange(own, whole, send, recv, base):
    f = lax.axis_index("fsdp")
    rows = whole.shape[0] // 4

    def one(at, source, owner, k):
        return pltpu.make_async_remote_copy(
            source, row_slice(whole, owner * rows, rows), send.at[base + at], recv.at[base + at],
            device_id={"fsdp": partner(k)}, device_id_type=MESH,
        )

    far = partner(2)
    return (
        one(0, own, f, 2), one(1, own, f, 1), one(2, row_slice(whole, far * rows, rows), far, 1),
    )


def forward_kernel(
    tokens_ref, cotangent_hbm, in_ref, out_ref, turn_ref, gain_in_ref, gain_ref, taps_ref, bias_ref,
    mask_ref, skip_ref, head_ref, shared_taps_ref, block_ref, count_ref,
    small_all, x_all, gate_all, out_all, cotangent_all, normed_t_all, x_part_all, states_all,
    gated_all, gated_t_all, y_grad_all, gate_grad_all,
    columns_ref, rows_ref, column_ref, keys_ref, queries_ref, queries_t_ref,
    shared_part_ref, shared_pre_ref, gain_grad_ref,
    small_cut, x_cut, gate_cut, out_low, normed, cotangent, small_weight, keys_t, shared_all,
    x_part, states, y, gate_part, gated_grad, weight, out_tile, turned, squares, products, stats, stats_in,
    back_tiles, back_tiles_t, padded, state,
    local_sem, swap_send, swap_recv, token_send, token_recv, ring_send, ring_recv,
    shared_send, shared_recv, stats_send, stats_recv, load_sem, store_sem,
):
    ring = Ring()
    d, f = ring.me, lax.axis_index("fsdp")
    tokens, length = tokens_ref.shape[0], normed.shape[0]
    sub, rows_out = in_ref.shape[0], out_ref.shape[0]
    width = x_cut.shape[2]
    groups, chunks = width // LANES, length // SPAN
    heads, shared = HEADS // 4, shared_taps_ref.shape[0]
    greet([{"fsdp": partner(k)} for k in (1, 2, 3)] + [ring.target(0), ring.target(1)])
    wholes = [small_all, x_all, gate_all, out_all]
    small_part, x_of, gate_of, out_of = range(4)
    rings = RingGather(ring, wholes, ring_send, ring_recv)
    cuts = [small_cut, x_cut, gate_cut]

    def own_copy(part):
        if part == out_of:
            source, target = out_low, row_slice(out_all, d * rows_out, rows_out)
        else:
            source = cuts[part].at[f]
            target = row_slice(wholes[part], (4 * d + f) * sub, sub)
        return pltpu.make_async_copy(source, target, local_sem.at[part])

    def swap(part, k):
        return pltpu.make_async_remote_copy(
            cuts[part].at[partner(k)], row_slice(wholes[part], (4 * d + f) * sub, sub),
            swap_send.at[3 * part + k - 1], swap_recv.at[3 * part + k - 1],
            device_id={"fsdp": partner(k)}, device_id_type=MESH,
        )

    def start_swaps(part):
        for k in (2, 3, 1):
            swap(part, k).start()
        own_copy(part).start()

    def start_ring(part):
        own_copy(part).wait()
        if part != out_of:
            for k in (1, 2, 3):
                swap(part, k).wait_recv()
        rings.start(part, 0)

    def cut_channels(target, low):
        for pair in range(INNER // PAIR):
            member, at = pair % 4, pair // 4
            target[member, :, at * PAIR : (at + 1) * PAIR] = in_ref[
                :, low + pair * PAIR : low + (pair + 1) * PAIR
            ].astype(bf16)

    out_low[...] = out_ref[...].astype(bf16)
    own_copy(out_of).start()
    pieces = dot_lanes(in_ref[:, 2 * INNER :].astype(bf16), turn_ref[...]).astype(bf16)
    for member in range(4):
        small_cut[member] = pieces[:, member * PAIR : (member + 1) * PAIR]
    start_swaps(small_part)
    cut_channels(x_cut, INNER)
    start_swaps(x_of)
    start_ring(out_of)
    inputs = tokens_ref[...].astype(f32)
    inverse = lax.rsqrt(jnp.sum(inputs * inputs, axis=1, keepdims=True) / D + norm_eps)
    own_rows = pl.ds(pl.multiple_of(f * tokens, tokens), tokens)
    normed[own_rows, :] = (inputs * inverse * gain_in_ref[...]).astype(bf16)
    normed_copies = tokens_exchange(normed.at[own_rows], normed, token_send, token_recv, 0)
    cotangent_copies = tokens_exchange(
        cotangent_hbm, cotangent, token_send, token_recv, 3
    )
    cotangent_own = pltpu.make_async_copy(cotangent_hbm, cotangent.at[own_rows], local_sem.at[4])
    cotangent_own.start()
    for copy in normed_copies[:2]:
        copy.start()
    start_ring(small_part)
    start_ring(x_of)
    cut_channels(gate_cut, 0)
    start_swaps(gate_of)
    rings.start(small_part, 1)
    rings.start(small_part, 2)
    rings.start(x_of, 1)
    rings.start(out_of, 1)
    for hop in range(3, ring.far):
        rings.start(small_part, hop)
    normed_copies[0].wait_recv()
    normed_copies[2].start()
    for copy in cotangent_copies[:2]:
        copy.start()
    rings.finish(small_part)
    load_small = pltpu.make_async_copy(small_all, small_weight, local_sem.at[5])
    load_small.start()
    for copy in normed_copies[1:]:
        copy.wait_recv()
    load_small.wait()

    small = dot_rows(normed[...], small_weight[...]).T
    part = small[0:shared]
    pre = shared_taps_ref[:, CONV : CONV + 1] + jnp.zeros_like(part)
    for k in range(CONV):
        pre = pre + shared_taps_ref[:, k : k + 1] * shifted(part, CONV - 1 - k)
    shared_part_ref[...] = part
    shared_pre_ref[...] = pre
    shared_all[f] = (pre * jax.nn.sigmoid(pre)).astype(bf16)

    def shared_copy(k):
        return pltpu.make_async_remote_copy(
            shared_all.at[f], shared_all.at[f], shared_send.at[k - 1], shared_recv.at[k - 1],
            device_id={"fsdp": partner(k)}, device_id_type=MESH,
        )

    for k in (2, 3, 1):
        shared_copy(k).start()
    rings.start(x_of, 2)
    rings.start(out_of, 2)
    head_mask, step_bias, decay = head_ref[:, 0:1], head_ref[:, 1:2], head_ref[:, 2:3]
    logits = small[shared : shared + heads] * head_mask + step_bias
    steps = jnp.maximum(logits, 0.0) + jnp.log1p(jnp.exp(-jnp.abs(logits)))
    at_row = lax.broadcasted_iota(jnp.int32, (SPAN, SPAN), 0)
    at_lane = lax.broadcasted_iota(jnp.int32, (SPAN, SPAN), 1)
    upto = (at_row <= at_lane).astype(f32)
    rates = steps * decay
    log_sums = jnp.concatenate(
        [
            jnp.dot(
                rates[:, c * SPAN : (c + 1) * SPAN], upto, precision=highest,
                preferred_element_type=f32,
            )
            for c in range(chunks)
        ],
        axis=1,
    )
    column = jnp.concatenate(
        [log_sums, steps, logits, jnp.zeros((PAIR - 3 * heads, length), f32)], axis=0
    ).T
    column_ref[...] = column
    for group in range(groups):
        rolled = column if group == 0 else pltpu.roll(column, PAIR - group * GROUP, 1)
        columns_ref[:, group * PAIR : (group + 1) * PAIR] = rolled
        rows_ref[group * 8 : group * 8 + 8, :] = jnp.zeros((8, length), f32)
        rows_ref[group * 8 : group * 8 + GROUP, :] = log_sums[group * GROUP : (group + 1) * GROUP]
    for k in (1, 2, 3):
        shared_copy(k).wait_recv()
    keys_t[0:shared, :] = shared_all[0]
    keys_t[shared:, :] = shared_all[1]
    queries_t_ref[0:shared, :] = shared_all[2]
    queries_t_ref[shared:, :] = shared_all[3]
    keys_ref[...] = keys_t[...].T
    queries_ref[...] = queries_t_ref[...].T
    for hop in range(3, ring.far):
        rings.start(x_of, hop)
        rings.start(out_of, hop)
    cotangent_copies[0].wait_recv()
    cotangent_copies[2].start()

    def store(source, target, slot):
        return pltpu.make_async_copy(source, target, store_sem.at[slot])

    quarter = D // 4

    def turned_store(i):
        return store(turned.at[i % 2], row_slice(normed_t_all, i * quarter, quarter), i)

    for i in range(4):
        if i >= 2:
            turned_store(i - 2).wait()
        turned[i % 2] = normed[:, i * quarter : (i + 1) * quarter].T
        turned_store(i).start()
    rings.finish(x_of)
    start_ring(gate_of)

    def lanes(group):
        return pl.ds(group * LANES, LANES)

    def load_columns(source, group):
        return pltpu.make_async_copy(
            source.at[:, lanes(group)], weight.at[group % 2], load_sem.at[group % 2]
        )

    def x_store(group):
        return store(x_part.at[group % 2], x_part_all.at[:, lanes(group)], 4 + group)

    def states_store(group):
        return store(states.at[group % 2], states_all.at[:, :, lanes(group)], 8 + group)

    load_columns(x_all, 0).start()
    for group in range(groups):
        if group + 1 < groups:
            load_columns(x_all, group + 1).start()
        load_columns(x_all, group).wait()
        if group >= 2:
            x_store(group - 2).wait()
            states_store(group - 2).wait()
        slot = group % 2
        x_part[slot] = dot_rows(normed[...], weight[slot])
        x_store(group).start()
        scan_forward_kernel(
            x_part.at[slot], taps_ref.at[:, lanes(group)], bias_ref.at[:, lanes(group)],
            mask_ref.at[:, lanes(group)], skip_ref.at[:, lanes(group)],
            columns_ref.at[:, pl.ds(group * PAIR, PAIR)], rows_ref.at[pl.ds(group * 8, 8)],
            keys_ref, queries_ref, keys_t, block_ref, y.at[:, lanes(group)], states.at[slot],
            padded, state,
        )
        states_store(group).start()
        if group % 2 == 1 and group // 2 + 1 < ring.far - 1:
            rings.start(gate_of, group // 2 + 1)

    for copy in cotangent_copies[1:]:
        copy.wait_recv()
    cotangent_own.wait()
    cotangent_store = store(cotangent, cotangent_all, 12)
    cotangent_store.start()
    rings.finish(out_of)

    def load_rows(group):
        return pltpu.make_async_copy(
            out_all.at[lanes(group)], out_tile.at[group % 2], load_sem.at[2 + group % 2]
        )

    load_rows(0).start()
    for group in range(groups):
        if group + 1 < groups:
            load_rows(group + 1).start()
        load_rows(group).wait()
        gated_grad[:, lanes(group)] = dot_lanes(cotangent[...], out_tile[group % 2])
    rings.start(gate_of, ring.far - 1)
    rings.finish(gate_of)

    load_columns(gate_all, 0).start()
    for group in range(groups):
        if group + 1 < groups:
            load_columns(gate_all, group + 1).start()
        load_columns(gate_all, group).wait()
        here = lanes(group)
        value = dot_rows(normed[...], weight[group % 2]) * mask_ref[:, here]
        gate_part[:, here] = value
        gated = y[:, here] * (value * jax.nn.sigmoid(value))
        product = gated * (gated_grad[:, here] * gain_ref[:, here])
        gated = gated * gated
        gated = gated[:, :PAIR] + gated[:, PAIR:]
        product = product[:, :PAIR] + product[:, PAIR:]
        squares[...] = gated if group == 0 else squares[...] + gated
        products[...] = product if group == 0 else products[...] + product
    lane = lax.broadcasted_iota(jnp.int32, (length, PAIR), 1)
    both = jnp.where(
        lane == 0,
        jnp.sum(squares[...], axis=1, keepdims=True),
        jnp.where(lane == 1, jnp.sum(products[...], axis=1, keepdims=True), 0.0),
    )
    stats[...] = both.T[0:8]

    def stats_copy(k):
        return pltpu.make_async_remote_copy(
            stats, stats_in.at[k - 1], stats_send.at[k - 1], stats_recv.at[k - 1],
            device_id={"fsdp": partner(k)}, device_id_type=MESH,
        )

    for k in (2, 3, 1):
        stats_copy(k).start()
    for k in (1, 2, 3):
        stats_copy(k).wait_recv()
    total = (stats[...] + stats_in[0]) + (stats_in[1] + stats_in[2])
    channel_count = count_ref[0:1, 0:1]
    inverse_out = lax.rsqrt(total[0:1] / channel_count + norm_eps)
    pulls = inverse_out * inverse_out * inverse_out / channel_count * total[1:2]
    scales = jnp.concatenate(
        [inverse_out, pulls, jnp.zeros((PAIR - 2, length), f32)], axis=0
    ).T
    inverse_out, pulls = scales[:, 0:1], scales[:, 1:2]

    def back_stores(group):
        slot, at, here = group % 2, 13 + 4 * group, lanes(group)
        return [
            store(back_tiles.at[slot, 0], gated_all.at[:, here], at),
            store(back_tiles.at[slot, 1], y_grad_all.at[:, here], at + 1),
            store(back_tiles.at[slot, 2], gate_grad_all.at[:, here], at + 2),
            store(back_tiles_t.at[slot], gated_t_all.at[here], at + 3),
        ]

    gain_grad_ref[...] = jnp.zeros_like(gain_grad_ref)
    for group in range(groups):
        here, slot = lanes(group), group % 2
        if group >= 2:
            for copy in back_stores(group - 2):
                copy.wait()
        value, grad, gain = gate_part[:, here], gated_grad[:, here], gain_ref[:, here]
        gate = jax.nn.sigmoid(value)
        silu = value * gate
        y_here = y[:, here]
        gated = y_here * silu
        scaled = gated * inverse_out
        gated_low = (scaled * gain).astype(bf16)
        back_tiles[slot, 0] = gated_low
        back_tiles_t[slot] = gated_low.T
        gain_grad_ref[0:1, here] = jnp.sum(grad * scaled, axis=0, keepdims=True)
        back = inverse_out * (grad * gain) - gated * pulls
        back_tiles[slot, 1] = (back * silu).astype(bf16)
        back_tiles[slot, 2] = (
            back * y_here * (gate * (1.0 + value * (1.0 - gate))) * mask_ref[:, here]
        ).astype(bf16)
        for copy in back_stores(group):
            copy.start()

    for i in (2, 3):
        turned_store(i).wait()
    for group in range(groups - 2, groups):
        x_store(group).wait()
        states_store(group).wait()
        for copy in back_stores(group):
            copy.wait()
    cotangent_store.wait()
    for copy in normed_copies + cotangent_copies:
        copy.wait_send()
    for k in (1, 2, 3):
        shared_copy(k).wait_send()
        stats_copy(k).wait_send()
        for i in (small_part, x_of, gate_of):
            swap(i, k).wait_send()


def forward(
    tokens, cotangent, in_weight, out_weight, gain_in, gain, taps, bias, mask, skip, head_consts,
    shared_taps, channel_count,
):
    count, members = lax.axis_size("dp"), lax.axis_size("fsdp")
    own, sub, rows_out = tokens.shape[0], in_weight.shape[0], out_weight.shape[0]
    length, inner, shared = own * members, INNER // members, 2 * STATE // members
    chunks, groups = length // SPAN, inner // LANES
    assert groups == 4 and count == 8 and members == 4
    source = jnp.arange(2 * STATE + HEADS)
    head = source - 2 * STATE
    target = jnp.where(
        source < 2 * STATE,
        source // shared * PAIR + source % shared,
        head // 2 % members * PAIR + shared + head // (2 * members) * 2 + head % 2,
    )
    turn = (jnp.arange(members * PAIR)[:, None] == target[None, :]).astype(bf16)
    sd, dma = jax.ShapeDtypeStruct, pltpu.SemaphoreType.DMA
    vmem = pltpu.VMEM
    return pl.pallas_call(
        forward_kernel,
        in_specs=[whole_spec()] + any_specs(1) + [whole_spec()] * 13,
        out_specs=any_specs(12) + [whole_spec()] * 9,
        out_shape=[
            sd((D, PAIR), bf16),
            sd((D, inner), bf16),
            sd((D, inner), bf16),
            sd((inner, D), bf16),
            sd((length, D), bf16),
            sd((D, length), bf16),
            sd((length, inner), f32),
            sd((chunks, STATE, inner), bf16),
            sd((length, inner), bf16),
            sd((inner, length), bf16),
            sd((length, inner), bf16),
            sd((length, inner), bf16),
            sd((length, groups * PAIR), f32),
            sd((groups * 8, length), f32),
            sd((length, PAIR), f32),
            sd((length, STATE), bf16),
            sd((length, STATE), bf16),
            sd((STATE, length), bf16),
            sd((shared, length), f32),
            sd((shared, length), f32),
            sd((8, inner), f32),
        ],
        scratch_shapes=[
            vmem((members, sub, PAIR), bf16),
            vmem((members, sub, inner), bf16),
            vmem((members, sub, inner), bf16),
            vmem((rows_out, D), bf16),
            vmem((length, D), bf16),
            vmem((length, D), bf16),
            vmem((D, PAIR), bf16),
            vmem((STATE, length), bf16),
            vmem((members, shared, length), bf16),
            vmem((2, length, LANES), f32),
            vmem((2, chunks, STATE, LANES), bf16),
            vmem((length, inner), f32),
            vmem((length, inner), f32),
            vmem((length, inner), f32),
            vmem((2, D, LANES), bf16),
            vmem((2, LANES, D), bf16),
            vmem((2, D // 4, length), bf16),
            vmem((length, PAIR), f32),
            vmem((length, PAIR), f32),
            vmem((8, length), f32),
            vmem((3, 8, length), f32),
            vmem((2, 3, length, LANES), bf16),
            vmem((2, LANES, length), bf16),
            vmem((length + 8, LANES), f32),
            vmem((STATE, LANES), f32),
            dma((6,)),
            dma((9,)),
            dma((9,)),
            dma((6,)),
            dma((6,)),
            RingGather.semaphores(4, count),
            RingGather.semaphores(4, count),
            dma((3,)),
            dma((3,)),
            dma((3,)),
            dma((3,)),
            dma((4,)),
            dma((13 + 4 * groups,)),
        ],
        compiler_params=pltpu.CompilerParams(
            collective_id=0, has_side_effects=True, vmem_limit_bytes=VMEM_BYTES
        ),
        name="forward",
    )(
        tokens, cotangent, in_weight, out_weight, turn, gain_in, gain, taps, bias, mask, skip,
        head_consts, shared_taps, block_mask(), jnp.broadcast_to(channel_count, (8, PAIR)),
    )


def total_squares(value):
    return jnp.sum(jnp.sum(value * value, axis=0, keepdims=True), axis=1, keepdims=True)


def scan_scatter_kernel(
    x_ref, taps_ref, bias_ref, mask_ref, skip_ref, column_ref, row_ref, key_ref, query_ref,
    query_t_ref, block_ref, pick_ref, grad_ref, states_ref,
    normed_t_ref, gate_grad_ref, gated_ref, gated_t_ref, cotangent_ref, weight_ref, tokens_ref,
    x_grad_ref, key_grad_ref, query_grad_ref, sums_ref, rest_ref, channel_ref,
    gate_raw_ref, out_raw_ref, layer_out_ref, squares_ref,
    padded, following, state_back, inner_grad, added, added_out, added_in, added_send, added_recv,
    *ring_scratch,
):
    ring = Ring()
    step = pl.program_id(0)
    steps = pl.num_programs(0)
    gate_ring = RingScatter(ring, *ring_scratch[:4])
    out_ring = RingScatter(ring, *ring_scratch[4:])
    rows_in, rows_out = gate_raw_ref.shape[0], out_raw_ref.shape[0]
    tokens = tokens_ref.shape[0]

    def gate_term(owner):
        here = pl.ds(pl.multiple_of(owner * rows_in, rows_in), rows_in)
        return dot_rows(normed_t_ref[here, :], gate_grad_ref[...])

    def out_term(owner):
        here = pl.ds(pl.multiple_of(owner * rows_out, rows_out), rows_out)
        return dot_rows(gated_t_ref[here, :], cotangent_ref[...])

    def added_block(flip):
        here = pl.ds(pl.multiple_of(partner(flip) * tokens, tokens), tokens)
        return dot_rows(gated_ref[here, :], weight_ref[...])

    def added_copy(i):
        return pltpu.make_async_remote_copy(
            added_out.at[i], added_in.at[i], added_send.at[i], added_recv.at[i],
            device_id={"fsdp": partner(2 if i == 2 else 1)}, device_id_type=MESH,
        )

    @pl.when(step == 0)
    def _():
        greet([{"fsdp": partner(k)} for k in (1, 2)] + [ring.target(0), ring.target(1)])

    for hop in range(ring.far):
        @pl.when(step == hop)
        def _(hop=hop):
            out_ring.start(hop, out_term)
            gate_ring.start(hop, gate_term)

    @pl.when(step == 0)
    def _():
        for i, flip in ((1, 3), (0, 1)):
            added_out[i] = added_block(flip).astype(bf16)
            added_copy(i).start()

    @pl.when(step == 1)
    def _():
        value = added_block(2)
        added_copy(1).wait_recv()
        added_out[2] = (value + added_in[1].astype(f32)).astype(bf16)
        added_copy(2).start()

    @pl.when(step == 2)
    def _():
        added[...] = added_block(0)

    scan_backward_kernel(
        x_ref, taps_ref, bias_ref, mask_ref, skip_ref, column_ref, row_ref, key_ref, query_ref,
        query_t_ref, block_ref, pick_ref, grad_ref, states_ref,
        x_grad_ref, key_grad_ref, query_grad_ref, sums_ref, rest_ref, channel_ref,
        padded, following, state_back, inner_grad,
    )

    @pl.when(step == steps - 1)
    def _():
        added_copy(0).wait_recv()
        added_copy(2).wait_recv()
        layer_out_ref[...] = (
            tokens_ref[...].astype(f32)
            + ((added[...] + added_in[0].astype(f32)) + added_in[2].astype(f32))
        ).astype(bf16)
        for i in range(3):
            added_copy(i).wait_send()
        out_raw = out_ring.finish(out_term)
        out_raw_ref[...] = out_raw
        gate_raw = gate_ring.finish(gate_term)
        gate_raw_ref[...] = gate_raw.astype(bf16)
        squares_ref[...] = jnp.broadcast_to(
            total_squares(out_raw) + total_squares(gate_raw), squares_ref.shape
        )


def scan_scatter(
    x, taps, bias, mask, skip, columns, rows, keys, queries, queries_t, grad, states,
    normed_t, gate_grad, gated, gated_t, cotangent, weight, tokens,
):
    length, width = x.shape
    chunks = length // SPAN
    groups = width // LANES
    count = lax.axis_size("dp")
    assert groups == count // 2
    rows_in, rows_out, own = D // count, width // count, tokens.shape[0]
    same = lambda g: (0, 0)
    return pl.pallas_call(
        scan_scatter_kernel,
        grid=(groups,),
        in_specs=head_specs(length)
        + [
            pl.BlockSpec((3, LANES, PAIR), lambda g: (g, 0, 0)),
            lane_spec(length),
            pl.BlockSpec((chunks, STATE, LANES), lambda g: (0, 0, g)),
        ]
        + [whole_spec()] * 7,
        out_specs=[
            lane_spec(length),
            pl.BlockSpec((length, STATE), same),
            pl.BlockSpec((length, STATE), same),
            pl.BlockSpec((length, PAIR), same),
            pl.BlockSpec((chunks, 1, LANES), lambda g: (0, 0, g)),
            lane_spec(8),
        ]
        + [whole_spec()] * 4,
        out_shape=[
            jax.ShapeDtypeStruct((length, width), bf16),
            jax.ShapeDtypeStruct((length, STATE), f32),
            jax.ShapeDtypeStruct((length, STATE), f32),
            jax.ShapeDtypeStruct((length, PAIR), f32),
            jax.ShapeDtypeStruct((chunks, 1, width), f32),
            jax.ShapeDtypeStruct((8, width), f32),
            jax.ShapeDtypeStruct((rows_in, width), bf16),
            jax.ShapeDtypeStruct((rows_out, D), f32),
            jax.ShapeDtypeStruct((own, D), bf16),
            jax.ShapeDtypeStruct((8, PAIR), f32),
        ],
        scratch_shapes=[
            pltpu.VMEM((length + 8, LANES), f32),
            pltpu.VMEM((8, LANES), f32),
            pltpu.VMEM((STATE, LANES), f32),
            pltpu.VMEM((chunks, SPAN, SPAN), f32),
            pltpu.VMEM((own, D), f32),
            pltpu.VMEM((3, own, D), bf16),
            pltpu.VMEM((3, own, D), bf16),
            pltpu.SemaphoreType.DMA((3,)),
            pltpu.SemaphoreType.DMA((3,)),
        ]
        + RingScatter.scratch(count, rows_in, width)
        + RingScatter.scratch(count, rows_out, D),
        compiler_params=pltpu.CompilerParams(
            collective_id=2, has_side_effects=True, vmem_limit_bytes=VMEM_BYTES
        ),
        name="scan_scatter",
    )(
        x, taps, bias, mask, skip, columns, rows, keys, queries, queries_t, block_mask(),
        pick_masks(groups), grad, states,
        normed_t, gate_grad, gated, gated_t, cotangent, weight, tokens,
    )


def flipped(member, flip):
    return member + flip - 2 * flip * lax.rem(lax.div(member, flip), 2)


def shifted(value, by):
    length = value.shape[1]
    lane = lax.broadcasted_iota(jnp.int32, value.shape, 1)
    if by == 0:
        return value
    if by > 0:
        return jnp.where(lane >= by, pltpu.roll(value, by, 1), 0.0)
    return jnp.where(lane < length + by, pltpu.roll(value, length + by, 1), 0.0)


def last_scatter_kernel(
    x_grad_ref, normed_t_ref, gate_grad_hbm, weight_gate_hbm, weight_x_hbm, weight_small_ref,
    key_grad_ref, query_grad_ref, sums_ref, rest_ref, head_pick_ref, steps_ref, heads_ref,
    shared_part_ref, shared_pre_ref, taps_ref, tokens_ref, cotangent_ref, inverse_ref, gain_ref,
    gate_raw_ref, channel_ref, gate_gain_ref, squares_ref,
    gate_back_ref, x_back_ref, small_back_ref, token_grad_ref, vectors_ref, total_ref,
    gate_grad, weight_gate, weight_x, load_sem,
    shared_own, shared_out, shared_in, swap_send, swap_recv, raw, small_t, small_n,
    kept, back_out, back_in, back_send, back_recv,
    vector_sum, vector_in, vector_send, vector_recv,
    x_out, small_out, return_send, return_recv, local_sem,
    scalar_out, scalar_in, scalar_send, scalar_recv,
    *ring_scratch,
):
    ring = Ring()
    d, f = ring.me, lax.axis_index("fsdp")
    count = ring.count
    x_ring = RingScatter(ring, *ring_scratch[:4])
    small_ring = RingScatter(ring, *ring_scratch[4:])
    loads = [
        pltpu.make_async_copy(source, target, load_sem.at[i])
        for i, (source, target) in enumerate(
            [(gate_grad_hbm, gate_grad), (weight_gate_hbm, weight_gate), (weight_x_hbm, weight_x)]
        )
    ]
    for load in loads:
        load.start()
    near = [{"fsdp": partner(k)} for k in (1, 2, 3)]
    over = [{"dp": lax.rem(d + k, count)} for k in range(1, count)]
    greet(near + over)
    length, shared = x_grad_ref.shape[0], shared_own.shape[1]
    rows, sub = x_out.shape[0], x_back_ref.shape[1]
    tokens = tokens_ref.shape[0]

    def rows_of(owner):
        return pl.ds(pl.multiple_of(owner * rows, rows), rows)

    def x_term(owner):
        return dot_rows(normed_t_ref[rows_of(owner), :], x_grad_ref[...])

    def small_term(owner):
        return dot_lanes(normed_t_ref[rows_of(owner), :], small_t[...])

    def to_partner(k, source, target, send, recv, at):
        return pltpu.make_async_remote_copy(
            source, target, send.at[at], recv.at[at],
            device_id={"fsdp": partner(k)}, device_id_type=MESH,
        )

    def return_copy(part, k):
        source = (gate_raw_ref, x_out, small_out)[part]
        target = (gate_back_ref, x_back_ref, small_back_ref)[part]
        return to_partner(
            k, row_slice(source, partner(k) * sub, sub), target.at[f],
            return_send, return_recv, part * 3 + k - 1,
        )

    def own_copy(part):
        source = (gate_raw_ref, x_out, small_out)[part]
        target = (gate_back_ref, x_back_ref, small_back_ref)[part]
        return pltpu.make_async_copy(
            row_slice(source, f * sub, sub), target.at[f], local_sem.at[part]
        )

    x_ring.start(0, x_term)

    for i, ref in ((0, key_grad_ref), (2, query_grad_ref)):
        turned = ref[...].T
        for j in (0, 1):
            shared_own[i + j] = turned[j * shared : (j + 1) * shared]
            shared_out[i + j] = turned[j * shared : (j + 1) * shared].astype(bf16)

    def shared_copy(k):
        return to_partner(
            k, shared_out.at[partner(k)], shared_in.at[k - 1], swap_send, swap_recv, k - 1
        )

    for k in (2, 3, 1):
        shared_copy(k).start()
    for k in (2, 3, 1):
        return_copy(0, k).start()
    own_copy(0).start()

    at_row = lax.broadcasted_iota(jnp.int32, (SPAN, SPAN), 0)
    at_lane = lax.broadcasted_iota(jnp.int32, (SPAN, SPAN), 1)
    later = (at_lane >= at_row).astype(f32)
    earlier = (at_lane < at_row).astype(f32)
    precise = partial(jnp.dot, precision=highest, preferred_element_type=f32)
    heads = HEADS // 4
    rest = precise(rest_ref[...], head_pick_ref[...])
    decay, head_mask = heads_ref[0:1, :], heads_ref[1:2, :]
    step_bias_grad = jnp.zeros((1, PAIR), f32)
    decay_grad = jnp.zeros((1, PAIR), f32)
    for c in range(length // SPAN):
        here = slice(c * SPAN, (c + 1) * SPAN)
        sums = sums_ref[here, :]
        log_grad = (
            precise(later, sums)
            + pltpu.roll(precise(earlier, sums), PAIR - heads, 1)
            + rest[c : c + 1]
        )
        steps = pltpu.roll(steps_ref[here, :], PAIR - heads, 1)
        logits = pltpu.roll(steps_ref[here, :], PAIR - 2 * heads, 1)
        raw_grad = (decay * log_grad + pltpu.roll(sums, PAIR - 2 * heads, 1)) * jax.nn.sigmoid(
            logits
        )
        step_bias_grad = step_bias_grad + jnp.sum(raw_grad, axis=0, keepdims=True)
        decay_grad = decay_grad + jnp.sum(steps * log_grad, axis=0, keepdims=True)
        raw[here, :] = raw_grad * head_mask
    decay_grad = decay_grad * decay

    x_ring.start(1, x_term)

    for k in (2, 3, 1):
        shared_copy(k).wait_recv()
    part, pre = shared_part_ref[...], shared_pre_ref[...]
    gate = jax.nn.sigmoid(pre)
    pre_grad = shared_own[f]
    for k in (1, 2, 3):
        pre_grad = pre_grad + shared_in[k - 1].astype(f32)
    pre_grad = pre_grad * (gate * (1.0 + pre * (1.0 - gate)))
    shared_grad = jnp.zeros_like(pre_grad)
    lane = lax.broadcasted_iota(jnp.int32, (shared, PAIR), 1)
    shared_sums = jnp.where(lane == CONV, jnp.sum(pre_grad, axis=1, keepdims=True), 0.0)
    for k in range(CONV):
        shift = CONV - 1 - k
        shared_grad = shared_grad + taps_ref[:, k : k + 1] * shifted(pre_grad, -shift)
        shared_sums = shared_sums + jnp.where(
            lane == k, jnp.sum(pre_grad * shifted(part, shift), axis=1, keepdims=True), 0.0
        )
    small_t[0:shared, :] = shared_grad.astype(bf16)
    small_t[shared:, :] = raw[...].T[0 : PAIR - shared].astype(bf16)
    small_n[...] = small_t[...].T
    small_ring.start(0, small_term)

    for load in loads:
        load.wait()

    def back_block(flip):
        here = pl.ds(pl.multiple_of(partner(flip) * tokens, tokens), tokens)
        return (
            dot_lanes(gate_grad[here, :], weight_gate[...])
            + dot_lanes(x_grad_ref[here, :], weight_x[...])
            + dot_lanes(small_n[here, :], weight_small_ref[...])
        )

    def back_copy(i):
        return to_partner(
            2 if i == 2 else 1, back_out.at[i], back_in.at[i], back_send, back_recv, i
        )

    for i, flip in ((1, 3), (0, 1)):
        back_out[i] = back_block(flip).astype(bf16)
        back_copy(i).start()
    value = back_block(2)
    back_copy(1).wait_recv()
    back_out[2] = (value + back_in[1].astype(f32)).astype(bf16)
    back_copy(2).start()
    x_ring.start(2, x_term)
    small_ring.start(1, small_term)
    kept[...] = back_block(0)
    for hop in range(3, ring.far):
        x_ring.start(hop, x_term)
        small_ring.start(hop - 1, small_term)
    back_copy(0).wait_recv()
    back_copy(2).wait_recv()
    inputs, inverse = tokens_ref[...].astype(f32), inverse_ref[...]
    normed_grad = (kept[...] + back_in[0].astype(f32)) + back_in[2].astype(f32)
    pulled = normed_grad * gain_ref[...]
    scaled = inputs * inverse
    input_grad = inverse * (
        pulled - scaled * (jnp.sum(pulled * scaled, axis=1, keepdims=True) / D)
    )
    token_grad_ref[...] = (cotangent_ref[...].astype(f32) + input_grad).astype(bf16)
    gain_grad = jnp.sum(normed_grad * scaled, axis=0, keepdims=True)

    width = vector_sum.shape[1]
    vector_sum[...] = jnp.zeros_like(vector_sum)
    vector_sum[0:1, :] = gate_gain_ref[0:1, :]
    vector_sum[1 : CONV + 3, :] = channel_ref[0 : CONV + 2, :]
    for i in range(D // width):
        vector_sum[CONV + 3 + i : CONV + 4 + i, :] = gain_grad[:, i * width : (i + 1) * width]
    vector_sum[15:16, 0:PAIR] = step_bias_grad
    vector_sum[15:16, PAIR : 2 * PAIR] = decay_grad
    wide = jnp.concatenate([shared_sums, jnp.zeros((PAIR - shared, PAIR), f32)], axis=0)
    vector_sum[16:24, 0:PAIR] = wide.T[0:8]

    def vector_copy(step, flip):
        return pltpu.make_async_remote_copy(
            vector_in.at[step, 0], vector_in.at[step, 1], vector_send.at[step],
            vector_recv.at[step],
            device_id={"dp": flipped(d, flip)}, device_id_type=MESH,
        )

    flips = []
    while 1 << len(flips) < count:
        flips.append(1 << len(flips))
    for step, flip in enumerate(flips):
        vector_in[step, 0] = vector_sum[...]
        vector_copy(step, flip).start()
        if step == 0:
            small_ring.start(ring.far - 1, small_term)
        vector_copy(step, flip).wait_recv()
        vector_sum[...] = vector_sum[...] + vector_in[step, 1]

    def vector_spread(k):
        return to_partner(
            k, vector_sum, vectors_ref.at[f], vector_send, vector_recv, len(flips) + k - 1
        )

    for k in (2, 3, 1):
        vector_spread(k).start()
    vectors_ref[f] = vector_sum[...]

    x_raw = x_ring.finish(x_term)
    x_out[...] = x_raw.astype(bf16)
    for k in (2, 3, 1):
        return_copy(1, k).start()
    own_copy(1).start()
    small_raw = small_ring.finish(small_term)
    small_out[...] = small_raw.astype(bf16)
    for k in (2, 3, 1):
        return_copy(2, k).start()
    own_copy(2).start()

    total = squares_ref[...] + jnp.broadcast_to(
        total_squares(x_raw) + total_squares(small_raw), squares_ref.shape
    )
    scalar_out[0] = total

    def near_scalar(k):
        return to_partner(
            k, scalar_out.at[0], scalar_in.at[k], scalar_send, scalar_recv, k
        )

    for k in (2, 3, 1):
        near_scalar(k).start()
    for k in (2, 3, 1):
        near_scalar(k).wait_recv()
    total = (total + scalar_in[1]) + (scalar_in[2] + scalar_in[3])
    scalar_out[1] = total

    def far_scalar(k):
        member = d
        for bit in flips:
            if k & bit:
                member = flipped(member, bit)
        return pltpu.make_async_remote_copy(
            scalar_out.at[1], scalar_in.at[3 + k], scalar_send.at[3 + k], scalar_recv.at[3 + k],
            device_id={"dp": member}, device_id_type=MESH,
        )

    for k in range(count - 1, 0, -1):
        far_scalar(k).start()
    parts = [total]
    for k in range(1, count):
        far_scalar(k).wait_recv()
        parts.append(scalar_in[3 + k])
    while len(parts) > 1:
        parts = [parts[i] + parts[i + 1] for i in range(0, len(parts), 2)]
    total_ref[...] = parts[0]

    for k in (1, 2, 3):
        vector_spread(k).wait_recv()
        vector_spread(k).wait_send()
        shared_copy(k).wait_send()
        near_scalar(k).wait_send()
        for i in range(3):
            return_copy(i, k).wait_recv()
            return_copy(i, k).wait_send()
    for k in range(1, count):
        far_scalar(k).wait_send()
    for i in range(3):
        back_copy(i).wait_send()
        own_copy(i).wait()
    for step, flip in enumerate(flips):
        vector_copy(step, flip).wait_send()


def last_scatter(
    x_grad, normed_t, gate_grad, weight_gate, weight_x, weight_small, key_grad, query_grad, sums,
    rest, steps, head_rows, shared_part, shared_pre, taps, tokens, cotangent, inverse, gain,
    gate_raw, channel, gate_gain, squares,
):
    length, width = x_grad.shape
    count, members = lax.axis_size("dp"), lax.axis_size("fsdp")
    rows = D // count
    sub, own, shared = rows // members, tokens.shape[0], shared_part.shape[0]
    hops = max(count - 1, 1).bit_length()
    head_pick = (
        jnp.arange(width)[:, None] // HEAD_DIM == jnp.arange(PAIR)[None, :]
    ).astype(f32)
    dma = pltpu.SemaphoreType.DMA
    sd = jax.ShapeDtypeStruct
    return pl.pallas_call(
        last_scatter_kernel,
        in_specs=[whole_spec()] * 2 + any_specs(3) + [whole_spec()] * 19,
        out_specs=[whole_spec()] * 6,
        out_shape=[
            sd((members, sub, width), bf16),
            sd((members, sub, width), bf16),
            sd((members, sub, PAIR), bf16),
            sd((own, D), bf16),
            sd((members, 24, width), f32),
            sd((8, PAIR), f32),
        ],
        scratch_shapes=[
            pltpu.VMEM((length, width), bf16),
            pltpu.VMEM((D, width), bf16),
            pltpu.VMEM((D, width), bf16),
            dma((3,)),
            pltpu.VMEM((members, shared, length), f32),
            pltpu.VMEM((members, shared, length), bf16),
            pltpu.VMEM((members - 1, shared, length), bf16),
            dma((3,)),
            dma((3,)),
            pltpu.VMEM((length, PAIR), f32),
            pltpu.VMEM((PAIR, length), bf16),
            pltpu.VMEM((length, PAIR), bf16),
            pltpu.VMEM((own, D), f32),
            pltpu.VMEM((3, own, D), bf16),
            pltpu.VMEM((3, own, D), bf16),
            dma((3,)),
            dma((3,)),
            pltpu.VMEM((24, width), f32),
            pltpu.VMEM((hops, 2, 24, width), f32),
            dma((hops + 3,)),
            dma((hops + 3,)),
            pltpu.VMEM((rows, width), bf16),
            pltpu.VMEM((rows, PAIR), bf16),
            dma((9,)),
            dma((9,)),
            dma((3,)),
            pltpu.VMEM((2, 8, PAIR), f32),
            pltpu.VMEM((3 + count, 8, PAIR), f32),
            dma((3 + count,)),
            dma((3 + count,)),
        ]
        + RingScatter.scratch(count, rows, width)
        + RingScatter.scratch(count, rows, PAIR),
        compiler_params=pltpu.CompilerParams(
            collective_id=3, has_side_effects=True, vmem_limit_bytes=VMEM_BYTES
        ),
        name="last_scatter",
    )(
        x_grad, normed_t, gate_grad, weight_gate, weight_x, weight_small, key_grad, query_grad,
        sums, rest, head_pick, steps, head_rows, shared_part, shared_pre, taps, tokens, cotangent,
        inverse, gain, gate_raw, channel, gate_gain, squares,
    )


COLUMN_TILE = 512


def step_in_kernel(
    factor_ref, gate_ref, x_ref, small_ref, turn_ref, weight_ref, first_ref, second_ref,
    grad_ref, moment_ref, square_ref, master_ref, rounded_ref, raw,
):
    step = pl.program_id(0)
    tiles = INNER // COLUMN_TILE

    def joined(ref):
        return jnp.concatenate([ref[i] for i in range(ref.shape[0])], axis=1)

    @pl.when(step < tiles)
    def _():
        raw[...] = joined(gate_ref).astype(f32)

    @pl.when((step >= tiles) & (step < 2 * tiles))
    def _():
        raw[...] = joined(x_ref).astype(f32)

    @pl.when(step == 2 * tiles)
    def _():
        raw[...] = dot_rows(joined(small_ref), turn_ref[...])

    grad = raw[...] * factor_ref[0:1, 0:1]
    moment, square, master = adamw(
        weight_ref[...], first_ref[...], second_ref[...], grad, rate_in_proj
    )
    grad_ref[...] = grad
    moment_ref[...] = moment
    square_ref[...] = square
    master_ref[...] = master
    rounded_ref[...] = master.astype(bf16)


def step_in(factor, gate, x, small, weight, first, second):
    members, rows, width = x.shape
    tiles = INNER // COLUMN_TILE
    shared, heads = 2 * STATE // members, HEADS // members
    target = jnp.arange(COLUMN_TILE)
    head = target - 2 * STATE
    source = jnp.where(
        target < 2 * STATE,
        target // shared * PAIR + target % shared,
        head // 2 % members * PAIR + shared + head // (2 * members) * 2 + head % 2,
    )
    turn = (
        (jnp.arange(members * PAIR)[:, None] == source[None, :])
        & (target < 2 * STATE + HEADS)[None, :]
    ).astype(bf16)
    piece = lambda low: pl.BlockSpec(
        (members, rows, PAIR), lambda j: (0, 0, jnp.clip(j - low, 0, tiles - 1))
    )
    flat = pl.BlockSpec((rows, COLUMN_TILE), lambda j: (0, j))
    shape = jax.ShapeDtypeStruct(weight.shape, f32)
    return pl.pallas_call(
        step_in_kernel,
        grid=(2 * tiles + 1,),
        in_specs=[whole_spec(), piece(0), piece(tiles), whole_spec(), whole_spec()] + [flat] * 3,
        out_specs=[flat] * 5,
        out_shape=[shape] * 4 + [jax.ShapeDtypeStruct(weight.shape, bf16)],
        scratch_shapes=[pltpu.VMEM((rows, COLUMN_TILE), f32)],
        compiler_params=pltpu.CompilerParams(vmem_limit_bytes=VMEM_BYTES),
        name="step_in",
    )(factor, gate, x, small, turn, weight, first, second)


def unpack(vectors):
    offset = D + INNER
    taps_end = offset + CONV * XBC
    heads_start = taps_end + XBC
    norm_gain = vectors[:D]
    gate_gain = vectors[D:offset]
    filter_taps = vectors[offset:taps_end].reshape(CONV, XBC)
    filter_bias = vectors[taps_end:heads_start]
    step_bias = vectors[heads_start : heads_start + HEADS]
    decay_log = vectors[heads_start + HEADS : heads_start + 2 * HEADS]
    skip_gain = vectors[heads_start + 2 * HEADS : heads_start + 3 * HEADS]
    return (norm_gain, gate_gain, filter_taps, filter_bias, step_bias, decay_log, skip_gain)


def adamw(weight, moment, square, gradient, step_rate):
    moment_new = beta_first * moment + (1.0 - beta_first) * gradient
    square_new = beta_second * square + (1.0 - beta_second) * gradient * gradient
    moment_hat = moment_new / (1.0 - beta_first**STEP)
    square_hat = square_new / (1.0 - beta_second**STEP)
    weight_new = weight - step_rate * (
        moment_hat / (jnp.sqrt(square_hat) + adam_eps) + weight_decay * weight
    )
    return (moment_new, square_new, weight_new)


def on_device(
    tokens,
    widths,
    cotangent,
    in_weight,
    in_first,
    in_second,
    out_weight,
    out_first,
    out_second,
    vectors,
    vector_first,
    vector_second,
):
    fsdp = lax.axis_size("fsdp")
    me = lax.axis_index("fsdp")
    heads = HEADS // fsdp
    inner = INNER // fsdp
    shared = 2 * STATE // fsdp
    pairs = HEADS // 2 // fsdp
    rows_in, rows_out = in_weight.shape[0], out_weight.shape[0]
    length = tokens.shape[0] * fsdp
    chunks = length // SPAN
    in_kernels = uses_ring("dp") and rows_out == PAIR and rows_in % 16 == 0

    def own_channels(v):
        lead = v.shape[:-1]
        cut = v.reshape(lead + (pairs, fsdp, PAIR))
        return lax.dynamic_index_in_dim(cut, me, len(lead) + 1, False).reshape(lead + (inner,))

    def own_heads(v):
        return lax.dynamic_index_in_dim(v.reshape(pairs, fsdp, 2), me, 1, False).reshape(heads)

    def own_shared(v):
        return lax.dynamic_slice_in_dim(v, me * shared, shared, v.ndim - 1)

    norm_gain, gate_gain, filter_taps, filter_bias, step_bias, decay_log, skip_gain = unpack(
        vectors
    )
    gain_own = own_channels(gate_gain)[None]
    taps_own = own_channels(filter_taps[:, :INNER])
    bias_own = own_channels(filter_bias[:INNER])[None]
    taps_shared = own_shared(filter_taps[:, INNER:])
    bias_shared = own_shared(filter_bias[INNER:])
    step_bias_own, decay_own = own_heads(step_bias), -jnp.exp(own_heads(decay_log))
    skip_own = jnp.repeat(own_heads(skip_gain), HEAD_DIM)[None]

    width_index = widths[0]
    active = HEADS // 8 * jnp.left_shift(jnp.int32(1), width_index)
    head_mask = (jnp.arange(heads, dtype=jnp.int32) < active // fsdp).astype(f32)
    mask = jnp.repeat(head_mask, HEAD_DIM)[None]
    channel_count = (active * HEAD_DIM).astype(f32)

    inputs = tokens.astype(f32)
    inverse_in = lax.rsqrt(jnp.mean(inputs * inputs, axis=-1, keepdims=True) + norm_eps)

    if in_kernels:
        head_consts = jnp.pad(
            jnp.stack([head_mask, step_bias_own, decay_own], axis=1), ((0, 0), (0, PAIR - 3))
        )
        shared_taps = jnp.pad(
            jnp.concatenate([taps_shared, bias_shared[None]]).T, ((0, 0), (0, PAIR - CONV - 1))
        )
        (
            weight_shared, weight_x, weight_gate, weight_out, cotangents, normed_t, x_part, states,
            gated_low, gated_t, y_grad, gate_grad, head_columns, head_rows, head_all, keys,
            queries, queries_t, shared_part, shared_pre, gain_grad,
        ) = forward(
            tokens, cotangent, in_weight, out_weight, norm_gain[None], gain_own, taps_own,
            bias_own, mask, skip_own, head_consts, shared_taps, channel_count,
        )
        scan_inputs = (taps_own, bias_own, mask, skip_own, head_columns, head_rows, keys, queries)
    else:
        in_low = in_weight.astype(bf16)
        shared_cut = jnp.concatenate(
            [
                in_low[:, 2 * INNER : 2 * INNER + 2 * STATE]
                .reshape(rows_in, fsdp, shared)
                .transpose(1, 0, 2),
                in_low[:, 2 * INNER + 2 * STATE :]
                .reshape(rows_in, pairs, fsdp, 2)
                .transpose(2, 0, 1, 3)
                .reshape(fsdp, rows_in, heads),
            ],
            axis=2,
        )

        def channel_cut(part):
            return (
                part.reshape(rows_in, pairs, fsdp, PAIR)
                .transpose(2, 0, 1, 3)
                .reshape(fsdp, rows_in, inner)
            )

        def gathered(cut):
            block = exchanged(cut, "fsdp")
            return gather_rows(block.reshape(fsdp * rows_in, cut.shape[2]), "dp")

        normed_own = (inputs * inverse_in * norm_gain[None, :]).astype(bf16)
        x_cut = channel_cut(in_low[:, INNER : 2 * INNER])
        gate_cut = channel_cut(in_low[:, :INNER])
        out_low = out_weight.astype(bf16)

        weight_shared = gathered(shared_cut)
        weight_x = gathered(x_cut)
        weight_gate = gathered(gate_cut)
        weight_out = lax.dynamic_index_in_dim(
            lax.all_gather(out_low, ("dp", "fsdp"), axis=0, tiled=True).reshape(
                pairs, fsdp, PAIR, D
            ),
            me,
            1,
            False,
        ).reshape(inner, D)
        normed = spread(normed_own, "fsdp").reshape(length, D)
        cotangents = spread(cotangent, "fsdp").reshape(length, D)

        small = lax.dot_general(
            weight_shared, normed, (((0,), (1,)), ((), ())), preferred_element_type=f32
        )
        shared_part = small[:shared]
        step_raw = small[shared : shared + heads] * head_mask[:, None]
        shared_padded = jnp.pad(shared_part, ((0, 0), (CONV - 1, 0)))
        shared_pre = bias_shared[:, None] + sum(
            taps_shared[k][:, None] * shared_padded[:, k : k + length] for k in range(CONV)
        )
        shared_gate = jax.nn.sigmoid(shared_pre)
        shared_all = spread_small((shared_pre * shared_gate).astype(bf16), "fsdp").reshape(
            2 * STATE, length
        )
        keys_t, queries_t = shared_all[:STATE], shared_all[STATE:]
        keys, queries = keys_t.T, queries_t.T
        step_logits = step_raw + step_bias_own[:, None]
        step_sizes = jax.nn.softplus(step_logits)
        upto = (jnp.arange(SPAN)[:, None] <= jnp.arange(SPAN)[None, :]).astype(f32)
        log_sums = jnp.dot(
            (step_sizes * decay_own[:, None]).reshape(heads, chunks, SPAN), upto, precision=highest
        ).reshape(heads, length)
        groups = heads // GROUP
        head_all = jnp.concatenate(
            [log_sums, step_sizes, step_logits, jnp.zeros((PAIR - 3 * heads, length), f32)]
        ).T
        head_columns = jnp.concatenate(
            [jnp.roll(head_all, -group * GROUP, axis=1) for group in range(groups)], axis=1
        )
        head_rows = jnp.pad(
            log_sums.reshape(groups, GROUP, length), ((0, 0), (0, 8 - GROUP), (0, 0))
        ).reshape(groups * 8, length)

        scan_inputs = (taps_own, bias_own, mask, skip_own, head_columns, head_rows, keys, queries)
        x_part = jnp.dot(normed, weight_x, preferred_element_type=f32)
        y, states = scan_forward(x_part, *scan_inputs, keys_t)
        gate_part, gated_grad, stats = gate_forward(
            normed, weight_gate, cotangents, weight_out, y, gain_own, mask
        )
        stats = summed(stats[:, :2].T, "fsdp")
        inverse_out = lax.rsqrt(stats[0] / channel_count + norm_eps)
        pull = inverse_out**3 / channel_count * stats[1]
        gated_low, y_grad, gate_grad, gain_grad = norm_back(
            y, gate_part, gated_grad, jnp.stack([inverse_out, pull], axis=1), gain_own, mask
        )

        def in_term(grad):
            return lax.dot_general(
                normed, grad, (((0,), (0,)), ((), ())), preferred_element_type=f32
            ).astype(bf16)

    if in_kernels:
        (
            x_grad, key_grad, query_grad, sums, rest, channel_grad, gate_raw, out_raw, layer_out,
            squares,
        ) = scan_scatter(
            x_part, *scan_inputs, queries_t, y_grad, states,
            normed_t, gate_grad, gated_low, gated_t, cotangents, weight_out, tokens,
        )
    else:
        out_term = lax.dot_general(
            gated_low, cotangents, (((0,), (0,)), ((), ())), preferred_element_type=f32
        )
        whole_term = jnp.zeros((pairs, fsdp, PAIR, D), f32)
        whole_term = lax.dynamic_update_slice(
            whole_term, out_term.reshape(pairs, 1, PAIR, D), (0, me, 0, 0)
        )
        out_raw = lax.psum_scatter(
            whole_term.reshape(INNER, D), ("dp", "fsdp"), scatter_dimension=0, tiled=True
        )
        added = halved(
            jnp.dot(gated_low, weight_out, preferred_element_type=f32)
            .astype(bf16)
            .reshape(fsdp, tokens.shape[0], D),
            "fsdp",
        )
        layer_out = (inputs + added).astype(bf16)
        gate_raw = scatter_rows(in_term(gate_grad), "dp")
        x_grad, key_grad, query_grad, sums, rest, channel_grad = scan_backward(
            x_part, *scan_inputs, queries_t, y_grad, states
        )
    if in_kernels:
        head_consts = jnp.pad(jnp.stack([decay_own, head_mask]), ((0, 6), (0, PAIR - heads)))
        gate_back, x_back, small_back, token_grad, vector_rows, squares = last_scatter(
            x_grad, normed_t, gate_grad, weight_gate, weight_x, weight_shared, key_grad,
            query_grad, sums, rest.reshape(chunks, inner), head_all, head_consts, shared_part,
            shared_pre, shared_taps, tokens, cotangent,
            inverse_in, norm_gain[None], gate_raw, channel_grad, gain_grad, squares,
        )
        squares = squares[0, 0]
    else:
        x_raw = scatter_rows(in_term(x_grad), "dp")

        shared_grads = jnp.concatenate([key_grad, query_grad], axis=1).T.astype(bf16)
        arrived = exchanged(shared_grads.reshape(fsdp, shared, length), "fsdp").astype(f32)
        activated_grad = jnp.sum(arrived, axis=0)
        shared_pre_grad = activated_grad * shared_gate * (1.0 + shared_pre * (1.0 - shared_gate))
        shared_ahead = jnp.pad(shared_pre_grad, ((0, 0), (0, CONV - 1)))
        shared_grad = sum(
            taps_shared[k][:, None] * shared_ahead[:, CONV - 1 - k : CONV - 1 - k + length]
            for k in range(CONV)
        )
        taps_shared_grad = jnp.stack(
            [
                jnp.sum(shared_pre_grad * shared_padded[:, k : k + length], axis=1)
                for k in range(CONV)
            ]
        )
        bias_shared_grad = jnp.sum(shared_pre_grad, axis=1)

        sums = sums.T[: 3 * heads].reshape(3, heads, chunks, SPAN)
        before = (jnp.arange(SPAN)[:, None] < jnp.arange(SPAN)[None, :]).astype(f32)
        rest = rest.reshape(chunks, heads, HEAD_DIM).sum(axis=2).T
        log_grad = (
            jnp.dot(sums[0], 1.0 - before, precision=highest)
            + jnp.dot(sums[1], before, precision=highest)
            + rest[:, :, None]
        ).reshape(heads, length)
        step_grad = decay_own[:, None] * log_grad + sums[2].reshape(heads, length)
        raw_grad = step_grad * jax.nn.sigmoid(step_logits)
        step_bias_grad = jnp.sum(raw_grad, axis=1)
        decay_grad = jnp.sum(step_sizes * log_grad, axis=1) * decay_own
        small_grad = jnp.concatenate([shared_grad, raw_grad * head_mask[:, None]], axis=0).astype(bf16)
        small_raw = scatter_rows(
            lax.dot_general(
                normed, small_grad, (((0,), (1,)), ((), ())), preferred_element_type=f32
            ).astype(bf16),
            "dp",
        )

        def in_back(grad, weight, grad_dim=1):
            return lax.dot_general(
                grad, weight, (((grad_dim,), (1,)), ((), ())), preferred_element_type=f32
            )

        normed_grad = halved(
            (
                in_back(gate_grad, weight_gate)
                + in_back(x_grad, weight_x)
                + in_back(small_grad, weight_shared, 0)
            )
            .astype(bf16)
            .reshape(fsdp, tokens.shape[0], D),
            "fsdp",
        )
        pulled = normed_grad * norm_gain[None, :]
        input_grad = inverse_in * pulled - inputs * (
            inverse_in**3 * jnp.mean(pulled * inputs, axis=-1, keepdims=True)
        )
        token_grad = (cotangent.astype(f32) + input_grad).astype(bf16)
        norm_gain_grad = jnp.sum(normed_grad * inputs * inverse_in, axis=0)

        head_row = jnp.concatenate(
            [jnp.pad(step_bias_grad, (0, PAIR - heads)), jnp.pad(decay_grad, (0, PAIR - heads))]
        )
        shared_rows = jnp.concatenate([taps_shared_grad, bias_shared_grad[None]])
        vector_rows = jnp.concatenate(
            [
                gain_grad[0:1],
                channel_grad[: CONV + 2],
                norm_gain_grad.reshape(-1, inner),
                jnp.zeros((15 - CONV - 3 - D // inner, inner), f32),
                jnp.pad(head_row, (0, inner - 2 * PAIR))[None],
                jnp.pad(shared_rows, ((0, 7 - CONV), (0, inner - shared))),
            ]
        )
        vector_rows = spread_small(summed_in_steps(vector_rows, "dp"), "fsdp")
        squares = (
            jnp.sum(gate_raw * gate_raw)
            + jnp.sum(x_raw * x_raw)
            + jnp.sum(small_raw * small_raw)
            + jnp.sum(out_raw * out_raw)
        )
        squares = summed(summed(jnp.broadcast_to(squares, (8, 128)), "fsdp"), "dp")[0, 0]

    def joined_channels(v):
        return v.reshape(fsdp, pairs, PAIR).transpose(1, 0, 2).reshape(INNER)

    def joined_heads(v):
        return v.reshape(fsdp, pairs, 2).transpose(1, 0, 2).reshape(HEADS)

    shared_all = vector_rows[:, 16 : 17 + CONV, :shared]
    bias_shared_all = shared_all[:, CONV].reshape(-1)
    taps_all = [
        jnp.concatenate([joined_channels(vector_rows[:, 1 + k]), shared_all[:, k].reshape(-1)])
        for k in range(CONV)
    ]
    bias_all = jnp.concatenate([joined_channels(vector_rows[:, CONV + 1]), bias_shared_all])
    norm_rows = vector_rows[:, CONV + 3 : CONV + 3 + D // inner].reshape(fsdp, D)
    norm_all = norm_rows[0]
    for member in range(1, fsdp):
        norm_all = norm_all + norm_rows[member]
    skip_all = vector_rows[:, CONV + 2].reshape(fsdp * heads, HEAD_DIM).sum(axis=1)
    vector_raw = jnp.concatenate(
        [norm_all, joined_channels(vector_rows[:, 0])]
        + taps_all
        + [
            bias_all,
            joined_heads(vector_rows[:, 15, :heads]),
            joined_heads(vector_rows[:, 15, PAIR : PAIR + heads]),
            joined_heads(skip_all),
        ]
    )

    grad_norm = jnp.sqrt(squares + jnp.sum(vector_raw * vector_raw))
    factor = jnp.minimum(1.0, clip_norm / (grad_norm + 1e-06))
    if in_kernels:
        in_grad, in_moment, in_square, in_master, in_rounded = step_in(
            jnp.broadcast_to(factor, (8, PAIR)), gate_back, x_back, small_back,
            in_weight, in_first, in_second,
        )
    else:

        def returned(raw):
            return exchanged(raw.astype(bf16).reshape(fsdp, rows_in, raw.shape[1]), "fsdp")

        def joined_columns(part):
            return (
                part.reshape(fsdp, rows_in, pairs, PAIR)
                .transpose(1, 2, 0, 3)
                .reshape(rows_in, INNER)
            )

        small_back = returned(small_raw)
        in_raw = jnp.concatenate(
            [
                joined_columns(returned(gate_raw)),
                joined_columns(returned(x_raw)),
                small_back[:, :, :shared].transpose(1, 0, 2).reshape(rows_in, 2 * STATE),
                small_back[:, :, shared:]
                .reshape(fsdp, rows_in, pairs, 2)
                .transpose(1, 2, 0, 3)
                .reshape(rows_in, HEADS),
            ],
            axis=1,
        ).astype(f32)
        in_grad = in_raw * factor
        in_moment, in_square, in_master = adamw(
            in_weight, in_first, in_second, in_grad, rate_in_proj
        )
        in_rounded = in_master.astype(bf16)
    out_grad = out_raw * factor
    vector_grad = vector_raw * factor
    out_moment, out_square, out_master = adamw(
        out_weight, out_first, out_second, out_grad, rate_out_proj
    )
    vector_moment, vector_square, vector_master = adamw(
        vectors, vector_first, vector_second, vector_grad, rate_vectors
    )
    return (
        layer_out,
        token_grad,
        in_grad,
        out_grad,
        vector_grad,
        grad_norm,
        in_moment,
        in_square,
        in_master,
        in_rounded,
        out_moment,
        out_square,
        out_master,
        out_master.astype(bf16),
        vector_moment,
        vector_square,
        vector_master,
    )


def solution(mesh):
    rows = P(("dp", "fsdp"), None)
    return jax.shard_map(
        on_device,
        mesh=mesh,
        in_specs=(rows, P("dp")) + (rows,) * 7 + (P(),) * 3,
        out_specs=(rows,) * 4 + (P(),) * 2 + (rows,) * 8 + (P(),) * 3,
        check_vma=False,
    )
```

```python
from functools import partial

import jax
import jax.numpy as jnp
import numpy as np
from jax import lax
from jax.experimental import pallas as pl
from jax.experimental.pallas import tpu as pltpu
from jax.sharding import PartitionSpec as P

D = 2048
HEADS = 64
HEAD_DIM = 64
STATE = 128
CONV = 4
SPAN = 128
STEP = 10
INNER = 4096
XBC = 4352
PAIR = 2 * HEAD_DIM
GROUP = 4
STEP_LANE = 16
TAPS_ROW = (D + INNER) // PAIR
LAST_ROW = TAPS_ROW + (CONV + 1) * XBC // PAIR
MASK_ROW, SKIP_ROW, GAIN_ROW = CONV + 1, CONV + 2, CONV + 3
LANES = GROUP * HEAD_DIM
ROW_TILE = 256
RING_LIMIT = 16

norm_eps = 1e-05
clip_norm = 1.0
beta_first = 0.5
beta_second = 0.5
adam_eps = 1e-08
weight_decay = 0.1
rate_in_proj = 0.03
rate_out_proj = 0.02
rate_vectors = 0.5
highest = lax.Precision.HIGHEST
f32 = jnp.float32
bf16 = jnp.bfloat16
VMEM_BYTES = 60 * 1024 * 1024


def ring_order(count):
    return list(range(0, count, 2)) + list(range(count - 1, 0, -2))


def ring_links(count):
    order = ring_order(count)
    right = [(order[i], order[(i + 1) % count]) for i in range(count)]
    return right, [(b, a) for a, b in right]


def ring_place(axis):
    count = lax.axis_size(axis)
    order = ring_order(count)
    places = [0] * count
    for place, member in enumerate(order):
        places[member] = place
    place = jnp.asarray(places, jnp.int32)[lax.axis_index(axis)]

    def member_at(distance):
        return jnp.asarray(order, jnp.int32)[lax.rem(place + distance + count, count)]

    return member_at


def uses_ring(axis):
    count = lax.axis_size(axis)
    return count % 2 == 0 and 4 <= count <= RING_LIMIT


def gather_rows(block, axis):
    count = lax.axis_size(axis)
    if not uses_ring(axis):
        return lax.all_gather(block, axis, axis=0, tiled=True)
    right, left = ring_links(count)
    member_at = ring_place(axis)
    rows, half = block.shape[0], block.shape[0] // 2
    whole = jnp.zeros((count * rows,) + block.shape[1:], block.dtype)
    columns = (0,) * (block.ndim - 1)

    def put(whole, piece, distance, shift=0):
        return lax.dynamic_update_slice(
            whole, piece, (member_at(distance) * rows + shift,) + columns
        )

    whole = put(whole, block, 0)
    going_right = going_left = block
    for hop in range(1, count // 2):
        going_right = lax.ppermute(going_right, axis, right)
        going_left = lax.ppermute(going_left, axis, left)
        whole = put(whole, going_right, -hop)
        whole = put(whole, going_left, hop)
    first = lax.ppermute(going_right[:half], axis, right)
    second = lax.ppermute(going_left[half:], axis, left)
    whole = put(whole, first, count // 2)
    return put(whole, second, count // 2, half)


def scatter_rows(terms, axis):
    count = lax.axis_size(axis)
    if not uses_ring(axis):
        return lax.psum_scatter(terms.astype(f32), axis, scatter_dimension=0, tiled=True)
    right, left = ring_links(count)
    member_at = ring_place(axis)
    rows = terms.shape[0] // count
    half = rows // 2

    def term(distance):
        return lax.dynamic_slice_in_dim(terms, member_at(distance) * rows, rows, 0).astype(f32)

    far = term(count // 2).astype(bf16)
    going_right = lax.ppermute(far[:half], axis, right)
    going_left = lax.ppermute(far[half:], axis, left)
    for distance in range(count // 2 - 1, 0, -1):
        to_right, to_left = term(distance), term(-distance)
        if distance == count // 2 - 1:
            to_right = jnp.concatenate([to_right[:half] + going_right, to_right[half:]])
            to_left = jnp.concatenate([to_left[:half], to_left[half:] + going_left])
        else:
            to_right, to_left = to_right + going_right, to_left + going_left
        going_right = lax.ppermute(to_right.astype(bf16), axis, right)
        going_left = lax.ppermute(to_left.astype(bf16), axis, left)
    return term(0) + going_right + going_left


def swapped(value, axis, flip):
    count = lax.axis_size(axis)
    return lax.ppermute(value, axis, [(i, i ^ flip) for i in range(count)])


def summed(value, axis):
    count = lax.axis_size(axis)
    if count <= 8:
        parts = [value] + [swapped(value, axis, flip) for flip in range(1, count)]
        while len(parts) > 1:
            parts = [parts[i] + parts[i + 1] for i in range(0, len(parts), 2)]
        return parts[0]
    return summed_in_steps(value, axis)


def summed_in_steps(value, axis):
    flip = 1
    while flip < lax.axis_size(axis):
        value = value + swapped(value, axis, flip)
        flip *= 2
    return value


def placed(parts, axis):
    count = lax.axis_size(axis)
    me = lax.axis_index(axis)
    whole = jnp.zeros((count,) + parts[0].shape, parts[0].dtype)
    for flip, part in enumerate(parts):
        whole = lax.dynamic_update_index_in_dim(whole, part, lax.bitwise_xor(me, flip), 0)
    return whole


def spread(value, axis):
    count = lax.axis_size(axis)
    parts = [value]
    flip = count // 2
    known = {0: value}
    while flip:
        fresh = {k ^ flip: swapped(v, axis, flip) for k, v in known.items()}
        known.update(fresh)
        flip //= 2
    parts = [known[k] for k in range(count)]
    return placed(parts, axis)


def spread_small(value, axis):
    count = lax.axis_size(axis)
    return placed([value] + [swapped(value, axis, k) for k in range(1, count)], axis)


def exchanged(blocks, axis):
    count = lax.axis_size(axis)
    me = lax.axis_index(axis)

    def block_for(flip):
        return lax.dynamic_index_in_dim(blocks, lax.bitwise_xor(me, flip), 0, False)

    return placed(
        [block_for(0)] + [swapped(block_for(k), axis, k) for k in range(1, count)], axis
    )


def halved(blocks, axis):
    count = lax.axis_size(axis)
    me = lax.axis_index(axis)
    held = {
        k: lax.dynamic_index_in_dim(blocks, lax.bitwise_xor(me, k), 0, False)
        for k in range(count)
    }
    flip = 1
    while flip < count:
        kept = {}
        for k in sorted(held):
            if k & flip:
                continue
            arrived = swapped(held[k ^ flip].astype(bf16), axis, flip)
            kept[k] = held[k].astype(f32) + arrived
        held = kept
        flip *= 2
    return held[0]


def dot_rows(a, b):
    return lax.dot_general(a, b, (((1,), (0,)), ((), ())), preferred_element_type=f32)


def dot_lanes(a, b):
    return lax.dot_general(a, b, (((1,), (1,)), ((), ())), preferred_element_type=f32)


def head_lanes(columns, base):
    rows = columns.shape[0]
    full = [
        jnp.broadcast_to(columns[:, base + j : base + j + 1], (rows, PAIR)) for j in range(GROUP)
    ]
    first = lax.broadcasted_iota(jnp.int32, (rows, PAIR), 1) < HEAD_DIM
    lanes = jnp.concatenate(
        [jnp.where(first, full[i], full[i + 1]) for i in range(0, GROUP, 2)], axis=1
    )
    return full, lanes


def stacked_heads(values, block_mask):
    return jnp.concatenate([values] * GROUP, axis=0) * block_mask


def filtered(window, taps, bias, rows):
    pre = bias + taps[CONV - 1 : CONV] * window[8 : 8 + rows]
    for k in range(CONV - 1):
        pre = pre + taps[k : k + 1] * window[5 + k : 5 + k + rows]
    return pre


def scan_forward_kernel(
    x_ref, consts_ref, column_ref, row_ref, key_ref, query_ref,
    key_t_ref, block_ref, y_ref, states_ref, padded, state,
):
    length = x_ref.shape[0]
    rows = SPAN
    mask = consts_ref[MASK_ROW : MASK_ROW + 1]
    padded[0:8, :] = jnp.zeros((8, LANES), f32)
    padded[8 : 8 + length, :] = x_ref[...] * mask
    state[...] = jnp.zeros_like(state)
    taps, bias = consts_ref[0:CONV], consts_ref[CONV : CONV + 1]
    skip = consts_ref[SKIP_ROW : SKIP_ROW + 1]
    causal = lax.broadcasted_iota(jnp.int32, (rows, rows), 0) >= lax.broadcasted_iota(
        jnp.int32, (rows, rows), 1
    )

    def chunk(c, carry):
        start = pl.multiple_of(c * rows, rows)
        here = pl.ds(start, rows)
        pre = filtered(padded[pl.ds(start, rows + 8), :], taps, bias, rows)
        values = pre * jax.nn.sigmoid(pre) * mask
        columns = column_ref[here, :]
        log_full, log_lanes = head_lanes(columns, 0)
        step_lanes = head_lanes(columns, STEP_LANE)[1]
        weighted = step_lanes * values
        weighted_low = weighted.astype(bf16)
        keys, queries, keys_t = key_ref[here, :], query_ref[here, :], key_t_ref[:, here]
        inner = dot_lanes(queries, keys)
        mixing = jnp.concatenate(
            [
                (
                    jnp.where(causal, jnp.exp(log_full[j] - row_ref[j : j + 1, here]), 0.0)
                    * inner
                ).astype(bf16)
                for j in range(GROUP)
            ],
            axis=1,
        )
        state_now = state[...]
        state_low = state_now.astype(bf16)
        states_ref[pl.ds(c, 1)] = state_low[None]
        y = dot_rows(mixing, stacked_heads(weighted_low, block_ref[...]))
        y = y + jnp.exp(log_lanes) * dot_rows(queries, state_low)
        y_ref[here, :] = y + skip * values
        log_last = log_lanes[rows - 1 : rows, :]
        tail = (weighted * jnp.exp(log_last - log_lanes)).astype(bf16)
        state[...] = jnp.exp(log_last) * state_now + dot_rows(keys_t, tail)
        return carry

    lax.fori_loop(0, length // rows, chunk, 0)


def scan_backward_kernel(
    x_ref, consts_ref, column_ref, row_ref, key_ref, query_ref,
    query_t_ref, block_ref, pick_ref, grad_ref, states_ref,
    x_grad_ref, key_grad_ref, query_grad_ref, sums_ref, rest_ref, channel_ref,
    padded, following, state_back, inner_grad,
):
    length = x_ref.shape[0]
    rows = SPAN
    chunks = length // rows
    group = pl.program_id(0)
    mask = consts_ref[MASK_ROW : MASK_ROW + 1]
    padded[0:8, :] = jnp.zeros((8, LANES), f32)
    padded[8 : 8 + length, :] = x_ref[...] * mask
    following[...] = jnp.zeros_like(following)
    state_back[...] = jnp.zeros_like(state_back)
    channel_ref[...] = jnp.zeros_like(channel_ref)

    @pl.when(group == 0)
    def _():
        key_grad_ref[...] = jnp.zeros_like(key_grad_ref)
        query_grad_ref[...] = jnp.zeros_like(query_grad_ref)
        inner_grad[...] = jnp.zeros_like(inner_grad)
        sums_ref[...] = jnp.zeros_like(sums_ref)

    taps, bias = consts_ref[0:CONV], consts_ref[CONV : CONV + 1]
    skip = consts_ref[SKIP_ROW : SKIP_ROW + 1]
    row_at = lax.broadcasted_iota(jnp.int32, (rows, rows), 0)
    lane_at = lax.broadcasted_iota(jnp.int32, (rows, rows), 1)
    causal, causal_t = row_at >= lane_at, lane_at >= row_at

    def chunk(lap, carry):
        c = chunks - 1 - lap
        start = pl.multiple_of(c * rows, rows)
        here = pl.ds(start, rows)
        window = padded[pl.ds(start, rows + 8), :]
        pre = filtered(window, taps, bias, rows)
        gate = jax.nn.sigmoid(pre)
        values = pre * gate * mask
        columns = column_ref[here, :]
        log_full, log_lanes = head_lanes(columns, 0)
        step_lanes = head_lanes(columns, STEP_LANE)[1]
        weighted = step_lanes * values
        weighted_low = weighted.astype(bf16)
        keys, queries, queries_t = key_ref[here, :], query_ref[here, :], query_t_ref[:, here]
        grad_low = grad_ref[here, :]
        grad = grad_low.astype(f32)
        inner, inner_t = dot_lanes(queries, keys), dot_lanes(keys, queries)
        blocks = block_ref[...]
        weighted_blocks = stacked_heads(weighted_low, blocks)
        grad_blocks = stacked_heads(grad_low, blocks)
        mixing_grad = dot_lanes(grad_low, weighted_blocks)
        mixing, mixing_t, inner_sum = [], [], jnp.zeros((rows, rows), f32)
        for j in range(GROUP):
            log_row = row_ref[j : j + 1, here]
            decay = jnp.where(causal, jnp.exp(log_full[j] - log_row), 0.0)
            decay_t = jnp.where(causal_t, jnp.exp(log_row - log_full[j]), 0.0)
            mixing.append((decay * inner).astype(bf16))
            mixing_t.append((decay_t * inner_t).astype(bf16))
            inner_sum = inner_sum + decay * mixing_grad[:, j * rows : (j + 1) * rows]
        inner_grad[pl.ds(c, 1)] = inner_grad[pl.ds(c, 1)] + inner_sum[None]
        y = dot_rows(jnp.concatenate(mixing, axis=1), weighted_blocks)
        state_low = states_ref[pl.ds(c, 1)][0]
        entry = jnp.exp(log_lanes)
        y = y + entry * dot_rows(queries, state_low)
        inside = dot_rows(jnp.concatenate(mixing_t, axis=1), grad_blocks)
        back = state_back[...]
        back_low = back.astype(bf16)
        log_last = log_lanes[rows - 1 : rows, :]
        tail = jnp.exp(log_last - log_lanes)
        outside = tail * dot_rows(keys, back_low)
        entry_grad = (grad * entry).astype(bf16)
        tail_low = (weighted * tail).astype(bf16)
        query_grad_ref[here, :] = query_grad_ref[here, :] + dot_lanes(entry_grad, state_low)
        key_grad_ref[here, :] = key_grad_ref[here, :] + dot_lanes(tail_low, back_low)
        last = jnp.exp(log_last)
        rest_ref[pl.ds(c, 1)] = (
            last * jnp.sum(state_low.astype(f32) * back, axis=0, keepdims=True)
        )[None]
        state_back[...] = last * back + dot_rows(queries_t, entry_grad)
        weighted_grad = inside + outside
        first = grad * y - weighted_low.astype(f32) * inside
        first_high = first.astype(bf16)
        first_rest = (first - first_high.astype(f32)).astype(bf16)
        sums_ref[here, :] = sums_ref[here, :] + (
            dot_rows(first_high, pick_ref[0])
            + dot_rows(first_rest, pick_ref[0])
            + dot_rows((weighted * outside).astype(bf16), pick_ref[1])
            + dot_rows((values * weighted_grad).astype(bf16), pick_ref[2])
        )
        values_grad = step_lanes * weighted_grad + skip * grad
        pre_grad = values_grad * mask * (gate * (1.0 + pre * (1.0 - gate)))
        channel_ref[CONV : CONV + 1, :] += jnp.sum(pre_grad, axis=0, keepdims=True)
        channel_ref[CONV + 1 : CONV + 2, :] += jnp.sum(grad * values, axis=0, keepdims=True)
        for k in range(CONV):
            channel_ref[k : k + 1, :] += jnp.sum(
                pre_grad * window[5 + k : 5 + k + rows], axis=0, keepdims=True
            )
        ahead = jnp.concatenate([pre_grad, following[...]], axis=0)
        following[...] = pre_grad[0:8]
        x_grad = taps[CONV - 1 : CONV] * ahead[0:rows]
        for k in range(CONV - 1):
            x_grad = x_grad + taps[k : k + 1] * ahead[CONV - 1 - k : CONV - 1 - k + rows]
        x_grad_ref[here, :] = (x_grad * mask).astype(bf16)
        return carry

    lax.fori_loop(0, chunks, chunk, 0)

    @pl.when(group == pl.num_programs(0) - 1)
    def _():
        def finish(c, carry):
            here = pl.ds(pl.multiple_of(c * rows, rows), rows)
            inner_low = inner_grad[pl.ds(c, 1)][0].astype(bf16)
            query_grad_ref[here, :] = query_grad_ref[here, :] + dot_rows(
                inner_low, key_ref[here, :]
            )
            key_grad_ref[here, :] = key_grad_ref[here, :] + lax.dot_general(
                inner_low, query_ref[here, :], (((0,), (0,)), ((), ())),
                preferred_element_type=f32,
            )
            return carry

        lax.fori_loop(0, chunks, finish, 0)


def block_mask():
    row = np.arange(GROUP * SPAN)[:, None] // SPAN
    lane = np.arange(LANES)[None, :] // HEAD_DIM
    return jnp.asarray((row == lane).astype(np.float32), bf16)


def pick_masks(groups):
    lane = np.arange(LANES)[:, None] // HEAD_DIM
    target = np.arange(PAIR)[None, :]
    masks = [
        target == (kind * groups + group) * GROUP + lane
        for group in range(groups)
        for kind in range(3)
    ]
    return jnp.asarray(np.stack(masks).astype(np.float32), bf16)


def whole_spec():
    return pl.BlockSpec(memory_space=pltpu.VMEM)


def lane_spec(rows):
    return pl.BlockSpec((rows, LANES), lambda g: (0, g))


def head_specs(length):
    return [
        lane_spec(length),
        lane_spec(8),
        pl.BlockSpec((length, PAIR), lambda g: (0, g)),
        pl.BlockSpec((8, length), lambda g: (g, 0)),
        whole_spec(),
        whole_spec(),
        whole_spec(),
        whole_spec(),
    ]


def scan_forward(x, consts, columns, rows, keys, queries, keys_t):
    length, width = x.shape
    chunks = length // SPAN
    return pl.pallas_call(
        scan_forward_kernel,
        grid=(width // LANES,),
        in_specs=head_specs(length),
        out_specs=[
            lane_spec(length),
            pl.BlockSpec((chunks, STATE, LANES), lambda g: (0, 0, g)),
        ],
        out_shape=[
            jax.ShapeDtypeStruct((length, width), f32),
            jax.ShapeDtypeStruct((chunks, STATE, width), bf16),
        ],
        scratch_shapes=[pltpu.VMEM((length + 8, LANES), f32), pltpu.VMEM((STATE, LANES), f32)],
        compiler_params=pltpu.CompilerParams(vmem_limit_bytes=VMEM_BYTES),
        cost_estimate=pl.CostEstimate(
            flops=10_000_000_000, bytes_accessed=12_000_000, transcendentals=4_000_000
        ),
        name="scan_forward",
    )(x, consts, columns, rows, keys, queries, keys_t, block_mask())


def scan_backward(
    x, consts, columns, rows, keys, queries, queries_t, grad, states
):
    length, width = x.shape
    chunks = length // SPAN
    groups = width // LANES
    same = lambda g: (0, 0)
    return pl.pallas_call(
        scan_backward_kernel,
        grid=(groups,),
        in_specs=head_specs(length)
        + [
            pl.BlockSpec((3, LANES, PAIR), lambda g: (g, 0, 0)),
            lane_spec(length),
            pl.BlockSpec((chunks, STATE, LANES), lambda g: (0, 0, g)),
        ],
        out_specs=[
            lane_spec(length),
            pl.BlockSpec((length, STATE), same),
            pl.BlockSpec((length, STATE), same),
            pl.BlockSpec((length, PAIR), same),
            pl.BlockSpec((chunks, 1, LANES), lambda g: (0, 0, g)),
            lane_spec(8),
        ],
        out_shape=[
            jax.ShapeDtypeStruct((length, width), bf16),
            jax.ShapeDtypeStruct((length, STATE), f32),
            jax.ShapeDtypeStruct((length, STATE), f32),
            jax.ShapeDtypeStruct((length, PAIR), f32),
            jax.ShapeDtypeStruct((chunks, 1, width), f32),
            jax.ShapeDtypeStruct((8, width), f32),
        ],
        scratch_shapes=[
            pltpu.VMEM((length + 8, LANES), f32),
            pltpu.VMEM((8, LANES), f32),
            pltpu.VMEM((STATE, LANES), f32),
            pltpu.VMEM((chunks, SPAN, SPAN), f32),
        ],
        compiler_params=pltpu.CompilerParams(vmem_limit_bytes=VMEM_BYTES),
        cost_estimate=pl.CostEstimate(
            flops=30_000_000_000, bytes_accessed=16_000_000, transcendentals=8_000_000
        ),
        name="scan_backward",
    )(
        x, consts, columns, rows, keys, queries, queries_t, block_mask(),
        pick_masks(groups), grad, states,
    )


def gate_kernel(
    normed_ref, weight_ref, cotangent_ref, out_ref, y_ref, gain_ref, mask_ref,
    gate_part_ref, gated_grad_ref, stats_ref,
):
    gate_part = dot_rows(normed_ref[...], weight_ref[...]) * mask_ref[...]
    gated_grad = dot_lanes(cotangent_ref[...], out_ref[...])
    gate_part_ref[...] = gate_part
    gated_grad_ref[...] = gated_grad
    gated = y_ref[...] * (gate_part * jax.nn.sigmoid(gate_part))
    squares = jnp.sum(gated * gated, axis=1, keepdims=True)
    products = jnp.sum(gated * gated_grad * gain_ref[...], axis=1, keepdims=True)
    lane = lax.broadcasted_iota(jnp.int32, stats_ref.shape, 1)
    stats_ref[...] = jnp.where(lane == 0, squares, products)


def gate_forward(normed, weight, cotangent, out_weight, y, gain, mask):
    length, width = y.shape
    rows = lambda lanes: pl.BlockSpec((ROW_TILE, lanes), lambda i: (i, 0))
    return pl.pallas_call(
        gate_kernel,
        grid=(length // ROW_TILE,),
        in_specs=[
            rows(D), whole_spec(), rows(D), whole_spec(), rows(width), whole_spec(), whole_spec(),
        ],
        out_specs=[rows(width), rows(width), rows(PAIR)],
        out_shape=[
            jax.ShapeDtypeStruct((length, width), f32),
            jax.ShapeDtypeStruct((length, width), f32),
            jax.ShapeDtypeStruct((length, PAIR), f32),
        ],
        compiler_params=pltpu.CompilerParams(vmem_limit_bytes=VMEM_BYTES),
        cost_estimate=pl.CostEstimate(
            flops=9_000_000_000, bytes_accessed=28_000_000, transcendentals=1_000_000
        ),
        name="gate_forward",
    )(normed, weight, cotangent, out_weight, y, gain, mask)


def norm_back_kernel(
    y_ref, gate_part_ref, gated_grad_ref, scale_ref, gain_ref, mask_ref,
    gated_ref, y_grad_ref, gate_grad_ref, gain_grad_ref,
):
    @pl.when(pl.program_id(0) == 0)
    def _():
        gain_grad_ref[...] = jnp.zeros_like(gain_grad_ref)

    y, gate_part, gated_grad = y_ref[...], gate_part_ref[...], gated_grad_ref[...]
    inverse, pull = scale_ref[:, 0:1], scale_ref[:, 1:2]
    gate = jax.nn.sigmoid(gate_part)
    silu = gate_part * gate
    gated = y * silu
    scaled = gated * inverse
    gain = gain_ref[...]
    gated_ref[...] = (scaled * gain).astype(bf16)
    gain_grad_ref[0:1, :] += jnp.sum(gated_grad * scaled, axis=0, keepdims=True)
    back = inverse * (gated_grad * gain) - gated * pull
    y_grad_ref[...] = (back * silu).astype(bf16)
    gate_grad_ref[...] = (
        back * y * (gate * (1.0 + gate_part * (1.0 - gate))) * mask_ref[...]
    ).astype(bf16)


def norm_back(y, gate_part, gated_grad, scales, gain, mask):
    length, width = y.shape
    rows = lambda lanes: pl.BlockSpec((ROW_TILE, lanes), lambda i: (i, 0))
    return pl.pallas_call(
        norm_back_kernel,
        grid=(length // ROW_TILE,),
        in_specs=[rows(width), rows(width), rows(width), rows(2), whole_spec(), whole_spec()],
        out_specs=[
            rows(width), rows(width), rows(width), pl.BlockSpec((8, width), lambda i: (0, 0)),
        ],
        out_shape=[
            jax.ShapeDtypeStruct((length, width), bf16),
            jax.ShapeDtypeStruct((length, width), bf16),
            jax.ShapeDtypeStruct((length, width), bf16),
            jax.ShapeDtypeStruct((8, width), f32),
        ],
        compiler_params=pltpu.CompilerParams(vmem_limit_bytes=VMEM_BYTES),
        cost_estimate=pl.CostEstimate(
            flops=30_000_000, bytes_accessed=18_000_000, transcendentals=1_000_000
        ),
        name="norm_back",
    )(y, gate_part, gated_grad, scales, gain, mask)


MESH = pl.DeviceIdType.MESH


class Ring:
    def __init__(self):
        self.count = lax.axis_size("dp")
        self.far = self.count // 2
        me = lax.axis_index("dp")
        odd = lax.rem(me, 2)
        self.me = me
        self.place = (1 - odd) * lax.div(me, 2) + odd * lax.div(2 * self.count - 1 - me, 2)

    def member(self, distance):
        n = self.count
        place = lax.rem(self.place + distance + n, n)
        back = lax.div(place, n // 2)
        return (1 - back) * 2 * place + back * (2 * n - 1 - 2 * place)

    def target(self, way):
        return {"dp": self.member(1 if way == 0 else -1)}


def partner(flip):
    f = lax.axis_index("fsdp")
    return (f, f + 1 - 2 * lax.rem(f, 2), lax.rem(f + 2, 4), 3 - f)[flip]


def greet(targets):
    barrier = pltpu.get_barrier_semaphore()
    for target in targets:
        pl.semaphore_signal(barrier, inc=1, device_id=target, device_id_type=MESH)
    pl.semaphore_wait(barrier, len(targets))


def row_slice(ref, start, size):
    return ref.at[pl.ds(pl.multiple_of(start, 16), size)]


class RingGather:
    def __init__(self, ring, wholes, send, recv):
        self.ring, self.wholes, self.send, self.recv = ring, wholes, send, recv

    @staticmethod
    def semaphores(parts, count):
        return pltpu.SemaphoreType.DMA((parts * 4 * (count // 2),))

    def copy(self, part, way, half, hop):
        whole = self.wholes[part]
        rows = whole.shape[0] // self.ring.count
        size = rows // 2
        owner = self.ring.member(-hop if way == 0 else hop)
        place = row_slice(whole, owner * rows + half * size, size)
        at = ((part * 2 + way) * 2 + half) * self.ring.far + hop
        return pltpu.make_async_remote_copy(
            place, place, self.send.at[at], self.recv.at[at],
            device_id=self.ring.target(way), device_id_type=MESH,
        )

    def pieces(self, hop):
        return [
            (way, half)
            for half in (0, 1)
            for way in (0, 1)
            if hop < self.ring.far - 1 or half == way
        ]

    def start(self, part, hop):
        for way, half in self.pieces(hop):
            if hop:
                self.copy(part, way, half, hop - 1).wait_recv()
            self.copy(part, way, half, hop).start()

    def finish(self, part):
        last = self.ring.far - 1
        for way, half in self.pieces(last):
            self.copy(part, way, half, last).wait_recv()
            if last:
                self.copy(part, way, 1 - half, last - 1).wait_recv()
        for hop in range(last + 1):
            for way, half in self.pieces(hop):
                self.copy(part, way, half, hop).wait_send()


class RingScatter:
    def __init__(self, ring, held, arrived, send, recv):
        self.ring, self.held, self.arrived = ring, held, arrived
        self.send, self.recv = send, recv

    @staticmethod
    def scratch(count, rows, columns):
        hops = count // 2
        return [
            pltpu.VMEM((2, 2, rows, columns), bf16),
            pltpu.VMEM((2, hops, rows, columns), bf16),
            pltpu.SemaphoreType.DMA((2 * hops,)),
            pltpu.SemaphoreType.DMA((2 * hops,)),
        ]

    def copy(self, way, hop):
        rows = self.held.shape[2]
        size = rows // 2 if hop == 0 else rows
        at = way * self.ring.far + hop
        return pltpu.make_async_remote_copy(
            self.held.at[way, hop % 2, pl.ds(0, size)],
            self.arrived.at[way, hop, pl.ds(0, size)],
            self.send.at[at], self.recv.at[at],
            device_id=self.ring.target(way), device_id_type=MESH,
        )

    def owner(self, way, hop):
        distance = self.ring.far - hop
        return self.ring.member(distance if way == 0 else -distance)

    def start(self, hop, term):
        rows = self.held.shape[2]
        half = rows // 2
        if hop == 0:
            value = term(self.owner(0, 0)).astype(bf16)
            self.held[0, 0, 0:half] = value[:half]
            self.copy(0, 0).start()
            self.held[1, 0, 0:half] = value[half:]
            self.copy(1, 0).start()
            return
        for way in (0, 1):
            value = term(self.owner(way, hop))
            self.copy(way, hop - 1).wait_recv()
            slot = hop % 2
            if hop >= 2:
                self.copy(way, hop - 2).wait_send()
            if hop == 1:
                low = slice(way * half, (way + 1) * half)
                rest = slice((1 - way) * half, (2 - way) * half)
                self.held[way, slot, low] = (
                    value[low] + self.arrived[way, 0, 0:half].astype(f32)
                ).astype(bf16)
                self.held[way, slot, rest] = value[rest].astype(bf16)
            else:
                self.held[way, slot] = (
                    value + self.arrived[way, hop - 1].astype(f32)
                ).astype(bf16)
            self.copy(way, hop).start()

    def finish(self, term):
        last = self.ring.far - 1
        value = term(self.ring.me)
        for way in (0, 1):
            self.copy(way, last).wait_recv()
            value = value + self.arrived[way, last].astype(f32)
        for hop in range(last - 1, last + 1):
            for way in (0, 1):
                self.copy(way, hop).wait_send()
        return value


def any_specs(count):
    return [pl.BlockSpec(memory_space=pl.ANY)] * count


def tokens_exchange(own, whole, send, recv, base):
    f = lax.axis_index("fsdp")
    rows = whole.shape[0] // 4

    def one(at, source, owner, k):
        return pltpu.make_async_remote_copy(
            source, row_slice(whole, owner * rows, rows), send.at[base + at], recv.at[base + at],
            device_id={"fsdp": partner(k)}, device_id_type=MESH,
        )

    far = partner(2)
    return (
        one(0, own, f, 2), one(1, own, f, 1), one(2, row_slice(whole, far * rows, rows), far, 1),
    )


def forward_kernel(
    tokens_ref, cotangent_hbm, in_ref, out_ref, turn_ref, vectors_ref, active_ref, block_ref,
    small_all, x_all, gate_all, out_all, cotangent_all, normed_t_all, x_part_all, states_all,
    gated_all, gated_t_all, y_grad_all, gate_grad_all,
    consts_ref, head_ref, shared_taps_ref, columns_ref, rows_ref, column_ref, keys_ref, queries_ref, queries_t_ref,
    shared_part_ref, shared_pre_ref, gain_grad_ref,
    small_cut, x_cut, gate_cut, out_low, normed, cotangent, small_weight, keys_t, shared_all,
    x_part, states, y, gate_part, gated_grad, weight, out_tile, turned, squares, products, stats, stats_in,
    back_tiles, back_tiles_t, padded, state, shared_wide,
    local_sem, swap_send, swap_recv, token_send, token_recv, ring_send, ring_recv,
    shared_send, shared_recv, stats_send, stats_recv, load_sem, store_sem,
):
    ring = Ring()
    d, f = ring.me, lax.axis_index("fsdp")
    tokens, length = tokens_ref.shape[0], normed.shape[0]
    sub, rows_out = in_ref.shape[0], out_ref.shape[0]
    width = x_cut.shape[2]
    groups, chunks = width // LANES, length // SPAN
    heads, shared = HEADS // 4, shared_taps_ref.shape[0]
    precise = partial(jnp.dot, precision=highest, preferred_element_type=f32)
    greet([{"fsdp": partner(k)} for k in (1, 2, 3)] + [ring.target(0), ring.target(1)])
    wholes = [small_all, x_all, gate_all, out_all]
    small_part, x_of, gate_of, out_of = range(4)
    rings = RingGather(ring, wholes, ring_send, ring_recv)
    cuts = [small_cut, x_cut, gate_cut]

    def own_copy(part):
        if part == out_of:
            source, target = out_low, row_slice(out_all, d * rows_out, rows_out)
        else:
            source = cuts[part].at[f]
            target = row_slice(wholes[part], (4 * d + f) * sub, sub)
        return pltpu.make_async_copy(source, target, local_sem.at[part])

    def swap(part, k):
        return pltpu.make_async_remote_copy(
            cuts[part].at[partner(k)], row_slice(wholes[part], (4 * d + f) * sub, sub),
            swap_send.at[3 * part + k - 1], swap_recv.at[3 * part + k - 1],
            device_id={"fsdp": partner(k)}, device_id_type=MESH,
        )

    def start_swaps(part):
        for k in (2, 3, 1):
            swap(part, k).start()
        own_copy(part).start()

    def start_ring(part):
        own_copy(part).wait()
        if part != out_of:
            for k in (1, 2, 3):
                swap(part, k).wait_recv()
        rings.start(part, 0)

    def cut_channels(target, low):
        for pair in range(INNER // PAIR):
            member, at = pair % 4, pair // 4
            target[member, :, at * PAIR : (at + 1) * PAIR] = in_ref[
                :, low + pair * PAIR : low + (pair + 1) * PAIR
            ].astype(bf16)

    out_low[...] = out_ref[...].astype(bf16)
    own_copy(out_of).start()
    pieces = dot_lanes(in_ref[:, 2 * INNER :].astype(bf16), turn_ref[...]).astype(bf16)
    for member in range(4):
        small_cut[member] = pieces[:, member * PAIR : (member + 1) * PAIR]
    start_swaps(small_part)
    cut_channels(x_cut, INNER)
    start_swaps(x_of)
    start_ring(out_of)
    inputs = tokens_ref[...].astype(f32)
    inverse = lax.rsqrt(jnp.sum(inputs * inputs, axis=1, keepdims=True) / D + norm_eps)
    own_rows = pl.ds(pl.multiple_of(f * tokens, tokens), tokens)
    normed[own_rows, :] = (inputs * inverse * norm_gain_row(vectors_ref)).astype(bf16)
    normed_copies = tokens_exchange(normed.at[own_rows], normed, token_send, token_recv, 0)
    cotangent_copies = tokens_exchange(
        cotangent_hbm, cotangent, token_send, token_recv, 3
    )
    cotangent_own = pltpu.make_async_copy(cotangent_hbm, cotangent.at[own_rows], local_sem.at[4])
    cotangent_own.start()
    for copy in normed_copies[:2]:
        copy.start()
    start_ring(small_part)
    start_ring(x_of)
    cut_channels(gate_cut, 0)
    start_swaps(gate_of)

    def vector_row(row):
        return vectors_ref[pl.ds(row, 1), :]

    def own_channels(first_row):
        return jnp.concatenate(
            [vector_row(first_row + 4 * pair + f) for pair in range(width // PAIR)], axis=1
        )

    active = active_ref[0:1, 0:1]
    for k in range(CONV + 1):
        consts_ref[k : k + 1, :] = own_channels(TAPS_ROW + k * (XBC // PAIR))
    channel_head = lax.broadcasted_iota(jnp.int32, (1, width), 1) // HEAD_DIM
    consts_ref[MASK_ROW : MASK_ROW + 1, :] = (channel_head.astype(f32) < active / 4).astype(f32)
    consts_ref[GAIN_ROW : GAIN_ROW + 1, :] = own_channels(D // PAIR)
    head_at = lax.broadcasted_iota(jnp.int32, (PAIR, PAIR), 0)
    local_at = lax.broadcasted_iota(jnp.int32, (PAIR, PAIR), 1)
    own_head = local_at // 2 * 8 + 2 * f + local_at % 2
    chosen = (head_at == own_head) & (local_at < heads)
    chosen_far = (head_at == own_head + HEADS) & (local_at < heads)
    last = vector_row(LAST_ROW)
    step_bias_row = precise(last, chosen.astype(f32))
    is_head = lax.broadcasted_iota(jnp.int32, (1, PAIR), 1) < heads
    decay_row = jnp.where(is_head, -jnp.exp(precise(last, chosen_far.astype(f32))), 0.0)
    head_mask_row = (
        lax.broadcasted_iota(jnp.int32, (1, PAIR), 1).astype(f32) < active / 4
    ).astype(f32)
    skip_row = precise(vector_row(LAST_ROW + 1), chosen.astype(f32))
    spread_head = (
        lax.broadcasted_iota(jnp.int32, (PAIR, width), 0)
        == lax.broadcasted_iota(jnp.int32, (PAIR, width), 1) // HEAD_DIM
    ).astype(f32)
    consts_ref[SKIP_ROW : SKIP_ROW + 1, :] = precise(skip_row, spread_head)
    head_ref[...] = jnp.concatenate(
        [decay_row, head_mask_row, step_bias_row, jnp.zeros((5, PAIR), f32)], axis=0
    )
    shared_rows = [
        vector_row(TAPS_ROW + k * (XBC // PAIR) + INNER // PAIR + f // 2) for k in range(CONV + 1)
    ]
    shared_wide[...] = jnp.concatenate(
        shared_rows + [jnp.zeros((PAIR - CONV - 1, PAIR), f32)], axis=0
    ).T
    shared_taps_ref[...] = shared_wide[pl.ds(pl.multiple_of(f % 2 * shared, shared), shared), :]
    rings.start(small_part, 1)
    rings.start(small_part, 2)
    rings.start(x_of, 1)
    rings.start(out_of, 1)
    for hop in range(3, ring.far):
        rings.start(small_part, hop)
    normed_copies[0].wait_recv()
    normed_copies[2].start()
    for copy in cotangent_copies[:2]:
        copy.start()
    rings.finish(small_part)
    load_small = pltpu.make_async_copy(small_all, small_weight, local_sem.at[5])
    load_small.start()
    for copy in normed_copies[1:]:
        copy.wait_recv()
    load_small.wait()

    small = dot_rows(normed[...], small_weight[...]).T
    part = small[0:shared]
    pre = shared_taps_ref[:, CONV : CONV + 1] + jnp.zeros_like(part)
    for k in range(CONV):
        pre = pre + shared_taps_ref[:, k : k + 1] * shifted(part, CONV - 1 - k)
    shared_part_ref[...] = part
    shared_pre_ref[...] = pre
    shared_all[f] = (pre * jax.nn.sigmoid(pre)).astype(bf16)

    def shared_copy(k):
        return pltpu.make_async_remote_copy(
            shared_all.at[f], shared_all.at[f], shared_send.at[k - 1], shared_recv.at[k - 1],
            device_id={"fsdp": partner(k)}, device_id_type=MESH,
        )

    for k in (2, 3, 1):
        shared_copy(k).start()
    rings.start(x_of, 2)
    rings.start(out_of, 2)
    head_columns = jnp.concatenate(
        [head_ref[...], jnp.zeros((PAIR - 8, PAIR), f32)], axis=0
    ).T[0:heads]
    decay, head_mask, step_bias = (head_columns[:, i : i + 1] for i in range(3))
    logits = small[shared : shared + heads] * head_mask + step_bias
    steps = jnp.maximum(logits, 0.0) + jnp.log1p(jnp.exp(-jnp.abs(logits)))
    at_row = lax.broadcasted_iota(jnp.int32, (SPAN, SPAN), 0)
    at_lane = lax.broadcasted_iota(jnp.int32, (SPAN, SPAN), 1)
    upto = (at_row <= at_lane).astype(f32)
    rates = steps * decay
    log_sums = jnp.concatenate(
        [
            jnp.dot(
                rates[:, c * SPAN : (c + 1) * SPAN], upto, precision=highest,
                preferred_element_type=f32,
            )
            for c in range(chunks)
        ],
        axis=1,
    )
    column = jnp.concatenate(
        [log_sums, steps, logits, jnp.zeros((PAIR - 3 * heads, length), f32)], axis=0
    ).T
    column_ref[...] = column
    for group in range(groups):
        rolled = column if group == 0 else pltpu.roll(column, PAIR - group * GROUP, 1)
        columns_ref[:, group * PAIR : (group + 1) * PAIR] = rolled
        rows_ref[group * 8 : group * 8 + 8, :] = jnp.zeros((8, length), f32)
        rows_ref[group * 8 : group * 8 + GROUP, :] = log_sums[group * GROUP : (group + 1) * GROUP]
    for k in (1, 2, 3):
        shared_copy(k).wait_recv()
    keys_t[0:shared, :] = shared_all[0]
    keys_t[shared:, :] = shared_all[1]
    queries_t_ref[0:shared, :] = shared_all[2]
    queries_t_ref[shared:, :] = shared_all[3]
    keys_ref[...] = keys_t[...].T
    queries_ref[...] = queries_t_ref[...].T
    for hop in range(3, ring.far):
        rings.start(x_of, hop)
        rings.start(out_of, hop)
    cotangent_copies[0].wait_recv()
    cotangent_copies[2].start()

    def store(source, target, slot):
        return pltpu.make_async_copy(source, target, store_sem.at[slot])

    quarter = D // 4

    def turned_store(i):
        return store(turned.at[i % 2], row_slice(normed_t_all, i * quarter, quarter), i)

    for i in range(4):
        if i >= 2:
            turned_store(i - 2).wait()
        turned[i % 2] = normed[:, i * quarter : (i + 1) * quarter].T
        turned_store(i).start()
    rings.finish(x_of)
    start_ring(gate_of)

    def lanes(group):
        return pl.ds(group * LANES, LANES)

    def load_columns(source, group):
        return pltpu.make_async_copy(
            source.at[:, lanes(group)], weight.at[group % 2], load_sem.at[group % 2]
        )

    def x_store(group):
        return store(x_part.at[group % 2], x_part_all.at[:, lanes(group)], 4 + group)

    def states_store(group):
        return store(states.at[group % 2], states_all.at[:, :, lanes(group)], 8 + group)

    load_columns(x_all, 0).start()
    for group in range(groups):
        if group + 1 < groups:
            load_columns(x_all, group + 1).start()
        load_columns(x_all, group).wait()
        if group >= 2:
            x_store(group - 2).wait()
            states_store(group - 2).wait()
        slot = group % 2
        x_part[slot] = dot_rows(normed[...], weight[slot])
        x_store(group).start()
        scan_forward_kernel(
            x_part.at[slot], consts_ref.at[:, lanes(group)],
            columns_ref.at[:, pl.ds(group * PAIR, PAIR)], rows_ref.at[pl.ds(group * 8, 8)],
            keys_ref, queries_ref, keys_t, block_ref, y.at[:, lanes(group)], states.at[slot],
            padded, state,
        )
        states_store(group).start()
        if group % 2 == 1 and group // 2 + 1 < ring.far - 1:
            rings.start(gate_of, group // 2 + 1)

    for copy in cotangent_copies[1:]:
        copy.wait_recv()
    cotangent_own.wait()
    cotangent_store = store(cotangent, cotangent_all, 12)
    cotangent_store.start()
    rings.finish(out_of)

    def load_rows(group):
        return pltpu.make_async_copy(
            out_all.at[lanes(group)], out_tile.at[group % 2], load_sem.at[2 + group % 2]
        )

    load_rows(0).start()
    for group in range(groups):
        if group + 1 < groups:
            load_rows(group + 1).start()
        load_rows(group).wait()
        gated_grad[:, lanes(group)] = dot_lanes(cotangent[...], out_tile[group % 2])
    rings.start(gate_of, ring.far - 1)
    rings.finish(gate_of)

    def const_row(row, here):
        return consts_ref[row : row + 1, here]

    load_columns(gate_all, 0).start()
    for group in range(groups):
        if group + 1 < groups:
            load_columns(gate_all, group + 1).start()
        load_columns(gate_all, group).wait()
        here = lanes(group)
        value = dot_rows(normed[...], weight[group % 2]) * const_row(MASK_ROW, here)
        gate_part[:, here] = value
        gated = y[:, here] * (value * jax.nn.sigmoid(value))
        product = gated * (gated_grad[:, here] * const_row(GAIN_ROW, here))
        gated = gated * gated
        gated = gated[:, :PAIR] + gated[:, PAIR:]
        product = product[:, :PAIR] + product[:, PAIR:]
        squares[...] = gated if group == 0 else squares[...] + gated
        products[...] = product if group == 0 else products[...] + product
    lane = lax.broadcasted_iota(jnp.int32, (length, PAIR), 1)
    both = jnp.where(
        lane == 0,
        jnp.sum(squares[...], axis=1, keepdims=True),
        jnp.where(lane == 1, jnp.sum(products[...], axis=1, keepdims=True), 0.0),
    )
    stats[...] = both.T[0:8]

    def stats_copy(k):
        return pltpu.make_async_remote_copy(
            stats, stats_in.at[k - 1], stats_send.at[k - 1], stats_recv.at[k - 1],
            device_id={"fsdp": partner(k)}, device_id_type=MESH,
        )

    for k in (2, 3, 1):
        stats_copy(k).start()
    for k in (1, 2, 3):
        stats_copy(k).wait_recv()
    total = (stats[...] + stats_in[0]) + (stats_in[1] + stats_in[2])
    channel_count = active * HEAD_DIM
    inverse_out = lax.rsqrt(total[0:1] / channel_count + norm_eps)
    pulls = inverse_out * inverse_out * inverse_out / channel_count * total[1:2]
    scales = jnp.concatenate(
        [inverse_out, pulls, jnp.zeros((PAIR - 2, length), f32)], axis=0
    ).T
    inverse_out, pulls = scales[:, 0:1], scales[:, 1:2]

    def back_stores(group):
        slot, at, here = group % 2, 13 + 4 * group, lanes(group)
        return [
            store(back_tiles.at[slot, 0], gated_all.at[:, here], at),
            store(back_tiles.at[slot, 1], y_grad_all.at[:, here], at + 1),
            store(back_tiles.at[slot, 2], gate_grad_all.at[:, here], at + 2),
            store(back_tiles_t.at[slot], gated_t_all.at[here], at + 3),
        ]

    gain_grad_ref[...] = jnp.zeros_like(gain_grad_ref)
    for group in range(groups):
        here, slot = lanes(group), group % 2
        if group >= 2:
            for copy in back_stores(group - 2):
                copy.wait()
        value, grad, gain = gate_part[:, here], gated_grad[:, here], const_row(GAIN_ROW, here)
        gate = jax.nn.sigmoid(value)
        silu = value * gate
        y_here = y[:, here]
        gated = y_here * silu
        scaled = gated * inverse_out
        gated_low = (scaled * gain).astype(bf16)
        back_tiles[slot, 0] = gated_low
        back_tiles_t[slot] = gated_low.T
        gain_grad_ref[0:1, here] = jnp.sum(grad * scaled, axis=0, keepdims=True)
        back = inverse_out * (grad * gain) - gated * pulls
        back_tiles[slot, 1] = (back * silu).astype(bf16)
        back_tiles[slot, 2] = (
            back * y_here * (gate * (1.0 + value * (1.0 - gate))) * const_row(MASK_ROW, here)
        ).astype(bf16)
        for copy in back_stores(group):
            copy.start()

    for i in (2, 3):
        turned_store(i).wait()
    for group in range(groups - 2, groups):
        x_store(group).wait()
        states_store(group).wait()
        for copy in back_stores(group):
            copy.wait()
    cotangent_store.wait()
    for copy in normed_copies + cotangent_copies:
        copy.wait_send()
    for k in (1, 2, 3):
        shared_copy(k).wait_send()
        stats_copy(k).wait_send()
        for i in (small_part, x_of, gate_of):
            swap(i, k).wait_send()


def last_columns(members):
    shared = 2 * STATE // members
    source = np.arange(2 * STATE + HEADS)
    head = source - 2 * STATE
    target = np.where(
        source < 2 * STATE,
        source // shared * PAIR + source % shared,
        head // 2 % members * PAIR + shared + head // (2 * members) * 2 + head % 2,
    )
    turn = np.arange(members * PAIR)[:, None] == target[None, :]
    return jnp.asarray(turn.astype(np.float32), bf16)


def norm_gain_row(vectors_ref):
    return jnp.concatenate([vectors_ref[i : i + 1, :] for i in range(D // PAIR)], axis=1)


def vector_tiles(vectors):
    rows = -(-vectors.shape[0] // PAIR)
    return jnp.pad(vectors, (0, rows * PAIR - vectors.shape[0])).reshape(rows, PAIR)


def forward(
    tokens, cotangent, in_weight, out_weight, vectors, active,
):
    count, members = lax.axis_size("dp"), lax.axis_size("fsdp")
    own, sub, rows_out = tokens.shape[0], in_weight.shape[0], out_weight.shape[0]
    length, inner, shared = own * members, INNER // members, 2 * STATE // members
    chunks, groups = length // SPAN, inner // LANES
    assert groups == 4 and count == 8 and members == 4
    turn = last_columns(members)
    sd, dma = jax.ShapeDtypeStruct, pltpu.SemaphoreType.DMA
    vmem = pltpu.VMEM
    return pl.pallas_call(
        forward_kernel,
        in_specs=[whole_spec()] + any_specs(1) + [whole_spec()] * 6,
        out_specs=any_specs(12) + [whole_spec()] * 12,
        out_shape=[
            sd((D, PAIR), bf16),
            sd((D, inner), bf16),
            sd((D, inner), bf16),
            sd((inner, D), bf16),
            sd((length, D), bf16),
            sd((D, length), bf16),
            sd((length, inner), f32),
            sd((chunks, STATE, inner), bf16),
            sd((length, inner), bf16),
            sd((inner, length), bf16),
            sd((length, inner), bf16),
            sd((length, inner), bf16),
            sd((8, inner), f32),
            sd((8, PAIR), f32),
            sd((shared, PAIR), f32),
            sd((length, groups * PAIR), f32),
            sd((groups * 8, length), f32),
            sd((length, PAIR), f32),
            sd((length, STATE), bf16),
            sd((length, STATE), bf16),
            sd((STATE, length), bf16),
            sd((shared, length), f32),
            sd((shared, length), f32),
            sd((8, inner), f32),
        ],
        scratch_shapes=[
            vmem((members, sub, PAIR), bf16),
            vmem((members, sub, inner), bf16),
            vmem((members, sub, inner), bf16),
            vmem((rows_out, D), bf16),
            vmem((length, D), bf16),
            vmem((length, D), bf16),
            vmem((D, PAIR), bf16),
            vmem((STATE, length), bf16),
            vmem((members, shared, length), bf16),
            vmem((2, length, LANES), f32),
            vmem((2, chunks, STATE, LANES), bf16),
            vmem((length, inner), f32),
            vmem((length, inner), f32),
            vmem((length, inner), f32),
            vmem((2, D, LANES), bf16),
            vmem((2, LANES, D), bf16),
            vmem((2, D // 4, length), bf16),
            vmem((length, PAIR), f32),
            vmem((length, PAIR), f32),
            vmem((8, length), f32),
            vmem((3, 8, length), f32),
            vmem((2, 3, length, LANES), bf16),
            vmem((2, LANES, length), bf16),
            vmem((length + 8, LANES), f32),
            vmem((STATE, LANES), f32),
            vmem((PAIR, PAIR), f32),
            dma((6,)),
            dma((9,)),
            dma((9,)),
            dma((6,)),
            dma((6,)),
            RingGather.semaphores(4, count),
            RingGather.semaphores(4, count),
            dma((3,)),
            dma((3,)),
            dma((3,)),
            dma((3,)),
            dma((4,)),
            dma((13 + 4 * groups,)),
        ],
        compiler_params=pltpu.CompilerParams(
            collective_id=0, has_side_effects=True, vmem_limit_bytes=VMEM_BYTES
        ),
        name="forward",
    )(
        tokens, cotangent, in_weight, out_weight, turn, vectors,
        jnp.broadcast_to(active.astype(f32), (8, PAIR)), block_mask(),
    )


def total_squares(value):
    return jnp.sum(jnp.sum(value * value, axis=0, keepdims=True), axis=1, keepdims=True)


def scan_scatter_kernel(
    x_ref, consts_ref, column_ref, row_ref, key_ref, query_ref,
    query_t_ref, block_ref, pick_ref, grad_ref, states_ref,
    normed_t_ref, gate_grad_ref, gated_ref, gated_t_ref, cotangent_ref, weight_ref, tokens_ref,
    x_grad_ref, key_grad_ref, query_grad_ref, sums_ref, rest_ref, channel_ref,
    gate_raw_ref, out_raw_ref, layer_out_ref, squares_ref,
    padded, following, state_back, inner_grad, added, added_out, added_in, added_send, added_recv,
    *ring_scratch,
):
    ring = Ring()
    step = pl.program_id(0)
    steps = pl.num_programs(0)
    gate_ring = RingScatter(ring, *ring_scratch[:4])
    out_ring = RingScatter(ring, *ring_scratch[4:])
    rows_in, rows_out = gate_raw_ref.shape[0], out_raw_ref.shape[0]
    tokens = tokens_ref.shape[0]

    def gate_term(owner):
        here = pl.ds(pl.multiple_of(owner * rows_in, rows_in), rows_in)
        return dot_rows(normed_t_ref[here, :], gate_grad_ref[...])

    def out_term(owner):
        here = pl.ds(pl.multiple_of(owner * rows_out, rows_out), rows_out)
        return dot_rows(gated_t_ref[here, :], cotangent_ref[...])

    def added_block(flip):
        here = pl.ds(pl.multiple_of(partner(flip) * tokens, tokens), tokens)
        return dot_rows(gated_ref[here, :], weight_ref[...])

    def added_copy(i):
        return pltpu.make_async_remote_copy(
            added_out.at[i], added_in.at[i], added_send.at[i], added_recv.at[i],
            device_id={"fsdp": partner(2 if i == 2 else 1)}, device_id_type=MESH,
        )

    @pl.when(step == 0)
    def _():
        greet([{"fsdp": partner(k)} for k in (1, 2)] + [ring.target(0), ring.target(1)])

    for hop in range(ring.far):
        @pl.when(step == hop)
        def _(hop=hop):
            out_ring.start(hop, out_term)
            gate_ring.start(hop, gate_term)

    @pl.when(step == 0)
    def _():
        for i, flip in ((1, 3), (0, 1)):
            added_out[i] = added_block(flip).astype(bf16)
            added_copy(i).start()

    @pl.when(step == 1)
    def _():
        value = added_block(2)
        added_copy(1).wait_recv()
        added_out[2] = (value + added_in[1].astype(f32)).astype(bf16)
        added_copy(2).start()

    @pl.when(step == 2)
    def _():
        added[...] = added_block(0)

    scan_backward_kernel(
        x_ref, consts_ref, column_ref, row_ref, key_ref, query_ref,
        query_t_ref, block_ref, pick_ref, grad_ref, states_ref,
        x_grad_ref, key_grad_ref, query_grad_ref, sums_ref, rest_ref, channel_ref,
        padded, following, state_back, inner_grad,
    )

    @pl.when(step == steps - 1)
    def _():
        added_copy(0).wait_recv()
        added_copy(2).wait_recv()
        layer_out_ref[...] = (
            tokens_ref[...].astype(f32)
            + ((added[...] + added_in[0].astype(f32)) + added_in[2].astype(f32))
        ).astype(bf16)
        for i in range(3):
            added_copy(i).wait_send()
        out_raw = out_ring.finish(out_term)
        out_raw_ref[...] = out_raw
        gate_raw = gate_ring.finish(gate_term)
        gate_raw_ref[...] = gate_raw.astype(bf16)
        squares_ref[...] = jnp.broadcast_to(
            total_squares(out_raw) + total_squares(gate_raw), squares_ref.shape
        )


def scan_scatter(
    x, consts, columns, rows, keys, queries, queries_t, grad, states,
    normed_t, gate_grad, gated, gated_t, cotangent, weight, tokens,
):
    length, width = x.shape
    chunks = length // SPAN
    groups = width // LANES
    count = lax.axis_size("dp")
    assert groups == count // 2
    rows_in, rows_out, own = D // count, width // count, tokens.shape[0]
    same = lambda g: (0, 0)
    return pl.pallas_call(
        scan_scatter_kernel,
        grid=(groups,),
        in_specs=head_specs(length)
        + [
            pl.BlockSpec((3, LANES, PAIR), lambda g: (g, 0, 0)),
            lane_spec(length),
            pl.BlockSpec((chunks, STATE, LANES), lambda g: (0, 0, g)),
        ]
        + [whole_spec()] * 7,
        out_specs=[
            lane_spec(length),
            pl.BlockSpec((length, STATE), same),
            pl.BlockSpec((length, STATE), same),
            pl.BlockSpec((length, PAIR), same),
            pl.BlockSpec((chunks, 1, LANES), lambda g: (0, 0, g)),
            lane_spec(8),
        ]
        + [whole_spec()] * 4,
        out_shape=[
            jax.ShapeDtypeStruct((length, width), bf16),
            jax.ShapeDtypeStruct((length, STATE), f32),
            jax.ShapeDtypeStruct((length, STATE), f32),
            jax.ShapeDtypeStruct((length, PAIR), f32),
            jax.ShapeDtypeStruct((chunks, 1, width), f32),
            jax.ShapeDtypeStruct((8, width), f32),
            jax.ShapeDtypeStruct((rows_in, width), bf16),
            jax.ShapeDtypeStruct((rows_out, D), f32),
            jax.ShapeDtypeStruct((own, D), bf16),
            jax.ShapeDtypeStruct((8, PAIR), f32),
        ],
        scratch_shapes=[
            pltpu.VMEM((length + 8, LANES), f32),
            pltpu.VMEM((8, LANES), f32),
            pltpu.VMEM((STATE, LANES), f32),
            pltpu.VMEM((chunks, SPAN, SPAN), f32),
            pltpu.VMEM((own, D), f32),
            pltpu.VMEM((3, own, D), bf16),
            pltpu.VMEM((3, own, D), bf16),
            pltpu.SemaphoreType.DMA((3,)),
            pltpu.SemaphoreType.DMA((3,)),
        ]
        + RingScatter.scratch(count, rows_in, width)
        + RingScatter.scratch(count, rows_out, D),
        compiler_params=pltpu.CompilerParams(
            collective_id=2, has_side_effects=True, vmem_limit_bytes=VMEM_BYTES
        ),
        name="scan_scatter",
    )(
        x, consts, columns, rows, keys, queries, queries_t, block_mask(),
        pick_masks(groups), grad, states,
        normed_t, gate_grad, gated, gated_t, cotangent, weight, tokens,
    )


def flipped(member, flip):
    return member + flip - 2 * flip * lax.rem(lax.div(member, flip), 2)


def shifted(value, by):
    length = value.shape[1]
    lane = lax.broadcasted_iota(jnp.int32, value.shape, 1)
    if by == 0:
        return value
    if by > 0:
        return jnp.where(lane >= by, pltpu.roll(value, by, 1), 0.0)
    return jnp.where(lane < length + by, pltpu.roll(value, length + by, 1), 0.0)


def last_scatter_kernel(
    x_grad_ref, normed_t_ref, gate_grad_hbm, weight_gate_hbm, weight_x_hbm, weight_small_ref,
    key_grad_ref, query_grad_ref, sums_ref, rest_ref, head_pick_ref, steps_ref, heads_ref,
    shared_part_ref, shared_pre_ref, taps_ref, tokens_ref, cotangent_ref, vectors_own_ref,
    gate_raw_ref, channel_ref, gate_gain_ref, squares_ref,
    gate_back_ref, x_back_ref, small_back_ref, token_grad_ref, vectors_ref, total_ref,
    gate_grad, weight_gate, weight_x, load_sem,
    shared_own, shared_out, shared_in, swap_send, swap_recv, raw, small_t, small_n,
    kept, back_out, back_in, back_send, back_recv,
    vector_sum, vector_in, vector_send, vector_recv,
    x_out, small_out, return_send, return_recv, local_sem,
    scalar_out, scalar_in, scalar_send, scalar_recv,
    *ring_scratch,
):
    ring = Ring()
    d, f = ring.me, lax.axis_index("fsdp")
    count = ring.count
    x_ring = RingScatter(ring, *ring_scratch[:4])
    small_ring = RingScatter(ring, *ring_scratch[4:])
    loads = [
        pltpu.make_async_copy(source, target, load_sem.at[i])
        for i, (source, target) in enumerate(
            [(gate_grad_hbm, gate_grad), (weight_gate_hbm, weight_gate), (weight_x_hbm, weight_x)]
        )
    ]
    for load in loads:
        load.start()
    near = [{"fsdp": partner(k)} for k in (1, 2, 3)]
    over = [{"dp": lax.rem(d + k, count)} for k in range(1, count)]
    greet(near + over)
    length, shared = x_grad_ref.shape[0], shared_own.shape[1]
    rows, sub = x_out.shape[0], x_back_ref.shape[1]
    tokens = tokens_ref.shape[0]

    def rows_of(owner):
        return pl.ds(pl.multiple_of(owner * rows, rows), rows)

    def x_term(owner):
        return dot_rows(normed_t_ref[rows_of(owner), :], x_grad_ref[...])

    def small_term(owner):
        return dot_lanes(normed_t_ref[rows_of(owner), :], small_t[...])

    def to_partner(k, source, target, send, recv, at):
        return pltpu.make_async_remote_copy(
            source, target, send.at[at], recv.at[at],
            device_id={"fsdp": partner(k)}, device_id_type=MESH,
        )

    def return_copy(part, k):
        source = (gate_raw_ref, x_out, small_out)[part]
        target = (gate_back_ref, x_back_ref, small_back_ref)[part]
        return to_partner(
            k, row_slice(source, partner(k) * sub, sub), target.at[f],
            return_send, return_recv, part * 3 + k - 1,
        )

    def own_copy(part):
        source = (gate_raw_ref, x_out, small_out)[part]
        target = (gate_back_ref, x_back_ref, small_back_ref)[part]
        return pltpu.make_async_copy(
            row_slice(source, f * sub, sub), target.at[f], local_sem.at[part]
        )

    x_ring.start(0, x_term)

    for i, ref in ((0, key_grad_ref), (2, query_grad_ref)):
        turned = ref[...].T
        for j in (0, 1):
            shared_own[i + j] = turned[j * shared : (j + 1) * shared]
            shared_out[i + j] = turned[j * shared : (j + 1) * shared].astype(bf16)

    def shared_copy(k):
        return to_partner(
            k, shared_out.at[partner(k)], shared_in.at[k - 1], swap_send, swap_recv, k - 1
        )

    for k in (2, 3, 1):
        shared_copy(k).start()
    for k in (2, 3, 1):
        return_copy(0, k).start()
    own_copy(0).start()

    at_row = lax.broadcasted_iota(jnp.int32, (SPAN, SPAN), 0)
    at_lane = lax.broadcasted_iota(jnp.int32, (SPAN, SPAN), 1)
    later = (at_lane >= at_row).astype(f32)
    earlier = (at_lane < at_row).astype(f32)
    precise = partial(jnp.dot, precision=highest, preferred_element_type=f32)
    heads = HEADS // 4
    rest = precise(rest_ref[...], head_pick_ref[...])
    decay, head_mask = heads_ref[0:1, :], heads_ref[1:2, :]
    step_bias_grad = jnp.zeros((1, PAIR), f32)
    decay_grad = jnp.zeros((1, PAIR), f32)
    for c in range(length // SPAN):
        here = slice(c * SPAN, (c + 1) * SPAN)
        sums = sums_ref[here, :]
        log_grad = (
            precise(later, sums)
            + pltpu.roll(precise(earlier, sums), PAIR - heads, 1)
            + rest[c : c + 1]
        )
        steps = pltpu.roll(steps_ref[here, :], PAIR - heads, 1)
        logits = pltpu.roll(steps_ref[here, :], PAIR - 2 * heads, 1)
        raw_grad = (decay * log_grad + pltpu.roll(sums, PAIR - 2 * heads, 1)) * jax.nn.sigmoid(
            logits
        )
        step_bias_grad = step_bias_grad + jnp.sum(raw_grad, axis=0, keepdims=True)
        decay_grad = decay_grad + jnp.sum(steps * log_grad, axis=0, keepdims=True)
        raw[here, :] = raw_grad * head_mask
    decay_grad = decay_grad * decay

    x_ring.start(1, x_term)

    for k in (2, 3, 1):
        shared_copy(k).wait_recv()
    part, pre = shared_part_ref[...], shared_pre_ref[...]
    gate = jax.nn.sigmoid(pre)
    pre_grad = shared_own[f]
    for k in (1, 2, 3):
        pre_grad = pre_grad + shared_in[k - 1].astype(f32)
    pre_grad = pre_grad * (gate * (1.0 + pre * (1.0 - gate)))
    shared_grad = jnp.zeros_like(pre_grad)
    lane = lax.broadcasted_iota(jnp.int32, (shared, PAIR), 1)
    shared_sums = jnp.where(lane == CONV, jnp.sum(pre_grad, axis=1, keepdims=True), 0.0)
    for k in range(CONV):
        shift = CONV - 1 - k
        shared_grad = shared_grad + taps_ref[:, k : k + 1] * shifted(pre_grad, -shift)
        shared_sums = shared_sums + jnp.where(
            lane == k, jnp.sum(pre_grad * shifted(part, shift), axis=1, keepdims=True), 0.0
        )
    small_t[0:shared, :] = shared_grad.astype(bf16)
    small_t[shared:, :] = raw[...].T[0 : PAIR - shared].astype(bf16)
    small_n[...] = small_t[...].T
    small_ring.start(0, small_term)

    for load in loads:
        load.wait()

    def back_block(flip):
        here = pl.ds(pl.multiple_of(partner(flip) * tokens, tokens), tokens)
        return (
            dot_lanes(gate_grad[here, :], weight_gate[...])
            + dot_lanes(x_grad_ref[here, :], weight_x[...])
            + dot_lanes(small_n[here, :], weight_small_ref[...])
        )

    def back_copy(i):
        return to_partner(
            2 if i == 2 else 1, back_out.at[i], back_in.at[i], back_send, back_recv, i
        )

    for i, flip in ((1, 3), (0, 1)):
        back_out[i] = back_block(flip).astype(bf16)
        back_copy(i).start()
    value = back_block(2)
    back_copy(1).wait_recv()
    back_out[2] = (value + back_in[1].astype(f32)).astype(bf16)
    back_copy(2).start()
    x_ring.start(2, x_term)
    small_ring.start(1, small_term)
    kept[...] = back_block(0)
    for hop in range(3, ring.far):
        x_ring.start(hop, x_term)
        small_ring.start(hop - 1, small_term)
    back_copy(0).wait_recv()
    back_copy(2).wait_recv()
    inputs = tokens_ref[...].astype(f32)
    inverse = lax.rsqrt(jnp.sum(inputs * inputs, axis=1, keepdims=True) / D + norm_eps)
    normed_grad = (kept[...] + back_in[0].astype(f32)) + back_in[2].astype(f32)
    pulled = normed_grad * norm_gain_row(vectors_own_ref)
    scaled = inputs * inverse
    input_grad = inverse * (
        pulled - scaled * (jnp.sum(pulled * scaled, axis=1, keepdims=True) / D)
    )
    token_grad_ref[...] = (cotangent_ref[...].astype(f32) + input_grad).astype(bf16)
    gain_grad = jnp.sum(normed_grad * scaled, axis=0, keepdims=True)

    width = vector_sum.shape[1]
    vector_sum[...] = jnp.zeros_like(vector_sum)
    vector_sum[0:1, :] = gate_gain_ref[0:1, :]
    vector_sum[1 : CONV + 3, :] = channel_ref[0 : CONV + 2, :]
    for i in range(D // width):
        vector_sum[CONV + 3 + i : CONV + 4 + i, :] = gain_grad[:, i * width : (i + 1) * width]
    vector_sum[15:16, 0:PAIR] = step_bias_grad
    vector_sum[15:16, PAIR : 2 * PAIR] = decay_grad
    wide = jnp.concatenate([shared_sums, jnp.zeros((PAIR - shared, PAIR), f32)], axis=0)
    vector_sum[16:24, 0:PAIR] = wide.T[0:8]

    def vector_copy(step, flip):
        return pltpu.make_async_remote_copy(
            vector_in.at[step, 0], vector_in.at[step, 1], vector_send.at[step],
            vector_recv.at[step],
            device_id={"dp": flipped(d, flip)}, device_id_type=MESH,
        )

    flips = []
    while 1 << len(flips) < count:
        flips.append(1 << len(flips))
    for step, flip in enumerate(flips):
        vector_in[step, 0] = vector_sum[...]
        vector_copy(step, flip).start()
        if step == 0:
            small_ring.start(ring.far - 1, small_term)
        vector_copy(step, flip).wait_recv()
        vector_sum[...] = vector_sum[...] + vector_in[step, 1]

    def vector_spread(k):
        return to_partner(
            k, vector_sum, vectors_ref.at[f], vector_send, vector_recv, len(flips) + k - 1
        )

    for k in (2, 3, 1):
        vector_spread(k).start()
    vectors_ref[f] = vector_sum[...]

    x_raw = x_ring.finish(x_term)
    x_out[...] = x_raw.astype(bf16)
    for k in (2, 3, 1):
        return_copy(1, k).start()
    own_copy(1).start()
    small_raw = small_ring.finish(small_term)
    small_out[...] = small_raw.astype(bf16)
    for k in (2, 3, 1):
        return_copy(2, k).start()
    own_copy(2).start()

    total = squares_ref[...] + jnp.broadcast_to(
        total_squares(x_raw) + total_squares(small_raw), squares_ref.shape
    )
    scalar_out[0] = total

    def near_scalar(k):
        return to_partner(
            k, scalar_out.at[0], scalar_in.at[k], scalar_send, scalar_recv, k
        )

    for k in (2, 3, 1):
        near_scalar(k).start()
    for k in (2, 3, 1):
        near_scalar(k).wait_recv()
    total = (total + scalar_in[1]) + (scalar_in[2] + scalar_in[3])
    scalar_out[1] = total

    def far_scalar(k):
        member = d
        for bit in flips:
            if k & bit:
                member = flipped(member, bit)
        return pltpu.make_async_remote_copy(
            scalar_out.at[1], scalar_in.at[3 + k], scalar_send.at[3 + k], scalar_recv.at[3 + k],
            device_id={"dp": member}, device_id_type=MESH,
        )

    for k in range(count - 1, 0, -1):
        far_scalar(k).start()
    parts = [total]
    for k in range(1, count):
        far_scalar(k).wait_recv()
        parts.append(scalar_in[3 + k])
    while len(parts) > 1:
        parts = [parts[i] + parts[i + 1] for i in range(0, len(parts), 2)]
    total_ref[...] = parts[0]

    for k in (1, 2, 3):
        vector_spread(k).wait_recv()
        vector_spread(k).wait_send()
        shared_copy(k).wait_send()
        near_scalar(k).wait_send()
        for i in range(3):
            return_copy(i, k).wait_recv()
            return_copy(i, k).wait_send()
    for k in range(1, count):
        far_scalar(k).wait_send()
    for i in range(3):
        back_copy(i).wait_send()
        own_copy(i).wait()
    for step, flip in enumerate(flips):
        vector_copy(step, flip).wait_send()


def last_scatter(
    x_grad, normed_t, gate_grad, weight_gate, weight_x, weight_small, key_grad, query_grad, sums,
    rest, steps, head_rows, shared_part, shared_pre, taps, tokens, cotangent, vectors,
    gate_raw, channel, gate_gain, squares,
):
    length, width = x_grad.shape
    count, members = lax.axis_size("dp"), lax.axis_size("fsdp")
    rows = D // count
    sub, own, shared = rows // members, tokens.shape[0], shared_part.shape[0]
    hops = max(count - 1, 1).bit_length()
    head_pick = jnp.asarray(
        (np.arange(width)[:, None] // HEAD_DIM == np.arange(PAIR)[None, :]).astype(np.float32)
    )
    dma = pltpu.SemaphoreType.DMA
    sd = jax.ShapeDtypeStruct
    return pl.pallas_call(
        last_scatter_kernel,
        in_specs=[whole_spec()] * 2 + any_specs(3) + [whole_spec()] * 18,
        out_specs=[whole_spec()] * 6,
        out_shape=[
            sd((members, sub, width), bf16),
            sd((members, sub, width), bf16),
            sd((members, sub, PAIR), bf16),
            sd((own, D), bf16),
            sd((members, 24, width), f32),
            sd((8, PAIR), f32),
        ],
        scratch_shapes=[
            pltpu.VMEM((length, width), bf16),
            pltpu.VMEM((D, width), bf16),
            pltpu.VMEM((D, width), bf16),
            dma((3,)),
            pltpu.VMEM((members, shared, length), f32),
            pltpu.VMEM((members, shared, length), bf16),
            pltpu.VMEM((members - 1, shared, length), bf16),
            dma((3,)),
            dma((3,)),
            pltpu.VMEM((length, PAIR), f32),
            pltpu.VMEM((PAIR, length), bf16),
            pltpu.VMEM((length, PAIR), bf16),
            pltpu.VMEM((own, D), f32),
            pltpu.VMEM((3, own, D), bf16),
            pltpu.VMEM((3, own, D), bf16),
            dma((3,)),
            dma((3,)),
            pltpu.VMEM((24, width), f32),
            pltpu.VMEM((hops, 2, 24, width), f32),
            dma((hops + 3,)),
            dma((hops + 3,)),
            pltpu.VMEM((rows, width), bf16),
            pltpu.VMEM((rows, PAIR), bf16),
            dma((9,)),
            dma((9,)),
            dma((3,)),
            pltpu.VMEM((2, 8, PAIR), f32),
            pltpu.VMEM((3 + count, 8, PAIR), f32),
            dma((3 + count,)),
            dma((3 + count,)),
        ]
        + RingScatter.scratch(count, rows, width)
        + RingScatter.scratch(count, rows, PAIR),
        compiler_params=pltpu.CompilerParams(
            collective_id=3, has_side_effects=True, vmem_limit_bytes=VMEM_BYTES
        ),
        name="last_scatter",
    )(
        x_grad, normed_t, gate_grad, weight_gate, weight_x, weight_small, key_grad, query_grad,
        sums, rest, head_pick, steps, head_rows, shared_part, shared_pre, taps, tokens, cotangent,
        vectors, gate_raw, channel, gate_gain, squares,
    )


OPTIMIZER_STEPS = 4


def optimizer_kernel(
    squares_ref, parts_ref, vector_ref, vector_first_ref, vector_second_ref, turn_ref,
    gate_ref, x_ref, small_ref, in_ref, in_first_ref, in_second_ref,
    out_raw_ref, out_ref, out_first_ref, out_second_ref,
    norm_ref, vector_grad_ref, vector_moment_ref, vector_square_ref, vector_master_ref,
    in_grad_ref, in_moment_ref, in_square_ref, in_master_ref, in_rounded_ref,
    out_grad_ref, out_moment_ref, out_square_ref, out_master_ref, out_rounded_ref,
    joined, factor_ref, in_raw,
):
    members = parts_ref.shape[0]
    pairs = INNER // PAIR
    shared, heads = 2 * STATE // members, HEADS // members

    @pl.when(pl.program_id(0) == 0)
    def _():
        joined[...] = jnp.zeros_like(joined)
        width = parts_ref.shape[2]
        for i in range(D // PAIR):
            row = CONV + 3 + i * PAIR // width
            lanes = slice(i * PAIR % width, i * PAIR % width + PAIR)
            value = parts_ref[0, row : row + 1, lanes]
            for member in range(1, members):
                value = value + parts_ref[member, row : row + 1, lanes]
            joined[i : i + 1, :] = value

        def put_channels(first_row, row):
            for pair in range(pairs):
                at = pair // members
                joined[first_row + pair : first_row + pair + 1, :] = parts_ref[
                    pair % members, row : row + 1, at * PAIR : (at + 1) * PAIR
                ]

        put_channels(D // PAIR, 0)
        each = PAIR // shared
        for k in range(CONV + 1):
            first_row = TAPS_ROW + k * (XBC // PAIR)
            put_channels(first_row, 1 + k)
            for i in range(members // each):
                joined[first_row + pairs + i : first_row + pairs + i + 1, :] = jnp.concatenate(
                    [
                        parts_ref[i * each + j, 16 + k : 17 + k, 0:shared]
                        for j in range(each)
                    ],
                    axis=1,
                )
        precise = partial(jnp.dot, precision=highest, preferred_element_type=f32)
        last, skips = jnp.zeros((1, PAIR), f32), jnp.zeros((1, PAIR), f32)
        local_at = lax.broadcasted_iota(jnp.int32, (PAIR, PAIR), 0)
        head_at = lax.broadcasted_iota(jnp.int32, (PAIR, PAIR), 1)
        channel_head = lax.broadcasted_iota(jnp.int32, (width, PAIR), 0) // HEAD_DIM
        wide_at = lax.broadcasted_iota(jnp.int32, (width, PAIR), 1)
        for member in range(members):
            home = local_at // 2 * 2 * members + 2 * member + local_at % 2
            known = local_at < heads
            biases = parts_ref[member, 15:16, 0:PAIR]
            decays = parts_ref[member, 15:16, PAIR : 2 * PAIR]
            last = last + precise(biases, ((head_at == home) & known).astype(f32))
            last = last + precise(decays, ((head_at == home + HEADS) & known).astype(f32))
            home = channel_head // 2 * 2 * members + 2 * member + channel_head % 2
            skips = skips + precise(
                parts_ref[member, CONV + 2 : CONV + 3, :], (wide_at == home).astype(f32)
            )
        joined[LAST_ROW : LAST_ROW + 1, :] = last
        joined[LAST_ROW + 1 : LAST_ROW + 2, :] = skips
        vector_raw = joined[...]
        norm = jnp.sqrt(squares_ref[...] + total_squares(vector_raw))
        norm_ref[...] = norm
        factor = jnp.minimum(1.0, clip_norm / (norm + 1e-06))
        factor_ref[...] = factor
        grad = vector_raw * factor[0:1, 0:1]
        vector_grad_ref[...] = grad
        vector_moment_ref[...], vector_square_ref[...], vector_master_ref[...] = adamw(
            vector_ref[...], vector_first_ref[...], vector_second_ref[...], grad, rate_vectors
        )

    factor = factor_ref[0:1, 0:1]
    for pair in range(pairs):
        at = pair // members
        lanes, held = slice(pair * PAIR, (pair + 1) * PAIR), slice(at * PAIR, (at + 1) * PAIR)
        in_raw[:, lanes] = gate_ref[pair % members, :, held].astype(f32)
        in_raw[:, INNER + pair * PAIR : INNER + (pair + 1) * PAIR] = x_ref[
            pair % members, :, held
        ].astype(f32)
    small = jnp.concatenate([small_ref[i] for i in range(members)], axis=1)
    in_raw[:, 2 * INNER :] = dot_rows(small, turn_ref[...])
    grad = in_raw[...] * factor
    in_grad_ref[...] = grad
    in_moment_ref[...], in_square_ref[...], master = adamw(
        in_ref[...], in_first_ref[...], in_second_ref[...], grad, rate_in_proj
    )
    in_master_ref[...] = master
    in_rounded_ref[...] = master.astype(bf16)
    grad = out_raw_ref[...] * factor
    out_grad_ref[...] = grad
    out_moment_ref[...], out_square_ref[...], master = adamw(
        out_ref[...], out_first_ref[...], out_second_ref[...], grad, rate_out_proj
    )
    out_master_ref[...] = master
    out_rounded_ref[...] = master.astype(bf16)


def optimizer(squares, parts, vectors, gate, x, small, in_state, out_raw, out_state):
    members, rows, width = x.shape
    in_shape, out_shape = in_state[0].shape, out_state[0].shape
    steps = OPTIMIZER_STEPS
    step_rows = rows // steps
    piece = lambda lanes: pl.BlockSpec((members, step_rows, lanes), lambda i: (0, i, 0))
    in_flat = pl.BlockSpec((step_rows, in_shape[1]), lambda i: (i, 0))
    out_flat = pl.BlockSpec((out_shape[0] // steps, out_shape[1]), lambda i: (i, 0))
    sd = jax.ShapeDtypeStruct
    vector_shape = sd(vectors[0].shape, f32)
    return pl.pallas_call(
        optimizer_kernel,
        grid=(steps,),
        in_specs=[whole_spec()] * 6
        + [piece(width), piece(width), piece(PAIR)]
        + [in_flat] * 3
        + [out_flat] * 4,
        out_specs=[whole_spec()] * 5 + [in_flat] * 5 + [out_flat] * 5,
        out_shape=[sd((8, PAIR), f32)]
        + [vector_shape] * 4
        + [sd(in_shape, f32)] * 4
        + [sd(in_shape, bf16)]
        + [sd(out_shape, f32)] * 4
        + [sd(out_shape, bf16)],
        scratch_shapes=[
            pltpu.VMEM(vectors[0].shape, f32),
            pltpu.VMEM((8, PAIR), f32),
            pltpu.VMEM((step_rows, in_shape[1]), f32),
        ],
        compiler_params=pltpu.CompilerParams(vmem_limit_bytes=VMEM_BYTES),
        name="optimizer",
    )(
        squares, parts, *vectors, last_columns(members), gate, x, small, *in_state, out_raw,
        *out_state,
    )


def unpack(vectors):
    offset = D + INNER
    taps_end = offset + CONV * XBC
    heads_start = taps_end + XBC
    norm_gain = vectors[:D]
    gate_gain = vectors[D:offset]
    filter_taps = vectors[offset:taps_end].reshape(CONV, XBC)
    filter_bias = vectors[taps_end:heads_start]
    step_bias = vectors[heads_start : heads_start + HEADS]
    decay_log = vectors[heads_start + HEADS : heads_start + 2 * HEADS]
    skip_gain = vectors[heads_start + 2 * HEADS : heads_start + 3 * HEADS]
    return (norm_gain, gate_gain, filter_taps, filter_bias, step_bias, decay_log, skip_gain)


def adamw(weight, moment, square, gradient, step_rate):
    moment_new = beta_first * moment + (1.0 - beta_first) * gradient
    square_new = beta_second * square + (1.0 - beta_second) * gradient * gradient
    moment_hat = moment_new / (1.0 - beta_first**STEP)
    square_hat = square_new / (1.0 - beta_second**STEP)
    weight_new = weight - step_rate * (
        moment_hat / (jnp.sqrt(square_hat) + adam_eps) + weight_decay * weight
    )
    return (moment_new, square_new, weight_new)


def on_device(
    tokens,
    widths,
    cotangent,
    in_weight,
    in_first,
    in_second,
    out_weight,
    out_first,
    out_second,
    vectors,
    vector_first,
    vector_second,
):
    fsdp = lax.axis_size("fsdp")
    me = lax.axis_index("fsdp")
    heads = HEADS // fsdp
    inner = INNER // fsdp
    shared = 2 * STATE // fsdp
    pairs = HEADS // 2 // fsdp
    rows_in, rows_out = in_weight.shape[0], out_weight.shape[0]
    length = tokens.shape[0] * fsdp
    chunks = length // SPAN
    in_kernels = uses_ring("dp") and rows_out == PAIR and rows_in % 16 == 0

    def own_channels(v):
        lead = v.shape[:-1]
        cut = v.reshape(lead + (pairs, fsdp, PAIR))
        return lax.dynamic_index_in_dim(cut, me, len(lead) + 1, False).reshape(lead + (inner,))

    def own_heads(v):
        return lax.dynamic_index_in_dim(v.reshape(pairs, fsdp, 2), me, 1, False).reshape(heads)

    def own_shared(v):
        return lax.dynamic_slice_in_dim(v, me * shared, shared, v.ndim - 1)

    norm_gain, gate_gain, filter_taps, filter_bias, step_bias, decay_log, skip_gain = unpack(
        vectors
    )
    gain_own = own_channels(gate_gain)[None]
    taps_own = own_channels(filter_taps[:, :INNER])
    bias_own = own_channels(filter_bias[:INNER])[None]
    taps_shared = own_shared(filter_taps[:, INNER:])
    bias_shared = own_shared(filter_bias[INNER:])
    step_bias_own, decay_own = own_heads(step_bias), -jnp.exp(own_heads(decay_log))
    skip_own = jnp.repeat(own_heads(skip_gain), HEAD_DIM)[None]

    width_index = widths[0]
    active = HEADS // 8 * jnp.left_shift(jnp.int32(1), width_index)
    head_mask = (jnp.arange(heads, dtype=jnp.int32) < active // fsdp).astype(f32)
    mask = jnp.repeat(head_mask, HEAD_DIM)[None]
    channel_count = (active * HEAD_DIM).astype(f32)

    inputs = tokens.astype(f32)
    inverse_in = lax.rsqrt(jnp.mean(inputs * inputs, axis=-1, keepdims=True) + norm_eps)

    if in_kernels:
        vector_state = [vector_tiles(v) for v in (vectors, vector_first, vector_second)]
        (
            weight_shared, weight_x, weight_gate, weight_out, cotangents, normed_t, x_part, states,
            gated_low, gated_t, y_grad, gate_grad, consts, head_consts, shared_taps, head_columns,
            head_rows, head_all, keys, queries, queries_t, shared_part, shared_pre, gain_grad,
        ) = forward(tokens, cotangent, in_weight, out_weight, vector_state[0], active)
        scan_inputs = (consts, head_columns, head_rows, keys, queries)
    else:
        in_low = in_weight.astype(bf16)
        shared_cut = jnp.concatenate(
            [
                in_low[:, 2 * INNER : 2 * INNER + 2 * STATE]
                .reshape(rows_in, fsdp, shared)
                .transpose(1, 0, 2),
                in_low[:, 2 * INNER + 2 * STATE :]
                .reshape(rows_in, pairs, fsdp, 2)
                .transpose(2, 0, 1, 3)
                .reshape(fsdp, rows_in, heads),
            ],
            axis=2,
        )

        def channel_cut(part):
            return (
                part.reshape(rows_in, pairs, fsdp, PAIR)
                .transpose(2, 0, 1, 3)
                .reshape(fsdp, rows_in, inner)
            )

        def gathered(cut):
            block = exchanged(cut, "fsdp")
            return gather_rows(block.reshape(fsdp * rows_in, cut.shape[2]), "dp")

        normed_own = (inputs * inverse_in * norm_gain[None, :]).astype(bf16)
        x_cut = channel_cut(in_low[:, INNER : 2 * INNER])
        gate_cut = channel_cut(in_low[:, :INNER])
        out_low = out_weight.astype(bf16)

        weight_shared = gathered(shared_cut)
        weight_x = gathered(x_cut)
        weight_gate = gathered(gate_cut)
        weight_out = lax.dynamic_index_in_dim(
            lax.all_gather(out_low, ("dp", "fsdp"), axis=0, tiled=True).reshape(
                pairs, fsdp, PAIR, D
            ),
            me,
            1,
            False,
        ).reshape(inner, D)
        normed = spread(normed_own, "fsdp").reshape(length, D)
        cotangents = spread(cotangent, "fsdp").reshape(length, D)

        small = lax.dot_general(
            weight_shared, normed, (((0,), (1,)), ((), ())), preferred_element_type=f32
        )
        shared_part = small[:shared]
        step_raw = small[shared : shared + heads] * head_mask[:, None]
        shared_padded = jnp.pad(shared_part, ((0, 0), (CONV - 1, 0)))
        shared_pre = bias_shared[:, None] + sum(
            taps_shared[k][:, None] * shared_padded[:, k : k + length] for k in range(CONV)
        )
        shared_gate = jax.nn.sigmoid(shared_pre)
        shared_all = spread_small((shared_pre * shared_gate).astype(bf16), "fsdp").reshape(
            2 * STATE, length
        )
        keys_t, queries_t = shared_all[:STATE], shared_all[STATE:]
        keys, queries = keys_t.T, queries_t.T
        step_logits = step_raw + step_bias_own[:, None]
        step_sizes = jax.nn.softplus(step_logits)
        upto = (jnp.arange(SPAN)[:, None] <= jnp.arange(SPAN)[None, :]).astype(f32)
        log_sums = jnp.dot(
            (step_sizes * decay_own[:, None]).reshape(heads, chunks, SPAN), upto, precision=highest
        ).reshape(heads, length)
        groups = heads // GROUP
        head_all = jnp.concatenate(
            [log_sums, step_sizes, step_logits, jnp.zeros((PAIR - 3 * heads, length), f32)]
        ).T
        head_columns = jnp.concatenate(
            [jnp.roll(head_all, -group * GROUP, axis=1) for group in range(groups)], axis=1
        )
        head_rows = jnp.pad(
            log_sums.reshape(groups, GROUP, length), ((0, 0), (0, 8 - GROUP), (0, 0))
        ).reshape(groups * 8, length)

        consts = jnp.concatenate([taps_own, bias_own, mask, skip_own, gain_own])
        scan_inputs = (consts, head_columns, head_rows, keys, queries)
        x_part = jnp.dot(normed, weight_x, preferred_element_type=f32)
        y, states = scan_forward(x_part, *scan_inputs, keys_t)
        gate_part, gated_grad, stats = gate_forward(
            normed, weight_gate, cotangents, weight_out, y, gain_own, mask
        )
        stats = summed(stats[:, :2].T, "fsdp")
        inverse_out = lax.rsqrt(stats[0] / channel_count + norm_eps)
        pull = inverse_out**3 / channel_count * stats[1]
        gated_low, y_grad, gate_grad, gain_grad = norm_back(
            y, gate_part, gated_grad, jnp.stack([inverse_out, pull], axis=1), gain_own, mask
        )

        def in_term(grad):
            return lax.dot_general(
                normed, grad, (((0,), (0,)), ((), ())), preferred_element_type=f32
            ).astype(bf16)

    if in_kernels:
        (
            x_grad, key_grad, query_grad, sums, rest, channel_grad, gate_raw, out_raw, layer_out,
            squares,
        ) = scan_scatter(
            x_part, *scan_inputs, queries_t, y_grad, states,
            normed_t, gate_grad, gated_low, gated_t, cotangents, weight_out, tokens,
        )
    else:
        out_term = lax.dot_general(
            gated_low, cotangents, (((0,), (0,)), ((), ())), preferred_element_type=f32
        )
        whole_term = jnp.zeros((pairs, fsdp, PAIR, D), f32)
        whole_term = lax.dynamic_update_slice(
            whole_term, out_term.reshape(pairs, 1, PAIR, D), (0, me, 0, 0)
        )
        out_raw = lax.psum_scatter(
            whole_term.reshape(INNER, D), ("dp", "fsdp"), scatter_dimension=0, tiled=True
        )
        added = halved(
            jnp.dot(gated_low, weight_out, preferred_element_type=f32)
            .astype(bf16)
            .reshape(fsdp, tokens.shape[0], D),
            "fsdp",
        )
        layer_out = (inputs + added).astype(bf16)
        gate_raw = scatter_rows(in_term(gate_grad), "dp")
        x_grad, key_grad, query_grad, sums, rest, channel_grad = scan_backward(
            x_part, *scan_inputs, queries_t, y_grad, states
        )
    if in_kernels:
        gate_back, x_back, small_back, token_grad, vector_rows, squares = last_scatter(
            x_grad, normed_t, gate_grad, weight_gate, weight_x, weight_shared, key_grad,
            query_grad, sums, rest.reshape(chunks, inner), head_all, head_consts, shared_part,
            shared_pre, shared_taps, tokens, cotangent, vector_state[0], gate_raw, channel_grad, gain_grad, squares,
        )
        norm, *rest = optimizer(
            squares, vector_rows, vector_state, gate_back, x_back, small_back,
            (in_weight, in_first, in_second), out_raw, (out_weight, out_first, out_second),
        )
        vector_out = [v.reshape(-1)[: vectors.shape[0]] for v in rest[:4]]
        in_grad, in_moment, in_square, in_master, in_rounded = rest[4:9]
        out_grad, out_moment, out_square, out_master, out_rounded = rest[9:]
        return (
            layer_out,
            token_grad,
            in_grad,
            out_grad,
            vector_out[0],
            norm[0, 0],
            in_moment,
            in_square,
            in_master,
            in_rounded,
            out_moment,
            out_square,
            out_master,
            out_rounded,
            *vector_out[1:],
        )
    else:
        x_raw = scatter_rows(in_term(x_grad), "dp")

        shared_grads = jnp.concatenate([key_grad, query_grad], axis=1).T.astype(bf16)
        arrived = exchanged(shared_grads.reshape(fsdp, shared, length), "fsdp").astype(f32)
        activated_grad = jnp.sum(arrived, axis=0)
        shared_pre_grad = activated_grad * shared_gate * (1.0 + shared_pre * (1.0 - shared_gate))
        shared_ahead = jnp.pad(shared_pre_grad, ((0, 0), (0, CONV - 1)))
        shared_grad = sum(
            taps_shared[k][:, None] * shared_ahead[:, CONV - 1 - k : CONV - 1 - k + length]
            for k in range(CONV)
        )
        taps_shared_grad = jnp.stack(
            [
                jnp.sum(shared_pre_grad * shared_padded[:, k : k + length], axis=1)
                for k in range(CONV)
            ]
        )
        bias_shared_grad = jnp.sum(shared_pre_grad, axis=1)

        sums = sums.T[: 3 * heads].reshape(3, heads, chunks, SPAN)
        before = (jnp.arange(SPAN)[:, None] < jnp.arange(SPAN)[None, :]).astype(f32)
        rest = rest.reshape(chunks, heads, HEAD_DIM).sum(axis=2).T
        log_grad = (
            jnp.dot(sums[0], 1.0 - before, precision=highest)
            + jnp.dot(sums[1], before, precision=highest)
            + rest[:, :, None]
        ).reshape(heads, length)
        step_grad = decay_own[:, None] * log_grad + sums[2].reshape(heads, length)
        raw_grad = step_grad * jax.nn.sigmoid(step_logits)
        step_bias_grad = jnp.sum(raw_grad, axis=1)
        decay_grad = jnp.sum(step_sizes * log_grad, axis=1) * decay_own
        small_grad = jnp.concatenate([shared_grad, raw_grad * head_mask[:, None]], axis=0).astype(bf16)
        small_raw = scatter_rows(
            lax.dot_general(
                normed, small_grad, (((0,), (1,)), ((), ())), preferred_element_type=f32
            ).astype(bf16),
            "dp",
        )

        def in_back(grad, weight, grad_dim=1):
            return lax.dot_general(
                grad, weight, (((grad_dim,), (1,)), ((), ())), preferred_element_type=f32
            )

        normed_grad = halved(
            (
                in_back(gate_grad, weight_gate)
                + in_back(x_grad, weight_x)
                + in_back(small_grad, weight_shared, 0)
            )
            .astype(bf16)
            .reshape(fsdp, tokens.shape[0], D),
            "fsdp",
        )
        pulled = normed_grad * norm_gain[None, :]
        input_grad = inverse_in * pulled - inputs * (
            inverse_in**3 * jnp.mean(pulled * inputs, axis=-1, keepdims=True)
        )
        token_grad = (cotangent.astype(f32) + input_grad).astype(bf16)
        norm_gain_grad = jnp.sum(normed_grad * inputs * inverse_in, axis=0)

        head_row = jnp.concatenate(
            [jnp.pad(step_bias_grad, (0, PAIR - heads)), jnp.pad(decay_grad, (0, PAIR - heads))]
        )
        shared_rows = jnp.concatenate([taps_shared_grad, bias_shared_grad[None]])
        vector_rows = jnp.concatenate(
            [
                gain_grad[0:1],
                channel_grad[: CONV + 2],
                norm_gain_grad.reshape(-1, inner),
                jnp.zeros((15 - CONV - 3 - D // inner, inner), f32),
                jnp.pad(head_row, (0, inner - 2 * PAIR))[None],
                jnp.pad(shared_rows, ((0, 7 - CONV), (0, inner - shared))),
            ]
        )
        vector_rows = spread_small(summed_in_steps(vector_rows, "dp"), "fsdp")
        squares = (
            jnp.sum(gate_raw * gate_raw)
            + jnp.sum(x_raw * x_raw)
            + jnp.sum(small_raw * small_raw)
            + jnp.sum(out_raw * out_raw)
        )
        squares = summed(summed(jnp.broadcast_to(squares, (8, 128)), "fsdp"), "dp")[0, 0]

    def joined_channels(v):
        return v.reshape(fsdp, pairs, PAIR).transpose(1, 0, 2).reshape(INNER)

    def joined_heads(v):
        return v.reshape(fsdp, pairs, 2).transpose(1, 0, 2).reshape(HEADS)

    shared_all = vector_rows[:, 16 : 17 + CONV, :shared]
    bias_shared_all = shared_all[:, CONV].reshape(-1)
    taps_all = [
        jnp.concatenate([joined_channels(vector_rows[:, 1 + k]), shared_all[:, k].reshape(-1)])
        for k in range(CONV)
    ]
    bias_all = jnp.concatenate([joined_channels(vector_rows[:, CONV + 1]), bias_shared_all])
    norm_rows = vector_rows[:, CONV + 3 : CONV + 3 + D // inner].reshape(fsdp, D)
    norm_all = norm_rows[0]
    for member in range(1, fsdp):
        norm_all = norm_all + norm_rows[member]
    skip_all = vector_rows[:, CONV + 2].reshape(fsdp * heads, HEAD_DIM).sum(axis=1)
    vector_raw = jnp.concatenate(
        [norm_all, joined_channels(vector_rows[:, 0])]
        + taps_all
        + [
            bias_all,
            joined_heads(vector_rows[:, 15, :heads]),
            joined_heads(vector_rows[:, 15, PAIR : PAIR + heads]),
            joined_heads(skip_all),
        ]
    )

    grad_norm = jnp.sqrt(squares + jnp.sum(vector_raw * vector_raw))
    factor = jnp.minimum(1.0, clip_norm / (grad_norm + 1e-06))
    def returned(raw):
        return exchanged(raw.astype(bf16).reshape(fsdp, rows_in, raw.shape[1]), "fsdp")

    def joined_columns(part):
        return (
            part.reshape(fsdp, rows_in, pairs, PAIR)
            .transpose(1, 2, 0, 3)
            .reshape(rows_in, INNER)
        )

    small_back = returned(small_raw)
    in_raw = jnp.concatenate(
        [
            joined_columns(returned(gate_raw)),
            joined_columns(returned(x_raw)),
            small_back[:, :, :shared].transpose(1, 0, 2).reshape(rows_in, 2 * STATE),
            small_back[:, :, shared:]
            .reshape(fsdp, rows_in, pairs, 2)
            .transpose(1, 2, 0, 3)
            .reshape(rows_in, HEADS),
        ],
        axis=1,
    ).astype(f32)
    in_grad = in_raw * factor
    in_moment, in_square, in_master = adamw(
        in_weight, in_first, in_second, in_grad, rate_in_proj
    )
    in_rounded = in_master.astype(bf16)
    out_grad = out_raw * factor
    vector_grad = vector_raw * factor
    out_moment, out_square, out_master = adamw(
        out_weight, out_first, out_second, out_grad, rate_out_proj
    )
    vector_moment, vector_square, vector_master = adamw(
        vectors, vector_first, vector_second, vector_grad, rate_vectors
    )
    return (
        layer_out,
        token_grad,
        in_grad,
        out_grad,
        vector_grad,
        grad_norm,
        in_moment,
        in_square,
        in_master,
        in_rounded,
        out_moment,
        out_square,
        out_master,
        out_master.astype(bf16),
        vector_moment,
        vector_square,
        vector_master,
    )


def solution(mesh):
    rows = P(("dp", "fsdp"), None)
    return jax.shard_map(
        on_device,
        mesh=mesh,
        in_specs=(rows, P("dp")) + (rows,) * 7 + (P(),) * 3,
        out_specs=(rows,) * 4 + (P(),) * 2 + (rows,) * 8 + (P(),) * 3,
        check_vma=False,
    )
```

```python
from functools import partial

import jax
import jax.numpy as jnp
import numpy as np
from jax import lax
from jax.experimental import pallas as pl
from jax.experimental.pallas import tpu as pltpu
from jax.sharding import PartitionSpec as P

D = 2048
HEADS = 64
HEAD_DIM = 64
STATE = 128
CONV = 4
SPAN = 128
STEP = 10
INNER = 4096
XBC = 4352
PAIR = 2 * HEAD_DIM
GROUP = 4
STEP_LANE = 16
TAPS_ROW = (D + INNER) // PAIR
LAST_ROW = TAPS_ROW + (CONV + 1) * XBC // PAIR
MASK_ROW, SKIP_ROW, GAIN_ROW = CONV + 1, CONV + 2, CONV + 3
LANES = GROUP * HEAD_DIM
ROW_TILE = 256
RING_LIMIT = 16

norm_eps = 1e-05
clip_norm = 1.0
beta_first = 0.5
beta_second = 0.5
adam_eps = 1e-08
weight_decay = 0.1
rate_in_proj = 0.03
rate_out_proj = 0.02
rate_vectors = 0.5
highest = lax.Precision.HIGHEST
f32 = jnp.float32
bf16 = jnp.bfloat16
VMEM_BYTES = 60 * 1024 * 1024
BACKWARD_VMEM_BYTES = 63 * 1024 * 1024


def ring_order(count):
    return list(range(0, count, 2)) + list(range(count - 1, 0, -2))


def ring_links(count):
    order = ring_order(count)
    right = [(order[i], order[(i + 1) % count]) for i in range(count)]
    return right, [(b, a) for a, b in right]


def ring_place(axis):
    count = lax.axis_size(axis)
    order = ring_order(count)
    places = [0] * count
    for place, member in enumerate(order):
        places[member] = place
    place = jnp.asarray(places, jnp.int32)[lax.axis_index(axis)]

    def member_at(distance):
        return jnp.asarray(order, jnp.int32)[lax.rem(place + distance + count, count)]

    return member_at


def uses_ring(axis):
    count = lax.axis_size(axis)
    return count % 2 == 0 and 4 <= count <= RING_LIMIT


def gather_rows(block, axis):
    count = lax.axis_size(axis)
    if not uses_ring(axis):
        return lax.all_gather(block, axis, axis=0, tiled=True)
    right, left = ring_links(count)
    member_at = ring_place(axis)
    rows, half = block.shape[0], block.shape[0] // 2
    whole = jnp.zeros((count * rows,) + block.shape[1:], block.dtype)
    columns = (0,) * (block.ndim - 1)

    def put(whole, piece, distance, shift=0):
        return lax.dynamic_update_slice(
            whole, piece, (member_at(distance) * rows + shift,) + columns
        )

    whole = put(whole, block, 0)
    going_right = going_left = block
    for hop in range(1, count // 2):
        going_right = lax.ppermute(going_right, axis, right)
        going_left = lax.ppermute(going_left, axis, left)
        whole = put(whole, going_right, -hop)
        whole = put(whole, going_left, hop)
    first = lax.ppermute(going_right[:half], axis, right)
    second = lax.ppermute(going_left[half:], axis, left)
    whole = put(whole, first, count // 2)
    return put(whole, second, count // 2, half)


def scatter_rows(terms, axis):
    count = lax.axis_size(axis)
    if not uses_ring(axis):
        return lax.psum_scatter(terms.astype(f32), axis, scatter_dimension=0, tiled=True)
    right, left = ring_links(count)
    member_at = ring_place(axis)
    rows = terms.shape[0] // count
    half = rows // 2

    def term(distance):
        return lax.dynamic_slice_in_dim(terms, member_at(distance) * rows, rows, 0).astype(f32)

    far = term(count // 2).astype(bf16)
    going_right = lax.ppermute(far[:half], axis, right)
    going_left = lax.ppermute(far[half:], axis, left)
    for distance in range(count // 2 - 1, 0, -1):
        to_right, to_left = term(distance), term(-distance)
        if distance == count // 2 - 1:
            to_right = jnp.concatenate([to_right[:half] + going_right, to_right[half:]])
            to_left = jnp.concatenate([to_left[:half], to_left[half:] + going_left])
        else:
            to_right, to_left = to_right + going_right, to_left + going_left
        going_right = lax.ppermute(to_right.astype(bf16), axis, right)
        going_left = lax.ppermute(to_left.astype(bf16), axis, left)
    return term(0) + going_right + going_left


def swapped(value, axis, flip):
    count = lax.axis_size(axis)
    return lax.ppermute(value, axis, [(i, i ^ flip) for i in range(count)])


def summed(value, axis):
    count = lax.axis_size(axis)
    if count <= 8:
        parts = [value] + [swapped(value, axis, flip) for flip in range(1, count)]
        while len(parts) > 1:
            parts = [parts[i] + parts[i + 1] for i in range(0, len(parts), 2)]
        return parts[0]
    return summed_in_steps(value, axis)


def summed_in_steps(value, axis):
    flip = 1
    while flip < lax.axis_size(axis):
        value = value + swapped(value, axis, flip)
        flip *= 2
    return value


def placed(parts, axis):
    count = lax.axis_size(axis)
    me = lax.axis_index(axis)
    whole = jnp.zeros((count,) + parts[0].shape, parts[0].dtype)
    for flip, part in enumerate(parts):
        whole = lax.dynamic_update_index_in_dim(whole, part, lax.bitwise_xor(me, flip), 0)
    return whole


def spread(value, axis):
    count = lax.axis_size(axis)
    parts = [value]
    flip = count // 2
    known = {0: value}
    while flip:
        fresh = {k ^ flip: swapped(v, axis, flip) for k, v in known.items()}
        known.update(fresh)
        flip //= 2
    parts = [known[k] for k in range(count)]
    return placed(parts, axis)


def spread_small(value, axis):
    count = lax.axis_size(axis)
    return placed([value] + [swapped(value, axis, k) for k in range(1, count)], axis)


def exchanged(blocks, axis):
    count = lax.axis_size(axis)
    me = lax.axis_index(axis)

    def block_for(flip):
        return lax.dynamic_index_in_dim(blocks, lax.bitwise_xor(me, flip), 0, False)

    return placed(
        [block_for(0)] + [swapped(block_for(k), axis, k) for k in range(1, count)], axis
    )


def halved(blocks, axis):
    count = lax.axis_size(axis)
    me = lax.axis_index(axis)
    held = {
        k: lax.dynamic_index_in_dim(blocks, lax.bitwise_xor(me, k), 0, False)
        for k in range(count)
    }
    flip = 1
    while flip < count:
        kept = {}
        for k in sorted(held):
            if k & flip:
                continue
            arrived = swapped(held[k ^ flip].astype(bf16), axis, flip)
            kept[k] = held[k].astype(f32) + arrived
        held = kept
        flip *= 2
    return held[0]


def dot_rows(a, b):
    return lax.dot_general(a, b, (((1,), (0,)), ((), ())), preferred_element_type=f32)


def dot_lanes(a, b):
    return lax.dot_general(a, b, (((1,), (1,)), ((), ())), preferred_element_type=f32)


def head_lanes(columns, base):
    rows = columns.shape[0]
    full = [
        jnp.broadcast_to(columns[:, base + j : base + j + 1], (rows, PAIR)) for j in range(GROUP)
    ]
    first = lax.broadcasted_iota(jnp.int32, (rows, PAIR), 1) < HEAD_DIM
    lanes = jnp.concatenate(
        [jnp.where(first, full[i], full[i + 1]) for i in range(0, GROUP, 2)], axis=1
    )
    return full, lanes


def stacked_heads(values, block_mask):
    return jnp.concatenate([values] * GROUP, axis=0) * block_mask


def filtered(window, taps, bias, rows):
    pre = bias + taps[CONV - 1 : CONV] * window[8 : 8 + rows]
    for k in range(CONV - 1):
        pre = pre + taps[k : k + 1] * window[5 + k : 5 + k + rows]
    return pre


def scan_forward_kernel(
    x_ref, consts_ref, column_ref, row_ref, key_ref, query_ref,
    key_t_ref, block_ref, y_ref, states_ref, padded, state,
):
    length = x_ref.shape[0]
    rows = SPAN
    mask = consts_ref[MASK_ROW : MASK_ROW + 1]
    padded[0:8, :] = jnp.zeros((8, LANES), f32)
    padded[8 : 8 + length, :] = x_ref[...] * mask
    state[...] = jnp.zeros_like(state)
    taps, bias = consts_ref[0:CONV], consts_ref[CONV : CONV + 1]
    skip = consts_ref[SKIP_ROW : SKIP_ROW + 1]
    causal = lax.broadcasted_iota(jnp.int32, (rows, rows), 0) >= lax.broadcasted_iota(
        jnp.int32, (rows, rows), 1
    )

    def chunk(c, carry):
        start = pl.multiple_of(c * rows, rows)
        here = pl.ds(start, rows)
        pre = filtered(padded[pl.ds(start, rows + 8), :], taps, bias, rows)
        values = pre * jax.nn.sigmoid(pre) * mask
        columns = column_ref[here, :]
        log_full, log_lanes = head_lanes(columns, 0)
        step_lanes = head_lanes(columns, STEP_LANE)[1]
        weighted = step_lanes * values
        weighted_low = weighted.astype(bf16)
        keys, queries, keys_t = key_ref[here, :], query_ref[here, :], key_t_ref[:, here]
        inner = dot_lanes(queries, keys)
        mixing = jnp.concatenate(
            [
                (
                    jnp.where(causal, jnp.exp(log_full[j] - row_ref[j : j + 1, here]), 0.0)
                    * inner
                ).astype(bf16)
                for j in range(GROUP)
            ],
            axis=1,
        )
        state_now = state[...]
        state_low = state_now.astype(bf16)
        states_ref[pl.ds(c, 1)] = state_low[None]
        y = dot_rows(mixing, stacked_heads(weighted_low, block_ref[...]))
        y = y + jnp.exp(log_lanes) * dot_rows(queries, state_low)
        y_ref[here, :] = y + skip * values
        log_last = log_lanes[rows - 1 : rows, :]
        tail = (weighted * jnp.exp(log_last - log_lanes)).astype(bf16)
        state[...] = jnp.exp(log_last) * state_now + dot_rows(keys_t, tail)
        return carry

    lax.fori_loop(0, length // rows, chunk, 0)


def scan_backward_group(
    x_ref, consts_ref, column_ref, row_ref, key_ref, query_ref,
    query_t_ref, block_ref, pick_ref, grad_ref, states_ref,
    x_grad_ref, key_grad_ref, query_grad_ref, sums_ref, rest_ref, channel_ref,
    padded, following, state_back, inner_grad,
):
    length = x_ref.shape[0]
    rows = SPAN
    chunks = length // rows
    mask = consts_ref[MASK_ROW : MASK_ROW + 1]
    padded[0:8, :] = jnp.zeros((8, LANES), f32)
    padded[8 : 8 + length, :] = x_ref[...] * mask
    following[...] = jnp.zeros_like(following)
    state_back[...] = jnp.zeros_like(state_back)
    channel_ref[...] = jnp.zeros_like(channel_ref)

    taps, bias = consts_ref[0:CONV], consts_ref[CONV : CONV + 1]
    skip = consts_ref[SKIP_ROW : SKIP_ROW + 1]
    row_at = lax.broadcasted_iota(jnp.int32, (rows, rows), 0)
    lane_at = lax.broadcasted_iota(jnp.int32, (rows, rows), 1)
    causal, causal_t = row_at >= lane_at, lane_at >= row_at

    def chunk(lap, carry):
        c = chunks - 1 - lap
        start = pl.multiple_of(c * rows, rows)
        here = pl.ds(start, rows)
        window = padded[pl.ds(start, rows + 8), :]
        pre = filtered(window, taps, bias, rows)
        gate = jax.nn.sigmoid(pre)
        values = pre * gate * mask
        columns = column_ref[here, :]
        log_full, log_lanes = head_lanes(columns, 0)
        step_lanes = head_lanes(columns, STEP_LANE)[1]
        weighted = step_lanes * values
        weighted_low = weighted.astype(bf16)
        keys, queries, queries_t = key_ref[here, :], query_ref[here, :], query_t_ref[:, here]
        grad_low = grad_ref[here, :]
        grad = grad_low.astype(f32)
        inner, inner_t = dot_lanes(queries, keys), dot_lanes(keys, queries)
        blocks = block_ref[...]
        weighted_blocks = stacked_heads(weighted_low, blocks)
        grad_blocks = stacked_heads(grad_low, blocks)
        mixing_grad = dot_lanes(grad_low, weighted_blocks)
        mixing, mixing_t, inner_sum = [], [], jnp.zeros((rows, rows), f32)
        for j in range(GROUP):
            log_row = row_ref[j : j + 1, here]
            decay = jnp.where(causal, jnp.exp(log_full[j] - log_row), 0.0)
            decay_t = jnp.where(causal_t, jnp.exp(log_row - log_full[j]), 0.0)
            mixing.append((decay * inner).astype(bf16))
            mixing_t.append((decay_t * inner_t).astype(bf16))
            inner_sum = inner_sum + decay * mixing_grad[:, j * rows : (j + 1) * rows]
        inner_grad[pl.ds(c, 1)] = inner_grad[pl.ds(c, 1)] + inner_sum[None]
        y = dot_rows(jnp.concatenate(mixing, axis=1), weighted_blocks)
        state_low = states_ref[pl.ds(c, 1)][0]
        entry = jnp.exp(log_lanes)
        y = y + entry * dot_rows(queries, state_low)
        inside = dot_rows(jnp.concatenate(mixing_t, axis=1), grad_blocks)
        back = state_back[...]
        back_low = back.astype(bf16)
        log_last = log_lanes[rows - 1 : rows, :]
        tail = jnp.exp(log_last - log_lanes)
        outside = tail * dot_rows(keys, back_low)
        entry_grad = (grad * entry).astype(bf16)
        tail_low = (weighted * tail).astype(bf16)
        query_grad_ref[here, :] = query_grad_ref[here, :] + dot_lanes(entry_grad, state_low)
        key_grad_ref[here, :] = key_grad_ref[here, :] + dot_lanes(tail_low, back_low)
        last = jnp.exp(log_last)
        rest_ref[pl.ds(c, 1)] = (
            last * jnp.sum(state_low.astype(f32) * back, axis=0, keepdims=True)
        )[None]
        state_back[...] = last * back + dot_rows(queries_t, entry_grad)
        weighted_grad = inside + outside
        first = grad * y - weighted_low.astype(f32) * inside
        first_high = first.astype(bf16)
        first_rest = (first - first_high.astype(f32)).astype(bf16)
        sums_ref[here, :] = sums_ref[here, :] + (
            dot_rows(first_high, pick_ref[0])
            + dot_rows(first_rest, pick_ref[0])
            + dot_rows((weighted * outside).astype(bf16), pick_ref[1])
            + dot_rows((values * weighted_grad).astype(bf16), pick_ref[2])
        )
        values_grad = step_lanes * weighted_grad + skip * grad
        pre_grad = values_grad * mask * (gate * (1.0 + pre * (1.0 - gate)))
        channel_ref[CONV : CONV + 1, :] += jnp.sum(pre_grad, axis=0, keepdims=True)
        channel_ref[CONV + 1 : CONV + 2, :] += jnp.sum(grad * values, axis=0, keepdims=True)
        for k in range(CONV):
            channel_ref[k : k + 1, :] += jnp.sum(
                pre_grad * window[5 + k : 5 + k + rows], axis=0, keepdims=True
            )
        ahead = jnp.concatenate([pre_grad, following[...]], axis=0)
        following[...] = pre_grad[0:8]
        x_grad = taps[CONV - 1 : CONV] * ahead[0:rows]
        for k in range(CONV - 1):
            x_grad = x_grad + taps[k : k + 1] * ahead[CONV - 1 - k : CONV - 1 - k + rows]
        x_grad_ref[here, :] = (x_grad * mask).astype(bf16)
        return carry

    lax.fori_loop(0, chunks, chunk, 0)


def scan_backward_start(key_grad_ref, query_grad_ref, sums_ref, inner_grad):
    key_grad_ref[...] = jnp.zeros_like(key_grad_ref)
    query_grad_ref[...] = jnp.zeros_like(query_grad_ref)
    inner_grad[...] = jnp.zeros_like(inner_grad)
    sums_ref[...] = jnp.zeros_like(sums_ref)


def scan_backward_finish(key_ref, query_ref, key_grad_ref, query_grad_ref, inner_grad):
    rows = SPAN

    def finish(c, carry):
        here = pl.ds(pl.multiple_of(c * rows, rows), rows)
        inner_low = inner_grad[pl.ds(c, 1)][0].astype(bf16)
        query_grad_ref[here, :] = query_grad_ref[here, :] + dot_rows(inner_low, key_ref[here, :])
        key_grad_ref[here, :] = key_grad_ref[here, :] + lax.dot_general(
            inner_low, query_ref[here, :], (((0,), (0,)), ((), ())), preferred_element_type=f32
        )
        return carry

    lax.fori_loop(0, key_ref.shape[0] // rows, finish, 0)


def scan_backward_kernel(*refs):
    key_ref, query_ref = refs[4:6]
    key_grad_ref, query_grad_ref, sums_ref = refs[12:15]
    inner_grad = refs[-1]

    @pl.when(pl.program_id(0) == 0)
    def _():
        scan_backward_start(key_grad_ref, query_grad_ref, sums_ref, inner_grad)

    scan_backward_group(*refs)

    @pl.when(pl.program_id(0) == pl.num_programs(0) - 1)
    def _():
        scan_backward_finish(key_ref, query_ref, key_grad_ref, query_grad_ref, inner_grad)


def block_mask():
    row = np.arange(GROUP * SPAN)[:, None] // SPAN
    lane = np.arange(LANES)[None, :] // HEAD_DIM
    return jnp.asarray((row == lane).astype(np.float32), bf16)


def pick_masks(groups):
    lane = np.arange(LANES)[:, None] // HEAD_DIM
    target = np.arange(PAIR)[None, :]
    masks = [
        target == (kind * groups + group) * GROUP + lane
        for group in range(groups)
        for kind in range(3)
    ]
    return jnp.asarray(np.stack(masks).astype(np.float32), bf16)


def whole_spec():
    return pl.BlockSpec(memory_space=pltpu.VMEM)


def lane_spec(rows):
    return pl.BlockSpec((rows, LANES), lambda g: (0, g))


def head_specs(length):
    return [
        lane_spec(length),
        lane_spec(8),
        pl.BlockSpec((length, PAIR), lambda g: (0, g)),
        pl.BlockSpec((8, length), lambda g: (g, 0)),
        whole_spec(),
        whole_spec(),
        whole_spec(),
        whole_spec(),
    ]


def scan_forward(x, consts, columns, rows, keys, queries, keys_t):
    length, width = x.shape
    chunks = length // SPAN
    return pl.pallas_call(
        scan_forward_kernel,
        grid=(width // LANES,),
        in_specs=head_specs(length),
        out_specs=[
            lane_spec(length),
            pl.BlockSpec((chunks, STATE, LANES), lambda g: (0, 0, g)),
        ],
        out_shape=[
            jax.ShapeDtypeStruct((length, width), f32),
            jax.ShapeDtypeStruct((chunks, STATE, width), bf16),
        ],
        scratch_shapes=[pltpu.VMEM((length + 8, LANES), f32), pltpu.VMEM((STATE, LANES), f32)],
        compiler_params=pltpu.CompilerParams(vmem_limit_bytes=VMEM_BYTES),
        cost_estimate=pl.CostEstimate(
            flops=10_000_000_000, bytes_accessed=12_000_000, transcendentals=4_000_000
        ),
        name="scan_forward",
    )(x, consts, columns, rows, keys, queries, keys_t, block_mask())


def scan_backward(
    x, consts, columns, rows, keys, queries, queries_t, grad, states
):
    length, width = x.shape
    chunks = length // SPAN
    groups = width // LANES
    same = lambda g: (0, 0)
    return pl.pallas_call(
        scan_backward_kernel,
        grid=(groups,),
        in_specs=head_specs(length)
        + [
            pl.BlockSpec((3, LANES, PAIR), lambda g: (g, 0, 0)),
            lane_spec(length),
            pl.BlockSpec((chunks, STATE, LANES), lambda g: (0, 0, g)),
        ],
        out_specs=[
            lane_spec(length),
            pl.BlockSpec((length, STATE), same),
            pl.BlockSpec((length, STATE), same),
            pl.BlockSpec((length, PAIR), same),
            pl.BlockSpec((chunks, 1, LANES), lambda g: (0, 0, g)),
            lane_spec(8),
        ],
        out_shape=[
            jax.ShapeDtypeStruct((length, width), bf16),
            jax.ShapeDtypeStruct((length, STATE), f32),
            jax.ShapeDtypeStruct((length, STATE), f32),
            jax.ShapeDtypeStruct((length, PAIR), f32),
            jax.ShapeDtypeStruct((chunks, 1, width), f32),
            jax.ShapeDtypeStruct((8, width), f32),
        ],
        scratch_shapes=[
            pltpu.VMEM((length + 8, LANES), f32),
            pltpu.VMEM((8, LANES), f32),
            pltpu.VMEM((STATE, LANES), f32),
            pltpu.VMEM((chunks, SPAN, SPAN), f32),
        ],
        compiler_params=pltpu.CompilerParams(vmem_limit_bytes=VMEM_BYTES),
        cost_estimate=pl.CostEstimate(
            flops=30_000_000_000, bytes_accessed=16_000_000, transcendentals=8_000_000
        ),
        name="scan_backward",
    )(
        x, consts, columns, rows, keys, queries, queries_t, block_mask(),
        pick_masks(groups), grad, states,
    )


def gate_kernel(
    normed_ref, weight_ref, cotangent_ref, out_ref, y_ref, gain_ref, mask_ref,
    gate_part_ref, gated_grad_ref, stats_ref,
):
    gate_part = dot_rows(normed_ref[...], weight_ref[...]) * mask_ref[...]
    gated_grad = dot_lanes(cotangent_ref[...], out_ref[...])
    gate_part_ref[...] = gate_part
    gated_grad_ref[...] = gated_grad
    gated = y_ref[...] * (gate_part * jax.nn.sigmoid(gate_part))
    squares = jnp.sum(gated * gated, axis=1, keepdims=True)
    products = jnp.sum(gated * gated_grad * gain_ref[...], axis=1, keepdims=True)
    lane = lax.broadcasted_iota(jnp.int32, stats_ref.shape, 1)
    stats_ref[...] = jnp.where(lane == 0, squares, products)


def gate_forward(normed, weight, cotangent, out_weight, y, gain, mask):
    length, width = y.shape
    rows = lambda lanes: pl.BlockSpec((ROW_TILE, lanes), lambda i: (i, 0))
    return pl.pallas_call(
        gate_kernel,
        grid=(length // ROW_TILE,),
        in_specs=[
            rows(D), whole_spec(), rows(D), whole_spec(), rows(width), whole_spec(), whole_spec(),
        ],
        out_specs=[rows(width), rows(width), rows(PAIR)],
        out_shape=[
            jax.ShapeDtypeStruct((length, width), f32),
            jax.ShapeDtypeStruct((length, width), f32),
            jax.ShapeDtypeStruct((length, PAIR), f32),
        ],
        compiler_params=pltpu.CompilerParams(vmem_limit_bytes=VMEM_BYTES),
        cost_estimate=pl.CostEstimate(
            flops=9_000_000_000, bytes_accessed=28_000_000, transcendentals=1_000_000
        ),
        name="gate_forward",
    )(normed, weight, cotangent, out_weight, y, gain, mask)


def norm_back_kernel(
    y_ref, gate_part_ref, gated_grad_ref, scale_ref, gain_ref, mask_ref,
    gated_ref, y_grad_ref, gate_grad_ref, gain_grad_ref,
):
    @pl.when(pl.program_id(0) == 0)
    def _():
        gain_grad_ref[...] = jnp.zeros_like(gain_grad_ref)

    y, gate_part, gated_grad = y_ref[...], gate_part_ref[...], gated_grad_ref[...]
    inverse, pull = scale_ref[:, 0:1], scale_ref[:, 1:2]
    gate = jax.nn.sigmoid(gate_part)
    silu = gate_part * gate
    gated = y * silu
    scaled = gated * inverse
    gain = gain_ref[...]
    gated_ref[...] = (scaled * gain).astype(bf16)
    gain_grad_ref[0:1, :] += jnp.sum(gated_grad * scaled, axis=0, keepdims=True)
    back = inverse * (gated_grad * gain) - gated * pull
    y_grad_ref[...] = (back * silu).astype(bf16)
    gate_grad_ref[...] = (
        back * y * (gate * (1.0 + gate_part * (1.0 - gate))) * mask_ref[...]
    ).astype(bf16)


def norm_back(y, gate_part, gated_grad, scales, gain, mask):
    length, width = y.shape
    rows = lambda lanes: pl.BlockSpec((ROW_TILE, lanes), lambda i: (i, 0))
    return pl.pallas_call(
        norm_back_kernel,
        grid=(length // ROW_TILE,),
        in_specs=[rows(width), rows(width), rows(width), rows(2), whole_spec(), whole_spec()],
        out_specs=[
            rows(width), rows(width), rows(width), pl.BlockSpec((8, width), lambda i: (0, 0)),
        ],
        out_shape=[
            jax.ShapeDtypeStruct((length, width), bf16),
            jax.ShapeDtypeStruct((length, width), bf16),
            jax.ShapeDtypeStruct((length, width), bf16),
            jax.ShapeDtypeStruct((8, width), f32),
        ],
        compiler_params=pltpu.CompilerParams(vmem_limit_bytes=VMEM_BYTES),
        cost_estimate=pl.CostEstimate(
            flops=30_000_000, bytes_accessed=18_000_000, transcendentals=1_000_000
        ),
        name="norm_back",
    )(y, gate_part, gated_grad, scales, gain, mask)


MESH = pl.DeviceIdType.MESH


class Ring:
    def __init__(self):
        self.count = lax.axis_size("dp")
        self.far = self.count // 2
        me = lax.axis_index("dp")
        odd = lax.rem(me, 2)
        self.me = me
        self.place = (1 - odd) * lax.div(me, 2) + odd * lax.div(2 * self.count - 1 - me, 2)

    def member(self, distance):
        n = self.count
        place = lax.rem(self.place + distance + n, n)
        back = lax.div(place, n // 2)
        return (1 - back) * 2 * place + back * (2 * n - 1 - 2 * place)

    def target(self, way):
        return {"dp": self.member(1 if way == 0 else -1)}


def partner(flip):
    f = lax.axis_index("fsdp")
    return (f, f + 1 - 2 * lax.rem(f, 2), lax.rem(f + 2, 4), 3 - f)[flip]


def greet(targets):
    barrier = pltpu.get_barrier_semaphore()
    for target in targets:
        pl.semaphore_signal(barrier, inc=1, device_id=target, device_id_type=MESH)
    pl.semaphore_wait(barrier, len(targets))


def row_slice(ref, start, size):
    return ref.at[pl.ds(pl.multiple_of(start, 16), size)]


class RingGather:
    def __init__(self, ring, wholes, send, recv):
        self.ring, self.wholes, self.send, self.recv = ring, wholes, send, recv

    @staticmethod
    def semaphores(parts, count):
        return pltpu.SemaphoreType.DMA((parts * 4 * (count // 2),))

    def copy(self, part, way, half, hop):
        whole = self.wholes[part]
        rows = whole.shape[0] // self.ring.count
        size = rows // 2
        owner = self.ring.member(-hop if way == 0 else hop)
        place = row_slice(whole, owner * rows + half * size, size)
        at = ((part * 2 + way) * 2 + half) * self.ring.far + hop
        return pltpu.make_async_remote_copy(
            place, place, self.send.at[at], self.recv.at[at],
            device_id=self.ring.target(way), device_id_type=MESH,
        )

    def pieces(self, hop):
        return [
            (way, half)
            for half in (0, 1)
            for way in (0, 1)
            if hop < self.ring.far - 1 or half == way
        ]

    def start(self, part, hop):
        for way, half in self.pieces(hop):
            if hop:
                self.copy(part, way, half, hop - 1).wait_recv()
            self.copy(part, way, half, hop).start()

    def finish(self, part):
        last = self.ring.far - 1
        for way, half in self.pieces(last):
            self.copy(part, way, half, last).wait_recv()
            if last:
                self.copy(part, way, 1 - half, last - 1).wait_recv()
        for hop in range(last + 1):
            for way, half in self.pieces(hop):
                self.copy(part, way, half, hop).wait_send()


class RingScatter:
    def __init__(self, ring, held, arrived, send, recv):
        self.ring, self.held, self.arrived = ring, held, arrived
        self.send, self.recv = send, recv

    @staticmethod
    def scratch(count, rows, columns):
        return [
            pltpu.VMEM((2, 2, rows, columns), bf16),
            pltpu.VMEM((2, count // 2 * rows - rows // 2, columns), bf16),
        ]

    def landing(self, way, hop):
        rows = self.held.shape[2]
        if hop == 0:
            return self.arrived.at[way, pl.ds((self.ring.far - 1) * rows, rows // 2)]
        return self.arrived.at[way, pl.ds((hop - 1) * rows, rows)]

    def copy(self, way, hop):
        rows = self.held.shape[2]
        size = rows // 2 if hop == 0 else rows
        at = way * self.ring.far + hop
        return pltpu.make_async_remote_copy(
            self.held.at[way, hop % 2, pl.ds(0, size)], self.landing(way, hop),
            self.send.at[at], self.recv.at[at],
            device_id=self.ring.target(way), device_id_type=MESH,
        )

    def owner(self, way, hop):
        distance = self.ring.far - hop
        return self.ring.member(distance if way == 0 else -distance)

    def start(self, hop, term):
        rows = self.held.shape[2]
        half = rows // 2
        if hop == 0:
            value = term(self.owner(0, 0), 0).astype(bf16)
            self.held[0, 0, 0:half] = value[:half]
            self.copy(0, 0).start()
            self.held[1, 0, 0:half] = value[half:]
            self.copy(1, 0).start()
            return
        for way in (0, 1):
            value = term(self.owner(way, hop), way)
            self.copy(way, hop - 1).wait_recv()
            slot = hop % 2
            if hop >= 2:
                self.copy(way, hop - 2).wait_send()
            if hop == 1:
                low = slice(way * half, (way + 1) * half)
                rest = slice((1 - way) * half, (2 - way) * half)
                self.held[way, slot, low] = (
                    value[low] + self.landing(way, 0)[...].astype(f32)
                ).astype(bf16)
                self.held[way, slot, rest] = value[rest].astype(bf16)
            else:
                self.held[way, slot] = (
                    value + self.landing(way, hop - 1)[...].astype(f32)
                ).astype(bf16)
            self.copy(way, hop).start()

    def finish(self, term):
        last = self.ring.far - 1
        value = term(self.ring.me, 0)
        for way in (0, 1):
            self.copy(way, last).wait_recv()
            value = value + self.landing(way, last)[...].astype(f32)
        for hop in range(last - 1, last + 1):
            for way in (0, 1):
                self.copy(way, hop).wait_send()
        return value


def any_specs(count):
    return [pl.BlockSpec(memory_space=pl.ANY)] * count


def tokens_exchange(own, whole, send, recv, base):
    f = lax.axis_index("fsdp")
    rows = whole.shape[0] // 4

    def one(at, source, owner, k):
        return pltpu.make_async_remote_copy(
            source, row_slice(whole, owner * rows, rows), send.at[base + at], recv.at[base + at],
            device_id={"fsdp": partner(k)}, device_id_type=MESH,
        )

    far = partner(2)
    return (
        one(0, own, f, 2), one(1, own, f, 1), one(2, row_slice(whole, far * rows, rows), far, 1),
    )


def forward_kernel(
    tokens_ref, cotangent_hbm, in_ref, out_ref, turn_ref, vectors_ref, active_ref, block_ref,
    small_all, x_all, gate_all, out_all, cotangent_all, normed_t_all, x_part_all, states_all,
    gated_all, gated_t_all, y_grad_all, gate_grad_all,
    consts_ref, head_ref, shared_taps_ref, columns_ref, rows_ref, column_ref, keys_ref, queries_ref, queries_t_ref,
    shared_part_ref, shared_pre_ref, gain_grad_ref,
    small_cut, x_cut, gate_cut, out_low, normed, cotangent, small_weight, keys_t, shared_all,
    x_part, states, y, gate_part, gated_grad, weight, out_tile, turned, squares, products, stats, stats_in,
    back_tiles, back_tiles_t, padded, state, shared_wide,
    local_sem, swap_send, swap_recv, token_send, token_recv, ring_send, ring_recv,
    shared_send, shared_recv, stats_send, stats_recv, load_sem, store_sem,
):
    ring = Ring()
    d, f = ring.me, lax.axis_index("fsdp")
    tokens, length = tokens_ref.shape[0], normed.shape[0]
    sub, rows_out = in_ref.shape[0], out_ref.shape[0]
    width = x_cut.shape[2]
    groups, chunks = width // LANES, length // SPAN
    heads, shared = HEADS // 4, shared_taps_ref.shape[0]
    precise = partial(jnp.dot, precision=highest, preferred_element_type=f32)
    greet([{"fsdp": partner(k)} for k in (1, 2, 3)] + [ring.target(0), ring.target(1)])
    wholes = [small_all, x_all, gate_all, out_all]
    small_part, x_of, gate_of, out_of = range(4)
    rings = RingGather(ring, wholes, ring_send, ring_recv)
    cuts = [small_cut, x_cut, gate_cut]

    def own_copy(part):
        if part == out_of:
            source, target = out_low, row_slice(out_all, d * rows_out, rows_out)
        else:
            source = cuts[part].at[f]
            target = row_slice(wholes[part], (4 * d + f) * sub, sub)
        return pltpu.make_async_copy(source, target, local_sem.at[part])

    def swap(part, k):
        return pltpu.make_async_remote_copy(
            cuts[part].at[partner(k)], row_slice(wholes[part], (4 * d + f) * sub, sub),
            swap_send.at[3 * part + k - 1], swap_recv.at[3 * part + k - 1],
            device_id={"fsdp": partner(k)}, device_id_type=MESH,
        )

    def start_swaps(part):
        for k in (2, 3, 1):
            swap(part, k).start()
        own_copy(part).start()

    def start_ring(part):
        own_copy(part).wait()
        if part != out_of:
            for k in (1, 2, 3):
                swap(part, k).wait_recv()
        rings.start(part, 0)

    def cut_channels(target, low):
        for pair in range(INNER // PAIR):
            member, at = pair % 4, pair // 4
            target[member, :, at * PAIR : (at + 1) * PAIR] = in_ref[
                :, low + pair * PAIR : low + (pair + 1) * PAIR
            ].astype(bf16)

    out_low[...] = out_ref[...].astype(bf16)
    own_copy(out_of).start()
    pieces = dot_lanes(in_ref[:, 2 * INNER :].astype(bf16), turn_ref[...]).astype(bf16)
    for member in range(4):
        small_cut[member] = pieces[:, member * PAIR : (member + 1) * PAIR]
    start_swaps(small_part)
    cut_channels(x_cut, INNER)
    start_swaps(x_of)
    start_ring(out_of)
    inputs = tokens_ref[...].astype(f32)
    inverse = lax.rsqrt(jnp.sum(inputs * inputs, axis=1, keepdims=True) / D + norm_eps)
    own_rows = pl.ds(pl.multiple_of(f * tokens, tokens), tokens)
    normed[own_rows, :] = (inputs * inverse * norm_gain_row(vectors_ref)).astype(bf16)
    normed_copies = tokens_exchange(normed.at[own_rows], normed, token_send, token_recv, 0)
    cotangent_copies = tokens_exchange(
        cotangent_hbm, cotangent, token_send, token_recv, 3
    )
    cotangent_own = pltpu.make_async_copy(cotangent_hbm, cotangent.at[own_rows], local_sem.at[4])
    cotangent_own.start()
    for copy in normed_copies[:2]:
        copy.start()
    start_ring(small_part)
    start_ring(x_of)
    cut_channels(gate_cut, 0)
    start_swaps(gate_of)

    def vector_row(row):
        return vectors_ref[pl.ds(row, 1), :]

    def own_channels(first_row):
        return jnp.concatenate(
            [vector_row(first_row + 4 * pair + f) for pair in range(width // PAIR)], axis=1
        )

    active = active_ref[0:1, 0:1]
    for k in range(CONV + 1):
        consts_ref[k : k + 1, :] = own_channels(TAPS_ROW + k * (XBC // PAIR))
    channel_head = lax.broadcasted_iota(jnp.int32, (1, width), 1) // HEAD_DIM
    consts_ref[MASK_ROW : MASK_ROW + 1, :] = (channel_head.astype(f32) < active / 4).astype(f32)
    consts_ref[GAIN_ROW : GAIN_ROW + 1, :] = own_channels(D // PAIR)
    head_at = lax.broadcasted_iota(jnp.int32, (PAIR, PAIR), 0)
    local_at = lax.broadcasted_iota(jnp.int32, (PAIR, PAIR), 1)
    own_head = local_at // 2 * 8 + 2 * f + local_at % 2
    chosen = (head_at == own_head) & (local_at < heads)
    chosen_far = (head_at == own_head + HEADS) & (local_at < heads)
    last = vector_row(LAST_ROW)
    step_bias_row = precise(last, chosen.astype(f32))
    is_head = lax.broadcasted_iota(jnp.int32, (1, PAIR), 1) < heads
    decay_row = jnp.where(is_head, -jnp.exp(precise(last, chosen_far.astype(f32))), 0.0)
    head_mask_row = (
        lax.broadcasted_iota(jnp.int32, (1, PAIR), 1).astype(f32) < active / 4
    ).astype(f32)
    skip_row = precise(vector_row(LAST_ROW + 1), chosen.astype(f32))
    spread_head = (
        lax.broadcasted_iota(jnp.int32, (PAIR, width), 0)
        == lax.broadcasted_iota(jnp.int32, (PAIR, width), 1) // HEAD_DIM
    ).astype(f32)
    consts_ref[SKIP_ROW : SKIP_ROW + 1, :] = precise(skip_row, spread_head)
    head_ref[...] = jnp.concatenate(
        [decay_row, head_mask_row, step_bias_row, jnp.zeros((5, PAIR), f32)], axis=0
    )
    shared_rows = [
        vector_row(TAPS_ROW + k * (XBC // PAIR) + INNER // PAIR + f // 2) for k in range(CONV + 1)
    ]
    shared_wide[...] = jnp.concatenate(
        shared_rows + [jnp.zeros((PAIR - CONV - 1, PAIR), f32)], axis=0
    ).T
    shared_taps_ref[...] = shared_wide[pl.ds(pl.multiple_of(f % 2 * shared, shared), shared), :]
    rings.start(small_part, 1)
    rings.start(small_part, 2)
    rings.start(x_of, 1)
    rings.start(out_of, 1)
    for hop in range(3, ring.far):
        rings.start(small_part, hop)
    normed_copies[0].wait_recv()
    normed_copies[2].start()
    for copy in cotangent_copies[:2]:
        copy.start()
    rings.finish(small_part)
    load_small = pltpu.make_async_copy(small_all, small_weight, local_sem.at[5])
    load_small.start()
    for copy in normed_copies[1:]:
        copy.wait_recv()
    load_small.wait()

    small = dot_rows(normed[...], small_weight[...]).T
    part = small[0:shared]
    pre = shared_taps_ref[:, CONV : CONV + 1] + jnp.zeros_like(part)
    for k in range(CONV):
        pre = pre + shared_taps_ref[:, k : k + 1] * shifted(part, CONV - 1 - k)
    shared_part_ref[...] = part
    shared_pre_ref[...] = pre
    shared_all[f] = (pre * jax.nn.sigmoid(pre)).astype(bf16)

    def shared_copy(k):
        return pltpu.make_async_remote_copy(
            shared_all.at[f], shared_all.at[f], shared_send.at[k - 1], shared_recv.at[k - 1],
            device_id={"fsdp": partner(k)}, device_id_type=MESH,
        )

    for k in (2, 3, 1):
        shared_copy(k).start()
    rings.start(x_of, 2)
    rings.start(out_of, 2)
    head_columns = jnp.concatenate(
        [head_ref[...], jnp.zeros((PAIR - 8, PAIR), f32)], axis=0
    ).T[0:heads]
    decay, head_mask, step_bias = (head_columns[:, i : i + 1] for i in range(3))
    logits = small[shared : shared + heads] * head_mask + step_bias
    steps = jnp.maximum(logits, 0.0) + jnp.log1p(jnp.exp(-jnp.abs(logits)))
    at_row = lax.broadcasted_iota(jnp.int32, (SPAN, SPAN), 0)
    at_lane = lax.broadcasted_iota(jnp.int32, (SPAN, SPAN), 1)
    upto = (at_row <= at_lane).astype(f32)
    rates = steps * decay
    log_sums = jnp.concatenate(
        [
            jnp.dot(
                rates[:, c * SPAN : (c + 1) * SPAN], upto, precision=highest,
                preferred_element_type=f32,
            )
            for c in range(chunks)
        ],
        axis=1,
    )
    column = jnp.concatenate(
        [log_sums, steps, logits, jnp.zeros((PAIR - 3 * heads, length), f32)], axis=0
    ).T
    column_ref[...] = column
    for group in range(groups):
        rolled = column if group == 0 else pltpu.roll(column, PAIR - group * GROUP, 1)
        columns_ref[:, group * PAIR : (group + 1) * PAIR] = rolled
        rows_ref[group * 8 : group * 8 + 8, :] = jnp.zeros((8, length), f32)
        rows_ref[group * 8 : group * 8 + GROUP, :] = log_sums[group * GROUP : (group + 1) * GROUP]
    for k in (1, 2, 3):
        shared_copy(k).wait_recv()
    keys_t[0:shared, :] = shared_all[0]
    keys_t[shared:, :] = shared_all[1]
    queries_t_ref[0:shared, :] = shared_all[2]
    queries_t_ref[shared:, :] = shared_all[3]
    keys_ref[...] = keys_t[...].T
    queries_ref[...] = queries_t_ref[...].T
    for hop in range(3, ring.far):
        rings.start(x_of, hop)
        rings.start(out_of, hop)
    cotangent_copies[0].wait_recv()
    cotangent_copies[2].start()

    def store(source, target, slot):
        return pltpu.make_async_copy(source, target, store_sem.at[slot])

    quarter = D // 4

    def turned_store(i):
        return store(turned.at[i % 2], row_slice(normed_t_all, i * quarter, quarter), i)

    for i in range(4):
        if i >= 2:
            turned_store(i - 2).wait()
        turned[i % 2] = normed[:, i * quarter : (i + 1) * quarter].T
        turned_store(i).start()
    rings.finish(x_of)
    start_ring(gate_of)

    def lanes(group):
        return pl.ds(group * LANES, LANES)

    def load_columns(source, group):
        return pltpu.make_async_copy(
            source.at[:, lanes(group)], weight.at[group % 2], load_sem.at[group % 2]
        )

    def x_store(group):
        return store(x_part.at[group % 2], x_part_all.at[:, lanes(group)], 4 + group)

    def states_store(group):
        return store(states.at[group % 2], states_all.at[:, :, lanes(group)], 8 + group)

    load_columns(x_all, 0).start()
    for group in range(groups):
        if group + 1 < groups:
            load_columns(x_all, group + 1).start()
        load_columns(x_all, group).wait()
        if group >= 2:
            x_store(group - 2).wait()
            states_store(group - 2).wait()
        slot = group % 2
        x_part[slot] = dot_rows(normed[...], weight[slot])
        x_store(group).start()
        scan_forward_kernel(
            x_part.at[slot], consts_ref.at[:, lanes(group)],
            columns_ref.at[:, pl.ds(group * PAIR, PAIR)], rows_ref.at[pl.ds(group * 8, 8)],
            keys_ref, queries_ref, keys_t, block_ref, y.at[:, lanes(group)], states.at[slot],
            padded, state,
        )
        states_store(group).start()
        if group % 2 == 1 and group // 2 + 1 < ring.far - 1:
            rings.start(gate_of, group // 2 + 1)

    for copy in cotangent_copies[1:]:
        copy.wait_recv()
    cotangent_own.wait()
    cotangent_store = store(cotangent, cotangent_all, 12)
    cotangent_store.start()
    rings.finish(out_of)

    def load_rows(group):
        return pltpu.make_async_copy(
            out_all.at[lanes(group)], out_tile.at[group % 2], load_sem.at[2 + group % 2]
        )

    load_rows(0).start()
    for group in range(groups):
        if group + 1 < groups:
            load_rows(group + 1).start()
        load_rows(group).wait()
        gated_grad[:, lanes(group)] = dot_lanes(cotangent[...], out_tile[group % 2])
    rings.start(gate_of, ring.far - 1)
    rings.finish(gate_of)

    def const_row(row, here):
        return consts_ref[row : row + 1, here]

    load_columns(gate_all, 0).start()
    for group in range(groups):
        if group + 1 < groups:
            load_columns(gate_all, group + 1).start()
        load_columns(gate_all, group).wait()
        here = lanes(group)
        value = dot_rows(normed[...], weight[group % 2]) * const_row(MASK_ROW, here)
        gate_part[:, here] = value
        gated = y[:, here] * (value * jax.nn.sigmoid(value))
        product = gated * (gated_grad[:, here] * const_row(GAIN_ROW, here))
        gated = gated * gated
        gated = gated[:, :PAIR] + gated[:, PAIR:]
        product = product[:, :PAIR] + product[:, PAIR:]
        squares[...] = gated if group == 0 else squares[...] + gated
        products[...] = product if group == 0 else products[...] + product
    lane = lax.broadcasted_iota(jnp.int32, (length, PAIR), 1)
    both = jnp.where(
        lane == 0,
        jnp.sum(squares[...], axis=1, keepdims=True),
        jnp.where(lane == 1, jnp.sum(products[...], axis=1, keepdims=True), 0.0),
    )
    stats[...] = both.T[0:8]

    def stats_copy(k):
        return pltpu.make_async_remote_copy(
            stats, stats_in.at[k - 1], stats_send.at[k - 1], stats_recv.at[k - 1],
            device_id={"fsdp": partner(k)}, device_id_type=MESH,
        )

    for k in (2, 3, 1):
        stats_copy(k).start()
    for k in (1, 2, 3):
        stats_copy(k).wait_recv()
    total = (stats[...] + stats_in[0]) + (stats_in[1] + stats_in[2])
    channel_count = active * HEAD_DIM
    inverse_out = lax.rsqrt(total[0:1] / channel_count + norm_eps)
    pulls = inverse_out * inverse_out * inverse_out / channel_count * total[1:2]
    scales = jnp.concatenate(
        [inverse_out, pulls, jnp.zeros((PAIR - 2, length), f32)], axis=0
    ).T
    inverse_out, pulls = scales[:, 0:1], scales[:, 1:2]

    def back_stores(group):
        slot, at, here = group % 2, 13 + 4 * group, lanes(group)
        return [
            store(back_tiles.at[slot, 0], gated_all.at[:, here], at),
            store(back_tiles.at[slot, 1], y_grad_all.at[:, here], at + 1),
            store(back_tiles.at[slot, 2], gate_grad_all.at[:, here], at + 2),
            store(back_tiles_t.at[slot], gated_t_all.at[here], at + 3),
        ]

    gain_grad_ref[...] = jnp.zeros_like(gain_grad_ref)
    for group in range(groups):
        here, slot = lanes(group), group % 2
        if group >= 2:
            for copy in back_stores(group - 2):
                copy.wait()
        value, grad, gain = gate_part[:, here], gated_grad[:, here], const_row(GAIN_ROW, here)
        gate = jax.nn.sigmoid(value)
        silu = value * gate
        y_here = y[:, here]
        gated = y_here * silu
        scaled = gated * inverse_out
        gated_low = (scaled * gain).astype(bf16)
        back_tiles[slot, 0] = gated_low
        back_tiles_t[slot] = gated_low.T
        gain_grad_ref[0:1, here] = jnp.sum(grad * scaled, axis=0, keepdims=True)
        back = inverse_out * (grad * gain) - gated * pulls
        back_tiles[slot, 1] = (back * silu).astype(bf16)
        back_tiles[slot, 2] = (
            back * y_here * (gate * (1.0 + value * (1.0 - gate))) * const_row(MASK_ROW, here)
        ).astype(bf16)
        for copy in back_stores(group):
            copy.start()

    for i in (2, 3):
        turned_store(i).wait()
    for group in range(groups - 2, groups):
        x_store(group).wait()
        states_store(group).wait()
        for copy in back_stores(group):
            copy.wait()
    cotangent_store.wait()
    for copy in normed_copies + cotangent_copies:
        copy.wait_send()
    for k in (1, 2, 3):
        shared_copy(k).wait_send()
        stats_copy(k).wait_send()
        for i in (small_part, x_of, gate_of):
            swap(i, k).wait_send()


def last_columns(members):
    shared = 2 * STATE // members
    source = np.arange(2 * STATE + HEADS)
    head = source - 2 * STATE
    target = np.where(
        source < 2 * STATE,
        source // shared * PAIR + source % shared,
        head // 2 % members * PAIR + shared + head // (2 * members) * 2 + head % 2,
    )
    turn = np.arange(members * PAIR)[:, None] == target[None, :]
    return jnp.asarray(turn.astype(np.float32), bf16)


def norm_gain_row(vectors_ref):
    return jnp.concatenate([vectors_ref[i : i + 1, :] for i in range(D // PAIR)], axis=1)


def vector_tiles(vectors):
    rows = -(-vectors.shape[0] // PAIR)
    return jnp.pad(vectors, (0, rows * PAIR - vectors.shape[0])).reshape(rows, PAIR)


def forward(
    tokens, cotangent, in_weight, out_weight, vectors, active,
):
    count, members = lax.axis_size("dp"), lax.axis_size("fsdp")
    own, sub, rows_out = tokens.shape[0], in_weight.shape[0], out_weight.shape[0]
    length, inner, shared = own * members, INNER // members, 2 * STATE // members
    chunks, groups = length // SPAN, inner // LANES
    assert groups == 4 and count == 8 and members == 4
    turn = last_columns(members)
    sd, dma = jax.ShapeDtypeStruct, pltpu.SemaphoreType.DMA
    vmem = pltpu.VMEM
    return pl.pallas_call(
        forward_kernel,
        in_specs=[whole_spec()] + any_specs(1) + [whole_spec()] * 6,
        out_specs=any_specs(12) + [whole_spec()] * 12,
        out_shape=[
            sd((D, PAIR), bf16),
            sd((D, inner), bf16),
            sd((D, inner), bf16),
            sd((inner, D), bf16),
            sd((length, D), bf16),
            sd((D, length), bf16),
            sd((length, inner), f32),
            sd((chunks, STATE, inner), bf16),
            sd((length, inner), bf16),
            sd((inner, length), bf16),
            sd((length, inner), bf16),
            sd((length, inner), bf16),
            sd((8, inner), f32),
            sd((8, PAIR), f32),
            sd((shared, PAIR), f32),
            sd((length, groups * PAIR), f32),
            sd((groups * 8, length), f32),
            sd((length, PAIR), f32),
            sd((length, STATE), bf16),
            sd((length, STATE), bf16),
            sd((STATE, length), bf16),
            sd((shared, length), f32),
            sd((shared, length), f32),
            sd((8, inner), f32),
        ],
        scratch_shapes=[
            vmem((members, sub, PAIR), bf16),
            vmem((members, sub, inner), bf16),
            vmem((members, sub, inner), bf16),
            vmem((rows_out, D), bf16),
            vmem((length, D), bf16),
            vmem((length, D), bf16),
            vmem((D, PAIR), bf16),
            vmem((STATE, length), bf16),
            vmem((members, shared, length), bf16),
            vmem((2, length, LANES), f32),
            vmem((2, chunks, STATE, LANES), bf16),
            vmem((length, inner), f32),
            vmem((length, inner), f32),
            vmem((length, inner), f32),
            vmem((2, D, LANES), bf16),
            vmem((2, LANES, D), bf16),
            vmem((2, D // 4, length), bf16),
            vmem((length, PAIR), f32),
            vmem((length, PAIR), f32),
            vmem((8, length), f32),
            vmem((3, 8, length), f32),
            vmem((2, 3, length, LANES), bf16),
            vmem((2, LANES, length), bf16),
            vmem((length + 8, LANES), f32),
            vmem((STATE, LANES), f32),
            vmem((PAIR, PAIR), f32),
            dma((6,)),
            dma((9,)),
            dma((9,)),
            dma((6,)),
            dma((6,)),
            RingGather.semaphores(4, count),
            RingGather.semaphores(4, count),
            dma((3,)),
            dma((3,)),
            dma((3,)),
            dma((3,)),
            dma((4,)),
            dma((13 + 4 * groups,)),
        ],
        compiler_params=pltpu.CompilerParams(
            collective_id=0, has_side_effects=True, vmem_limit_bytes=VMEM_BYTES
        ),
        name="forward",
    )(
        tokens, cotangent, in_weight, out_weight, turn, vectors,
        jnp.broadcast_to(active.astype(f32), (8, PAIR)), block_mask(),
    )


def total_squares(value):
    return jnp.sum(jnp.sum(value * value, axis=0, keepdims=True), axis=1, keepdims=True)


def flipped(member, flip):
    return member + flip - 2 * flip * lax.rem(lax.div(member, flip), 2)


def shifted(value, by):
    length = value.shape[1]
    lane = lax.broadcasted_iota(jnp.int32, value.shape, 1)
    if by == 0:
        return value
    if by > 0:
        return jnp.where(lane >= by, pltpu.roll(value, by, 1), 0.0)
    return jnp.where(lane < length + by, pltpu.roll(value, length + by, 1), 0.0)


def backward_kernel(
    rows_ref, key_ref, query_ref, query_t_ref, block_ref, pick_ref, consts_ref, column_ref, heads_ref,
    head_pick_ref, shared_part_ref, shared_pre_ref, taps_ref, vectors_own_ref, gate_gain_ref,
    weight_small_ref,
    tokens_hbm, x_hbm, y_grad_hbm, states_hbm, columns_hbm, gated_hbm, gated_t_hbm, gate_grad_hbm, normed_t_hbm,
    cotangents_hbm, cotangent_hbm, weight_out_hbm, weight_gate_hbm, weight_x_hbm,
    layer_out_hbm, token_grad_hbm, gate_back, x_back, small_back,
    out_raw_ref, vectors_ref, total_ref,
    x_part, y_grad, states, columns, padded, following, state_back, inner_grad,
    x_grad, key_grad, query_grad, sums_ref, rest_ref, channel_ref,
    normed_t, gate_grad, gated_t, cotangent, wide,
    kept, near_out, near_in,
    shared_out, shared_in, raw, small_t, small_n,
    vector_sum, vector_in, gate_out, x_out, small_out, scalar_out, scalar_in,
    first_held, first_arrived, gate_held, gate_arrived, small_held, small_arrived,
    load_sem, scan_sem, chunk_sem, store_sem, local_sem,
    near_send, near_recv, swap_send, swap_recv, vector_send, vector_recv, return_send, return_recv,
    scalar_send, scalar_recv, ring_send, ring_recv, ring_free, near_free,
):
    ring = Ring()
    d, f, count, far = ring.me, lax.axis_index("fsdp"), ring.count, ring.far
    length, width = x_grad.shape
    groups, chunks = width // LANES, length // SPAN
    rows, rows_out, tokens = D // count, width // count, tokens_hbm.shape[0]
    sub, shared, heads = gate_back.shape[1], shared_part_ref.shape[0], HEADS // 4
    precise = partial(jnp.dot, precision=highest, preferred_element_type=f32)
    out_ring, gate_ring, x_ring, small_ring = (
        RingScatter(ring, held, arrived, ring_send.at[i], ring_recv.at[i])
        for i, (held, arrived) in enumerate(
            [
                (first_held, first_arrived),
                (gate_held, gate_arrived),
                (first_held, first_arrived),
                (small_held, small_arrived),
            ]
        )
    )

    def load(source, target, at):
        return pltpu.make_async_copy(source, target, load_sem.at[at])

    def lanes(group):
        return pl.ds(group * LANES, LANES)

    def scan_loads(group):
        slot = group % 2
        return [
            pltpu.make_async_copy(source, target, scan_sem.at[slot, i])
            for i, (source, target) in enumerate(
                [
                    (y_grad_hbm.at[:, lanes(group)], y_grad.at[slot]),
                    (states_hbm.at[:, :, lanes(group)], states.at[slot]),
                    (columns_hbm.at[:, pl.ds(group * PAIR, PAIR)], columns.at[slot]),
                ]
            )
        ]

    def x_load(group):
        return pltpu.make_async_copy(x_hbm.at[:, lanes(group)], x_part, scan_sem.at[2, 0])

    def chunk_load(owner, slot):
        return pltpu.make_async_copy(
            row_slice(gated_t_hbm, owner * rows_out, rows_out), gated_t.at[slot],
            chunk_sem.at[slot],
        )

    def hop_loads(hop):
        if hop == far:
            return [chunk_load(d, 2 * (hop % 2))]
        ways = (0,) if hop == 0 else (0, 1)
        return [chunk_load(out_ring.owner(way, hop), 2 * (hop % 2) + way) for way in ways]

    gated_blocks = [x_out, gate_out]

    def gated_load(i, flip):
        return load(
            row_slice(gated_hbm, partner(flip) * tokens, tokens), gated_blocks[i], 4 + i
        )

    cotangent_load = load(cotangents_hbm, cotangent, 0)
    normed_load = load(normed_t_hbm, normed_t, 1)
    gate_grad_load = load(gate_grad_hbm, gate_grad, 2)
    out_load = load(weight_out_hbm, wide, 3)
    for copy in hop_loads(0) + [cotangent_load, normed_load, gate_grad_load, out_load]:
        copy.start()
    gated_load(0, 3).start()
    gated_load(1, 1).start()
    x_load(0).start()
    for copy in scan_loads(0):
        copy.start()
    greet(
        [{"fsdp": partner(k)} for k in (1, 2, 3)]
        + [{"dp": lax.rem(d + k, count)} for k in range(1, count)]
    )

    def rows_of(owner):
        return pl.ds(pl.multiple_of(owner * rows, rows), rows)

    def out_term(hop):
        def term(owner, way):
            value = dot_rows(gated_t[2 * (hop % 2) + way], cotangent[...])
            return jnp.concatenate([value[:, :width], value[:, width:]], axis=0)

        return term

    def out_hop(hop):
        for copy in hop_loads(hop):
            copy.wait()
        out_ring.start(hop, out_term(hop))
        for copy in hop_loads(hop + 1):
            copy.start()

    def gate_term(owner, way):
        return dot_rows(normed_t[rows_of(owner), :], gate_grad[...])

    def x_term(owner, way):
        return dot_rows(normed_t[rows_of(owner), :], x_grad[...])

    def small_term(owner, way):
        return dot_lanes(normed_t[rows_of(owner), :], small_t[...])

    def to_partner(k, source, target, send, recv, at):
        return pltpu.make_async_remote_copy(
            source, target, send.at[at], recv.at[at],
            device_id={"fsdp": partner(k)}, device_id_type=MESH,
        )

    def near_copy(use, i):
        return to_partner(
            2 if i == 2 else 1, near_out.at[i], near_in.at[i], near_send, near_recv, 3 * use + i
        )

    def scan(group):
        slot = group % 2
        x_load(group).wait()
        for copy in scan_loads(group):
            copy.wait()
        if group + 1 < groups:
            for copy in scan_loads(group + 1):
                copy.start()
        here = lanes(group)
        scan_backward_group(
            x_part, consts_ref.at[:, here], columns.at[slot], rows_ref.at[pl.ds(group * 8, 8)],
            key_ref, query_ref, query_t_ref, block_ref, pick_ref.at[pl.ds(3 * group, 3)],
            y_grad.at[slot], states.at[slot],
            x_grad.at[:, here], key_grad, query_grad, sums_ref, rest_ref.at[:, :, here],
            channel_ref.at[:, here], padded, following, state_back, inner_grad,
        )
        if group + 1 < groups:
            x_load(group + 1).start()

    scan_backward_start(key_grad, query_grad, sums_ref, inner_grad)
    cotangent_load.wait()
    out_hop(0)
    normed_load.wait()
    gate_grad_load.wait()
    gate_ring.start(0, gate_term)

    def added_block(i):
        return dot_rows(gated_blocks[i][...], wide[...])

    out_load.wait()
    for i, flip in ((0, 3), (1, 1)):
        gated_load(i, flip).wait()
        near_out[1 - i] = added_block(i).astype(bf16)
        near_copy(0, 1 - i).start()
        gated_load(i, (2, 0)[i]).start()
    scan(0)
    out_hop(1)
    gated_load(0, 2).wait()
    value = added_block(0)
    near_copy(0, 1).wait_recv()
    near_out[2] = (value + near_in[1].astype(f32)).astype(bf16)
    near_copy(0, 2).start()
    gated_load(1, 0).wait()
    kept[...] = added_block(1)
    half = D // 4

    def weight_tiles(source, target, at):
        return [
            load(
                source.at[pl.ds(i * half, half)],
                target.at[pl.ds(i // 2 * half, half), pl.ds(i % 2 * width, width)], at + i,
            )
            for i in range(4)
        ]

    gate_tiles = weight_tiles(weight_gate_hbm, wide, 6)
    for copy in gate_tiles:
        copy.start()
    scan(1)
    gate_ring.start(1, gate_term)
    scan(2)
    out_hop(2)
    scan(3)
    scan_backward_finish(key_ref, query_ref, key_grad, query_grad, inner_grad)

    for i, ref in ((0, key_grad), (2, query_grad)):
        across = ref[...].T
        for j in (0, 1):
            shared_out[i + j] = across[j * shared : (j + 1) * shared].astype(bf16)

    def shared_copy(k):
        return to_partner(
            k, shared_out.at[partner(k)], shared_in.at[k - 1], swap_send, swap_recv, k - 1
        )

    for k in (2, 3, 1):
        shared_copy(k).start()
    for hop in range(3, far):
        out_hop(hop)
    gate_ring.start(2, gate_term)

    at_row = lax.broadcasted_iota(jnp.int32, (SPAN, SPAN), 0)
    at_lane = lax.broadcasted_iota(jnp.int32, (SPAN, SPAN), 1)
    later = (at_lane >= at_row).astype(f32)
    earlier = (at_lane < at_row).astype(f32)
    rest = precise(
        jnp.concatenate([rest_ref[c] for c in range(chunks)], axis=0), head_pick_ref[...]
    )
    decay, head_mask = heads_ref[0:1, :], heads_ref[1:2, :]
    step_bias_grad = jnp.zeros((1, PAIR), f32)
    decay_grad = jnp.zeros((1, PAIR), f32)
    for c in range(chunks):
        here = slice(c * SPAN, (c + 1) * SPAN)
        sums = sums_ref[here, :]
        log_grad = (
            precise(later, sums)
            + pltpu.roll(precise(earlier, sums), PAIR - heads, 1)
            + rest[c : c + 1]
        )
        steps = pltpu.roll(column_ref[here, :], PAIR - heads, 1)
        logits = pltpu.roll(column_ref[here, :], PAIR - 2 * heads, 1)
        raw_grad = (decay * log_grad + pltpu.roll(sums, PAIR - 2 * heads, 1)) * jax.nn.sigmoid(
            logits
        )
        step_bias_grad = step_bias_grad + jnp.sum(raw_grad, axis=0, keepdims=True)
        decay_grad = decay_grad + jnp.sum(steps * log_grad, axis=0, keepdims=True)
        raw[here, :] = raw_grad * head_mask
    decay_grad = decay_grad * decay

    for k in (2, 3, 1):
        shared_copy(k).wait_recv()
    part, pre = shared_part_ref[...], shared_pre_ref[...]
    gate = jax.nn.sigmoid(pre)
    pre_grad = shared_out[f].astype(f32)
    for k in (1, 2, 3):
        pre_grad = pre_grad + shared_in[k - 1].astype(f32)
    pre_grad = pre_grad * (gate * (1.0 + pre * (1.0 - gate)))
    shared_grad = jnp.zeros_like(pre_grad)
    lane = lax.broadcasted_iota(jnp.int32, (shared, PAIR), 1)
    shared_sums = jnp.where(lane == CONV, jnp.sum(pre_grad, axis=1, keepdims=True), 0.0)
    for k in range(CONV):
        shift = CONV - 1 - k
        shared_grad = shared_grad + taps_ref[:, k : k + 1] * shifted(pre_grad, -shift)
        shared_sums = shared_sums + jnp.where(
            lane == k, jnp.sum(pre_grad * shifted(part, shift), axis=1, keepdims=True), 0.0
        )
    small_t[0:shared, :] = shared_grad.astype(bf16)
    small_t[shared:, :] = raw[...].T[0 : PAIR - shared].astype(bf16)
    small_n[...] = small_t[...].T
    small_ring.start(0, small_term)

    near_copy(0, 0).wait_send()
    tokens_load = load(tokens_hbm, near_out.at[0], 15)
    tokens_load.start()
    near_copy(0, 0).wait_recv()
    near_copy(0, 2).wait_recv()
    tokens_load.wait()
    value = near_out[0].astype(f32) + (
        (kept[...] + near_in[0].astype(f32)) + near_in[2].astype(f32)
    )
    for k in (0, 1):
        pl.semaphore_signal(
            near_free.at[k], inc=1, device_id={"fsdp": partner(k + 1)}, device_id_type=MESH
        )
    for i in (1, 2):
        near_copy(0, i).wait_send()
    near_out[2] = value.astype(bf16)
    layer_store = pltpu.make_async_copy(near_out.at[2], layer_out_hbm, store_sem.at[0])
    layer_store.start()

    for copy in hop_loads(far):
        copy.wait()
    value = out_ring.finish(out_term(far))
    out_raw_ref[...] = jnp.concatenate([value[:rows_out], value[rows_out:]], axis=1)
    squares = total_squares(value)
    for way in (0, 1):
        pl.semaphore_signal(
            ring_free.at[way], inc=1, device_id=ring.target(1 - way), device_id_type=MESH
        )
    x_tiles = weight_tiles(weight_x_hbm, cotangent, 10)
    for copy in x_tiles:
        copy.start()
    for way in (0, 1):
        pl.semaphore_wait(ring_free.at[way], 1)
    x_ring.start(0, x_term)
    for hop in range(3, far):
        gate_ring.start(hop, gate_term)

    for copy in gate_tiles + x_tiles:
        copy.wait()

    def back_block(flip, target, kind):
        here = pl.ds(pl.multiple_of(partner(flip) * tokens, tokens), tokens)
        for i in range(4):
            at = (slice(i // 2 * half, (i // 2 + 1) * half), slice(i % 2 * width, (i % 2 + 1) * width))
            value = (
                dot_lanes(gate_grad[here, :], wide[at])
                + dot_lanes(x_grad[here, :], cotangent[at])
                + dot_lanes(small_n[here, :], weight_small_ref[i * half : (i + 1) * half, :])
            )
            target[:, i * half : (i + 1) * half] = value.astype(kind)

    for k in (0, 1):
        pl.semaphore_wait(near_free.at[k], 1)
    for i, flip in ((1, 3), (0, 1)):
        back_block(flip, near_out.at[i], bf16)
        near_copy(1, i).start()
    small_ring.start(1, small_term)
    back_block(2, kept, f32)
    near_copy(1, 1).wait_recv()
    layer_store.wait()
    near_out[2] = (kept[...] + near_in[1].astype(f32)).astype(bf16)
    near_copy(1, 2).start()
    x_ring.start(1, x_term)
    back_block(0, kept, f32)
    near_copy(1, 1).wait_send()
    own_load = load(cotangent_hbm, near_out.at[1], 14)
    own_load.start()
    near_copy(1, 0).wait_send()
    tokens_load = load(tokens_hbm, near_out.at[0], 15)
    tokens_load.start()

    def return_copy(part, k):
        source = (gate_out, x_out, small_out)[part]
        target = (gate_back, x_back, small_back)[part]
        return to_partner(
            k, row_slice(source, partner(k) * sub, sub), target.at[f],
            return_send, return_recv, part * 3 + k - 1,
        )

    def own_copy(part):
        source = (gate_out, x_out, small_out)[part]
        target = (gate_back, x_back, small_back)[part]
        return pltpu.make_async_copy(
            row_slice(source, f * sub, sub), target.at[f], local_sem.at[part]
        )

    def give_back(part, value):
        (gate_out, x_out, small_out)[part][...] = value.astype(bf16)
        for k in (2, 3, 1):
            return_copy(part, k).start()
        own_copy(part).start()

    value = gate_ring.finish(gate_term)
    squares = squares + total_squares(value)
    give_back(0, value)
    small_ring.start(2, small_term)
    x_ring.start(2, x_term)
    near_copy(1, 0).wait_recv()
    near_copy(1, 2).wait_recv()
    own_load.wait()
    tokens_load.wait()
    inputs = near_out[0].astype(f32)
    inverse = lax.rsqrt(jnp.sum(inputs * inputs, axis=1, keepdims=True) / D + norm_eps)
    normed_grad = (kept[...] + near_in[0].astype(f32)) + near_in[2].astype(f32)
    pulled = normed_grad * norm_gain_row(vectors_own_ref)
    scaled = inputs * inverse
    input_grad = inverse * (
        pulled - scaled * (jnp.sum(pulled * scaled, axis=1, keepdims=True) / D)
    )
    near_out[1] = (near_out[1].astype(f32) + input_grad).astype(bf16)
    token_store = pltpu.make_async_copy(near_out.at[1], token_grad_hbm, store_sem.at[1])
    token_store.start()
    gain_grad = jnp.sum(normed_grad * scaled, axis=0, keepdims=True)

    vector_sum[...] = jnp.zeros_like(vector_sum)
    vector_sum[0:1, :] = gate_gain_ref[0:1, :]
    vector_sum[1 : CONV + 3, :] = channel_ref[0 : CONV + 2, :]
    for i in range(D // width):
        vector_sum[CONV + 3 + i : CONV + 4 + i, :] = gain_grad[:, i * width : (i + 1) * width]
    vector_sum[15:16, 0:PAIR] = step_bias_grad
    vector_sum[15:16, PAIR : 2 * PAIR] = decay_grad
    across = jnp.concatenate([shared_sums, jnp.zeros((PAIR - shared, PAIR), f32)], axis=0)
    vector_sum[16:24, 0:PAIR] = across.T[0:8]

    def vector_copy(step, flip):
        return pltpu.make_async_remote_copy(
            vector_in.at[step, 0], vector_in.at[step, 1], vector_send.at[step],
            vector_recv.at[step],
            device_id={"dp": flipped(d, flip)}, device_id_type=MESH,
        )

    flips = []
    while 1 << len(flips) < count:
        flips.append(1 << len(flips))
    for step, flip in enumerate(flips):
        vector_in[step, 0] = vector_sum[...]
        vector_copy(step, flip).start()
        if step == 0:
            for hop in range(3, far):
                small_ring.start(hop, small_term)
        if step == 1:
            for hop in range(3, far):
                x_ring.start(hop, x_term)
        vector_copy(step, flip).wait_recv()
        vector_sum[...] = vector_sum[...] + vector_in[step, 1]

    def vector_spread(k):
        return to_partner(
            k, vector_sum, vectors_ref.at[f], vector_send, vector_recv, len(flips) + k - 1
        )

    for k in (2, 3, 1):
        vector_spread(k).start()
    vectors_ref[f] = vector_sum[...]

    value = small_ring.finish(small_term)
    squares = squares + total_squares(value)
    give_back(2, value)
    value = x_ring.finish(x_term)
    give_back(1, value)
    squares = squares + total_squares(value)

    total = jnp.broadcast_to(squares, (8, PAIR))
    scalar_out[0] = total

    def near_scalar(k):
        return to_partner(
            k, scalar_out.at[0], scalar_in.at[k], scalar_send, scalar_recv, k
        )

    for k in (2, 3, 1):
        near_scalar(k).start()
    for k in (2, 3, 1):
        near_scalar(k).wait_recv()
    total = (total + scalar_in[1]) + (scalar_in[2] + scalar_in[3])
    scalar_out[1] = total

    def far_scalar(k):
        member = d
        for bit in flips:
            if k & bit:
                member = flipped(member, bit)
        return pltpu.make_async_remote_copy(
            scalar_out.at[1], scalar_in.at[3 + k], scalar_send.at[3 + k], scalar_recv.at[3 + k],
            device_id={"dp": member}, device_id_type=MESH,
        )

    for k in range(count - 1, 0, -1):
        far_scalar(k).start()
    parts = [total]
    for k in range(1, count):
        far_scalar(k).wait_recv()
        parts.append(scalar_in[3 + k])
    while len(parts) > 1:
        parts = [parts[i] + parts[i + 1] for i in range(0, len(parts), 2)]
    total_ref[...] = parts[0]

    for k in (1, 2, 3):
        vector_spread(k).wait_recv()
        vector_spread(k).wait_send()
        shared_copy(k).wait_send()
        near_scalar(k).wait_send()
        for i in range(3):
            return_copy(i, k).wait_recv()
            return_copy(i, k).wait_send()
    for k in range(1, count):
        far_scalar(k).wait_send()
    near_copy(1, 2).wait_send()
    for i in range(3):
        own_copy(i).wait()
    for step, flip in enumerate(flips):
        vector_copy(step, flip).wait_send()
    token_store.wait()


def backward(
    scan_inputs, queries_t, column, heads, shared_part, shared_pre, taps, vectors, gate_gain, tokens,
    weight_small, x, y_grad, states, gated, gated_t, gate_grad, normed_t, cotangents, cotangent,
    weight_out, weight_gate, weight_x,
):
    consts, columns, rows_t, keys, queries = scan_inputs
    length, width = x.shape
    chunks, groups = length // SPAN, width // LANES
    count, members = lax.axis_size("dp"), lax.axis_size("fsdp")
    rows, rows_out = D // count, width // count
    sub, own, shared = rows // members, tokens.shape[0], shared_part.shape[0]
    far = count // 2
    hops = max(count - 1, 1).bit_length()
    assert groups == 4 and count == 8 and members == 4 and 2 * rows_out == rows and 2 * width == D
    head_pick = jnp.asarray(
        (np.arange(width)[:, None] // HEAD_DIM == np.arange(PAIR)[None, :]).astype(np.float32)
    )
    dma, vmem, sd = pltpu.SemaphoreType.DMA, pltpu.VMEM, jax.ShapeDtypeStruct
    return pl.pallas_call(
        backward_kernel,
        in_specs=[whole_spec()] * 16 + any_specs(14),
        out_specs=any_specs(5) + [whole_spec()] * 3,
        out_shape=[
            sd((own, D), bf16),
            sd((own, D), bf16),
            sd((members, sub, width), bf16),
            sd((members, sub, width), bf16),
            sd((members, sub, PAIR), bf16),
            sd((rows_out, D), f32),
            sd((members, 24, width), f32),
            sd((8, PAIR), f32),
        ],
        scratch_shapes=[
            vmem((length, LANES), f32),
            vmem((2, length, LANES), bf16),
            vmem((2, chunks, STATE, LANES), bf16),
            vmem((2, length, PAIR), f32),
            vmem((length + 8, LANES), f32),
            vmem((8, LANES), f32),
            vmem((STATE, LANES), f32),
            vmem((chunks, SPAN, SPAN), f32),
            vmem((length, width), bf16),
            vmem((length, STATE), f32),
            vmem((length, STATE), f32),
            vmem((length, PAIR), f32),
            vmem((chunks, 1, width), f32),
            vmem((8, width), f32),
            vmem((D, length), bf16),
            vmem((length, width), bf16),
            vmem((4, rows_out, length), bf16),
            vmem((length, D), bf16),
            vmem((width, D), bf16),
            vmem((own, D), f32),
            vmem((3, own, D), bf16),
            vmem((3, own, D), bf16),
            vmem((members, shared, length), bf16),
            vmem((members - 1, shared, length), bf16),
            vmem((length, PAIR), f32),
            vmem((PAIR, length), bf16),
            vmem((length, PAIR), bf16),
            vmem((24, width), f32),
            vmem((hops, 2, 24, width), f32),
            vmem((rows, width), bf16),
            vmem((rows, width), bf16),
            vmem((rows, PAIR), bf16),
            vmem((2, 8, PAIR), f32),
            vmem((3 + count, 8, PAIR), f32),
        ]
        + RingScatter.scratch(count, rows, width) * 2
        + RingScatter.scratch(count, rows, PAIR)
        + [
            dma((16,)),
            dma((3, 3)),
            dma((4,)),
            dma((2,)),
            dma((3,)),
            dma((6,)),
            dma((6,)),
            dma((3,)),
            dma((3,)),
            dma((hops + 3,)),
            dma((hops + 3,)),
            dma((9,)),
            dma((9,)),
            dma((3 + count,)),
            dma((3 + count,)),
            dma((4, 2 * far)),
            dma((4, 2 * far)),
            pltpu.SemaphoreType.REGULAR((2,)),
            pltpu.SemaphoreType.REGULAR((2,)),
        ],
        compiler_params=pltpu.CompilerParams(
            collective_id=1, has_side_effects=True, vmem_limit_bytes=BACKWARD_VMEM_BYTES
        ),
        name="backward",
    )(
        rows_t, keys, queries, queries_t, block_mask(), pick_masks(groups), consts, column, heads,
        head_pick, shared_part, shared_pre, taps, vectors, gate_gain, weight_small,
        tokens, x, y_grad, states, columns, gated, gated_t, gate_grad, normed_t, cotangents, cotangent,
        weight_out, weight_gate, weight_x,
    )


OPTIMIZER_STEPS = 4


def optimizer_kernel(
    squares_ref, parts_ref, vector_ref, vector_first_ref, vector_second_ref, turn_ref,
    gate_ref, x_ref, small_ref, in_ref, in_first_ref, in_second_ref,
    out_raw_ref, out_ref, out_first_ref, out_second_ref,
    norm_ref, vector_grad_ref, vector_moment_ref, vector_square_ref, vector_master_ref,
    in_grad_ref, in_moment_ref, in_square_ref, in_master_ref, in_rounded_ref,
    out_grad_ref, out_moment_ref, out_square_ref, out_master_ref, out_rounded_ref,
    joined, factor_ref, in_raw,
):
    members = parts_ref.shape[0]
    pairs = INNER // PAIR
    shared, heads = 2 * STATE // members, HEADS // members

    @pl.when(pl.program_id(0) == 0)
    def _():
        joined[...] = jnp.zeros_like(joined)
        width = parts_ref.shape[2]
        for i in range(D // PAIR):
            row = CONV + 3 + i * PAIR // width
            lanes = slice(i * PAIR % width, i * PAIR % width + PAIR)
            value = parts_ref[0, row : row + 1, lanes]
            for member in range(1, members):
                value = value + parts_ref[member, row : row + 1, lanes]
            joined[i : i + 1, :] = value

        def put_channels(first_row, row):
            for pair in range(pairs):
                at = pair // members
                joined[first_row + pair : first_row + pair + 1, :] = parts_ref[
                    pair % members, row : row + 1, at * PAIR : (at + 1) * PAIR
                ]

        put_channels(D // PAIR, 0)
        each = PAIR // shared
        for k in range(CONV + 1):
            first_row = TAPS_ROW + k * (XBC // PAIR)
            put_channels(first_row, 1 + k)
            for i in range(members // each):
                joined[first_row + pairs + i : first_row + pairs + i + 1, :] = jnp.concatenate(
                    [
                        parts_ref[i * each + j, 16 + k : 17 + k, 0:shared]
                        for j in range(each)
                    ],
                    axis=1,
                )
        precise = partial(jnp.dot, precision=highest, preferred_element_type=f32)
        last, skips = jnp.zeros((1, PAIR), f32), jnp.zeros((1, PAIR), f32)
        local_at = lax.broadcasted_iota(jnp.int32, (PAIR, PAIR), 0)
        head_at = lax.broadcasted_iota(jnp.int32, (PAIR, PAIR), 1)
        channel_head = lax.broadcasted_iota(jnp.int32, (width, PAIR), 0) // HEAD_DIM
        wide_at = lax.broadcasted_iota(jnp.int32, (width, PAIR), 1)
        for member in range(members):
            home = local_at // 2 * 2 * members + 2 * member + local_at % 2
            known = local_at < heads
            biases = parts_ref[member, 15:16, 0:PAIR]
            decays = parts_ref[member, 15:16, PAIR : 2 * PAIR]
            last = last + precise(biases, ((head_at == home) & known).astype(f32))
            last = last + precise(decays, ((head_at == home + HEADS) & known).astype(f32))
            home = channel_head // 2 * 2 * members + 2 * member + channel_head % 2
            skips = skips + precise(
                parts_ref[member, CONV + 2 : CONV + 3, :], (wide_at == home).astype(f32)
            )
        joined[LAST_ROW : LAST_ROW + 1, :] = last
        joined[LAST_ROW + 1 : LAST_ROW + 2, :] = skips
        vector_raw = joined[...]
        norm = jnp.sqrt(squares_ref[...] + total_squares(vector_raw))
        norm_ref[...] = norm
        factor = jnp.minimum(1.0, clip_norm / (norm + 1e-06))
        factor_ref[...] = factor
        grad = vector_raw * factor[0:1, 0:1]
        vector_grad_ref[...] = grad
        vector_moment_ref[...], vector_square_ref[...], vector_master_ref[...] = adamw(
            vector_ref[...], vector_first_ref[...], vector_second_ref[...], grad, rate_vectors
        )

    factor = factor_ref[0:1, 0:1]
    for pair in range(pairs):
        at = pair // members
        lanes, held = slice(pair * PAIR, (pair + 1) * PAIR), slice(at * PAIR, (at + 1) * PAIR)
        in_raw[:, lanes] = gate_ref[pair % members, :, held].astype(f32)
        in_raw[:, INNER + pair * PAIR : INNER + (pair + 1) * PAIR] = x_ref[
            pair % members, :, held
        ].astype(f32)
    small = jnp.concatenate([small_ref[i] for i in range(members)], axis=1)
    in_raw[:, 2 * INNER :] = dot_rows(small, turn_ref[...])
    grad = in_raw[...] * factor
    in_grad_ref[...] = grad
    in_moment_ref[...], in_square_ref[...], master = adamw(
        in_ref[...], in_first_ref[...], in_second_ref[...], grad, rate_in_proj
    )
    in_master_ref[...] = master
    in_rounded_ref[...] = master.astype(bf16)
    grad = out_raw_ref[...] * factor
    out_grad_ref[...] = grad
    out_moment_ref[...], out_square_ref[...], master = adamw(
        out_ref[...], out_first_ref[...], out_second_ref[...], grad, rate_out_proj
    )
    out_master_ref[...] = master
    out_rounded_ref[...] = master.astype(bf16)


def optimizer(squares, parts, vectors, gate, x, small, in_state, out_raw, out_state):
    members, rows, width = x.shape
    in_shape, out_shape = in_state[0].shape, out_state[0].shape
    steps = OPTIMIZER_STEPS
    step_rows = rows // steps
    piece = lambda lanes: pl.BlockSpec((members, step_rows, lanes), lambda i: (0, i, 0))
    in_flat = pl.BlockSpec((step_rows, in_shape[1]), lambda i: (i, 0))
    out_flat = pl.BlockSpec((out_shape[0] // steps, out_shape[1]), lambda i: (i, 0))
    sd = jax.ShapeDtypeStruct
    vector_shape = sd(vectors[0].shape, f32)
    return pl.pallas_call(
        optimizer_kernel,
        grid=(steps,),
        in_specs=[whole_spec()] * 6
        + [piece(width), piece(width), piece(PAIR)]
        + [in_flat] * 3
        + [out_flat] * 4,
        out_specs=[whole_spec()] * 5 + [in_flat] * 5 + [out_flat] * 5,
        out_shape=[sd((8, PAIR), f32)]
        + [vector_shape] * 4
        + [sd(in_shape, f32)] * 4
        + [sd(in_shape, bf16)]
        + [sd(out_shape, f32)] * 4
        + [sd(out_shape, bf16)],
        scratch_shapes=[
            pltpu.VMEM(vectors[0].shape, f32),
            pltpu.VMEM((8, PAIR), f32),
            pltpu.VMEM((step_rows, in_shape[1]), f32),
        ],
        compiler_params=pltpu.CompilerParams(vmem_limit_bytes=VMEM_BYTES),
        name="optimizer",
    )(
        squares, parts, *vectors, last_columns(members), gate, x, small, *in_state, out_raw,
        *out_state,
    )


def unpack(vectors):
    offset = D + INNER
    taps_end = offset + CONV * XBC
    heads_start = taps_end + XBC
    norm_gain = vectors[:D]
    gate_gain = vectors[D:offset]
    filter_taps = vectors[offset:taps_end].reshape(CONV, XBC)
    filter_bias = vectors[taps_end:heads_start]
    step_bias = vectors[heads_start : heads_start + HEADS]
    decay_log = vectors[heads_start + HEADS : heads_start + 2 * HEADS]
    skip_gain = vectors[heads_start + 2 * HEADS : heads_start + 3 * HEADS]
    return (norm_gain, gate_gain, filter_taps, filter_bias, step_bias, decay_log, skip_gain)


def adamw(weight, moment, square, gradient, step_rate):
    moment_new = beta_first * moment + (1.0 - beta_first) * gradient
    square_new = beta_second * square + (1.0 - beta_second) * gradient * gradient
    moment_hat = moment_new / (1.0 - beta_first**STEP)
    square_hat = square_new / (1.0 - beta_second**STEP)
    weight_new = weight - step_rate * (
        moment_hat / (jnp.sqrt(square_hat) + adam_eps) + weight_decay * weight
    )
    return (moment_new, square_new, weight_new)


def on_device(
    tokens,
    widths,
    cotangent,
    in_weight,
    in_first,
    in_second,
    out_weight,
    out_first,
    out_second,
    vectors,
    vector_first,
    vector_second,
):
    fsdp = lax.axis_size("fsdp")
    me = lax.axis_index("fsdp")
    heads = HEADS // fsdp
    inner = INNER // fsdp
    shared = 2 * STATE // fsdp
    pairs = HEADS // 2 // fsdp
    rows_in, rows_out = in_weight.shape[0], out_weight.shape[0]
    length = tokens.shape[0] * fsdp
    chunks = length // SPAN
    in_kernels = uses_ring("dp") and rows_out == PAIR and rows_in % 16 == 0

    def own_channels(v):
        lead = v.shape[:-1]
        cut = v.reshape(lead + (pairs, fsdp, PAIR))
        return lax.dynamic_index_in_dim(cut, me, len(lead) + 1, False).reshape(lead + (inner,))

    def own_heads(v):
        return lax.dynamic_index_in_dim(v.reshape(pairs, fsdp, 2), me, 1, False).reshape(heads)

    def own_shared(v):
        return lax.dynamic_slice_in_dim(v, me * shared, shared, v.ndim - 1)

    norm_gain, gate_gain, filter_taps, filter_bias, step_bias, decay_log, skip_gain = unpack(
        vectors
    )
    gain_own = own_channels(gate_gain)[None]
    taps_own = own_channels(filter_taps[:, :INNER])
    bias_own = own_channels(filter_bias[:INNER])[None]
    taps_shared = own_shared(filter_taps[:, INNER:])
    bias_shared = own_shared(filter_bias[INNER:])
    step_bias_own, decay_own = own_heads(step_bias), -jnp.exp(own_heads(decay_log))
    skip_own = jnp.repeat(own_heads(skip_gain), HEAD_DIM)[None]

    width_index = widths[0]
    active = HEADS // 8 * jnp.left_shift(jnp.int32(1), width_index)
    head_mask = (jnp.arange(heads, dtype=jnp.int32) < active // fsdp).astype(f32)
    mask = jnp.repeat(head_mask, HEAD_DIM)[None]
    channel_count = (active * HEAD_DIM).astype(f32)

    inputs = tokens.astype(f32)
    inverse_in = lax.rsqrt(jnp.mean(inputs * inputs, axis=-1, keepdims=True) + norm_eps)

    if in_kernels:
        vector_state = [vector_tiles(v) for v in (vectors, vector_first, vector_second)]
        (
            weight_shared, weight_x, weight_gate, weight_out, cotangents, normed_t, x_part, states,
            gated_low, gated_t, y_grad, gate_grad, consts, head_consts, shared_taps, head_columns,
            head_rows, head_all, keys, queries, queries_t, shared_part, shared_pre, gain_grad,
        ) = forward(tokens, cotangent, in_weight, out_weight, vector_state[0], active)
        scan_inputs = (consts, head_columns, head_rows, keys, queries)
    else:
        in_low = in_weight.astype(bf16)
        shared_cut = jnp.concatenate(
            [
                in_low[:, 2 * INNER : 2 * INNER + 2 * STATE]
                .reshape(rows_in, fsdp, shared)
                .transpose(1, 0, 2),
                in_low[:, 2 * INNER + 2 * STATE :]
                .reshape(rows_in, pairs, fsdp, 2)
                .transpose(2, 0, 1, 3)
                .reshape(fsdp, rows_in, heads),
            ],
            axis=2,
        )

        def channel_cut(part):
            return (
                part.reshape(rows_in, pairs, fsdp, PAIR)
                .transpose(2, 0, 1, 3)
                .reshape(fsdp, rows_in, inner)
            )

        def gathered(cut):
            block = exchanged(cut, "fsdp")
            return gather_rows(block.reshape(fsdp * rows_in, cut.shape[2]), "dp")

        normed_own = (inputs * inverse_in * norm_gain[None, :]).astype(bf16)
        x_cut = channel_cut(in_low[:, INNER : 2 * INNER])
        gate_cut = channel_cut(in_low[:, :INNER])
        out_low = out_weight.astype(bf16)

        weight_shared = gathered(shared_cut)
        weight_x = gathered(x_cut)
        weight_gate = gathered(gate_cut)
        weight_out = lax.dynamic_index_in_dim(
            lax.all_gather(out_low, ("dp", "fsdp"), axis=0, tiled=True).reshape(
                pairs, fsdp, PAIR, D
            ),
            me,
            1,
            False,
        ).reshape(inner, D)
        normed = spread(normed_own, "fsdp").reshape(length, D)
        cotangents = spread(cotangent, "fsdp").reshape(length, D)

        small = lax.dot_general(
            weight_shared, normed, (((0,), (1,)), ((), ())), preferred_element_type=f32
        )
        shared_part = small[:shared]
        step_raw = small[shared : shared + heads] * head_mask[:, None]
        shared_padded = jnp.pad(shared_part, ((0, 0), (CONV - 1, 0)))
        shared_pre = bias_shared[:, None] + sum(
            taps_shared[k][:, None] * shared_padded[:, k : k + length] for k in range(CONV)
        )
        shared_gate = jax.nn.sigmoid(shared_pre)
        shared_all = spread_small((shared_pre * shared_gate).astype(bf16), "fsdp").reshape(
            2 * STATE, length
        )
        keys_t, queries_t = shared_all[:STATE], shared_all[STATE:]
        keys, queries = keys_t.T, queries_t.T
        step_logits = step_raw + step_bias_own[:, None]
        step_sizes = jax.nn.softplus(step_logits)
        upto = (jnp.arange(SPAN)[:, None] <= jnp.arange(SPAN)[None, :]).astype(f32)
        log_sums = jnp.dot(
            (step_sizes * decay_own[:, None]).reshape(heads, chunks, SPAN), upto, precision=highest
        ).reshape(heads, length)
        groups = heads // GROUP
        head_all = jnp.concatenate(
            [log_sums, step_sizes, step_logits, jnp.zeros((PAIR - 3 * heads, length), f32)]
        ).T
        head_columns = jnp.concatenate(
            [jnp.roll(head_all, -group * GROUP, axis=1) for group in range(groups)], axis=1
        )
        head_rows = jnp.pad(
            log_sums.reshape(groups, GROUP, length), ((0, 0), (0, 8 - GROUP), (0, 0))
        ).reshape(groups * 8, length)

        consts = jnp.concatenate([taps_own, bias_own, mask, skip_own, gain_own])
        scan_inputs = (consts, head_columns, head_rows, keys, queries)
        x_part = jnp.dot(normed, weight_x, preferred_element_type=f32)
        y, states = scan_forward(x_part, *scan_inputs, keys_t)
        gate_part, gated_grad, stats = gate_forward(
            normed, weight_gate, cotangents, weight_out, y, gain_own, mask
        )
        stats = summed(stats[:, :2].T, "fsdp")
        inverse_out = lax.rsqrt(stats[0] / channel_count + norm_eps)
        pull = inverse_out**3 / channel_count * stats[1]
        gated_low, y_grad, gate_grad, gain_grad = norm_back(
            y, gate_part, gated_grad, jnp.stack([inverse_out, pull], axis=1), gain_own, mask
        )

        def in_term(grad):
            return lax.dot_general(
                normed, grad, (((0,), (0,)), ((), ())), preferred_element_type=f32
            ).astype(bf16)

    if in_kernels:
        (
            layer_out, token_grad, gate_back, x_back, small_back, out_raw, vector_rows, squares,
        ) = backward(
            scan_inputs, queries_t, head_all, head_consts, shared_part, shared_pre, shared_taps,
            vector_state[0], gain_grad, tokens, weight_shared, x_part, y_grad, states, gated_low,
            gated_t, gate_grad, normed_t, cotangents, cotangent, weight_out, weight_gate, weight_x,
        )
        norm, *rest = optimizer(
            squares, vector_rows, vector_state, gate_back, x_back, small_back,
            (in_weight, in_first, in_second), out_raw, (out_weight, out_first, out_second),
        )
        vector_out = [v.reshape(-1)[: vectors.shape[0]] for v in rest[:4]]
        in_grad, in_moment, in_square, in_master, in_rounded = rest[4:9]
        out_grad, out_moment, out_square, out_master, out_rounded = rest[9:]
        return (
            layer_out,
            token_grad,
            in_grad,
            out_grad,
            vector_out[0],
            norm[0, 0],
            in_moment,
            in_square,
            in_master,
            in_rounded,
            out_moment,
            out_square,
            out_master,
            out_rounded,
            *vector_out[1:],
        )
    else:
        out_term = lax.dot_general(
            gated_low, cotangents, (((0,), (0,)), ((), ())), preferred_element_type=f32
        )
        whole_term = jnp.zeros((pairs, fsdp, PAIR, D), f32)
        whole_term = lax.dynamic_update_slice(
            whole_term, out_term.reshape(pairs, 1, PAIR, D), (0, me, 0, 0)
        )
        out_raw = lax.psum_scatter(
            whole_term.reshape(INNER, D), ("dp", "fsdp"), scatter_dimension=0, tiled=True
        )
        added = halved(
            jnp.dot(gated_low, weight_out, preferred_element_type=f32)
            .astype(bf16)
            .reshape(fsdp, tokens.shape[0], D),
            "fsdp",
        )
        layer_out = (inputs + added).astype(bf16)
        gate_raw = scatter_rows(in_term(gate_grad), "dp")
        x_grad, key_grad, query_grad, sums, rest, channel_grad = scan_backward(
            x_part, *scan_inputs, queries_t, y_grad, states
        )
        x_raw = scatter_rows(in_term(x_grad), "dp")

        shared_grads = jnp.concatenate([key_grad, query_grad], axis=1).T.astype(bf16)
        arrived = exchanged(shared_grads.reshape(fsdp, shared, length), "fsdp").astype(f32)
        activated_grad = jnp.sum(arrived, axis=0)
        shared_pre_grad = activated_grad * shared_gate * (1.0 + shared_pre * (1.0 - shared_gate))
        shared_ahead = jnp.pad(shared_pre_grad, ((0, 0), (0, CONV - 1)))
        shared_grad = sum(
            taps_shared[k][:, None] * shared_ahead[:, CONV - 1 - k : CONV - 1 - k + length]
            for k in range(CONV)
        )
        taps_shared_grad = jnp.stack(
            [
                jnp.sum(shared_pre_grad * shared_padded[:, k : k + length], axis=1)
                for k in range(CONV)
            ]
        )
        bias_shared_grad = jnp.sum(shared_pre_grad, axis=1)

        sums = sums.T[: 3 * heads].reshape(3, heads, chunks, SPAN)
        before = (jnp.arange(SPAN)[:, None] < jnp.arange(SPAN)[None, :]).astype(f32)
        rest = rest.reshape(chunks, heads, HEAD_DIM).sum(axis=2).T
        log_grad = (
            jnp.dot(sums[0], 1.0 - before, precision=highest)
            + jnp.dot(sums[1], before, precision=highest)
            + rest[:, :, None]
        ).reshape(heads, length)
        step_grad = decay_own[:, None] * log_grad + sums[2].reshape(heads, length)
        raw_grad = step_grad * jax.nn.sigmoid(step_logits)
        step_bias_grad = jnp.sum(raw_grad, axis=1)
        decay_grad = jnp.sum(step_sizes * log_grad, axis=1) * decay_own
        small_grad = jnp.concatenate([shared_grad, raw_grad * head_mask[:, None]], axis=0).astype(bf16)
        small_raw = scatter_rows(
            lax.dot_general(
                normed, small_grad, (((0,), (1,)), ((), ())), preferred_element_type=f32
            ).astype(bf16),
            "dp",
        )

        def in_back(grad, weight, grad_dim=1):
            return lax.dot_general(
                grad, weight, (((grad_dim,), (1,)), ((), ())), preferred_element_type=f32
            )

        normed_grad = halved(
            (
                in_back(gate_grad, weight_gate)
                + in_back(x_grad, weight_x)
                + in_back(small_grad, weight_shared, 0)
            )
            .astype(bf16)
            .reshape(fsdp, tokens.shape[0], D),
            "fsdp",
        )
        pulled = normed_grad * norm_gain[None, :]
        input_grad = inverse_in * pulled - inputs * (
            inverse_in**3 * jnp.mean(pulled * inputs, axis=-1, keepdims=True)
        )
        token_grad = (cotangent.astype(f32) + input_grad).astype(bf16)
        norm_gain_grad = jnp.sum(normed_grad * inputs * inverse_in, axis=0)

        head_row = jnp.concatenate(
            [jnp.pad(step_bias_grad, (0, PAIR - heads)), jnp.pad(decay_grad, (0, PAIR - heads))]
        )
        shared_rows = jnp.concatenate([taps_shared_grad, bias_shared_grad[None]])
        vector_rows = jnp.concatenate(
            [
                gain_grad[0:1],
                channel_grad[: CONV + 2],
                norm_gain_grad.reshape(-1, inner),
                jnp.zeros((15 - CONV - 3 - D // inner, inner), f32),
                jnp.pad(head_row, (0, inner - 2 * PAIR))[None],
                jnp.pad(shared_rows, ((0, 7 - CONV), (0, inner - shared))),
            ]
        )
        vector_rows = spread_small(summed_in_steps(vector_rows, "dp"), "fsdp")
        squares = (
            jnp.sum(gate_raw * gate_raw)
            + jnp.sum(x_raw * x_raw)
            + jnp.sum(small_raw * small_raw)
            + jnp.sum(out_raw * out_raw)
        )
        squares = summed(summed(jnp.broadcast_to(squares, (8, 128)), "fsdp"), "dp")[0, 0]

    def joined_channels(v):
        return v.reshape(fsdp, pairs, PAIR).transpose(1, 0, 2).reshape(INNER)

    def joined_heads(v):
        return v.reshape(fsdp, pairs, 2).transpose(1, 0, 2).reshape(HEADS)

    shared_all = vector_rows[:, 16 : 17 + CONV, :shared]
    bias_shared_all = shared_all[:, CONV].reshape(-1)
    taps_all = [
        jnp.concatenate([joined_channels(vector_rows[:, 1 + k]), shared_all[:, k].reshape(-1)])
        for k in range(CONV)
    ]
    bias_all = jnp.concatenate([joined_channels(vector_rows[:, CONV + 1]), bias_shared_all])
    norm_rows = vector_rows[:, CONV + 3 : CONV + 3 + D // inner].reshape(fsdp, D)
    norm_all = norm_rows[0]
    for member in range(1, fsdp):
        norm_all = norm_all + norm_rows[member]
    skip_all = vector_rows[:, CONV + 2].reshape(fsdp * heads, HEAD_DIM).sum(axis=1)
    vector_raw = jnp.concatenate(
        [norm_all, joined_channels(vector_rows[:, 0])]
        + taps_all
        + [
            bias_all,
            joined_heads(vector_rows[:, 15, :heads]),
            joined_heads(vector_rows[:, 15, PAIR : PAIR + heads]),
            joined_heads(skip_all),
        ]
    )

    grad_norm = jnp.sqrt(squares + jnp.sum(vector_raw * vector_raw))
    factor = jnp.minimum(1.0, clip_norm / (grad_norm + 1e-06))
    def returned(raw):
        return exchanged(raw.astype(bf16).reshape(fsdp, rows_in, raw.shape[1]), "fsdp")

    def joined_columns(part):
        return (
            part.reshape(fsdp, rows_in, pairs, PAIR)
            .transpose(1, 2, 0, 3)
            .reshape(rows_in, INNER)
        )

    small_back = returned(small_raw)
    in_raw = jnp.concatenate(
        [
            joined_columns(returned(gate_raw)),
            joined_columns(returned(x_raw)),
            small_back[:, :, :shared].transpose(1, 0, 2).reshape(rows_in, 2 * STATE),
            small_back[:, :, shared:]
            .reshape(fsdp, rows_in, pairs, 2)
            .transpose(1, 2, 0, 3)
            .reshape(rows_in, HEADS),
        ],
        axis=1,
    ).astype(f32)
    in_grad = in_raw * factor
    in_moment, in_square, in_master = adamw(
        in_weight, in_first, in_second, in_grad, rate_in_proj
    )
    in_rounded = in_master.astype(bf16)
    out_grad = out_raw * factor
    vector_grad = vector_raw * factor
    out_moment, out_square, out_master = adamw(
        out_weight, out_first, out_second, out_grad, rate_out_proj
    )
    vector_moment, vector_square, vector_master = adamw(
        vectors, vector_first, vector_second, vector_grad, rate_vectors
    )
    return (
        layer_out,
        token_grad,
        in_grad,
        out_grad,
        vector_grad,
        grad_norm,
        in_moment,
        in_square,
        in_master,
        in_rounded,
        out_moment,
        out_square,
        out_master,
        out_master.astype(bf16),
        vector_moment,
        vector_square,
        vector_master,
    )


def solution(mesh):
    rows = P(("dp", "fsdp"), None)
    return jax.shard_map(
        on_device,
        mesh=mesh,
        in_specs=(rows, P("dp")) + (rows,) * 7 + (P(),) * 3,
        out_specs=(rows,) * 4 + (P(),) * 2 + (rows,) * 8 + (P(),) * 3,
        check_vma=False,
    )
```

```python
from functools import partial

import jax
import jax.numpy as jnp
import numpy as np
from jax import lax
from jax.experimental import pallas as pl
from jax.experimental.pallas import tpu as pltpu
from jax.sharding import PartitionSpec as P

D = 2048
HEADS = 64
HEAD_DIM = 64
STATE = 128
CONV = 4
SPAN = 128
STEP = 10
INNER = 4096
XBC = 4352
PAIR = 2 * HEAD_DIM
GROUP = 4
STEP_LANE = 16
TAPS_ROW = (D + INNER) // PAIR
LAST_ROW = TAPS_ROW + (CONV + 1) * XBC // PAIR
MASK_ROW, SKIP_ROW, GAIN_ROW = CONV + 1, CONV + 2, CONV + 3
LANES = GROUP * HEAD_DIM
ROW_TILE = 256
RING_LIMIT = 16

norm_eps = 1e-05
clip_norm = 1.0
beta_first = 0.5
beta_second = 0.5
adam_eps = 1e-08
weight_decay = 0.1
rate_in_proj = 0.03
rate_out_proj = 0.02
rate_vectors = 0.5
highest = lax.Precision.HIGHEST
f32 = jnp.float32
bf16 = jnp.bfloat16
VMEM_BYTES = 63 * 1024 * 1024


def ring_order(count):
    return list(range(0, count, 2)) + list(range(count - 1, 0, -2))


def ring_links(count):
    order = ring_order(count)
    right = [(order[i], order[(i + 1) % count]) for i in range(count)]
    return right, [(b, a) for a, b in right]


def ring_place(axis):
    count = lax.axis_size(axis)
    order = ring_order(count)
    places = [0] * count
    for place, member in enumerate(order):
        places[member] = place
    place = jnp.asarray(places, jnp.int32)[lax.axis_index(axis)]

    def member_at(distance):
        return jnp.asarray(order, jnp.int32)[lax.rem(place + distance + count, count)]

    return member_at


def uses_ring(axis):
    count = lax.axis_size(axis)
    return count % 2 == 0 and 4 <= count <= RING_LIMIT


def gather_rows(block, axis):
    count = lax.axis_size(axis)
    if not uses_ring(axis):
        return lax.all_gather(block, axis, axis=0, tiled=True)
    right, left = ring_links(count)
    member_at = ring_place(axis)
    rows, half = block.shape[0], block.shape[0] // 2
    whole = jnp.zeros((count * rows,) + block.shape[1:], block.dtype)
    columns = (0,) * (block.ndim - 1)

    def put(whole, piece, distance, shift=0):
        return lax.dynamic_update_slice(
            whole, piece, (member_at(distance) * rows + shift,) + columns
        )

    whole = put(whole, block, 0)
    going_right = going_left = block
    for hop in range(1, count // 2):
        going_right = lax.ppermute(going_right, axis, right)
        going_left = lax.ppermute(going_left, axis, left)
        whole = put(whole, going_right, -hop)
        whole = put(whole, going_left, hop)
    first = lax.ppermute(going_right[:half], axis, right)
    second = lax.ppermute(going_left[half:], axis, left)
    whole = put(whole, first, count // 2)
    return put(whole, second, count // 2, half)


def scatter_rows(terms, axis):
    count = lax.axis_size(axis)
    if not uses_ring(axis):
        return lax.psum_scatter(terms.astype(f32), axis, scatter_dimension=0, tiled=True)
    right, left = ring_links(count)
    member_at = ring_place(axis)
    rows = terms.shape[0] // count
    half = rows // 2

    def term(distance):
        return lax.dynamic_slice_in_dim(terms, member_at(distance) * rows, rows, 0).astype(f32)

    far = term(count // 2).astype(bf16)
    going_right = lax.ppermute(far[:half], axis, right)
    going_left = lax.ppermute(far[half:], axis, left)
    for distance in range(count // 2 - 1, 0, -1):
        to_right, to_left = term(distance), term(-distance)
        if distance == count // 2 - 1:
            to_right = jnp.concatenate([to_right[:half] + going_right, to_right[half:]])
            to_left = jnp.concatenate([to_left[:half], to_left[half:] + going_left])
        else:
            to_right, to_left = to_right + going_right, to_left + going_left
        going_right = lax.ppermute(to_right.astype(bf16), axis, right)
        going_left = lax.ppermute(to_left.astype(bf16), axis, left)
    return term(0) + going_right + going_left


def swapped(value, axis, flip):
    count = lax.axis_size(axis)
    return lax.ppermute(value, axis, [(i, i ^ flip) for i in range(count)])


def summed(value, axis):
    count = lax.axis_size(axis)
    if count <= 8:
        parts = [value] + [swapped(value, axis, flip) for flip in range(1, count)]
        while len(parts) > 1:
            parts = [parts[i] + parts[i + 1] for i in range(0, len(parts), 2)]
        return parts[0]
    return summed_in_steps(value, axis)


def summed_in_steps(value, axis):
    flip = 1
    while flip < lax.axis_size(axis):
        value = value + swapped(value, axis, flip)
        flip *= 2
    return value


def placed(parts, axis):
    count = lax.axis_size(axis)
    me = lax.axis_index(axis)
    whole = jnp.zeros((count,) + parts[0].shape, parts[0].dtype)
    for flip, part in enumerate(parts):
        whole = lax.dynamic_update_index_in_dim(whole, part, lax.bitwise_xor(me, flip), 0)
    return whole


def spread(value, axis):
    count = lax.axis_size(axis)
    parts = [value]
    flip = count // 2
    known = {0: value}
    while flip:
        fresh = {k ^ flip: swapped(v, axis, flip) for k, v in known.items()}
        known.update(fresh)
        flip //= 2
    parts = [known[k] for k in range(count)]
    return placed(parts, axis)


def spread_small(value, axis):
    count = lax.axis_size(axis)
    return placed([value] + [swapped(value, axis, k) for k in range(1, count)], axis)


def exchanged(blocks, axis):
    count = lax.axis_size(axis)
    me = lax.axis_index(axis)

    def block_for(flip):
        return lax.dynamic_index_in_dim(blocks, lax.bitwise_xor(me, flip), 0, False)

    return placed(
        [block_for(0)] + [swapped(block_for(k), axis, k) for k in range(1, count)], axis
    )


def halved(blocks, axis):
    count = lax.axis_size(axis)
    me = lax.axis_index(axis)
    held = {
        k: lax.dynamic_index_in_dim(blocks, lax.bitwise_xor(me, k), 0, False)
        for k in range(count)
    }
    flip = 1
    while flip < count:
        kept = {}
        for k in sorted(held):
            if k & flip:
                continue
            arrived = swapped(held[k ^ flip].astype(bf16), axis, flip)
            kept[k] = held[k].astype(f32) + arrived
        held = kept
        flip *= 2
    return held[0]


def dot_rows(a, b):
    return lax.dot_general(a, b, (((1,), (0,)), ((), ())), preferred_element_type=f32)


def dot_lanes(a, b):
    return lax.dot_general(a, b, (((1,), (1,)), ((), ())), preferred_element_type=f32)


def head_lanes(columns, base):
    rows = columns.shape[0]
    full = [
        jnp.broadcast_to(columns[:, base + j : base + j + 1], (rows, PAIR)) for j in range(GROUP)
    ]
    first = lax.broadcasted_iota(jnp.int32, (rows, PAIR), 1) < HEAD_DIM
    lanes = jnp.concatenate(
        [jnp.where(first, full[i], full[i + 1]) for i in range(0, GROUP, 2)], axis=1
    )
    return full, lanes


def stacked_heads(values, block_mask):
    return jnp.concatenate([values] * GROUP, axis=0) * block_mask


def filtered(window, taps, bias, rows):
    pre = bias + taps[CONV - 1 : CONV] * window[8 : 8 + rows]
    for k in range(CONV - 1):
        pre = pre + taps[k : k + 1] * window[5 + k : 5 + k + rows]
    return pre


def scan_forward_kernel(
    x_ref, consts_ref, column_ref, row_ref, key_ref, query_ref,
    key_t_ref, block_ref, y_ref, states_ref, padded, state,
):
    length = x_ref.shape[0]
    rows = SPAN
    mask = consts_ref[MASK_ROW : MASK_ROW + 1]
    padded[0:8, :] = jnp.zeros((8, LANES), f32)
    padded[8 : 8 + length, :] = x_ref[...] * mask
    state[...] = jnp.zeros_like(state)
    taps, bias = consts_ref[0:CONV], consts_ref[CONV : CONV + 1]
    skip = consts_ref[SKIP_ROW : SKIP_ROW + 1]
    causal = lax.broadcasted_iota(jnp.int32, (rows, rows), 0) >= lax.broadcasted_iota(
        jnp.int32, (rows, rows), 1
    )

    def chunk(c, carry):
        start = pl.multiple_of(c * rows, rows)
        here = pl.ds(start, rows)
        pre = filtered(padded[pl.ds(start, rows + 8), :], taps, bias, rows)
        values = pre * jax.nn.sigmoid(pre) * mask
        columns = column_ref[here, :]
        log_full, log_lanes = head_lanes(columns, 0)
        step_lanes = head_lanes(columns, STEP_LANE)[1]
        weighted = step_lanes * values
        weighted_low = weighted.astype(bf16)
        keys, queries, keys_t = key_ref[here, :], query_ref[here, :], key_t_ref[:, here]
        inner = dot_lanes(queries, keys)
        mixing = jnp.concatenate(
            [
                (
                    jnp.where(causal, jnp.exp(log_full[j] - row_ref[j : j + 1, here]), 0.0)
                    * inner
                ).astype(bf16)
                for j in range(GROUP)
            ],
            axis=1,
        )
        state_now = state[...]
        state_low = state_now.astype(bf16)
        states_ref[pl.ds(c, 1)] = state_low[None]
        y = dot_rows(mixing, stacked_heads(weighted_low, block_ref[...]))
        y = y + jnp.exp(log_lanes) * dot_rows(queries, state_low)
        y_ref[here, :] = y + skip * values
        log_last = log_lanes[rows - 1 : rows, :]
        tail = (weighted * jnp.exp(log_last - log_lanes)).astype(bf16)
        state[...] = jnp.exp(log_last) * state_now + dot_rows(keys_t, tail)
        return carry

    lax.fori_loop(0, length // rows, chunk, 0)


def scan_backward_group(
    x_ref, consts_ref, column_ref, row_ref, key_ref, query_ref,
    query_t_ref, block_ref, pick_ref, grad_ref, states_ref,
    x_grad_ref, key_grad_ref, query_grad_ref, sums_ref, rest_ref, channel_ref,
    padded, following, state_back, inner_grad,
):
    length = x_ref.shape[0]
    rows = SPAN
    chunks = length // rows
    mask = consts_ref[MASK_ROW : MASK_ROW + 1]
    padded[0:8, :] = jnp.zeros((8, LANES), f32)
    padded[8 : 8 + length, :] = x_ref[...] * mask
    following[...] = jnp.zeros_like(following)
    state_back[...] = jnp.zeros_like(state_back)
    channel_ref[...] = jnp.zeros_like(channel_ref)

    taps, bias = consts_ref[0:CONV], consts_ref[CONV : CONV + 1]
    skip = consts_ref[SKIP_ROW : SKIP_ROW + 1]
    row_at = lax.broadcasted_iota(jnp.int32, (rows, rows), 0)
    lane_at = lax.broadcasted_iota(jnp.int32, (rows, rows), 1)
    causal, causal_t = row_at >= lane_at, lane_at >= row_at

    def chunk(lap, carry):
        c = chunks - 1 - lap
        start = pl.multiple_of(c * rows, rows)
        here = pl.ds(start, rows)
        window = padded[pl.ds(start, rows + 8), :]
        pre = filtered(window, taps, bias, rows)
        gate = jax.nn.sigmoid(pre)
        values = pre * gate * mask
        columns = column_ref[here, :]
        log_full, log_lanes = head_lanes(columns, 0)
        step_lanes = head_lanes(columns, STEP_LANE)[1]
        weighted = step_lanes * values
        weighted_low = weighted.astype(bf16)
        keys, queries, queries_t = key_ref[here, :], query_ref[here, :], query_t_ref[:, here]
        grad_low = grad_ref[here, :]
        grad = grad_low.astype(f32)
        inner, inner_t = dot_lanes(queries, keys), dot_lanes(keys, queries)
        blocks = block_ref[...]
        weighted_blocks = stacked_heads(weighted_low, blocks)
        grad_blocks = stacked_heads(grad_low, blocks)
        mixing_grad = dot_lanes(grad_low, weighted_blocks)
        mixing, mixing_t, inner_sum = [], [], jnp.zeros((rows, rows), f32)
        for j in range(GROUP):
            log_row = row_ref[j : j + 1, here]
            decay = jnp.where(causal, jnp.exp(log_full[j] - log_row), 0.0)
            decay_t = jnp.where(causal_t, jnp.exp(log_row - log_full[j]), 0.0)
            mixing.append((decay * inner).astype(bf16))
            mixing_t.append((decay_t * inner_t).astype(bf16))
            inner_sum = inner_sum + decay * mixing_grad[:, j * rows : (j + 1) * rows]
        inner_grad[pl.ds(c, 1)] = inner_grad[pl.ds(c, 1)] + inner_sum[None]
        y = dot_rows(jnp.concatenate(mixing, axis=1), weighted_blocks)
        state_low = states_ref[pl.ds(c, 1)][0]
        entry = jnp.exp(log_lanes)
        y = y + entry * dot_rows(queries, state_low)
        inside = dot_rows(jnp.concatenate(mixing_t, axis=1), grad_blocks)
        back = state_back[...]
        back_low = back.astype(bf16)
        log_last = log_lanes[rows - 1 : rows, :]
        tail = jnp.exp(log_last - log_lanes)
        outside = tail * dot_rows(keys, back_low)
        entry_grad = (grad * entry).astype(bf16)
        tail_low = (weighted * tail).astype(bf16)
        query_grad_ref[here, :] = query_grad_ref[here, :] + dot_lanes(entry_grad, state_low)
        key_grad_ref[here, :] = key_grad_ref[here, :] + dot_lanes(tail_low, back_low)
        last = jnp.exp(log_last)
        rest_ref[pl.ds(c, 1)] = (
            last * jnp.sum(state_low.astype(f32) * back, axis=0, keepdims=True)
        )[None]
        state_back[...] = last * back + dot_rows(queries_t, entry_grad)
        weighted_grad = inside + outside
        first = grad * y - weighted_low.astype(f32) * inside
        first_high = first.astype(bf16)
        first_rest = (first - first_high.astype(f32)).astype(bf16)
        sums_ref[here, :] = sums_ref[here, :] + (
            dot_rows(first_high, pick_ref[0])
            + dot_rows(first_rest, pick_ref[0])
            + dot_rows((weighted * outside).astype(bf16), pick_ref[1])
            + dot_rows((values * weighted_grad).astype(bf16), pick_ref[2])
        )
        values_grad = step_lanes * weighted_grad + skip * grad
        pre_grad = values_grad * mask * (gate * (1.0 + pre * (1.0 - gate)))
        channel_ref[CONV : CONV + 1, :] += jnp.sum(pre_grad, axis=0, keepdims=True)
        channel_ref[CONV + 1 : CONV + 2, :] += jnp.sum(grad * values, axis=0, keepdims=True)
        for k in range(CONV):
            channel_ref[k : k + 1, :] += jnp.sum(
                pre_grad * window[5 + k : 5 + k + rows], axis=0, keepdims=True
            )
        ahead = jnp.concatenate([pre_grad, following[...]], axis=0)
        following[...] = pre_grad[0:8]
        x_grad = taps[CONV - 1 : CONV] * ahead[0:rows]
        for k in range(CONV - 1):
            x_grad = x_grad + taps[k : k + 1] * ahead[CONV - 1 - k : CONV - 1 - k + rows]
        x_grad_ref[here, :] = (x_grad * mask).astype(bf16)
        return carry

    lax.fori_loop(0, chunks, chunk, 0)


def scan_backward_start(key_grad_ref, query_grad_ref, sums_ref, inner_grad):
    key_grad_ref[...] = jnp.zeros_like(key_grad_ref)
    query_grad_ref[...] = jnp.zeros_like(query_grad_ref)
    inner_grad[...] = jnp.zeros_like(inner_grad)
    sums_ref[...] = jnp.zeros_like(sums_ref)


def scan_backward_finish(key_ref, query_ref, key_grad_ref, query_grad_ref, inner_grad):
    rows = SPAN

    def finish(c, carry):
        here = pl.ds(pl.multiple_of(c * rows, rows), rows)
        inner_low = inner_grad[pl.ds(c, 1)][0].astype(bf16)
        query_grad_ref[here, :] = query_grad_ref[here, :] + dot_rows(inner_low, key_ref[here, :])
        key_grad_ref[here, :] = key_grad_ref[here, :] + lax.dot_general(
            inner_low, query_ref[here, :], (((0,), (0,)), ((), ())), preferred_element_type=f32
        )
        return carry

    lax.fori_loop(0, key_ref.shape[0] // rows, finish, 0)


def scan_backward_kernel(*refs):
    key_ref, query_ref = refs[4:6]
    key_grad_ref, query_grad_ref, sums_ref = refs[12:15]
    inner_grad = refs[-1]

    @pl.when(pl.program_id(0) == 0)
    def _():
        scan_backward_start(key_grad_ref, query_grad_ref, sums_ref, inner_grad)

    scan_backward_group(*refs)

    @pl.when(pl.program_id(0) == pl.num_programs(0) - 1)
    def _():
        scan_backward_finish(key_ref, query_ref, key_grad_ref, query_grad_ref, inner_grad)


def block_mask():
    row = np.arange(GROUP * SPAN)[:, None] // SPAN
    lane = np.arange(LANES)[None, :] // HEAD_DIM
    return jnp.asarray((row == lane).astype(np.float32), bf16)


def pick_masks(groups):
    lane = np.arange(LANES)[:, None] // HEAD_DIM
    target = np.arange(PAIR)[None, :]
    masks = [
        target == (kind * groups + group) * GROUP + lane
        for group in range(groups)
        for kind in range(3)
    ]
    return jnp.asarray(np.stack(masks).astype(np.float32), bf16)


def whole_spec():
    return pl.BlockSpec(memory_space=pltpu.VMEM)


def lane_spec(rows):
    return pl.BlockSpec((rows, LANES), lambda g: (0, g))


def head_specs(length):
    return [
        lane_spec(length),
        lane_spec(8),
        pl.BlockSpec((length, PAIR), lambda g: (0, g)),
        pl.BlockSpec((8, length), lambda g: (g, 0)),
        whole_spec(),
        whole_spec(),
        whole_spec(),
        whole_spec(),
    ]


def scan_forward(x, consts, columns, rows, keys, queries, keys_t):
    length, width = x.shape
    chunks = length // SPAN
    return pl.pallas_call(
        scan_forward_kernel,
        grid=(width // LANES,),
        in_specs=head_specs(length),
        out_specs=[
            lane_spec(length),
            pl.BlockSpec((chunks, STATE, LANES), lambda g: (0, 0, g)),
        ],
        out_shape=[
            jax.ShapeDtypeStruct((length, width), f32),
            jax.ShapeDtypeStruct((chunks, STATE, width), bf16),
        ],
        scratch_shapes=[pltpu.VMEM((length + 8, LANES), f32), pltpu.VMEM((STATE, LANES), f32)],
        compiler_params=pltpu.CompilerParams(vmem_limit_bytes=VMEM_BYTES),
        cost_estimate=pl.CostEstimate(
            flops=10_000_000_000, bytes_accessed=12_000_000, transcendentals=4_000_000
        ),
        name="scan_forward",
    )(x, consts, columns, rows, keys, queries, keys_t, block_mask())


def scan_backward(
    x, consts, columns, rows, keys, queries, queries_t, grad, states
):
    length, width = x.shape
    chunks = length // SPAN
    groups = width // LANES
    same = lambda g: (0, 0)
    return pl.pallas_call(
        scan_backward_kernel,
        grid=(groups,),
        in_specs=head_specs(length)
        + [
            pl.BlockSpec((3, LANES, PAIR), lambda g: (g, 0, 0)),
            lane_spec(length),
            pl.BlockSpec((chunks, STATE, LANES), lambda g: (0, 0, g)),
        ],
        out_specs=[
            lane_spec(length),
            pl.BlockSpec((length, STATE), same),
            pl.BlockSpec((length, STATE), same),
            pl.BlockSpec((length, PAIR), same),
            pl.BlockSpec((chunks, 1, LANES), lambda g: (0, 0, g)),
            lane_spec(8),
        ],
        out_shape=[
            jax.ShapeDtypeStruct((length, width), bf16),
            jax.ShapeDtypeStruct((length, STATE), f32),
            jax.ShapeDtypeStruct((length, STATE), f32),
            jax.ShapeDtypeStruct((length, PAIR), f32),
            jax.ShapeDtypeStruct((chunks, 1, width), f32),
            jax.ShapeDtypeStruct((8, width), f32),
        ],
        scratch_shapes=[
            pltpu.VMEM((length + 8, LANES), f32),
            pltpu.VMEM((8, LANES), f32),
            pltpu.VMEM((STATE, LANES), f32),
            pltpu.VMEM((chunks, SPAN, SPAN), f32),
        ],
        compiler_params=pltpu.CompilerParams(vmem_limit_bytes=VMEM_BYTES),
        cost_estimate=pl.CostEstimate(
            flops=30_000_000_000, bytes_accessed=16_000_000, transcendentals=8_000_000
        ),
        name="scan_backward",
    )(
        x, consts, columns, rows, keys, queries, queries_t, block_mask(),
        pick_masks(groups), grad, states,
    )


def gate_kernel(
    normed_ref, weight_ref, cotangent_ref, out_ref, y_ref, gain_ref, mask_ref,
    gate_part_ref, gated_grad_ref, stats_ref,
):
    gate_part = dot_rows(normed_ref[...], weight_ref[...]) * mask_ref[...]
    gated_grad = dot_lanes(cotangent_ref[...], out_ref[...])
    gate_part_ref[...] = gate_part
    gated_grad_ref[...] = gated_grad
    gated = y_ref[...] * (gate_part * jax.nn.sigmoid(gate_part))
    squares = jnp.sum(gated * gated, axis=1, keepdims=True)
    products = jnp.sum(gated * gated_grad * gain_ref[...], axis=1, keepdims=True)
    lane = lax.broadcasted_iota(jnp.int32, stats_ref.shape, 1)
    stats_ref[...] = jnp.where(lane == 0, squares, products)


def gate_forward(normed, weight, cotangent, out_weight, y, gain, mask):
    length, width = y.shape
    rows = lambda lanes: pl.BlockSpec((ROW_TILE, lanes), lambda i: (i, 0))
    return pl.pallas_call(
        gate_kernel,
        grid=(length // ROW_TILE,),
        in_specs=[
            rows(D), whole_spec(), rows(D), whole_spec(), rows(width), whole_spec(), whole_spec(),
        ],
        out_specs=[rows(width), rows(width), rows(PAIR)],
        out_shape=[
            jax.ShapeDtypeStruct((length, width), f32),
            jax.ShapeDtypeStruct((length, width), f32),
            jax.ShapeDtypeStruct((length, PAIR), f32),
        ],
        compiler_params=pltpu.CompilerParams(vmem_limit_bytes=VMEM_BYTES),
        cost_estimate=pl.CostEstimate(
            flops=9_000_000_000, bytes_accessed=28_000_000, transcendentals=1_000_000
        ),
        name="gate_forward",
    )(normed, weight, cotangent, out_weight, y, gain, mask)


def norm_back_kernel(
    y_ref, gate_part_ref, gated_grad_ref, scale_ref, gain_ref, mask_ref,
    gated_ref, y_grad_ref, gate_grad_ref, gain_grad_ref,
):
    @pl.when(pl.program_id(0) == 0)
    def _():
        gain_grad_ref[...] = jnp.zeros_like(gain_grad_ref)

    y, gate_part, gated_grad = y_ref[...], gate_part_ref[...], gated_grad_ref[...]
    inverse, pull = scale_ref[:, 0:1], scale_ref[:, 1:2]
    gate = jax.nn.sigmoid(gate_part)
    silu = gate_part * gate
    gated = y * silu
    scaled = gated * inverse
    gain = gain_ref[...]
    gated_ref[...] = (scaled * gain).astype(bf16)
    gain_grad_ref[0:1, :] += jnp.sum(gated_grad * scaled, axis=0, keepdims=True)
    back = inverse * (gated_grad * gain) - gated * pull
    y_grad_ref[...] = (back * silu).astype(bf16)
    gate_grad_ref[...] = (
        back * y * (gate * (1.0 + gate_part * (1.0 - gate))) * mask_ref[...]
    ).astype(bf16)


def norm_back(y, gate_part, gated_grad, scales, gain, mask):
    length, width = y.shape
    rows = lambda lanes: pl.BlockSpec((ROW_TILE, lanes), lambda i: (i, 0))
    return pl.pallas_call(
        norm_back_kernel,
        grid=(length // ROW_TILE,),
        in_specs=[rows(width), rows(width), rows(width), rows(2), whole_spec(), whole_spec()],
        out_specs=[
            rows(width), rows(width), rows(width), pl.BlockSpec((8, width), lambda i: (0, 0)),
        ],
        out_shape=[
            jax.ShapeDtypeStruct((length, width), bf16),
            jax.ShapeDtypeStruct((length, width), bf16),
            jax.ShapeDtypeStruct((length, width), bf16),
            jax.ShapeDtypeStruct((8, width), f32),
        ],
        compiler_params=pltpu.CompilerParams(vmem_limit_bytes=VMEM_BYTES),
        cost_estimate=pl.CostEstimate(
            flops=30_000_000, bytes_accessed=18_000_000, transcendentals=1_000_000
        ),
        name="norm_back",
    )(y, gate_part, gated_grad, scales, gain, mask)


MESH = pl.DeviceIdType.MESH


class Ring:
    def __init__(self):
        self.count = lax.axis_size("dp")
        self.far = self.count // 2
        me = lax.axis_index("dp")
        odd = lax.rem(me, 2)
        self.me = me
        self.place = (1 - odd) * lax.div(me, 2) + odd * lax.div(2 * self.count - 1 - me, 2)

    def member(self, distance):
        n = self.count
        place = lax.rem(self.place + distance + n, n)
        back = lax.div(place, n // 2)
        return (1 - back) * 2 * place + back * (2 * n - 1 - 2 * place)

    def target(self, way):
        return {"dp": self.member(1 if way == 0 else -1)}


def partner(flip):
    f = lax.axis_index("fsdp")
    return (f, f + 1 - 2 * lax.rem(f, 2), lax.rem(f + 2, 4), 3 - f)[flip]


def greet(targets):
    barrier = pltpu.get_barrier_semaphore()
    for target in targets:
        pl.semaphore_signal(barrier, inc=1, device_id=target, device_id_type=MESH)
    pl.semaphore_wait(barrier, len(targets))


def row_slice(ref, start, size):
    return ref.at[pl.ds(pl.multiple_of(start, 16), size)]


class RingGather:
    def __init__(self, ring, wholes, send, recv, first):
        self.ring, self.wholes, self.send, self.recv = ring, wholes, send, recv
        self.first = first

    @staticmethod
    def semaphores(parts, count):
        return pltpu.SemaphoreType.DMA((parts * 4 * (count // 2),))

    def copy(self, part, way, half, hop):
        whole = self.wholes[part]
        rows = whole.shape[0] // self.ring.count
        size = rows // 2
        owner = self.ring.member(-hop if way == 0 else hop)
        place = row_slice(whole, owner * rows + half * size, size)
        at = ((part * 2 + way) * 2 + half) * self.ring.far + hop
        source = place
        if hop == 0 and part in self.first:
            source = row_slice(self.first[part], half * size, size)
        return pltpu.make_async_remote_copy(
            source, place, self.send.at[at], self.recv.at[at],
            device_id=self.ring.target(way), device_id_type=MESH,
        )

    def pieces(self, hop):
        return [
            (way, half)
            for half in (0, 1)
            for way in (0, 1)
            if hop < self.ring.far - 1 or half == way
        ]

    def start(self, part, hop):
        for way, half in self.pieces(hop):
            if hop:
                self.copy(part, way, half, hop - 1).wait_recv()
            self.copy(part, way, half, hop).start()

    def settle(self, part):
        last = self.ring.far - 1
        for way, half in self.pieces(last):
            self.copy(part, way, 1 - half, last - 1).wait_recv()

    def finish(self, part):
        last = self.ring.far - 1
        for way, half in self.pieces(last):
            self.copy(part, way, half, last).wait_recv()
        for hop in range(last + 1):
            for way, half in self.pieces(hop):
                self.copy(part, way, half, hop).wait_send()


class RingScatter:
    def __init__(self, ring, held, arrived, send, recv):
        self.ring, self.held, self.arrived = ring, held, arrived
        self.send, self.recv = send, recv

    @staticmethod
    def scratch(count, rows, columns):
        return [
            pltpu.VMEM((2, 2, rows, columns), bf16),
            pltpu.VMEM((2, count // 2 * rows - rows // 2, columns), bf16),
        ]

    def landing(self, way, hop):
        rows = self.held.shape[2]
        if hop == 0:
            return self.arrived.at[way, pl.ds((self.ring.far - 1) * rows, rows // 2)]
        return self.arrived.at[way, pl.ds((hop - 1) * rows, rows)]

    def copy(self, way, hop):
        rows = self.held.shape[2]
        size = rows // 2 if hop == 0 else rows
        at = way * self.ring.far + hop
        return pltpu.make_async_remote_copy(
            self.held.at[way, hop % 2, pl.ds(0, size)], self.landing(way, hop),
            self.send.at[at], self.recv.at[at],
            device_id=self.ring.target(way), device_id_type=MESH,
        )

    def owner(self, way, hop):
        distance = self.ring.far - hop
        return self.ring.member(distance if way == 0 else -distance)

    def start(self, hop, term):
        rows = self.held.shape[2]
        half = rows // 2
        if hop == 0:
            value = term(self.owner(0, 0), 0).astype(bf16)
            self.held[0, 0, 0:half] = value[:half]
            self.copy(0, 0).start()
            self.held[1, 0, 0:half] = value[half:]
            self.copy(1, 0).start()
            return
        for way in (0, 1):
            value = term(self.owner(way, hop), way)
            self.copy(way, hop - 1).wait_recv()
            slot = hop % 2
            if hop >= 2:
                self.copy(way, hop - 2).wait_send()
            if hop == 1:
                low = slice(way * half, (way + 1) * half)
                rest = slice((1 - way) * half, (2 - way) * half)
                self.held[way, slot, low] = (
                    value[low] + self.landing(way, 0)[...].astype(f32)
                ).astype(bf16)
                self.held[way, slot, rest] = value[rest].astype(bf16)
            else:
                self.held[way, slot] = (
                    value + self.landing(way, hop - 1)[...].astype(f32)
                ).astype(bf16)
            self.copy(way, hop).start()

    def finish(self, term):
        last = self.ring.far - 1
        value = term(self.ring.me, 0)
        for way in (0, 1):
            self.copy(way, last).wait_recv()
            value = value + self.landing(way, last)[...].astype(f32)
        for hop in range(last - 1, last + 1):
            for way in (0, 1):
                self.copy(way, hop).wait_send()
        return value


def any_specs(count):
    return [pl.BlockSpec(memory_space=pl.ANY)] * count


def tokens_exchange(own, whole, send, recv, base):
    f = lax.axis_index("fsdp")
    rows = whole.shape[0] // 4

    def one(at, source, owner, k):
        return pltpu.make_async_remote_copy(
            source, row_slice(whole, owner * rows, rows), send.at[base + at], recv.at[base + at],
            device_id={"fsdp": partner(k)}, device_id_type=MESH,
        )

    far = partner(2)
    return (
        one(0, own, f, 2), one(1, own, f, 1), one(2, row_slice(whole, far * rows, rows), far, 1),
    )


def forward_kernel(
    tokens_ref, cotangent_hbm, in_ref, out_ref, turn_ref, vectors_ref, active_ref, block_ref,
    small_all, x_all, gate_all, out_all, cotangent_all, normed_t_all, x_part_all, states_all,
    gated_all, gated_t_all, y_grad_all, gate_grad_all,
    consts_ref, head_ref, shared_taps_ref, columns_ref, rows_ref, column_ref, keys_ref, queries_ref, queries_t_ref,
    shared_part_ref, shared_pre_ref, gain_grad_ref,
    small_cut, x_cut, gate_cut, out_low, normed, cotangent, small_weight, keys_t, shared_all,
    x_part, states, y, gate_part, gated_grad, weight, gate_weight, far_weight, out_tile, turned, squares, products, stats, stats_in,
    back_tiles, back_tiles_t, padded, state, shared_wide,
    local_sem, swap_send, swap_recv, token_send, token_recv, ring_send, ring_recv,
    shared_send, shared_recv, stats_send, stats_recv, load_sem, gate_sem, store_sem,
):
    ring = Ring()
    d, f = ring.me, lax.axis_index("fsdp")
    tokens, length = tokens_ref.shape[0], normed.shape[0]
    sub, rows_out = in_ref.shape[0], out_ref.shape[0]
    width = x_cut.shape[2]
    groups, chunks = width // LANES, length // SPAN
    heads, shared = HEADS // 4, shared_taps_ref.shape[0]
    precise = partial(jnp.dot, precision=highest, preferred_element_type=f32)
    greet([{"fsdp": partner(k)} for k in (1, 2, 3)] + [ring.target(0), ring.target(1)])
    wholes = [small_all, x_all, gate_all, out_all]
    small_part, x_of, gate_of, out_of = range(4)
    rings = RingGather(ring, wholes, ring_send, ring_recv, {out_of: out_low})
    cuts = [small_cut, x_cut, gate_cut]

    def own_copy(part):
        if part == out_of:
            source, target = out_low, row_slice(out_all, d * rows_out, rows_out)
        else:
            source = cuts[part].at[f]
            target = row_slice(wholes[part], (4 * d + f) * sub, sub)
        return pltpu.make_async_copy(source, target, local_sem.at[part])

    def swap(part, k):
        return pltpu.make_async_remote_copy(
            cuts[part].at[partner(k)], row_slice(wholes[part], (4 * d + f) * sub, sub),
            swap_send.at[3 * part + k - 1], swap_recv.at[3 * part + k - 1],
            device_id={"fsdp": partner(k)}, device_id_type=MESH,
        )

    def start_swaps(part):
        for k in (2, 3, 1):
            swap(part, k).start()
        own_copy(part).start()

    def start_ring(part):
        if part != out_of:
            own_copy(part).wait()
            for k in (1, 2, 3):
                swap(part, k).wait_recv()
        rings.start(part, 0)

    def cut_channels(target, low):
        for pair in range(INNER // PAIR):
            member, at = pair % 4, pair // 4
            target[member, :, at * PAIR : (at + 1) * PAIR] = in_ref[
                :, low + pair * PAIR : low + (pair + 1) * PAIR
            ].astype(bf16)

    out_low[...] = out_ref[...].astype(bf16)
    own_copy(out_of).start()
    start_ring(out_of)
    pieces = dot_lanes(in_ref[:, 2 * INNER :].astype(bf16), turn_ref[...]).astype(bf16)
    for member in range(4):
        small_cut[member] = pieces[:, member * PAIR : (member + 1) * PAIR]
    start_swaps(small_part)
    cut_channels(x_cut, INNER)
    start_swaps(x_of)
    inputs = tokens_ref[...].astype(f32)
    inverse = lax.rsqrt(jnp.sum(inputs * inputs, axis=1, keepdims=True) / D + norm_eps)
    own_rows = pl.ds(pl.multiple_of(f * tokens, tokens), tokens)
    normed[own_rows, :] = (inputs * inverse * norm_gain_row(vectors_ref)).astype(bf16)
    normed_copies = tokens_exchange(normed.at[own_rows], normed, token_send, token_recv, 0)
    cotangent_copies = tokens_exchange(
        cotangent_hbm, cotangent, token_send, token_recv, 3
    )
    cotangent_own = pltpu.make_async_copy(cotangent_hbm, cotangent.at[own_rows], local_sem.at[4])
    cotangent_own.start()
    for copy in normed_copies[:2]:
        copy.start()
    start_ring(small_part)
    start_ring(x_of)
    cut_channels(gate_cut, 0)
    start_swaps(gate_of)

    def vector_row(row):
        return vectors_ref[pl.ds(row, 1), :]

    def own_channels(first_row):
        return jnp.concatenate(
            [vector_row(first_row + 4 * pair + f) for pair in range(width // PAIR)], axis=1
        )

    active = active_ref[0:1, 0:1]
    for k in range(CONV + 1):
        consts_ref[k : k + 1, :] = own_channels(TAPS_ROW + k * (XBC // PAIR))
    channel_head = lax.broadcasted_iota(jnp.int32, (1, width), 1) // HEAD_DIM
    consts_ref[MASK_ROW : MASK_ROW + 1, :] = (channel_head.astype(f32) < active / 4).astype(f32)
    consts_ref[GAIN_ROW : GAIN_ROW + 1, :] = own_channels(D // PAIR)
    head_at = lax.broadcasted_iota(jnp.int32, (PAIR, PAIR), 0)
    local_at = lax.broadcasted_iota(jnp.int32, (PAIR, PAIR), 1)
    own_head = local_at // 2 * 8 + 2 * f + local_at % 2
    chosen = (head_at == own_head) & (local_at < heads)
    chosen_far = (head_at == own_head + HEADS) & (local_at < heads)
    last = vector_row(LAST_ROW)
    step_bias_row = precise(last, chosen.astype(f32))
    is_head = lax.broadcasted_iota(jnp.int32, (1, PAIR), 1) < heads
    decay_row = jnp.where(is_head, -jnp.exp(precise(last, chosen_far.astype(f32))), 0.0)
    head_mask_row = (
        lax.broadcasted_iota(jnp.int32, (1, PAIR), 1).astype(f32) < active / 4
    ).astype(f32)
    skip_row = precise(vector_row(LAST_ROW + 1), chosen.astype(f32))
    spread_head = (
        lax.broadcasted_iota(jnp.int32, (PAIR, width), 0)
        == lax.broadcasted_iota(jnp.int32, (PAIR, width), 1) // HEAD_DIM
    ).astype(f32)
    consts_ref[SKIP_ROW : SKIP_ROW + 1, :] = precise(skip_row, spread_head)
    head_ref[...] = jnp.concatenate(
        [decay_row, head_mask_row, step_bias_row, jnp.zeros((5, PAIR), f32)], axis=0
    )
    shared_rows = [
        vector_row(TAPS_ROW + k * (XBC // PAIR) + INNER // PAIR + f // 2) for k in range(CONV + 1)
    ]
    shared_wide[...] = jnp.concatenate(
        shared_rows + [jnp.zeros((PAIR - CONV - 1, PAIR), f32)], axis=0
    ).T
    shared_taps_ref[...] = shared_wide[pl.ds(pl.multiple_of(f % 2 * shared, shared), shared), :]
    rings.start(small_part, 1)
    rings.start(out_of, 1)
    rings.start(small_part, 2)
    rings.start(x_of, 1)
    for hop in range(3, ring.far):
        rings.start(small_part, hop)
    normed_copies[0].wait_recv()
    normed_copies[2].start()
    for copy in cotangent_copies[:2]:
        copy.start()
    rings.settle(small_part)
    rings.finish(small_part)
    load_small = pltpu.make_async_copy(small_all, small_weight, local_sem.at[5])
    load_small.start()
    for copy in normed_copies[1:]:
        copy.wait_recv()
    load_small.wait()

    small = dot_rows(normed[...], small_weight[...]).T
    part = small[0:shared]
    pre = shared_taps_ref[:, CONV : CONV + 1] + jnp.zeros_like(part)
    for k in range(CONV):
        pre = pre + shared_taps_ref[:, k : k + 1] * shifted(part, CONV - 1 - k)
    shared_part_ref[...] = part
    shared_pre_ref[...] = pre
    shared_all[f] = (pre * jax.nn.sigmoid(pre)).astype(bf16)

    def shared_copy(k):
        return pltpu.make_async_remote_copy(
            shared_all.at[f], shared_all.at[f], shared_send.at[k - 1], shared_recv.at[k - 1],
            device_id={"fsdp": partner(k)}, device_id_type=MESH,
        )

    for k in (2, 3, 1):
        shared_copy(k).start()
    rings.start(out_of, 2)
    rings.start(x_of, 2)
    head_columns = jnp.concatenate(
        [head_ref[...], jnp.zeros((PAIR - 8, PAIR), f32)], axis=0
    ).T[0:heads]
    decay, head_mask, step_bias = (head_columns[:, i : i + 1] for i in range(3))
    logits = small[shared : shared + heads] * head_mask + step_bias
    steps = jnp.maximum(logits, 0.0) + jnp.log1p(jnp.exp(-jnp.abs(logits)))
    at_row = lax.broadcasted_iota(jnp.int32, (SPAN, SPAN), 0)
    at_lane = lax.broadcasted_iota(jnp.int32, (SPAN, SPAN), 1)
    upto = (at_row <= at_lane).astype(f32)
    rates = steps * decay
    log_sums = jnp.concatenate(
        [
            jnp.dot(
                rates[:, c * SPAN : (c + 1) * SPAN], upto, precision=highest,
                preferred_element_type=f32,
            )
            for c in range(chunks)
        ],
        axis=1,
    )
    column = jnp.concatenate(
        [log_sums, steps, logits, jnp.zeros((PAIR - 3 * heads, length), f32)], axis=0
    ).T
    column_ref[...] = column
    for group in range(groups):
        rolled = column if group == 0 else pltpu.roll(column, PAIR - group * GROUP, 1)
        columns_ref[:, group * PAIR : (group + 1) * PAIR] = rolled
        rows_ref[group * 8 : group * 8 + 8, :] = jnp.zeros((8, length), f32)
        rows_ref[group * 8 : group * 8 + GROUP, :] = log_sums[group * GROUP : (group + 1) * GROUP]
    for k in (1, 2, 3):
        shared_copy(k).wait_recv()
    keys_t[0:shared, :] = shared_all[0]
    keys_t[shared:, :] = shared_all[1]
    queries_t_ref[0:shared, :] = shared_all[2]
    queries_t_ref[shared:, :] = shared_all[3]
    keys_ref[...] = keys_t[...].T
    queries_ref[...] = queries_t_ref[...].T
    for hop in range(3, ring.far):
        rings.start(out_of, hop)
        rings.start(x_of, hop)
    start_ring(gate_of)
    cotangent_copies[0].wait_recv()
    cotangent_copies[2].start()

    def store(source, target, slot):
        return pltpu.make_async_copy(source, target, store_sem.at[slot])

    quarter = D // 4

    def turned_store(i):
        return store(turned.at[i % 2], row_slice(normed_t_all, i * quarter, quarter), i)

    for i in range(4):
        if i >= 2:
            turned_store(i - 2).wait()
        turned[i % 2] = normed[:, i * quarter : (i + 1) * quarter].T
        turned_store(i).start()
    rings.settle(x_of)
    rings.finish(x_of)

    def gate_load(distance, slot):
        owner = ring.member(distance)
        size = 4 * sub
        return pltpu.make_async_copy(
            row_slice(gate_all, owner * size, size), row_slice(gate_weight, owner * size, size),
            gate_sem.at[slot],
        )

    def start_gate(hop):
        rings.start(gate_of, hop)
        if hop == ring.far - 1:
            rings.settle(gate_of)
        if hop == 1:
            gate_load(0, 0).start()
        gate_load(-hop, 2 * hop - 1).start()
        gate_load(hop, 2 * hop).start()

    def lanes(group):
        return pl.ds(group * LANES, LANES)

    def load_columns(source, group):
        return pltpu.make_async_copy(
            source.at[:, lanes(group)], weight.at[group % 2], load_sem.at[group % 2]
        )

    def x_store(group):
        return store(x_part.at[group % 2], x_part_all.at[:, lanes(group)], 4 + group)

    def states_store(group):
        return store(states.at[group % 2], states_all.at[:, :, lanes(group)], 8 + group)

    load_columns(x_all, 0).start()
    for group in range(groups):
        if group + 1 < groups:
            load_columns(x_all, group + 1).start()
        load_columns(x_all, group).wait()
        if group >= 2:
            x_store(group - 2).wait()
            states_store(group - 2).wait()
        slot = group % 2
        x_part[slot] = dot_rows(normed[...], weight[slot])
        x_store(group).start()
        scan_forward_kernel(
            x_part.at[slot], consts_ref.at[:, lanes(group)],
            columns_ref.at[:, pl.ds(group * PAIR, PAIR)], rows_ref.at[pl.ds(group * 8, 8)],
            keys_ref, queries_ref, keys_t, block_ref, y.at[:, lanes(group)], states.at[slot],
            padded, state,
        )
        states_store(group).start()
        if group % 2 == 1 and group // 2 + 1 < ring.far - 1:
            start_gate(group // 2 + 1)

    for copy in cotangent_copies[1:]:
        copy.wait_recv()
    cotangent_own.wait()
    cotangent_store = store(cotangent, cotangent_all, 12)
    cotangent_store.start()
    rings.settle(out_of)
    rings.finish(out_of)
    own_copy(out_of).wait()

    def load_rows(group):
        return pltpu.make_async_copy(
            out_all.at[lanes(group)], out_tile.at[group % 2], load_sem.at[2 + group % 2]
        )

    load_rows(0).start()
    for group in range(groups):
        if group + 1 < groups:
            load_rows(group + 1).start()
        load_rows(group).wait()
        gated_grad[:, lanes(group)] = dot_lanes(cotangent[...], out_tile[group % 2])
    start_gate(ring.far - 1)
    far_size = 4 * sub
    far_rows = pl.ds(pl.multiple_of(ring.member(ring.far) * far_size, far_size), far_size)
    gate_weight[far_rows, :] = jnp.zeros((far_size, width), bf16)
    for hop in range(1, ring.far):
        if hop == 1:
            gate_load(0, 0).wait()
        gate_load(-hop, 2 * hop - 1).wait()
        gate_load(hop, 2 * hop).wait()
    for group in range(groups):
        gate_part[:, lanes(group)] = dot_rows(normed[...], gate_weight[:, lanes(group)])
    rings.finish(gate_of)

    def const_row(row, here):
        return consts_ref[row : row + 1, here]

    far_load = pltpu.make_async_copy(gate_all.at[far_rows], far_weight, gate_sem.at[7])
    far_load.start()
    far_load.wait()
    for group in range(groups):
        here = lanes(group)
        value = gate_part[:, here] + dot_rows(normed[:, far_rows], far_weight[:, here])
        value = value * const_row(MASK_ROW, here)
        gate_part[:, here] = value
        gated = y[:, here] * (value * jax.nn.sigmoid(value))
        product = gated * (gated_grad[:, here] * const_row(GAIN_ROW, here))
        gated = gated * gated
        gated = gated[:, :PAIR] + gated[:, PAIR:]
        product = product[:, :PAIR] + product[:, PAIR:]
        squares[...] = gated if group == 0 else squares[...] + gated
        products[...] = product if group == 0 else products[...] + product
    lane = lax.broadcasted_iota(jnp.int32, (length, PAIR), 1)
    both = jnp.where(
        lane == 0,
        jnp.sum(squares[...], axis=1, keepdims=True),
        jnp.where(lane == 1, jnp.sum(products[...], axis=1, keepdims=True), 0.0),
    )
    stats[...] = both.T[0:8]

    def stats_copy(k):
        return pltpu.make_async_remote_copy(
            stats, stats_in.at[k - 1], stats_send.at[k - 1], stats_recv.at[k - 1],
            device_id={"fsdp": partner(k)}, device_id_type=MESH,
        )

    for k in (2, 3, 1):
        stats_copy(k).start()
    for k in (1, 2, 3):
        stats_copy(k).wait_recv()
    total = (stats[...] + stats_in[0]) + (stats_in[1] + stats_in[2])
    channel_count = active * HEAD_DIM
    inverse_out = lax.rsqrt(total[0:1] / channel_count + norm_eps)
    pulls = inverse_out * inverse_out * inverse_out / channel_count * total[1:2]
    scales = jnp.concatenate(
        [inverse_out, pulls, jnp.zeros((PAIR - 2, length), f32)], axis=0
    ).T
    inverse_out, pulls = scales[:, 0:1], scales[:, 1:2]

    def back_stores(group):
        slot, at, here = group % 2, 13 + 4 * group, lanes(group)
        return [
            store(back_tiles.at[slot, 0], gated_all.at[:, here], at),
            store(back_tiles.at[slot, 1], y_grad_all.at[:, here], at + 1),
            store(back_tiles.at[slot, 2], gate_grad_all.at[:, here], at + 2),
            store(back_tiles_t.at[slot], gated_t_all.at[here], at + 3),
        ]

    gain_grad_ref[...] = jnp.zeros_like(gain_grad_ref)
    for group in range(groups):
        here, slot = lanes(group), group % 2
        if group >= 2:
            for copy in back_stores(group - 2):
                copy.wait()
        value, grad, gain = gate_part[:, here], gated_grad[:, here], const_row(GAIN_ROW, here)
        gate = jax.nn.sigmoid(value)
        silu = value * gate
        y_here = y[:, here]
        gated = y_here * silu
        scaled = gated * inverse_out
        gated_low = (scaled * gain).astype(bf16)
        back_tiles[slot, 0] = gated_low
        back_tiles_t[slot] = gated_low.T
        gain_grad_ref[0:1, here] = jnp.sum(grad * scaled, axis=0, keepdims=True)
        back = inverse_out * (grad * gain) - gated * pulls
        back_tiles[slot, 1] = (back * silu).astype(bf16)
        back_tiles[slot, 2] = (
            back * y_here * (gate * (1.0 + value * (1.0 - gate))) * const_row(MASK_ROW, here)
        ).astype(bf16)
        for copy in back_stores(group):
            copy.start()

    for i in (2, 3):
        turned_store(i).wait()
    for group in range(groups - 2, groups):
        x_store(group).wait()
        states_store(group).wait()
        for copy in back_stores(group):
            copy.wait()
    cotangent_store.wait()
    for copy in normed_copies + cotangent_copies:
        copy.wait_send()
    for k in (1, 2, 3):
        shared_copy(k).wait_send()
        stats_copy(k).wait_send()
        for i in (small_part, x_of, gate_of):
            swap(i, k).wait_send()


def last_columns(members):
    shared = 2 * STATE // members
    source = np.arange(2 * STATE + HEADS)
    head = source - 2 * STATE
    target = np.where(
        source < 2 * STATE,
        source // shared * PAIR + source % shared,
        head // 2 % members * PAIR + shared + head // (2 * members) * 2 + head % 2,
    )
    turn = np.arange(members * PAIR)[:, None] == target[None, :]
    return jnp.asarray(turn.astype(np.float32), bf16)


def norm_gain_row(vectors_ref):
    return jnp.concatenate([vectors_ref[i : i + 1, :] for i in range(D // PAIR)], axis=1)


def vector_tiles(vectors):
    rows = -(-vectors.shape[0] // PAIR)
    return jnp.pad(vectors, (0, rows * PAIR - vectors.shape[0])).reshape(rows, PAIR)


def forward(
    tokens, cotangent, in_weight, out_weight, vectors, active,
):
    count, members = lax.axis_size("dp"), lax.axis_size("fsdp")
    own, sub, rows_out = tokens.shape[0], in_weight.shape[0], out_weight.shape[0]
    length, inner, shared = own * members, INNER // members, 2 * STATE // members
    chunks, groups = length // SPAN, inner // LANES
    assert groups == 4 and count == 8 and members == 4
    turn = last_columns(members)
    sd, dma = jax.ShapeDtypeStruct, pltpu.SemaphoreType.DMA
    vmem = pltpu.VMEM
    return pl.pallas_call(
        forward_kernel,
        in_specs=[whole_spec()] + any_specs(1) + [whole_spec()] * 6,
        out_specs=any_specs(12) + [whole_spec()] * 12,
        out_shape=[
            sd((D, PAIR), bf16),
            sd((D, inner), bf16),
            sd((D, inner), bf16),
            sd((inner, D), bf16),
            sd((length, D), bf16),
            sd((D, length), bf16),
            sd((length, inner), f32),
            sd((chunks, STATE, inner), bf16),
            sd((length, inner), bf16),
            sd((inner, length), bf16),
            sd((length, inner), bf16),
            sd((length, inner), bf16),
            sd((8, inner), f32),
            sd((8, PAIR), f32),
            sd((shared, PAIR), f32),
            sd((length, groups * PAIR), f32),
            sd((groups * 8, length), f32),
            sd((length, PAIR), f32),
            sd((length, STATE), bf16),
            sd((length, STATE), bf16),
            sd((STATE, length), bf16),
            sd((shared, length), f32),
            sd((shared, length), f32),
            sd((8, inner), f32),
        ],
        scratch_shapes=[
            vmem((members, sub, PAIR), bf16),
            vmem((members, sub, inner), bf16),
            vmem((members, sub, inner), bf16),
            vmem((rows_out, D), bf16),
            vmem((length, D), bf16),
            vmem((length, D), bf16),
            vmem((D, PAIR), bf16),
            vmem((STATE, length), bf16),
            vmem((members, shared, length), bf16),
            vmem((2, length, LANES), f32),
            vmem((2, chunks, STATE, LANES), bf16),
            vmem((length, inner), f32),
            vmem((length, inner), f32),
            vmem((length, inner), f32),
            vmem((2, D, LANES), bf16),
            vmem((D, inner), bf16),
            vmem((D // count, inner), bf16),
            vmem((2, LANES, D), bf16),
            vmem((2, D // 4, length), bf16),
            vmem((length, PAIR), f32),
            vmem((length, PAIR), f32),
            vmem((8, length), f32),
            vmem((3, 8, length), f32),
            vmem((2, 3, length, LANES), bf16),
            vmem((2, LANES, length), bf16),
            vmem((length + 8, LANES), f32),
            vmem((STATE, LANES), f32),
            vmem((PAIR, PAIR), f32),
            dma((6,)),
            dma((9,)),
            dma((9,)),
            dma((6,)),
            dma((6,)),
            RingGather.semaphores(4, count),
            RingGather.semaphores(4, count),
            dma((3,)),
            dma((3,)),
            dma((3,)),
            dma((3,)),
            dma((4,)),
            dma((8,)),
            dma((13 + 4 * groups,)),
        ],
        compiler_params=pltpu.CompilerParams(
            collective_id=0, has_side_effects=True, vmem_limit_bytes=VMEM_BYTES
        ),
        name="forward",
    )(
        tokens, cotangent, in_weight, out_weight, turn, vectors,
        jnp.broadcast_to(active.astype(f32), (8, PAIR)), block_mask(),
    )


def total_squares(value):
    return jnp.sum(jnp.sum(value * value, axis=0, keepdims=True), axis=1, keepdims=True)


def flipped(member, flip):
    return member + flip - 2 * flip * lax.rem(lax.div(member, flip), 2)


def shifted(value, by):
    length = value.shape[1]
    lane = lax.broadcasted_iota(jnp.int32, value.shape, 1)
    if by == 0:
        return value
    if by > 0:
        return jnp.where(lane >= by, pltpu.roll(value, by, 1), 0.0)
    return jnp.where(lane < length + by, pltpu.roll(value, length + by, 1), 0.0)


def backward_kernel(
    rows_ref, key_ref, query_ref, query_t_ref, block_ref, pick_ref, consts_ref, column_ref, heads_ref,
    head_pick_ref, shared_part_ref, shared_pre_ref, taps_ref, vectors_own_ref, gate_gain_ref,
    weight_small_ref,
    tokens_hbm, x_hbm, y_grad_hbm, states_hbm, columns_hbm, gated_hbm, gated_t_hbm, gate_grad_hbm, normed_t_hbm,
    cotangents_hbm, cotangent_hbm, weight_out_hbm, weight_gate_hbm, weight_x_hbm,
    layer_out_hbm, token_grad_hbm, gate_back, x_back, small_back,
    out_raw_ref, vectors_ref, gains_ref, total_ref,
    x_part, y_grad, states, columns, padded, following, state_back, inner_grad,
    x_grad, key_grad, query_grad, sums_ref, rest_ref, channel_ref,
    normed_t, gate_grad, gated_t, cotangent, wide,
    kept, near_out, near_in,
    shared_out, shared_in, raw, small_t, small_n,
    vector_sum, vector_in, gain_parts, gain_total, gate_out, x_out, small_out, scalar_out, scalar_in,
    first_held, first_arrived, gate_held, gate_arrived, small_held, small_arrived,
    load_sem, scan_sem, chunk_sem, store_sem, local_sem,
    near_send, near_recv, swap_send, swap_recv, vector_send, vector_recv, gain_send, gain_recv, return_send, return_recv,
    scalar_send, scalar_recv, ring_send, ring_recv, ring_free, near_free,
):
    ring = Ring()
    d, f, count, far = ring.me, lax.axis_index("fsdp"), ring.count, ring.far
    length, width = x_grad.shape
    groups, chunks = width // LANES, length // SPAN
    rows, rows_out, tokens = D // count, width // count, tokens_hbm.shape[0]
    sub, shared, heads = gate_back.shape[1], shared_part_ref.shape[0], HEADS // 4
    precise = partial(jnp.dot, precision=highest, preferred_element_type=f32)
    halves = [pl.ds(0, width // 2), pl.ds(width // 2, width // 2)]
    out_ring, gate_ring, small_ring, *x_rings = (
        RingScatter(ring, held, arrived, ring_send.at[i], ring_recv.at[i])
        for i, (held, arrived) in enumerate(
            [
                (first_held, first_arrived),
                (gate_held, gate_arrived),
                (small_held, small_arrived),
            ]
            + [(first_held.at[:, :, :, at], first_arrived.at[:, :, at]) for at in halves]
        )
    )

    def load(source, target, at):
        return pltpu.make_async_copy(source, target, load_sem.at[at])

    def lanes(group):
        return pl.ds(group * LANES, LANES)

    def scan_loads(group):
        slot = group % 2
        return [
            pltpu.make_async_copy(source, target, scan_sem.at[slot, i])
            for i, (source, target) in enumerate(
                [
                    (y_grad_hbm.at[:, lanes(group)], y_grad.at[slot]),
                    (states_hbm.at[:, :, lanes(group)], states.at[slot]),
                    (columns_hbm.at[:, pl.ds(group * PAIR, PAIR)], columns.at[slot]),
                ]
            )
        ]

    def x_load(group):
        return pltpu.make_async_copy(x_hbm.at[:, lanes(group)], x_part, scan_sem.at[2, 0])

    def chunk_load(owner, slot):
        return pltpu.make_async_copy(
            row_slice(gated_t_hbm, owner * rows_out, rows_out), gated_t.at[slot],
            chunk_sem.at[slot],
        )

    def hop_loads(hop):
        if hop == far:
            return [chunk_load(d, 2 * (hop % 2))]
        ways = (0,) if hop == 0 else (0, 1)
        return [chunk_load(out_ring.owner(way, hop), 2 * (hop % 2) + way) for way in ways]

    gated_blocks = [x_out, gate_out]

    def gated_load(i, flip):
        return load(
            row_slice(gated_hbm, partner(flip) * tokens, tokens), gated_blocks[i], 4 + i
        )

    cotangent_load = load(cotangents_hbm, cotangent, 0)
    normed_load = load(normed_t_hbm, normed_t, 1)
    gate_grad_load = load(gate_grad_hbm, gate_grad, 2)
    out_load = load(weight_out_hbm, wide, 3)
    for copy in hop_loads(0) + [cotangent_load]:
        copy.start()
    greet(
        [{"fsdp": partner(k)} for k in (1, 2, 3)]
        + [{"dp": lax.rem(d + k, count)} for k in range(1, count)]
    )

    def rows_of(owner):
        return pl.ds(pl.multiple_of(owner * rows, rows), rows)

    def out_term(hop):
        def term(owner, way):
            value = dot_rows(gated_t[2 * (hop % 2) + way], cotangent[...])
            return jnp.concatenate([value[:, :width], value[:, width:]], axis=0)

        return term

    def out_hop(hop):
        for copy in hop_loads(hop):
            copy.wait()
        out_ring.start(hop, out_term(hop))
        for copy in hop_loads(hop + 1):
            copy.start()

    def gate_term(owner, way):
        return dot_rows(normed_t[rows_of(owner), :], gate_grad[...])

    def x_term(at):
        return lambda owner, way: dot_rows(normed_t[rows_of(owner), :], x_grad[:, at])

    def x_hop(hop):
        for x_ring, at in zip(x_rings, halves):
            x_ring.start(hop, x_term(at))

    def small_term(owner, way):
        return dot_lanes(normed_t[rows_of(owner), :], small_t[...])

    def to_partner(k, source, target, send, recv, at):
        return pltpu.make_async_remote_copy(
            source, target, send.at[at], recv.at[at],
            device_id={"fsdp": partner(k)}, device_id_type=MESH,
        )

    def near_copy(use, i):
        return to_partner(
            2 if i == 2 else 1, near_out.at[i], near_in.at[i], near_send, near_recv, 3 * use + i
        )

    def scan(group):
        slot = group % 2
        x_load(group).wait()
        for copy in scan_loads(group):
            copy.wait()
        if group + 1 < groups:
            for copy in scan_loads(group + 1):
                copy.start()
        here = lanes(group)
        scan_backward_group(
            x_part, consts_ref.at[:, here], columns.at[slot], rows_ref.at[pl.ds(group * 8, 8)],
            key_ref, query_ref, query_t_ref, block_ref, pick_ref.at[pl.ds(3 * group, 3)],
            y_grad.at[slot], states.at[slot],
            x_grad.at[:, here], key_grad, query_grad, sums_ref, rest_ref.at[:, :, here],
            channel_ref.at[:, here], padded, following, state_back, inner_grad,
        )
        if group + 1 < groups:
            x_load(group + 1).start()

    cotangent_load.wait()
    normed_load.start()
    gate_grad_load.start()
    out_hop(0)
    out_load.start()
    gated_load(0, 3).start()
    gated_load(1, 1).start()
    x_load(0).start()
    for copy in scan_loads(0):
        copy.start()
    scan_backward_start(key_grad, query_grad, sums_ref, inner_grad)
    normed_load.wait()
    gate_grad_load.wait()
    gate_ring.start(0, gate_term)

    def added_block(i):
        return dot_rows(gated_blocks[i][...], wide[...])

    out_load.wait()
    for i, flip in ((0, 3), (1, 1)):
        gated_load(i, flip).wait()
        near_out[1 - i] = added_block(i).astype(bf16)
        near_copy(0, 1 - i).start()
        gated_load(i, (2, 0)[i]).start()
    out_hop(1)
    scan(0)
    gate_ring.start(1, gate_term)
    gated_load(0, 2).wait()
    value = added_block(0)
    near_copy(0, 1).wait_recv()
    near_out[2] = (value + near_in[1].astype(f32)).astype(bf16)
    near_copy(0, 2).start()
    gated_load(1, 0).wait()
    kept[...] = added_block(1)
    half = D // 4

    def weight_tiles(source, target, at):
        return [
            load(
                source.at[pl.ds(i * half, half)],
                target.at[pl.ds(i // 2 * half, half), pl.ds(i % 2 * width, width)], at + i,
            )
            for i in range(4)
        ]

    gate_tiles = weight_tiles(weight_gate_hbm, wide, 6)
    for copy in gate_tiles:
        copy.start()
    out_hop(2)
    scan(1)
    gate_ring.start(2, gate_term)
    scan(2)
    for hop in range(3, far):
        out_hop(hop)
    scan(3)
    scan_backward_finish(key_ref, query_ref, key_grad, query_grad, inner_grad)

    for i, ref in ((0, key_grad), (2, query_grad)):
        across = ref[...].T
        for j in (0, 1):
            shared_out[i + j] = across[j * shared : (j + 1) * shared].astype(bf16)

    def shared_copy(k):
        return to_partner(
            k, shared_out.at[partner(k)], shared_in.at[k - 1], swap_send, swap_recv, k - 1
        )

    for k in (2, 3, 1):
        shared_copy(k).start()
    for copy in hop_loads(far):
        copy.wait()
    value = out_ring.finish(out_term(far))
    out_raw_ref[...] = jnp.concatenate([value[:rows_out], value[rows_out:]], axis=1)
    squares = total_squares(value)
    for way in (0, 1):
        pl.semaphore_signal(
            ring_free.at[way], inc=1, device_id=ring.target(1 - way), device_id_type=MESH
        )
    x_tiles = weight_tiles(weight_x_hbm, cotangent, 10)
    for copy in x_tiles:
        copy.start()
    for way in (0, 1):
        pl.semaphore_wait(ring_free.at[way], 1)
    x_hop(0)

    for hop in range(3, far):
        gate_ring.start(hop, gate_term)

    at_row = lax.broadcasted_iota(jnp.int32, (SPAN, SPAN), 0)
    at_lane = lax.broadcasted_iota(jnp.int32, (SPAN, SPAN), 1)
    later = (at_lane >= at_row).astype(f32)
    earlier = (at_lane < at_row).astype(f32)
    rest = precise(
        jnp.concatenate([rest_ref[c] for c in range(chunks)], axis=0), head_pick_ref[...]
    )
    decay, head_mask = heads_ref[0:1, :], heads_ref[1:2, :]
    step_bias_grad = jnp.zeros((1, PAIR), f32)
    decay_grad = jnp.zeros((1, PAIR), f32)
    for c in range(chunks):
        here = slice(c * SPAN, (c + 1) * SPAN)
        sums = sums_ref[here, :]
        log_grad = (
            precise(later, sums)
            + pltpu.roll(precise(earlier, sums), PAIR - heads, 1)
            + rest[c : c + 1]
        )
        steps = pltpu.roll(column_ref[here, :], PAIR - heads, 1)
        logits = pltpu.roll(column_ref[here, :], PAIR - 2 * heads, 1)
        raw_grad = (decay * log_grad + pltpu.roll(sums, PAIR - 2 * heads, 1)) * jax.nn.sigmoid(
            logits
        )
        step_bias_grad = step_bias_grad + jnp.sum(raw_grad, axis=0, keepdims=True)
        decay_grad = decay_grad + jnp.sum(steps * log_grad, axis=0, keepdims=True)
        raw[here, :] = raw_grad * head_mask
    decay_grad = decay_grad * decay

    for k in (2, 3, 1):
        shared_copy(k).wait_recv()
    part, pre = shared_part_ref[...], shared_pre_ref[...]
    gate = jax.nn.sigmoid(pre)
    pre_grad = shared_out[f].astype(f32)
    for k in (1, 2, 3):
        pre_grad = pre_grad + shared_in[k - 1].astype(f32)
    pre_grad = pre_grad * (gate * (1.0 + pre * (1.0 - gate)))
    shared_grad = jnp.zeros_like(pre_grad)
    lane = lax.broadcasted_iota(jnp.int32, (shared, PAIR), 1)
    shared_sums = jnp.where(lane == CONV, jnp.sum(pre_grad, axis=1, keepdims=True), 0.0)
    for k in range(CONV):
        shift = CONV - 1 - k
        shared_grad = shared_grad + taps_ref[:, k : k + 1] * shifted(pre_grad, -shift)
        shared_sums = shared_sums + jnp.where(
            lane == k, jnp.sum(pre_grad * shifted(part, shift), axis=1, keepdims=True), 0.0
        )
    small_t[0:shared, :] = shared_grad.astype(bf16)
    small_t[shared:, :] = raw[...].T[0 : PAIR - shared].astype(bf16)
    small_n[...] = small_t[...].T
    small_ring.start(0, small_term)

    vector_sum[...] = jnp.zeros_like(vector_sum)
    vector_sum[0:1, :] = gate_gain_ref[0:1, :]
    vector_sum[1 : CONV + 3, :] = channel_ref[0 : CONV + 2, :]
    vector_sum[15:16, 0:PAIR] = step_bias_grad
    vector_sum[15:16, PAIR : 2 * PAIR] = decay_grad
    across = jnp.concatenate([shared_sums, jnp.zeros((PAIR - shared, PAIR), f32)], axis=0)
    vector_sum[16:24, 0:PAIR] = across.T[0:8]
    flips = []
    while 1 << len(flips) < count:
        flips.append(1 << len(flips))

    def vector_copy(step):
        return pltpu.make_async_remote_copy(
            vector_in.at[step, 0], vector_in.at[step, 1], vector_send.at[step],
            vector_recv.at[step],
            device_id={"dp": flipped(d, flips[step])}, device_id_type=MESH,
        )

    def vector_step(step):
        if step:
            vector_copy(step - 1).wait_recv()
            vector_sum[...] = vector_sum[...] + vector_in[step - 1, 1]
        if step < len(flips):
            vector_in[step, 0] = vector_sum[...]
            vector_copy(step).start()

    def vector_spread(k):
        return to_partner(
            k, vector_sum, vectors_ref.at[f], vector_send, vector_recv, len(flips) + k - 1
        )

    vector_step(0)

    near_copy(0, 0).wait_send()
    tokens_load = load(tokens_hbm, near_out.at[0], 15)
    tokens_load.start()
    near_copy(0, 0).wait_recv()
    near_copy(0, 2).wait_recv()
    tokens_load.wait()
    value = near_out[0].astype(f32) + (
        (kept[...] + near_in[0].astype(f32)) + near_in[2].astype(f32)
    )
    for k in (0, 1):
        pl.semaphore_signal(
            near_free.at[k], inc=1, device_id={"fsdp": partner(k + 1)}, device_id_type=MESH
        )
    for i in (1, 2):
        near_copy(0, i).wait_send()
    near_out[2] = value.astype(bf16)
    layer_store = pltpu.make_async_copy(near_out.at[2], layer_out_hbm, store_sem.at[0])
    layer_store.start()

    for copy in gate_tiles + x_tiles:
        copy.wait()

    def back_block(flip, target, kind):
        here = pl.ds(pl.multiple_of(partner(flip) * tokens, tokens), tokens)
        for i in range(4):
            at = (slice(i // 2 * half, (i // 2 + 1) * half), slice(i % 2 * width, (i % 2 + 1) * width))
            value = (
                dot_lanes(gate_grad[here, :], wide[at])
                + dot_lanes(x_grad[here, :], cotangent[at])
                + dot_lanes(small_n[here, :], weight_small_ref[i * half : (i + 1) * half, :])
            )
            target[:, i * half : (i + 1) * half] = value.astype(kind)

    for k in (0, 1):
        pl.semaphore_wait(near_free.at[k], 1)
    for i, flip in ((1, 3), (0, 1)):
        back_block(flip, near_out.at[i], bf16)
        near_copy(1, i).start()
    small_ring.start(1, small_term)
    vector_step(1)
    back_block(2, kept, f32)
    near_copy(1, 1).wait_recv()
    layer_store.wait()
    near_out[2] = (kept[...] + near_in[1].astype(f32)).astype(bf16)
    near_copy(1, 2).start()
    x_hop(1)
    vector_step(2)
    back_block(0, kept, f32)
    near_copy(1, 1).wait_send()
    own_load = load(cotangent_hbm, near_out.at[1], 14)
    own_load.start()
    near_copy(1, 0).wait_send()
    tokens_load = load(tokens_hbm, near_out.at[0], 15)
    tokens_load.start()

    returned = [(gate_out, gate_back), (small_out, small_back)] + [
        (x_out.at[:, at], x_back.at[:, :, at]) for at in halves
    ]

    def return_copy(part, k):
        source, target = returned[part]
        return to_partner(
            k, row_slice(source, partner(k) * sub, sub), target.at[f],
            return_send, return_recv, part * 3 + k - 1,
        )

    def own_copy(part):
        source, target = returned[part]
        return pltpu.make_async_copy(
            row_slice(source, f * sub, sub), target.at[f], local_sem.at[part]
        )

    def give_back(part, value):
        returned[part][0][...] = value.astype(bf16)
        for k in (2, 3, 1):
            return_copy(part, k).start()
        own_copy(part).start()

    value = gate_ring.finish(gate_term)
    squares = squares + total_squares(value)
    give_back(0, value)
    small_ring.start(2, small_term)
    x_hop(2)
    vector_step(3)
    for k in (2, 3, 1):
        vector_spread(k).start()
    vectors_ref[f] = vector_sum[...]
    near_copy(1, 0).wait_recv()
    near_copy(1, 2).wait_recv()
    own_load.wait()
    tokens_load.wait()
    inputs = near_out[0].astype(f32)
    inverse = lax.rsqrt(jnp.sum(inputs * inputs, axis=1, keepdims=True) / D + norm_eps)
    normed_grad = (kept[...] + near_in[0].astype(f32)) + near_in[2].astype(f32)
    pulled = normed_grad * norm_gain_row(vectors_own_ref)
    scaled = inputs * inverse
    input_grad = inverse * (
        pulled - scaled * (jnp.sum(pulled * scaled, axis=1, keepdims=True) / D)
    )
    near_out[1] = (near_out[1].astype(f32) + input_grad).astype(bf16)
    token_store = pltpu.make_async_copy(near_out.at[1], token_grad_hbm, store_sem.at[1])
    token_store.start()
    gain_grad = jnp.sum(normed_grad * scaled, axis=0, keepdims=True)

    for i in range(8):
        gain_parts[0, i : i + 1, :] = gain_grad[:, i * (D // 8) : (i + 1) * (D // 8)]

    def over_dp(k, source, target, send, recv, at):
        member = d
        for bit in flips:
            if k & bit:
                member = flipped(member, bit)
        return pltpu.make_async_remote_copy(
            source, target, send.at[at], recv.at[at],
            device_id={"dp": member}, device_id_type=MESH,
        )

    def gain_copy(k):
        return over_dp(k, gain_parts.at[0], gain_parts.at[k], gain_send, gain_recv, k)

    def paired(parts):
        while len(parts) > 1:
            parts = [parts[i] + parts[i + 1] for i in range(0, len(parts), 2)]
        return parts[0]

    for k in range(count - 1, 0, -1):
        gain_copy(k).start()
    for hop in range(3, far):
        small_ring.start(hop, small_term)
        x_hop(hop)
    for k in range(1, count):
        gain_copy(k).wait_recv()
    gain_total[...] = paired([gain_parts[k] for k in range(count)])

    def gain_spread(k):
        return to_partner(
            k, gain_total, gains_ref.at[f], gain_send, gain_recv, count + k - 1
        )

    for k in (2, 3, 1):
        gain_spread(k).start()
    gains_ref[f] = gain_total[...]

    value = small_ring.finish(small_term)
    squares = squares + total_squares(value)
    give_back(1, value)
    for part, (x_ring, at) in enumerate(zip(x_rings, halves)):
        value = x_ring.finish(x_term(at))
        give_back(2 + part, value)
        squares = squares + total_squares(value)

    total = jnp.broadcast_to(squares, (8, PAIR))
    scalar_out[0] = total

    def near_scalar(k):
        return to_partner(
            k, scalar_out.at[0], scalar_in.at[k], scalar_send, scalar_recv, k
        )

    for k in (2, 3, 1):
        near_scalar(k).start()
    for k in (2, 3, 1):
        near_scalar(k).wait_recv()
    total = (total + scalar_in[1]) + (scalar_in[2] + scalar_in[3])
    scalar_out[1] = total

    def far_scalar(k):
        return over_dp(
            k, scalar_out.at[1], scalar_in.at[3 + k], scalar_send, scalar_recv, 3 + k
        )

    for k in range(count - 1, 0, -1):
        far_scalar(k).start()
    parts = [total]
    for k in range(1, count):
        far_scalar(k).wait_recv()
        parts.append(scalar_in[3 + k])
    total_ref[...] = paired(parts)

    for k in (1, 2, 3):
        vector_spread(k).wait_recv()
        vector_spread(k).wait_send()
        gain_spread(k).wait_recv()
        gain_spread(k).wait_send()
        shared_copy(k).wait_send()
        near_scalar(k).wait_send()
        for i in range(4):
            return_copy(i, k).wait_recv()
            return_copy(i, k).wait_send()
    for k in range(1, count):
        far_scalar(k).wait_send()
        gain_copy(k).wait_send()
    near_copy(1, 2).wait_send()
    for i in range(4):
        own_copy(i).wait()
    for step in range(len(flips)):
        vector_copy(step).wait_send()
    token_store.wait()


def backward(
    scan_inputs, queries_t, column, heads, shared_part, shared_pre, taps, vectors, gate_gain, tokens,
    weight_small, x, y_grad, states, gated, gated_t, gate_grad, normed_t, cotangents, cotangent,
    weight_out, weight_gate, weight_x,
):
    consts, columns, rows_t, keys, queries = scan_inputs
    length, width = x.shape
    chunks, groups = length // SPAN, width // LANES
    count, members = lax.axis_size("dp"), lax.axis_size("fsdp")
    rows, rows_out = D // count, width // count
    sub, own, shared = rows // members, tokens.shape[0], shared_part.shape[0]
    far = count // 2
    hops = max(count - 1, 1).bit_length()
    assert groups == 4 and count == 8 and members == 4 and 2 * rows_out == rows and 2 * width == D
    head_pick = jnp.asarray(
        (np.arange(width)[:, None] // HEAD_DIM == np.arange(PAIR)[None, :]).astype(np.float32)
    )
    dma, vmem, sd = pltpu.SemaphoreType.DMA, pltpu.VMEM, jax.ShapeDtypeStruct
    return pl.pallas_call(
        backward_kernel,
        in_specs=[whole_spec()] * 16 + any_specs(14),
        out_specs=any_specs(5) + [whole_spec()] * 4,
        out_shape=[
            sd((own, D), bf16),
            sd((own, D), bf16),
            sd((members, sub, width), bf16),
            sd((members, sub, width), bf16),
            sd((members, sub, PAIR), bf16),
            sd((rows_out, D), f32),
            sd((members, 24, width), f32),
            sd((members, 8, D // 8), f32),
            sd((8, PAIR), f32),
        ],
        scratch_shapes=[
            vmem((length, LANES), f32),
            vmem((2, length, LANES), bf16),
            vmem((2, chunks, STATE, LANES), bf16),
            vmem((2, length, PAIR), f32),
            vmem((length + 8, LANES), f32),
            vmem((8, LANES), f32),
            vmem((STATE, LANES), f32),
            vmem((chunks, SPAN, SPAN), f32),
            vmem((length, width), bf16),
            vmem((length, STATE), f32),
            vmem((length, STATE), f32),
            vmem((length, PAIR), f32),
            vmem((chunks, 1, width), f32),
            vmem((8, width), f32),
            vmem((D, length), bf16),
            vmem((length, width), bf16),
            vmem((4, rows_out, length), bf16),
            vmem((length, D), bf16),
            vmem((width, D), bf16),
            vmem((own, D), f32),
            vmem((3, own, D), bf16),
            vmem((3, own, D), bf16),
            vmem((members, shared, length), bf16),
            vmem((members - 1, shared, length), bf16),
            vmem((length, PAIR), f32),
            vmem((PAIR, length), bf16),
            vmem((length, PAIR), bf16),
            vmem((24, width), f32),
            vmem((hops, 2, 24, width), f32),
            vmem((count, 8, D // 8), f32),
            vmem((8, D // 8), f32),
            vmem((rows, width), bf16),
            vmem((rows, width), bf16),
            vmem((rows, PAIR), bf16),
            vmem((2, 8, PAIR), f32),
            vmem((3 + count, 8, PAIR), f32),
        ]
        + RingScatter.scratch(count, rows, width) * 2
        + RingScatter.scratch(count, rows, PAIR)
        + [
            dma((16,)),
            dma((3, 3)),
            dma((4,)),
            dma((2,)),
            dma((4,)),
            dma((6,)),
            dma((6,)),
            dma((3,)),
            dma((3,)),
            dma((hops + 3,)),
            dma((hops + 3,)),
            dma((count + 3,)),
            dma((count + 3,)),
            dma((12,)),
            dma((12,)),
            dma((3 + count,)),
            dma((3 + count,)),
            dma((5, 2 * far)),
            dma((5, 2 * far)),
            pltpu.SemaphoreType.REGULAR((2,)),
            pltpu.SemaphoreType.REGULAR((2,)),
        ],
        compiler_params=pltpu.CompilerParams(
            collective_id=1, has_side_effects=True, vmem_limit_bytes=VMEM_BYTES
        ),
        name="backward",
    )(
        rows_t, keys, queries, queries_t, block_mask(), pick_masks(groups), consts, column, heads,
        head_pick, shared_part, shared_pre, taps, vectors, gate_gain, weight_small,
        tokens, x, y_grad, states, columns, gated, gated_t, gate_grad, normed_t, cotangents, cotangent,
        weight_out, weight_gate, weight_x,
    )


OPTIMIZER_STEPS = 4


def optimizer_kernel(
    squares_ref, parts_ref, gains_ref, vector_ref, vector_first_ref, vector_second_ref, turn_ref,
    gate_ref, x_ref, small_ref, in_ref, in_first_ref, in_second_ref,
    out_raw_ref, out_ref, out_first_ref, out_second_ref, layer_ref, token_ref,
    norm_ref, vector_grad_ref, vector_moment_ref, vector_square_ref, vector_master_ref,
    in_grad_ref, in_moment_ref, in_square_ref, in_master_ref, in_rounded_ref,
    out_grad_ref, out_moment_ref, out_square_ref, out_master_ref, out_rounded_ref,
    layer_out_ref, token_out_ref,
    joined, factor_ref, in_raw,
):
    members = parts_ref.shape[0]
    pairs = INNER // PAIR
    shared, heads = 2 * STATE // members, HEADS // members
    layer_out_ref[...] = layer_ref[...]
    token_out_ref[...] = token_ref[...]

    @pl.when(pl.program_id(0) == 0)
    def _():
        joined[...] = jnp.zeros_like(joined)
        width = parts_ref.shape[2]
        for i in range(D // PAIR):
            row = i * PAIR // (D // 8)
            lanes = slice(i * PAIR % (D // 8), i * PAIR % (D // 8) + PAIR)
            value = gains_ref[0, row : row + 1, lanes]
            for member in range(1, members):
                value = value + gains_ref[member, row : row + 1, lanes]
            joined[i : i + 1, :] = value

        def put_channels(first_row, row):
            for pair in range(pairs):
                at = pair // members
                joined[first_row + pair : first_row + pair + 1, :] = parts_ref[
                    pair % members, row : row + 1, at * PAIR : (at + 1) * PAIR
                ]

        put_channels(D // PAIR, 0)
        each = PAIR // shared
        for k in range(CONV + 1):
            first_row = TAPS_ROW + k * (XBC // PAIR)
            put_channels(first_row, 1 + k)
            for i in range(members // each):
                joined[first_row + pairs + i : first_row + pairs + i + 1, :] = jnp.concatenate(
                    [
                        parts_ref[i * each + j, 16 + k : 17 + k, 0:shared]
                        for j in range(each)
                    ],
                    axis=1,
                )
        precise = partial(jnp.dot, precision=highest, preferred_element_type=f32)
        last, skips = jnp.zeros((1, PAIR), f32), jnp.zeros((1, PAIR), f32)
        local_at = lax.broadcasted_iota(jnp.int32, (PAIR, PAIR), 0)
        head_at = lax.broadcasted_iota(jnp.int32, (PAIR, PAIR), 1)
        channel_head = lax.broadcasted_iota(jnp.int32, (width, PAIR), 0) // HEAD_DIM
        wide_at = lax.broadcasted_iota(jnp.int32, (width, PAIR), 1)
        for member in range(members):
            home = local_at // 2 * 2 * members + 2 * member + local_at % 2
            known = local_at < heads
            biases = parts_ref[member, 15:16, 0:PAIR]
            decays = parts_ref[member, 15:16, PAIR : 2 * PAIR]
            last = last + precise(biases, ((head_at == home) & known).astype(f32))
            last = last + precise(decays, ((head_at == home + HEADS) & known).astype(f32))
            home = channel_head // 2 * 2 * members + 2 * member + channel_head % 2
            skips = skips + precise(
                parts_ref[member, CONV + 2 : CONV + 3, :], (wide_at == home).astype(f32)
            )
        joined[LAST_ROW : LAST_ROW + 1, :] = last
        joined[LAST_ROW + 1 : LAST_ROW + 2, :] = skips
        vector_raw = joined[...]
        norm = jnp.sqrt(squares_ref[...] + total_squares(vector_raw))
        norm_ref[0, 0] = norm[0, 0]
        factor = jnp.minimum(1.0, clip_norm / (norm + 1e-06))
        factor_ref[...] = factor
        grad = vector_raw * factor[0:1, 0:1]
        vector_grad_ref[...] = grad
        vector_moment_ref[...], vector_square_ref[...], vector_master_ref[...] = adamw(
            vector_ref[...], vector_first_ref[...], vector_second_ref[...], grad, rate_vectors
        )

    factor = factor_ref[0:1, 0:1]
    for pair in range(pairs):
        at = pair // members
        lanes, held = slice(pair * PAIR, (pair + 1) * PAIR), slice(at * PAIR, (at + 1) * PAIR)
        in_raw[:, lanes] = gate_ref[pair % members, :, held].astype(f32)
        in_raw[:, INNER + pair * PAIR : INNER + (pair + 1) * PAIR] = x_ref[
            pair % members, :, held
        ].astype(f32)
    small = jnp.concatenate([small_ref[i] for i in range(members)], axis=1)
    in_raw[:, 2 * INNER :] = dot_rows(small, turn_ref[...])
    grad = in_raw[...] * factor
    in_grad_ref[...] = grad
    in_moment_ref[...], in_square_ref[...], master = adamw(
        in_ref[...], in_first_ref[...], in_second_ref[...], grad, rate_in_proj
    )
    in_master_ref[...] = master
    in_rounded_ref[...] = master.astype(bf16)
    grad = out_raw_ref[...] * factor
    out_grad_ref[...] = grad
    out_moment_ref[...], out_square_ref[...], master = adamw(
        out_ref[...], out_first_ref[...], out_second_ref[...], grad, rate_out_proj
    )
    out_master_ref[...] = master
    out_rounded_ref[...] = master.astype(bf16)


def optimizer(squares, parts, gains, vectors, gate, x, small, in_state, out_raw, out_state, passed):
    members, rows, width = x.shape
    in_shape, out_shape = in_state[0].shape, out_state[0].shape
    steps = OPTIMIZER_STEPS
    step_rows = rows // steps
    piece = lambda lanes: pl.BlockSpec((members, step_rows, lanes), lambda i: (0, i, 0))
    in_flat = pl.BlockSpec((step_rows, in_shape[1]), lambda i: (i, 0))
    out_flat = pl.BlockSpec((out_shape[0] // steps, out_shape[1]), lambda i: (i, 0))
    row_flat = pl.BlockSpec((passed[0].shape[0] // steps, D), lambda i: (i, 0))
    sd = jax.ShapeDtypeStruct
    vector_shape = sd(vectors[0].shape, f32)
    return pl.pallas_call(
        optimizer_kernel,
        grid=(steps,),
        in_specs=[whole_spec()] * 7
        + [piece(width), piece(width), piece(PAIR)]
        + [in_flat] * 3
        + [out_flat] * 4
        + [row_flat] * 2,
        out_specs=[pl.BlockSpec(memory_space=pltpu.SMEM)]
        + [whole_spec()] * 4
        + [in_flat] * 5
        + [out_flat] * 5
        + [row_flat] * 2,
        out_shape=[sd((1, 1), f32)]
        + [vector_shape] * 4
        + [sd(in_shape, f32)] * 4
        + [sd(in_shape, bf16)]
        + [sd(out_shape, f32)] * 4
        + [sd(out_shape, bf16)]
        + [sd(v.shape, v.dtype) for v in passed],
        scratch_shapes=[
            pltpu.VMEM(vectors[0].shape, f32),
            pltpu.VMEM((8, PAIR), f32),
            pltpu.VMEM((step_rows, in_shape[1]), f32),
        ],
        compiler_params=pltpu.CompilerParams(vmem_limit_bytes=VMEM_BYTES),
        name="optimizer",
    )(
        squares, parts, gains, *vectors, last_columns(members), gate, x, small, *in_state, out_raw,
        *out_state, *passed,
    )


def unpack(vectors):
    offset = D + INNER
    taps_end = offset + CONV * XBC
    heads_start = taps_end + XBC
    norm_gain = vectors[:D]
    gate_gain = vectors[D:offset]
    filter_taps = vectors[offset:taps_end].reshape(CONV, XBC)
    filter_bias = vectors[taps_end:heads_start]
    step_bias = vectors[heads_start : heads_start + HEADS]
    decay_log = vectors[heads_start + HEADS : heads_start + 2 * HEADS]
    skip_gain = vectors[heads_start + 2 * HEADS : heads_start + 3 * HEADS]
    return (norm_gain, gate_gain, filter_taps, filter_bias, step_bias, decay_log, skip_gain)


def adamw(weight, moment, square, gradient, step_rate):
    moment_new = beta_first * moment + (1.0 - beta_first) * gradient
    square_new = beta_second * square + (1.0 - beta_second) * gradient * gradient
    moment_hat = moment_new / (1.0 - beta_first**STEP)
    square_hat = square_new / (1.0 - beta_second**STEP)
    weight_new = weight - step_rate * (
        moment_hat / (jnp.sqrt(square_hat) + adam_eps) + weight_decay * weight
    )
    return (moment_new, square_new, weight_new)


def on_device(
    tokens,
    widths,
    cotangent,
    in_weight,
    in_first,
    in_second,
    out_weight,
    out_first,
    out_second,
    vectors,
    vector_first,
    vector_second,
):
    fsdp = lax.axis_size("fsdp")
    me = lax.axis_index("fsdp")
    heads = HEADS // fsdp
    inner = INNER // fsdp
    shared = 2 * STATE // fsdp
    pairs = HEADS // 2 // fsdp
    rows_in, rows_out = in_weight.shape[0], out_weight.shape[0]
    length = tokens.shape[0] * fsdp
    chunks = length // SPAN
    in_kernels = uses_ring("dp") and rows_out == PAIR and rows_in % 16 == 0

    def own_channels(v):
        lead = v.shape[:-1]
        cut = v.reshape(lead + (pairs, fsdp, PAIR))
        return lax.dynamic_index_in_dim(cut, me, len(lead) + 1, False).reshape(lead + (inner,))

    def own_heads(v):
        return lax.dynamic_index_in_dim(v.reshape(pairs, fsdp, 2), me, 1, False).reshape(heads)

    def own_shared(v):
        return lax.dynamic_slice_in_dim(v, me * shared, shared, v.ndim - 1)

    norm_gain, gate_gain, filter_taps, filter_bias, step_bias, decay_log, skip_gain = unpack(
        vectors
    )
    gain_own = own_channels(gate_gain)[None]
    taps_own = own_channels(filter_taps[:, :INNER])
    bias_own = own_channels(filter_bias[:INNER])[None]
    taps_shared = own_shared(filter_taps[:, INNER:])
    bias_shared = own_shared(filter_bias[INNER:])
    step_bias_own, decay_own = own_heads(step_bias), -jnp.exp(own_heads(decay_log))
    skip_own = jnp.repeat(own_heads(skip_gain), HEAD_DIM)[None]

    width_index = widths[0]
    active = HEADS // 8 * jnp.left_shift(jnp.int32(1), width_index)
    head_mask = (jnp.arange(heads, dtype=jnp.int32) < active // fsdp).astype(f32)
    mask = jnp.repeat(head_mask, HEAD_DIM)[None]
    channel_count = (active * HEAD_DIM).astype(f32)

    inputs = tokens.astype(f32)
    inverse_in = lax.rsqrt(jnp.mean(inputs * inputs, axis=-1, keepdims=True) + norm_eps)

    if in_kernels:
        vector_state = [vector_tiles(v) for v in (vectors, vector_first, vector_second)]
        (
            weight_shared, weight_x, weight_gate, weight_out, cotangents, normed_t, x_part, states,
            gated_low, gated_t, y_grad, gate_grad, consts, head_consts, shared_taps, head_columns,
            head_rows, head_all, keys, queries, queries_t, shared_part, shared_pre, gain_grad,
        ) = forward(tokens, cotangent, in_weight, out_weight, vector_state[0], active)
        scan_inputs = (consts, head_columns, head_rows, keys, queries)
    else:
        in_low = in_weight.astype(bf16)
        shared_cut = jnp.concatenate(
            [
                in_low[:, 2 * INNER : 2 * INNER + 2 * STATE]
                .reshape(rows_in, fsdp, shared)
                .transpose(1, 0, 2),
                in_low[:, 2 * INNER + 2 * STATE :]
                .reshape(rows_in, pairs, fsdp, 2)
                .transpose(2, 0, 1, 3)
                .reshape(fsdp, rows_in, heads),
            ],
            axis=2,
        )

        def channel_cut(part):
            return (
                part.reshape(rows_in, pairs, fsdp, PAIR)
                .transpose(2, 0, 1, 3)
                .reshape(fsdp, rows_in, inner)
            )

        def gathered(cut):
            block = exchanged(cut, "fsdp")
            return gather_rows(block.reshape(fsdp * rows_in, cut.shape[2]), "dp")

        normed_own = (inputs * inverse_in * norm_gain[None, :]).astype(bf16)
        x_cut = channel_cut(in_low[:, INNER : 2 * INNER])
        gate_cut = channel_cut(in_low[:, :INNER])
        out_low = out_weight.astype(bf16)

        weight_shared = gathered(shared_cut)
        weight_x = gathered(x_cut)
        weight_gate = gathered(gate_cut)
        weight_out = lax.dynamic_index_in_dim(
            lax.all_gather(out_low, ("dp", "fsdp"), axis=0, tiled=True).reshape(
                pairs, fsdp, PAIR, D
            ),
            me,
            1,
            False,
        ).reshape(inner, D)
        normed = spread(normed_own, "fsdp").reshape(length, D)
        cotangents = spread(cotangent, "fsdp").reshape(length, D)

        small = lax.dot_general(
            weight_shared, normed, (((0,), (1,)), ((), ())), preferred_element_type=f32
        )
        shared_part = small[:shared]
        step_raw = small[shared : shared + heads] * head_mask[:, None]
        shared_padded = jnp.pad(shared_part, ((0, 0), (CONV - 1, 0)))
        shared_pre = bias_shared[:, None] + sum(
            taps_shared[k][:, None] * shared_padded[:, k : k + length] for k in range(CONV)
        )
        shared_gate = jax.nn.sigmoid(shared_pre)
        shared_all = spread_small((shared_pre * shared_gate).astype(bf16), "fsdp").reshape(
            2 * STATE, length
        )
        keys_t, queries_t = shared_all[:STATE], shared_all[STATE:]
        keys, queries = keys_t.T, queries_t.T
        step_logits = step_raw + step_bias_own[:, None]
        step_sizes = jax.nn.softplus(step_logits)
        upto = (jnp.arange(SPAN)[:, None] <= jnp.arange(SPAN)[None, :]).astype(f32)
        log_sums = jnp.dot(
            (step_sizes * decay_own[:, None]).reshape(heads, chunks, SPAN), upto, precision=highest
        ).reshape(heads, length)
        groups = heads // GROUP
        head_all = jnp.concatenate(
            [log_sums, step_sizes, step_logits, jnp.zeros((PAIR - 3 * heads, length), f32)]
        ).T
        head_columns = jnp.concatenate(
            [jnp.roll(head_all, -group * GROUP, axis=1) for group in range(groups)], axis=1
        )
        head_rows = jnp.pad(
            log_sums.reshape(groups, GROUP, length), ((0, 0), (0, 8 - GROUP), (0, 0))
        ).reshape(groups * 8, length)

        consts = jnp.concatenate([taps_own, bias_own, mask, skip_own, gain_own])
        scan_inputs = (consts, head_columns, head_rows, keys, queries)
        x_part = jnp.dot(normed, weight_x, preferred_element_type=f32)
        y, states = scan_forward(x_part, *scan_inputs, keys_t)
        gate_part, gated_grad, stats = gate_forward(
            normed, weight_gate, cotangents, weight_out, y, gain_own, mask
        )
        stats = summed(stats[:, :2].T, "fsdp")
        inverse_out = lax.rsqrt(stats[0] / channel_count + norm_eps)
        pull = inverse_out**3 / channel_count * stats[1]
        gated_low, y_grad, gate_grad, gain_grad = norm_back(
            y, gate_part, gated_grad, jnp.stack([inverse_out, pull], axis=1), gain_own, mask
        )

        def in_term(grad):
            return lax.dot_general(
                normed, grad, (((0,), (0,)), ((), ())), preferred_element_type=f32
            ).astype(bf16)

    if in_kernels:
        (
            layer_out, token_grad, gate_back, x_back, small_back, out_raw, vector_rows, gains,
            squares,
        ) = backward(
            scan_inputs, queries_t, head_all, head_consts, shared_part, shared_pre, shared_taps,
            vector_state[0], gain_grad, tokens, weight_shared, x_part, y_grad, states, gated_low,
            gated_t, gate_grad, normed_t, cotangents, cotangent, weight_out, weight_gate, weight_x,
        )
        norm, *rest = optimizer(
            squares, vector_rows, gains, vector_state, gate_back, x_back, small_back,
            (in_weight, in_first, in_second), out_raw, (out_weight, out_first, out_second),
            (layer_out, token_grad),
        )
        vector_out = [v.reshape(-1)[: vectors.shape[0]] for v in rest[:4]]
        in_grad, in_moment, in_square, in_master, in_rounded = rest[4:9]
        out_grad, out_moment, out_square, out_master, out_rounded = rest[9:14]
        layer_out, token_grad = rest[14:]
        return (
            layer_out,
            token_grad,
            in_grad,
            out_grad,
            vector_out[0],
            norm[0, 0],
            in_moment,
            in_square,
            in_master,
            in_rounded,
            out_moment,
            out_square,
            out_master,
            out_rounded,
            *vector_out[1:],
        )
    else:
        out_term = lax.dot_general(
            gated_low, cotangents, (((0,), (0,)), ((), ())), preferred_element_type=f32
        )
        whole_term = jnp.zeros((pairs, fsdp, PAIR, D), f32)
        whole_term = lax.dynamic_update_slice(
            whole_term, out_term.reshape(pairs, 1, PAIR, D), (0, me, 0, 0)
        )
        out_raw = lax.psum_scatter(
            whole_term.reshape(INNER, D), ("dp", "fsdp"), scatter_dimension=0, tiled=True
        )
        added = halved(
            jnp.dot(gated_low, weight_out, preferred_element_type=f32)
            .astype(bf16)
            .reshape(fsdp, tokens.shape[0], D),
            "fsdp",
        )
        layer_out = (inputs + added).astype(bf16)
        gate_raw = scatter_rows(in_term(gate_grad), "dp")
        x_grad, key_grad, query_grad, sums, rest, channel_grad = scan_backward(
            x_part, *scan_inputs, queries_t, y_grad, states
        )
        x_raw = scatter_rows(in_term(x_grad), "dp")

        shared_grads = jnp.concatenate([key_grad, query_grad], axis=1).T.astype(bf16)
        arrived = exchanged(shared_grads.reshape(fsdp, shared, length), "fsdp").astype(f32)
        activated_grad = jnp.sum(arrived, axis=0)
        shared_pre_grad = activated_grad * shared_gate * (1.0 + shared_pre * (1.0 - shared_gate))
        shared_ahead = jnp.pad(shared_pre_grad, ((0, 0), (0, CONV - 1)))
        shared_grad = sum(
            taps_shared[k][:, None] * shared_ahead[:, CONV - 1 - k : CONV - 1 - k + length]
            for k in range(CONV)
        )
        taps_shared_grad = jnp.stack(
            [
                jnp.sum(shared_pre_grad * shared_padded[:, k : k + length], axis=1)
                for k in range(CONV)
            ]
        )
        bias_shared_grad = jnp.sum(shared_pre_grad, axis=1)

        sums = sums.T[: 3 * heads].reshape(3, heads, chunks, SPAN)
        before = (jnp.arange(SPAN)[:, None] < jnp.arange(SPAN)[None, :]).astype(f32)
        rest = rest.reshape(chunks, heads, HEAD_DIM).sum(axis=2).T
        log_grad = (
            jnp.dot(sums[0], 1.0 - before, precision=highest)
            + jnp.dot(sums[1], before, precision=highest)
            + rest[:, :, None]
        ).reshape(heads, length)
        step_grad = decay_own[:, None] * log_grad + sums[2].reshape(heads, length)
        raw_grad = step_grad * jax.nn.sigmoid(step_logits)
        step_bias_grad = jnp.sum(raw_grad, axis=1)
        decay_grad = jnp.sum(step_sizes * log_grad, axis=1) * decay_own
        small_grad = jnp.concatenate([shared_grad, raw_grad * head_mask[:, None]], axis=0).astype(bf16)
        small_raw = scatter_rows(
            lax.dot_general(
                normed, small_grad, (((0,), (1,)), ((), ())), preferred_element_type=f32
            ).astype(bf16),
            "dp",
        )

        def in_back(grad, weight, grad_dim=1):
            return lax.dot_general(
                grad, weight, (((grad_dim,), (1,)), ((), ())), preferred_element_type=f32
            )

        normed_grad = halved(
            (
                in_back(gate_grad, weight_gate)
                + in_back(x_grad, weight_x)
                + in_back(small_grad, weight_shared, 0)
            )
            .astype(bf16)
            .reshape(fsdp, tokens.shape[0], D),
            "fsdp",
        )
        pulled = normed_grad * norm_gain[None, :]
        input_grad = inverse_in * pulled - inputs * (
            inverse_in**3 * jnp.mean(pulled * inputs, axis=-1, keepdims=True)
        )
        token_grad = (cotangent.astype(f32) + input_grad).astype(bf16)
        norm_gain_grad = jnp.sum(normed_grad * inputs * inverse_in, axis=0)

        head_row = jnp.concatenate(
            [jnp.pad(step_bias_grad, (0, PAIR - heads)), jnp.pad(decay_grad, (0, PAIR - heads))]
        )
        shared_rows = jnp.concatenate([taps_shared_grad, bias_shared_grad[None]])
        vector_rows = jnp.concatenate(
            [
                gain_grad[0:1],
                channel_grad[: CONV + 2],
                norm_gain_grad.reshape(-1, inner),
                jnp.zeros((15 - CONV - 3 - D // inner, inner), f32),
                jnp.pad(head_row, (0, inner - 2 * PAIR))[None],
                jnp.pad(shared_rows, ((0, 7 - CONV), (0, inner - shared))),
            ]
        )
        vector_rows = spread_small(summed_in_steps(vector_rows, "dp"), "fsdp")
        squares = (
            jnp.sum(gate_raw * gate_raw)
            + jnp.sum(x_raw * x_raw)
            + jnp.sum(small_raw * small_raw)
            + jnp.sum(out_raw * out_raw)
        )
        squares = summed(summed(jnp.broadcast_to(squares, (8, 128)), "fsdp"), "dp")[0, 0]

    def joined_channels(v):
        return v.reshape(fsdp, pairs, PAIR).transpose(1, 0, 2).reshape(INNER)

    def joined_heads(v):
        return v.reshape(fsdp, pairs, 2).transpose(1, 0, 2).reshape(HEADS)

    shared_all = vector_rows[:, 16 : 17 + CONV, :shared]
    bias_shared_all = shared_all[:, CONV].reshape(-1)
    taps_all = [
        jnp.concatenate([joined_channels(vector_rows[:, 1 + k]), shared_all[:, k].reshape(-1)])
        for k in range(CONV)
    ]
    bias_all = jnp.concatenate([joined_channels(vector_rows[:, CONV + 1]), bias_shared_all])
    norm_rows = vector_rows[:, CONV + 3 : CONV + 3 + D // inner].reshape(fsdp, D)
    norm_all = norm_rows[0]
    for member in range(1, fsdp):
        norm_all = norm_all + norm_rows[member]
    skip_all = vector_rows[:, CONV + 2].reshape(fsdp * heads, HEAD_DIM).sum(axis=1)
    vector_raw = jnp.concatenate(
        [norm_all, joined_channels(vector_rows[:, 0])]
        + taps_all
        + [
            bias_all,
            joined_heads(vector_rows[:, 15, :heads]),
            joined_heads(vector_rows[:, 15, PAIR : PAIR + heads]),
            joined_heads(skip_all),
        ]
    )

    grad_norm = jnp.sqrt(squares + jnp.sum(vector_raw * vector_raw))
    factor = jnp.minimum(1.0, clip_norm / (grad_norm + 1e-06))
    def returned(raw):
        return exchanged(raw.astype(bf16).reshape(fsdp, rows_in, raw.shape[1]), "fsdp")

    def joined_columns(part):
        return (
            part.reshape(fsdp, rows_in, pairs, PAIR)
            .transpose(1, 2, 0, 3)
            .reshape(rows_in, INNER)
        )

    small_back = returned(small_raw)
    in_raw = jnp.concatenate(
        [
            joined_columns(returned(gate_raw)),
            joined_columns(returned(x_raw)),
            small_back[:, :, :shared].transpose(1, 0, 2).reshape(rows_in, 2 * STATE),
            small_back[:, :, shared:]
            .reshape(fsdp, rows_in, pairs, 2)
            .transpose(1, 2, 0, 3)
            .reshape(rows_in, HEADS),
        ],
        axis=1,
    ).astype(f32)
    in_grad = in_raw * factor
    in_moment, in_square, in_master = adamw(
        in_weight, in_first, in_second, in_grad, rate_in_proj
    )
    in_rounded = in_master.astype(bf16)
    out_grad = out_raw * factor
    vector_grad = vector_raw * factor
    out_moment, out_square, out_master = adamw(
        out_weight, out_first, out_second, out_grad, rate_out_proj
    )
    vector_moment, vector_square, vector_master = adamw(
        vectors, vector_first, vector_second, vector_grad, rate_vectors
    )
    return (
        layer_out,
        token_grad,
        in_grad,
        out_grad,
        vector_grad,
        grad_norm,
        in_moment,
        in_square,
        in_master,
        in_rounded,
        out_moment,
        out_square,
        out_master,
        out_master.astype(bf16),
        vector_moment,
        vector_square,
        vector_master,
    )


def solution(mesh):
    rows = P(("dp", "fsdp"), None)
    return jax.shard_map(
        on_device,
        mesh=mesh,
        in_specs=(rows, P("dp")) + (rows,) * 7 + (P(),) * 3,
        out_specs=(rows,) * 4 + (P(),) * 2 + (rows,) * 8 + (P(),) * 3,
        check_vma=False,
    )
```

```python
from functools import partial

import jax
import jax.numpy as jnp
import numpy as np
from jax import lax
from jax.experimental import pallas as pl
from jax.experimental.pallas import tpu as pltpu
from jax.sharding import PartitionSpec as P

D = 2048
HEADS = 64
HEAD_DIM = 64
STATE = 128
CONV = 4
SPAN = 128
STEP = 10
INNER = 4096
XBC = 4352
PAIR = 2 * HEAD_DIM
GROUP = 4
STEP_LANE = 16
TAPS_ROW = (D + INNER) // PAIR
LAST_ROW = TAPS_ROW + (CONV + 1) * XBC // PAIR
MASK_ROW, SKIP_ROW, GAIN_ROW = CONV + 1, CONV + 2, CONV + 3
LANES = GROUP * HEAD_DIM
ROW_TILE = 256
RING_LIMIT = 16

norm_eps = 1e-05
clip_norm = 1.0
beta_first = 0.5
beta_second = 0.5
adam_eps = 1e-08
weight_decay = 0.1
rate_in_proj = 0.03
rate_out_proj = 0.02
rate_vectors = 0.5
highest = lax.Precision.HIGHEST
f32 = jnp.float32
bf16 = jnp.bfloat16
VMEM_BYTES = 63 * 1024 * 1024


def ring_order(count):
    return list(range(0, count, 2)) + list(range(count - 1, 0, -2))


def ring_links(count):
    order = ring_order(count)
    right = [(order[i], order[(i + 1) % count]) for i in range(count)]
    return right, [(b, a) for a, b in right]


def ring_place(axis):
    count = lax.axis_size(axis)
    order = ring_order(count)
    places = [0] * count
    for place, member in enumerate(order):
        places[member] = place
    place = jnp.asarray(places, jnp.int32)[lax.axis_index(axis)]

    def member_at(distance):
        return jnp.asarray(order, jnp.int32)[lax.rem(place + distance + count, count)]

    return member_at


def uses_ring(axis):
    count = lax.axis_size(axis)
    return count % 2 == 0 and 4 <= count <= RING_LIMIT


def gather_rows(block, axis):
    count = lax.axis_size(axis)
    if not uses_ring(axis):
        return lax.all_gather(block, axis, axis=0, tiled=True)
    right, left = ring_links(count)
    member_at = ring_place(axis)
    rows, half = block.shape[0], block.shape[0] // 2
    whole = jnp.zeros((count * rows,) + block.shape[1:], block.dtype)
    columns = (0,) * (block.ndim - 1)

    def put(whole, piece, distance, shift=0):
        return lax.dynamic_update_slice(
            whole, piece, (member_at(distance) * rows + shift,) + columns
        )

    whole = put(whole, block, 0)
    going_right = going_left = block
    for hop in range(1, count // 2):
        going_right = lax.ppermute(going_right, axis, right)
        going_left = lax.ppermute(going_left, axis, left)
        whole = put(whole, going_right, -hop)
        whole = put(whole, going_left, hop)
    first = lax.ppermute(going_right[:half], axis, right)
    second = lax.ppermute(going_left[half:], axis, left)
    whole = put(whole, first, count // 2)
    return put(whole, second, count // 2, half)


def scatter_rows(terms, axis):
    count = lax.axis_size(axis)
    if not uses_ring(axis):
        return lax.psum_scatter(terms.astype(f32), axis, scatter_dimension=0, tiled=True)
    right, left = ring_links(count)
    member_at = ring_place(axis)
    rows = terms.shape[0] // count
    half = rows // 2

    def term(distance):
        return lax.dynamic_slice_in_dim(terms, member_at(distance) * rows, rows, 0).astype(f32)

    far = term(count // 2).astype(bf16)
    going_right = lax.ppermute(far[:half], axis, right)
    going_left = lax.ppermute(far[half:], axis, left)
    for distance in range(count // 2 - 1, 0, -1):
        to_right, to_left = term(distance), term(-distance)
        if distance == count // 2 - 1:
            to_right = jnp.concatenate([to_right[:half] + going_right, to_right[half:]])
            to_left = jnp.concatenate([to_left[:half], to_left[half:] + going_left])
        else:
            to_right, to_left = to_right + going_right, to_left + going_left
        going_right = lax.ppermute(to_right.astype(bf16), axis, right)
        going_left = lax.ppermute(to_left.astype(bf16), axis, left)
    return term(0) + going_right + going_left


def swapped(value, axis, flip):
    count = lax.axis_size(axis)
    return lax.ppermute(value, axis, [(i, i ^ flip) for i in range(count)])


def summed(value, axis):
    count = lax.axis_size(axis)
    if count <= 8:
        parts = [value] + [swapped(value, axis, flip) for flip in range(1, count)]
        while len(parts) > 1:
            parts = [parts[i] + parts[i + 1] for i in range(0, len(parts), 2)]
        return parts[0]
    return summed_in_steps(value, axis)


def summed_in_steps(value, axis):
    flip = 1
    while flip < lax.axis_size(axis):
        value = value + swapped(value, axis, flip)
        flip *= 2
    return value


def placed(parts, axis):
    count = lax.axis_size(axis)
    me = lax.axis_index(axis)
    whole = jnp.zeros((count,) + parts[0].shape, parts[0].dtype)
    for flip, part in enumerate(parts):
        whole = lax.dynamic_update_index_in_dim(whole, part, lax.bitwise_xor(me, flip), 0)
    return whole


def spread(value, axis):
    count = lax.axis_size(axis)
    parts = [value]
    flip = count // 2
    known = {0: value}
    while flip:
        fresh = {k ^ flip: swapped(v, axis, flip) for k, v in known.items()}
        known.update(fresh)
        flip //= 2
    parts = [known[k] for k in range(count)]
    return placed(parts, axis)


def spread_small(value, axis):
    count = lax.axis_size(axis)
    return placed([value] + [swapped(value, axis, k) for k in range(1, count)], axis)


def exchanged(blocks, axis):
    count = lax.axis_size(axis)
    me = lax.axis_index(axis)

    def block_for(flip):
        return lax.dynamic_index_in_dim(blocks, lax.bitwise_xor(me, flip), 0, False)

    return placed(
        [block_for(0)] + [swapped(block_for(k), axis, k) for k in range(1, count)], axis
    )


def halved(blocks, axis):
    count = lax.axis_size(axis)
    me = lax.axis_index(axis)
    held = {
        k: lax.dynamic_index_in_dim(blocks, lax.bitwise_xor(me, k), 0, False)
        for k in range(count)
    }
    flip = 1
    while flip < count:
        kept = {}
        for k in sorted(held):
            if k & flip:
                continue
            arrived = swapped(held[k ^ flip].astype(bf16), axis, flip)
            kept[k] = held[k].astype(f32) + arrived
        held = kept
        flip *= 2
    return held[0]


def dot_rows(a, b):
    return lax.dot_general(a, b, (((1,), (0,)), ((), ())), preferred_element_type=f32)


def dot_lanes(a, b):
    return lax.dot_general(a, b, (((1,), (1,)), ((), ())), preferred_element_type=f32)


def head_lanes(columns, base):
    rows = columns.shape[0]
    full = [
        jnp.broadcast_to(columns[:, base + j : base + j + 1], (rows, PAIR)) for j in range(GROUP)
    ]
    first = lax.broadcasted_iota(jnp.int32, (rows, PAIR), 1) < HEAD_DIM
    lanes = jnp.concatenate(
        [jnp.where(first, full[i], full[i + 1]) for i in range(0, GROUP, 2)], axis=1
    )
    return full, lanes


def stacked_heads(values, block_mask):
    return jnp.concatenate([values] * GROUP, axis=0) * block_mask


def filtered(window, taps, bias, rows):
    pre = bias + taps[CONV - 1 : CONV] * window[8 : 8 + rows]
    for k in range(CONV - 1):
        pre = pre + taps[k : k + 1] * window[5 + k : 5 + k + rows]
    return pre


def scan_forward_kernel(
    x_ref, consts_ref, column_ref, row_ref, key_ref, query_ref,
    key_t_ref, block_ref, y_ref, states_ref, padded, state,
):
    length = x_ref.shape[0]
    rows = SPAN
    mask = consts_ref[MASK_ROW : MASK_ROW + 1]
    padded[0:8, :] = jnp.zeros((8, LANES), f32)
    padded[8 : 8 + length, :] = x_ref[...] * mask
    state[...] = jnp.zeros_like(state)
    taps, bias = consts_ref[0:CONV], consts_ref[CONV : CONV + 1]
    skip = consts_ref[SKIP_ROW : SKIP_ROW + 1]
    causal = lax.broadcasted_iota(jnp.int32, (rows, rows), 0) >= lax.broadcasted_iota(
        jnp.int32, (rows, rows), 1
    )

    def chunk(c, carry):
        start = pl.multiple_of(c * rows, rows)
        here = pl.ds(start, rows)
        pre = filtered(padded[pl.ds(start, rows + 8), :], taps, bias, rows)
        values = pre * jax.nn.sigmoid(pre) * mask
        columns = column_ref[here, :]
        log_full, log_lanes = head_lanes(columns, 0)
        step_lanes = head_lanes(columns, STEP_LANE)[1]
        weighted = step_lanes * values
        weighted_low = weighted.astype(bf16)
        keys, queries, keys_t = key_ref[here, :], query_ref[here, :], key_t_ref[:, here]
        inner = dot_lanes(queries, keys)
        mixing = jnp.concatenate(
            [
                (
                    jnp.where(causal, jnp.exp(log_full[j] - row_ref[j : j + 1, here]), 0.0)
                    * inner
                ).astype(bf16)
                for j in range(GROUP)
            ],
            axis=1,
        )
        state_now = state[...]
        state_low = state_now.astype(bf16)
        states_ref[pl.ds(c, 1)] = state_low[None]
        y = dot_rows(mixing, stacked_heads(weighted_low, block_ref[...]))
        y = y + jnp.exp(log_lanes) * dot_rows(queries, state_low)
        y_ref[here, :] = y + skip * values
        log_last = log_lanes[rows - 1 : rows, :]
        tail = (weighted * jnp.exp(log_last - log_lanes)).astype(bf16)
        state[...] = jnp.exp(log_last) * state_now + dot_rows(keys_t, tail)
        return carry

    lax.fori_loop(0, length // rows, chunk, 0)


def scan_backward_group(
    x_ref, consts_ref, column_ref, row_ref, key_ref, query_ref,
    query_t_ref, block_ref, pick_ref, grad_ref, states_ref,
    x_grad_ref, key_grad_ref, query_grad_ref, sums_ref, rest_ref, channel_ref,
    padded, following, state_back, inner_grad,
):
    length = x_ref.shape[0]
    rows = SPAN
    chunks = length // rows
    mask = consts_ref[MASK_ROW : MASK_ROW + 1]
    padded[0:8, :] = jnp.zeros((8, LANES), f32)
    padded[8 : 8 + length, :] = x_ref[...] * mask
    following[...] = jnp.zeros_like(following)
    state_back[...] = jnp.zeros_like(state_back)
    channel_ref[...] = jnp.zeros_like(channel_ref)

    taps, bias = consts_ref[0:CONV], consts_ref[CONV : CONV + 1]
    skip = consts_ref[SKIP_ROW : SKIP_ROW + 1]
    row_at = lax.broadcasted_iota(jnp.int32, (rows, rows), 0)
    lane_at = lax.broadcasted_iota(jnp.int32, (rows, rows), 1)
    causal, causal_t = row_at >= lane_at, lane_at >= row_at

    def chunk(lap, carry):
        c = chunks - 1 - lap
        start = pl.multiple_of(c * rows, rows)
        here = pl.ds(start, rows)
        window = padded[pl.ds(start, rows + 8), :]
        pre = filtered(window, taps, bias, rows)
        gate = jax.nn.sigmoid(pre)
        values = pre * gate * mask
        columns = column_ref[here, :]
        log_full, log_lanes = head_lanes(columns, 0)
        step_lanes = head_lanes(columns, STEP_LANE)[1]
        weighted = step_lanes * values
        weighted_low = weighted.astype(bf16)
        keys, queries, queries_t = key_ref[here, :], query_ref[here, :], query_t_ref[:, here]
        grad_low = grad_ref[here, :]
        grad = grad_low.astype(f32)
        inner, inner_t = dot_lanes(queries, keys), dot_lanes(keys, queries)
        blocks = block_ref[...]
        weighted_blocks = stacked_heads(weighted_low, blocks)
        grad_blocks = stacked_heads(grad_low, blocks)
        mixing_grad = dot_lanes(grad_low, weighted_blocks)
        mixing, mixing_t, inner_sum = [], [], jnp.zeros((rows, rows), f32)
        for j in range(GROUP):
            log_row = row_ref[j : j + 1, here]
            decay = jnp.where(causal, jnp.exp(log_full[j] - log_row), 0.0)
            decay_t = jnp.where(causal_t, jnp.exp(log_row - log_full[j]), 0.0)
            mixing.append((decay * inner).astype(bf16))
            mixing_t.append((decay_t * inner_t).astype(bf16))
            inner_sum = inner_sum + decay * mixing_grad[:, j * rows : (j + 1) * rows]
        inner_grad[pl.ds(c, 1)] = inner_grad[pl.ds(c, 1)] + inner_sum[None]
        y = dot_rows(jnp.concatenate(mixing, axis=1), weighted_blocks)
        state_low = states_ref[pl.ds(c, 1)][0]
        entry = jnp.exp(log_lanes)
        y = y + entry * dot_rows(queries, state_low)
        inside = dot_rows(jnp.concatenate(mixing_t, axis=1), grad_blocks)
        back = state_back[...]
        back_low = back.astype(bf16)
        log_last = log_lanes[rows - 1 : rows, :]
        tail = jnp.exp(log_last - log_lanes)
        outside = tail * dot_rows(keys, back_low)
        entry_grad = (grad * entry).astype(bf16)
        tail_low = (weighted * tail).astype(bf16)
        query_grad_ref[here, :] = query_grad_ref[here, :] + dot_lanes(entry_grad, state_low)
        key_grad_ref[here, :] = key_grad_ref[here, :] + dot_lanes(tail_low, back_low)
        last = jnp.exp(log_last)
        rest_ref[pl.ds(c, 1)] = (
            last * jnp.sum(state_low.astype(f32) * back, axis=0, keepdims=True)
        )[None]
        state_back[...] = last * back + dot_rows(queries_t, entry_grad)
        weighted_grad = inside + outside
        first = grad * y - weighted_low.astype(f32) * inside
        first_high = first.astype(bf16)
        first_rest = (first - first_high.astype(f32)).astype(bf16)
        sums_ref[here, :] = sums_ref[here, :] + (
            dot_rows(first_high, pick_ref[0])
            + dot_rows(first_rest, pick_ref[0])
            + dot_rows((weighted * outside).astype(bf16), pick_ref[1])
            + dot_rows((values * weighted_grad).astype(bf16), pick_ref[2])
        )
        values_grad = step_lanes * weighted_grad + skip * grad
        pre_grad = values_grad * mask * (gate * (1.0 + pre * (1.0 - gate)))
        channel_ref[CONV : CONV + 1, :] += jnp.sum(pre_grad, axis=0, keepdims=True)
        channel_ref[CONV + 1 : CONV + 2, :] += jnp.sum(grad * values, axis=0, keepdims=True)
        for k in range(CONV):
            channel_ref[k : k + 1, :] += jnp.sum(
                pre_grad * window[5 + k : 5 + k + rows], axis=0, keepdims=True
            )
        ahead = jnp.concatenate([pre_grad, following[...]], axis=0)
        following[...] = pre_grad[0:8]
        x_grad = taps[CONV - 1 : CONV] * ahead[0:rows]
        for k in range(CONV - 1):
            x_grad = x_grad + taps[k : k + 1] * ahead[CONV - 1 - k : CONV - 1 - k + rows]
        x_grad_ref[here, :] = (x_grad * mask).astype(bf16)
        return carry

    lax.fori_loop(0, chunks, chunk, 0)


def scan_backward_start(key_grad_ref, query_grad_ref, sums_ref, inner_grad):
    key_grad_ref[...] = jnp.zeros_like(key_grad_ref)
    query_grad_ref[...] = jnp.zeros_like(query_grad_ref)
    inner_grad[...] = jnp.zeros_like(inner_grad)
    sums_ref[...] = jnp.zeros_like(sums_ref)


def scan_backward_finish(key_ref, query_ref, key_grad_ref, query_grad_ref, inner_grad):
    rows = SPAN

    def finish(c, carry):
        here = pl.ds(pl.multiple_of(c * rows, rows), rows)
        inner_low = inner_grad[pl.ds(c, 1)][0].astype(bf16)
        query_grad_ref[here, :] = query_grad_ref[here, :] + dot_rows(inner_low, key_ref[here, :])
        key_grad_ref[here, :] = key_grad_ref[here, :] + lax.dot_general(
            inner_low, query_ref[here, :], (((0,), (0,)), ((), ())), preferred_element_type=f32
        )
        return carry

    lax.fori_loop(0, key_ref.shape[0] // rows, finish, 0)


def scan_backward_kernel(*refs):
    key_ref, query_ref = refs[4:6]
    key_grad_ref, query_grad_ref, sums_ref = refs[12:15]
    inner_grad = refs[-1]

    @pl.when(pl.program_id(0) == 0)
    def _():
        scan_backward_start(key_grad_ref, query_grad_ref, sums_ref, inner_grad)

    scan_backward_group(*refs)

    @pl.when(pl.program_id(0) == pl.num_programs(0) - 1)
    def _():
        scan_backward_finish(key_ref, query_ref, key_grad_ref, query_grad_ref, inner_grad)


def block_mask():
    row = np.arange(GROUP * SPAN)[:, None] // SPAN
    lane = np.arange(LANES)[None, :] // HEAD_DIM
    return jnp.asarray((row == lane).astype(np.float32), bf16)


def pick_masks(groups):
    lane = np.arange(LANES)[:, None] // HEAD_DIM
    target = np.arange(PAIR)[None, :]
    masks = [
        target == (kind * groups + group) * GROUP + lane
        for group in range(groups)
        for kind in range(3)
    ]
    return jnp.asarray(np.stack(masks).astype(np.float32), bf16)


def whole_spec():
    return pl.BlockSpec(memory_space=pltpu.VMEM)


def lane_spec(rows):
    return pl.BlockSpec((rows, LANES), lambda g: (0, g))


def head_specs(length):
    return [
        lane_spec(length),
        lane_spec(8),
        pl.BlockSpec((length, PAIR), lambda g: (0, g)),
        pl.BlockSpec((8, length), lambda g: (g, 0)),
        whole_spec(),
        whole_spec(),
        whole_spec(),
        whole_spec(),
    ]


def scan_forward(x, consts, columns, rows, keys, queries, keys_t):
    length, width = x.shape
    chunks = length // SPAN
    return pl.pallas_call(
        scan_forward_kernel,
        grid=(width // LANES,),
        in_specs=head_specs(length),
        out_specs=[
            lane_spec(length),
            pl.BlockSpec((chunks, STATE, LANES), lambda g: (0, 0, g)),
        ],
        out_shape=[
            jax.ShapeDtypeStruct((length, width), f32),
            jax.ShapeDtypeStruct((chunks, STATE, width), bf16),
        ],
        scratch_shapes=[pltpu.VMEM((length + 8, LANES), f32), pltpu.VMEM((STATE, LANES), f32)],
        compiler_params=pltpu.CompilerParams(vmem_limit_bytes=VMEM_BYTES),
        cost_estimate=pl.CostEstimate(
            flops=10_000_000_000, bytes_accessed=12_000_000, transcendentals=4_000_000
        ),
        name="scan_forward",
    )(x, consts, columns, rows, keys, queries, keys_t, block_mask())


def scan_backward(
    x, consts, columns, rows, keys, queries, queries_t, grad, states
):
    length, width = x.shape
    chunks = length // SPAN
    groups = width // LANES
    same = lambda g: (0, 0)
    return pl.pallas_call(
        scan_backward_kernel,
        grid=(groups,),
        in_specs=head_specs(length)
        + [
            pl.BlockSpec((3, LANES, PAIR), lambda g: (g, 0, 0)),
            lane_spec(length),
            pl.BlockSpec((chunks, STATE, LANES), lambda g: (0, 0, g)),
        ],
        out_specs=[
            lane_spec(length),
            pl.BlockSpec((length, STATE), same),
            pl.BlockSpec((length, STATE), same),
            pl.BlockSpec((length, PAIR), same),
            pl.BlockSpec((chunks, 1, LANES), lambda g: (0, 0, g)),
            lane_spec(8),
        ],
        out_shape=[
            jax.ShapeDtypeStruct((length, width), bf16),
            jax.ShapeDtypeStruct((length, STATE), f32),
            jax.ShapeDtypeStruct((length, STATE), f32),
            jax.ShapeDtypeStruct((length, PAIR), f32),
            jax.ShapeDtypeStruct((chunks, 1, width), f32),
            jax.ShapeDtypeStruct((8, width), f32),
        ],
        scratch_shapes=[
            pltpu.VMEM((length + 8, LANES), f32),
            pltpu.VMEM((8, LANES), f32),
            pltpu.VMEM((STATE, LANES), f32),
            pltpu.VMEM((chunks, SPAN, SPAN), f32),
        ],
        compiler_params=pltpu.CompilerParams(vmem_limit_bytes=VMEM_BYTES),
        cost_estimate=pl.CostEstimate(
            flops=30_000_000_000, bytes_accessed=16_000_000, transcendentals=8_000_000
        ),
        name="scan_backward",
    )(
        x, consts, columns, rows, keys, queries, queries_t, block_mask(),
        pick_masks(groups), grad, states,
    )


def gate_kernel(
    normed_ref, weight_ref, cotangent_ref, out_ref, y_ref, gain_ref, mask_ref,
    gate_part_ref, gated_grad_ref, stats_ref,
):
    gate_part = dot_rows(normed_ref[...], weight_ref[...]) * mask_ref[...]
    gated_grad = dot_lanes(cotangent_ref[...], out_ref[...])
    gate_part_ref[...] = gate_part
    gated_grad_ref[...] = gated_grad
    gated = y_ref[...] * (gate_part * jax.nn.sigmoid(gate_part))
    squares = jnp.sum(gated * gated, axis=1, keepdims=True)
    products = jnp.sum(gated * gated_grad * gain_ref[...], axis=1, keepdims=True)
    lane = lax.broadcasted_iota(jnp.int32, stats_ref.shape, 1)
    stats_ref[...] = jnp.where(lane == 0, squares, products)


def gate_forward(normed, weight, cotangent, out_weight, y, gain, mask):
    length, width = y.shape
    rows = lambda lanes: pl.BlockSpec((ROW_TILE, lanes), lambda i: (i, 0))
    return pl.pallas_call(
        gate_kernel,
        grid=(length // ROW_TILE,),
        in_specs=[
            rows(D), whole_spec(), rows(D), whole_spec(), rows(width), whole_spec(), whole_spec(),
        ],
        out_specs=[rows(width), rows(width), rows(PAIR)],
        out_shape=[
            jax.ShapeDtypeStruct((length, width), f32),
            jax.ShapeDtypeStruct((length, width), f32),
            jax.ShapeDtypeStruct((length, PAIR), f32),
        ],
        compiler_params=pltpu.CompilerParams(vmem_limit_bytes=VMEM_BYTES),
        cost_estimate=pl.CostEstimate(
            flops=9_000_000_000, bytes_accessed=28_000_000, transcendentals=1_000_000
        ),
        name="gate_forward",
    )(normed, weight, cotangent, out_weight, y, gain, mask)


def norm_back_kernel(
    y_ref, gate_part_ref, gated_grad_ref, scale_ref, gain_ref, mask_ref,
    gated_ref, y_grad_ref, gate_grad_ref, gain_grad_ref,
):
    @pl.when(pl.program_id(0) == 0)
    def _():
        gain_grad_ref[...] = jnp.zeros_like(gain_grad_ref)

    y, gate_part, gated_grad = y_ref[...], gate_part_ref[...], gated_grad_ref[...]
    inverse, pull = scale_ref[:, 0:1], scale_ref[:, 1:2]
    gate = jax.nn.sigmoid(gate_part)
    silu = gate_part * gate
    gated = y * silu
    scaled = gated * inverse
    gain = gain_ref[...]
    gated_ref[...] = (scaled * gain).astype(bf16)
    gain_grad_ref[0:1, :] += jnp.sum(gated_grad * scaled, axis=0, keepdims=True)
    back = inverse * (gated_grad * gain) - gated * pull
    y_grad_ref[...] = (back * silu).astype(bf16)
    gate_grad_ref[...] = (
        back * y * (gate * (1.0 + gate_part * (1.0 - gate))) * mask_ref[...]
    ).astype(bf16)


def norm_back(y, gate_part, gated_grad, scales, gain, mask):
    length, width = y.shape
    rows = lambda lanes: pl.BlockSpec((ROW_TILE, lanes), lambda i: (i, 0))
    return pl.pallas_call(
        norm_back_kernel,
        grid=(length // ROW_TILE,),
        in_specs=[rows(width), rows(width), rows(width), rows(2), whole_spec(), whole_spec()],
        out_specs=[
            rows(width), rows(width), rows(width), pl.BlockSpec((8, width), lambda i: (0, 0)),
        ],
        out_shape=[
            jax.ShapeDtypeStruct((length, width), bf16),
            jax.ShapeDtypeStruct((length, width), bf16),
            jax.ShapeDtypeStruct((length, width), bf16),
            jax.ShapeDtypeStruct((8, width), f32),
        ],
        compiler_params=pltpu.CompilerParams(vmem_limit_bytes=VMEM_BYTES),
        cost_estimate=pl.CostEstimate(
            flops=30_000_000, bytes_accessed=18_000_000, transcendentals=1_000_000
        ),
        name="norm_back",
    )(y, gate_part, gated_grad, scales, gain, mask)


MESH = pl.DeviceIdType.MESH


class Ring:
    def __init__(self):
        self.count = lax.axis_size("dp")
        self.far = self.count // 2
        me = lax.axis_index("dp")
        odd = lax.rem(me, 2)
        self.me = me
        self.place = (1 - odd) * lax.div(me, 2) + odd * lax.div(2 * self.count - 1 - me, 2)

    def member(self, distance):
        n = self.count
        place = lax.rem(self.place + distance + n, n)
        back = lax.div(place, n // 2)
        return (1 - back) * 2 * place + back * (2 * n - 1 - 2 * place)

    def target(self, way):
        return {"dp": self.member(1 if way == 0 else -1)}


def partner(flip):
    f = lax.axis_index("fsdp")
    return (f, f + 1 - 2 * lax.rem(f, 2), lax.rem(f + 2, 4), 3 - f)[flip]


def greet(targets):
    barrier = pltpu.get_barrier_semaphore()
    for target in targets:
        pl.semaphore_signal(barrier, inc=1, device_id=target, device_id_type=MESH)
    pl.semaphore_wait(barrier, len(targets))


def row_slice(ref, start, size):
    return ref.at[pl.ds(pl.multiple_of(start, 16), size)]


class RingGather:
    def __init__(self, ring, wholes, send, recv, first):
        self.ring, self.wholes, self.send, self.recv = ring, wholes, send, recv
        self.first = first

    @staticmethod
    def semaphores(parts, count):
        return pltpu.SemaphoreType.DMA((parts * 4 * (count // 2),))

    def copy(self, part, way, half, hop):
        whole = self.wholes[part]
        rows = whole.shape[0] // self.ring.count
        size = rows // 2
        owner = self.ring.member(-hop if way == 0 else hop)
        place = row_slice(whole, owner * rows + half * size, size)
        at = ((part * 2 + way) * 2 + half) * self.ring.far + hop
        source = place
        if hop == 0 and part in self.first:
            source = row_slice(self.first[part], half * size, size)
        return pltpu.make_async_remote_copy(
            source, place, self.send.at[at], self.recv.at[at],
            device_id=self.ring.target(way), device_id_type=MESH,
        )

    def pieces(self, hop):
        return [
            (way, half)
            for half in (0, 1)
            for way in (0, 1)
            if hop < self.ring.far - 1 or half == way
        ]

    def start(self, part, hop):
        for way, half in self.pieces(hop):
            if hop:
                self.copy(part, way, half, hop - 1).wait_recv()
            self.copy(part, way, half, hop).start()

    def settle(self, part):
        last = self.ring.far - 1
        for way, half in self.pieces(last):
            self.copy(part, way, 1 - half, last - 1).wait_recv()

    def finish(self, part):
        last = self.ring.far - 1
        for way, half in self.pieces(last):
            self.copy(part, way, half, last).wait_recv()
        for hop in range(last + 1):
            for way, half in self.pieces(hop):
                self.copy(part, way, half, hop).wait_send()


class RingScatter:
    def __init__(self, ring, held, arrived, send, recv):
        self.ring, self.held, self.arrived = ring, held, arrived
        self.send, self.recv = send, recv

    @staticmethod
    def scratch(count, rows, columns):
        return [
            pltpu.VMEM((2, 2, rows, columns), bf16),
            pltpu.VMEM((2, count // 2 * rows - rows // 2, columns), bf16),
        ]

    def landing(self, way, hop):
        rows = self.held.shape[2]
        if hop == 0:
            return self.arrived.at[way, pl.ds((self.ring.far - 1) * rows, rows // 2)]
        return self.arrived.at[way, pl.ds((hop - 1) * rows, rows)]

    def copy(self, way, hop):
        rows = self.held.shape[2]
        size = rows // 2 if hop == 0 else rows
        at = way * self.ring.far + hop
        return pltpu.make_async_remote_copy(
            self.held.at[way, hop % 2, pl.ds(0, size)], self.landing(way, hop),
            self.send.at[at], self.recv.at[at],
            device_id=self.ring.target(way), device_id_type=MESH,
        )

    def owner(self, way, hop):
        distance = self.ring.far - hop
        return self.ring.member(distance if way == 0 else -distance)

    def start(self, hop, term):
        rows = self.held.shape[2]
        half = rows // 2
        if hop == 0:
            value = term(self.owner(0, 0), 0).astype(bf16)
            self.held[0, 0, 0:half] = value[:half]
            self.copy(0, 0).start()
            self.held[1, 0, 0:half] = value[half:]
            self.copy(1, 0).start()
            return
        for way in (0, 1):
            value = term(self.owner(way, hop), way)
            self.copy(way, hop - 1).wait_recv()
            slot = hop % 2
            if hop >= 2:
                self.copy(way, hop - 2).wait_send()
            if hop == 1:
                low = slice(way * half, (way + 1) * half)
                rest = slice((1 - way) * half, (2 - way) * half)
                self.held[way, slot, low] = (
                    value[low] + self.landing(way, 0)[...].astype(f32)
                ).astype(bf16)
                self.held[way, slot, rest] = value[rest].astype(bf16)
            else:
                self.held[way, slot] = (
                    value + self.landing(way, hop - 1)[...].astype(f32)
                ).astype(bf16)
            self.copy(way, hop).start()

    def finish(self, term):
        last = self.ring.far - 1
        value = term(self.ring.me, 0)
        for way in (0, 1):
            self.copy(way, last).wait_recv()
            value = value + self.landing(way, last)[...].astype(f32)
        for hop in range(last - 1, last + 1):
            for way in (0, 1):
                self.copy(way, hop).wait_send()
        return value


def any_specs(count):
    return [pl.BlockSpec(memory_space=pl.ANY)] * count


def tokens_exchange(own, whole, send, recv, base):
    f = lax.axis_index("fsdp")
    rows = whole.shape[0] // 4

    def one(at, source, owner, k):
        return pltpu.make_async_remote_copy(
            source, row_slice(whole, owner * rows, rows), send.at[base + at], recv.at[base + at],
            device_id={"fsdp": partner(k)}, device_id_type=MESH,
        )

    far = partner(2)
    return (
        one(0, own, f, 2), one(1, own, f, 1), one(2, row_slice(whole, far * rows, rows), far, 1),
    )


def forward_kernel(
    tokens_ref, cotangent_hbm, in_ref, out_ref, turn_ref, vectors_ref, active_ref, block_ref,
    small_all, x_all, gate_all, out_all, cotangent_all, normed_t_all, x_part_all, states_all,
    gated_all, gated_t_all, y_grad_all, gate_grad_all,
    consts_ref, head_ref, shared_taps_ref, columns_ref, rows_ref, column_ref, keys_ref, queries_ref, queries_t_ref,
    shared_part_ref, shared_pre_ref, gain_grad_ref,
    small_cut, x_cut, gate_cut, out_low, normed, cotangent, small_weight, keys_t, shared_all,
    x_part, states, y, gate_part, gated_grad, weight, gate_weight, far_weight, out_tile, turned, squares, products, stats, stats_in,
    back_tiles, back_tiles_t, padded, state, shared_wide,
    local_sem, swap_send, swap_recv, token_send, token_recv, ring_send, ring_recv,
    shared_send, shared_recv, stats_send, stats_recv, load_sem, gate_sem, store_sem,
):
    ring = Ring()
    d, f = ring.me, lax.axis_index("fsdp")
    tokens, length = tokens_ref.shape[0], normed.shape[0]
    sub, rows_out = in_ref.shape[0], out_ref.shape[0]
    width = x_cut.shape[2]
    groups, chunks = width // LANES, length // SPAN
    heads, shared = HEADS // 4, shared_taps_ref.shape[0]
    precise = partial(jnp.dot, precision=highest, preferred_element_type=f32)
    greet([{"fsdp": partner(k)} for k in (1, 2, 3)] + [ring.target(0), ring.target(1)])
    wholes = [small_all, x_all, gate_all, out_all]
    small_part, x_of, gate_of, out_of = range(4)
    rings = RingGather(ring, wholes, ring_send, ring_recv, {out_of: out_low})
    cuts = [small_cut, x_cut, gate_cut]

    def own_copy(part):
        if part == out_of:
            source, target = out_low, row_slice(out_all, d * rows_out, rows_out)
        else:
            source = cuts[part].at[f]
            target = row_slice(wholes[part], (4 * d + f) * sub, sub)
        return pltpu.make_async_copy(source, target, local_sem.at[part])

    def swap(part, k):
        return pltpu.make_async_remote_copy(
            cuts[part].at[partner(k)], row_slice(wholes[part], (4 * d + f) * sub, sub),
            swap_send.at[3 * part + k - 1], swap_recv.at[3 * part + k - 1],
            device_id={"fsdp": partner(k)}, device_id_type=MESH,
        )

    def start_swaps(part):
        for k in (2, 3, 1):
            swap(part, k).start()
        own_copy(part).start()

    def start_ring(part):
        if part != out_of:
            own_copy(part).wait()
            for k in (1, 2, 3):
                swap(part, k).wait_recv()
        rings.start(part, 0)

    def cut_channels(target, low):
        for pair in range(INNER // PAIR):
            member, at = pair % 4, pair // 4
            target[member, :, at * PAIR : (at + 1) * PAIR] = in_ref[
                :, low + pair * PAIR : low + (pair + 1) * PAIR
            ].astype(bf16)

    out_low[...] = out_ref[...].astype(bf16)
    own_copy(out_of).start()
    start_ring(out_of)
    pieces = dot_lanes(in_ref[:, 2 * INNER :].astype(bf16), turn_ref[...]).astype(bf16)
    for member in range(4):
        small_cut[member] = pieces[:, member * PAIR : (member + 1) * PAIR]
    start_swaps(small_part)
    cut_channels(x_cut, INNER)
    start_swaps(x_of)
    inputs = tokens_ref[...].astype(f32)
    inverse = lax.rsqrt(jnp.sum(inputs * inputs, axis=1, keepdims=True) / D + norm_eps)
    own_rows = pl.ds(pl.multiple_of(f * tokens, tokens), tokens)
    normed[own_rows, :] = (inputs * inverse * norm_gain_row(vectors_ref)).astype(bf16)
    normed_copies = tokens_exchange(normed.at[own_rows], normed, token_send, token_recv, 0)
    cotangent_copies = tokens_exchange(
        cotangent_hbm, cotangent, token_send, token_recv, 3
    )
    cotangent_own = pltpu.make_async_copy(cotangent_hbm, cotangent.at[own_rows], local_sem.at[4])
    cotangent_own.start()
    for copy in normed_copies[:2]:
        copy.start()
    start_ring(small_part)
    start_ring(x_of)
    cut_channels(gate_cut, 0)
    start_swaps(gate_of)

    def vector_row(row):
        return vectors_ref[pl.ds(row, 1), :]

    def own_channels(first_row):
        return jnp.concatenate(
            [vector_row(first_row + 4 * pair + f) for pair in range(width // PAIR)], axis=1
        )

    active = active_ref[0:1, 0:1]
    for k in range(CONV + 1):
        consts_ref[k : k + 1, :] = own_channels(TAPS_ROW + k * (XBC // PAIR))
    channel_head = lax.broadcasted_iota(jnp.int32, (1, width), 1) // HEAD_DIM
    consts_ref[MASK_ROW : MASK_ROW + 1, :] = (channel_head.astype(f32) < active / 4).astype(f32)
    consts_ref[GAIN_ROW : GAIN_ROW + 1, :] = own_channels(D // PAIR)
    head_at = lax.broadcasted_iota(jnp.int32, (PAIR, PAIR), 0)
    local_at = lax.broadcasted_iota(jnp.int32, (PAIR, PAIR), 1)
    own_head = local_at // 2 * 8 + 2 * f + local_at % 2
    chosen = (head_at == own_head) & (local_at < heads)
    chosen_far = (head_at == own_head + HEADS) & (local_at < heads)
    last = vector_row(LAST_ROW)
    step_bias_row = precise(last, chosen.astype(f32))
    is_head = lax.broadcasted_iota(jnp.int32, (1, PAIR), 1) < heads
    decay_row = jnp.where(is_head, -jnp.exp(precise(last, chosen_far.astype(f32))), 0.0)
    head_mask_row = (
        lax.broadcasted_iota(jnp.int32, (1, PAIR), 1).astype(f32) < active / 4
    ).astype(f32)
    skip_row = precise(vector_row(LAST_ROW + 1), chosen.astype(f32))
    spread_head = (
        lax.broadcasted_iota(jnp.int32, (PAIR, width), 0)
        == lax.broadcasted_iota(jnp.int32, (PAIR, width), 1) // HEAD_DIM
    ).astype(f32)
    consts_ref[SKIP_ROW : SKIP_ROW + 1, :] = precise(skip_row, spread_head)
    head_ref[...] = jnp.concatenate(
        [decay_row, head_mask_row, step_bias_row, jnp.zeros((5, PAIR), f32)], axis=0
    )
    shared_rows = [
        vector_row(TAPS_ROW + k * (XBC // PAIR) + INNER // PAIR + f // 2) for k in range(CONV + 1)
    ]
    shared_wide[...] = jnp.concatenate(
        shared_rows + [jnp.zeros((PAIR - CONV - 1, PAIR), f32)], axis=0
    ).T
    shared_taps_ref[...] = shared_wide[pl.ds(pl.multiple_of(f % 2 * shared, shared), shared), :]
    rings.start(small_part, 1)
    rings.start(out_of, 1)
    rings.start(small_part, 2)
    rings.start(x_of, 1)
    for hop in range(3, ring.far):
        rings.start(small_part, hop)
    normed_copies[0].wait_recv()
    normed_copies[2].start()
    for copy in cotangent_copies[:2]:
        copy.start()
    rings.settle(small_part)
    rings.finish(small_part)
    load_small = pltpu.make_async_copy(small_all, small_weight, local_sem.at[5])
    load_small.start()
    for copy in normed_copies[1:]:
        copy.wait_recv()
    load_small.wait()

    small = dot_rows(normed[...], small_weight[...]).T
    part = small[0:shared]
    pre = shared_taps_ref[:, CONV : CONV + 1] + jnp.zeros_like(part)
    for k in range(CONV):
        pre = pre + shared_taps_ref[:, k : k + 1] * shifted(part, CONV - 1 - k)
    shared_part_ref[...] = part
    shared_pre_ref[...] = pre
    shared_all[f] = (pre * jax.nn.sigmoid(pre)).astype(bf16)

    def shared_copy(k):
        return pltpu.make_async_remote_copy(
            shared_all.at[f], shared_all.at[f], shared_send.at[k - 1], shared_recv.at[k - 1],
            device_id={"fsdp": partner(k)}, device_id_type=MESH,
        )

    for k in (2, 3, 1):
        shared_copy(k).start()
    rings.start(out_of, 2)
    rings.start(x_of, 2)
    head_columns = jnp.concatenate(
        [head_ref[...], jnp.zeros((PAIR - 8, PAIR), f32)], axis=0
    ).T[0:heads]
    decay, head_mask, step_bias = (head_columns[:, i : i + 1] for i in range(3))
    logits = small[shared : shared + heads] * head_mask + step_bias
    steps = jnp.maximum(logits, 0.0) + jnp.log1p(jnp.exp(-jnp.abs(logits)))
    at_row = lax.broadcasted_iota(jnp.int32, (SPAN, SPAN), 0)
    at_lane = lax.broadcasted_iota(jnp.int32, (SPAN, SPAN), 1)
    upto = (at_row <= at_lane).astype(f32)
    rates = steps * decay
    log_sums = jnp.concatenate(
        [
            jnp.dot(
                rates[:, c * SPAN : (c + 1) * SPAN], upto, precision=highest,
                preferred_element_type=f32,
            )
            for c in range(chunks)
        ],
        axis=1,
    )
    column = jnp.concatenate(
        [log_sums, steps, logits, jnp.zeros((PAIR - 3 * heads, length), f32)], axis=0
    ).T
    column_ref[...] = column
    for group in range(groups):
        rolled = column if group == 0 else pltpu.roll(column, PAIR - group * GROUP, 1)
        columns_ref[:, group * PAIR : (group + 1) * PAIR] = rolled
        rows_ref[group * 8 : group * 8 + 8, :] = jnp.zeros((8, length), f32)
        rows_ref[group * 8 : group * 8 + GROUP, :] = log_sums[group * GROUP : (group + 1) * GROUP]
    for k in (1, 2, 3):
        shared_copy(k).wait_recv()
    keys_t[0:shared, :] = shared_all[0]
    keys_t[shared:, :] = shared_all[1]
    queries_t_ref[0:shared, :] = shared_all[2]
    queries_t_ref[shared:, :] = shared_all[3]
    keys_ref[...] = keys_t[...].T
    queries_ref[...] = queries_t_ref[...].T
    for hop in range(3, ring.far):
        rings.start(out_of, hop)
        rings.start(x_of, hop)
    start_ring(gate_of)
    cotangent_copies[0].wait_recv()
    cotangent_copies[2].start()

    def store(source, target, slot):
        return pltpu.make_async_copy(source, target, store_sem.at[slot])

    quarter = D // 4

    def turned_store(i):
        return store(turned.at[i % 2], row_slice(normed_t_all, i * quarter, quarter), i)

    for i in range(4):
        if i >= 2:
            turned_store(i - 2).wait()
        turned[i % 2] = normed[:, i * quarter : (i + 1) * quarter].T
        turned_store(i).start()
    rings.settle(x_of)
    rings.finish(x_of)

    def gate_load(distance, slot):
        owner = ring.member(distance)
        size = 4 * sub
        return pltpu.make_async_copy(
            row_slice(gate_all, owner * size, size), row_slice(gate_weight, owner * size, size),
            gate_sem.at[slot],
        )

    def start_gate(hop):
        rings.start(gate_of, hop)
        if hop == ring.far - 1:
            rings.settle(gate_of)
        if hop == 1:
            gate_load(0, 0).start()
        gate_load(-hop, 2 * hop - 1).start()
        gate_load(hop, 2 * hop).start()

    def lanes(group):
        return pl.ds(group * LANES, LANES)

    def load_columns(source, group):
        return pltpu.make_async_copy(
            source.at[:, lanes(group)], weight.at[group % 2], load_sem.at[group % 2]
        )

    def x_store(group):
        return store(x_part.at[group % 2], x_part_all.at[:, lanes(group)], 4 + group)

    def states_store(group):
        return store(states.at[group % 2], states_all.at[:, :, lanes(group)], 8 + group)

    load_columns(x_all, 0).start()
    for group in range(groups):
        if group + 1 < groups:
            load_columns(x_all, group + 1).start()
        load_columns(x_all, group).wait()
        if group >= 2:
            x_store(group - 2).wait()
            states_store(group - 2).wait()
        slot = group % 2
        x_part[slot] = dot_rows(normed[...], weight[slot])
        x_store(group).start()
        scan_forward_kernel(
            x_part.at[slot], consts_ref.at[:, lanes(group)],
            columns_ref.at[:, pl.ds(group * PAIR, PAIR)], rows_ref.at[pl.ds(group * 8, 8)],
            keys_ref, queries_ref, keys_t, block_ref, y.at[:, lanes(group)], states.at[slot],
            padded, state,
        )
        states_store(group).start()
        if group % 2 == 1 and group // 2 + 1 < ring.far - 1:
            start_gate(group // 2 + 1)

    for copy in cotangent_copies[1:]:
        copy.wait_recv()
    cotangent_own.wait()
    cotangent_store = store(cotangent, cotangent_all, 12)
    cotangent_store.start()
    rings.settle(out_of)
    rings.finish(out_of)
    own_copy(out_of).wait()

    def load_rows(group):
        return pltpu.make_async_copy(
            out_all.at[lanes(group)], out_tile.at[group % 2], load_sem.at[2 + group % 2]
        )

    load_rows(0).start()
    for group in range(groups):
        if group + 1 < groups:
            load_rows(group + 1).start()
        load_rows(group).wait()
        gated_grad[:, lanes(group)] = dot_lanes(cotangent[...], out_tile[group % 2])
    start_gate(ring.far - 1)
    far_size = 4 * sub
    far_rows = pl.ds(pl.multiple_of(ring.member(ring.far) * far_size, far_size), far_size)
    gate_weight[far_rows, :] = jnp.zeros((far_size, width), bf16)
    for hop in range(1, ring.far):
        if hop == 1:
            gate_load(0, 0).wait()
        gate_load(-hop, 2 * hop - 1).wait()
        gate_load(hop, 2 * hop).wait()
    for group in range(groups):
        gate_part[:, lanes(group)] = dot_rows(normed[...], gate_weight[:, lanes(group)])
    rings.finish(gate_of)

    def const_row(row, here):
        return consts_ref[row : row + 1, here]

    far_load = pltpu.make_async_copy(gate_all.at[far_rows], far_weight, gate_sem.at[7])
    far_load.start()
    far_load.wait()
    for group in range(groups):
        here = lanes(group)
        value = gate_part[:, here] + dot_rows(normed[:, far_rows], far_weight[:, here])
        value = value * const_row(MASK_ROW, here)
        gate_part[:, here] = value
        gated = y[:, here] * (value * jax.nn.sigmoid(value))
        product = gated * (gated_grad[:, here] * const_row(GAIN_ROW, here))
        gated = gated * gated
        gated = gated[:, :PAIR] + gated[:, PAIR:]
        product = product[:, :PAIR] + product[:, PAIR:]
        squares[...] = gated if group == 0 else squares[...] + gated
        products[...] = product if group == 0 else products[...] + product
    lane = lax.broadcasted_iota(jnp.int32, (length, PAIR), 1)
    both = jnp.where(
        lane == 0,
        jnp.sum(squares[...], axis=1, keepdims=True),
        jnp.where(lane == 1, jnp.sum(products[...], axis=1, keepdims=True), 0.0),
    )
    stats[...] = both.T[0:8]

    def stats_copy(k):
        return pltpu.make_async_remote_copy(
            stats, stats_in.at[k - 1], stats_send.at[k - 1], stats_recv.at[k - 1],
            device_id={"fsdp": partner(k)}, device_id_type=MESH,
        )

    for k in (2, 3, 1):
        stats_copy(k).start()
    for k in (1, 2, 3):
        stats_copy(k).wait_recv()
    total = (stats[...] + stats_in[0]) + (stats_in[1] + stats_in[2])
    channel_count = active * HEAD_DIM
    inverse_out = lax.rsqrt(total[0:1] / channel_count + norm_eps)
    pulls = inverse_out * inverse_out * inverse_out / channel_count * total[1:2]
    scales = jnp.concatenate(
        [inverse_out, pulls, jnp.zeros((PAIR - 2, length), f32)], axis=0
    ).T
    inverse_out, pulls = scales[:, 0:1], scales[:, 1:2]

    def back_stores(group):
        slot, at, here = group % 2, 13 + 4 * group, lanes(group)
        return [
            store(back_tiles.at[slot, 0], gated_all.at[:, here], at),
            store(back_tiles.at[slot, 1], y_grad_all.at[:, here], at + 1),
            store(back_tiles.at[slot, 2], gate_grad_all.at[:, here], at + 2),
            store(back_tiles_t.at[slot], gated_t_all.at[here], at + 3),
        ]

    gain_grad_ref[...] = jnp.zeros_like(gain_grad_ref)
    for group in range(groups):
        here, slot = lanes(group), group % 2
        if group >= 2:
            for copy in back_stores(group - 2):
                copy.wait()
        value, grad, gain = gate_part[:, here], gated_grad[:, here], const_row(GAIN_ROW, here)
        gate = jax.nn.sigmoid(value)
        silu = value * gate
        y_here = y[:, here]
        gated = y_here * silu
        scaled = gated * inverse_out
        gated_low = (scaled * gain).astype(bf16)
        back_tiles[slot, 0] = gated_low
        back_tiles_t[slot] = gated_low.T
        gain_grad_ref[0:1, here] = jnp.sum(grad * scaled, axis=0, keepdims=True)
        back = inverse_out * (grad * gain) - gated * pulls
        back_tiles[slot, 1] = (back * silu).astype(bf16)
        back_tiles[slot, 2] = (
            back * y_here * (gate * (1.0 + value * (1.0 - gate))) * const_row(MASK_ROW, here)
        ).astype(bf16)
        for copy in back_stores(group):
            copy.start()

    for i in (2, 3):
        turned_store(i).wait()
    for group in range(groups - 2, groups):
        x_store(group).wait()
        states_store(group).wait()
        for copy in back_stores(group):
            copy.wait()
    cotangent_store.wait()
    for copy in normed_copies + cotangent_copies:
        copy.wait_send()
    for k in (1, 2, 3):
        shared_copy(k).wait_send()
        stats_copy(k).wait_send()
        for i in (small_part, x_of, gate_of):
            swap(i, k).wait_send()


def last_columns(members):
    shared = 2 * STATE // members
    source = np.arange(2 * STATE + HEADS)
    head = source - 2 * STATE
    target = np.where(
        source < 2 * STATE,
        source // shared * PAIR + source % shared,
        head // 2 % members * PAIR + shared + head // (2 * members) * 2 + head % 2,
    )
    turn = np.arange(members * PAIR)[:, None] == target[None, :]
    return jnp.asarray(turn.astype(np.float32), bf16)


def norm_gain_row(vectors_ref):
    return jnp.concatenate([vectors_ref[i : i + 1, :] for i in range(D // PAIR)], axis=1)


def vector_tiles(vectors):
    rows = -(-vectors.shape[0] // PAIR)
    return jnp.pad(vectors, (0, rows * PAIR - vectors.shape[0])).reshape(rows, PAIR)


def forward(
    tokens, cotangent, in_weight, out_weight, vectors, active,
):
    count, members = lax.axis_size("dp"), lax.axis_size("fsdp")
    own, sub, rows_out = tokens.shape[0], in_weight.shape[0], out_weight.shape[0]
    length, inner, shared = own * members, INNER // members, 2 * STATE // members
    chunks, groups = length // SPAN, inner // LANES
    assert groups == 4 and count == 8 and members == 4
    turn = last_columns(members)
    sd, dma = jax.ShapeDtypeStruct, pltpu.SemaphoreType.DMA
    vmem = pltpu.VMEM
    return pl.pallas_call(
        forward_kernel,
        in_specs=[whole_spec()] + any_specs(1) + [whole_spec()] * 6,
        out_specs=any_specs(12) + [whole_spec()] * 12,
        out_shape=[
            sd((D, PAIR), bf16),
            sd((D, inner), bf16),
            sd((D, inner), bf16),
            sd((inner, D), bf16),
            sd((length, D), bf16),
            sd((D, length), bf16),
            sd((length, inner), f32),
            sd((chunks, STATE, inner), bf16),
            sd((length, inner), bf16),
            sd((inner, length), bf16),
            sd((length, inner), bf16),
            sd((length, inner), bf16),
            sd((8, inner), f32),
            sd((8, PAIR), f32),
            sd((shared, PAIR), f32),
            sd((length, groups * PAIR), f32),
            sd((groups * 8, length), f32),
            sd((length, PAIR), f32),
            sd((length, STATE), bf16),
            sd((length, STATE), bf16),
            sd((STATE, length), bf16),
            sd((shared, length), f32),
            sd((shared, length), f32),
            sd((8, inner), f32),
        ],
        scratch_shapes=[
            vmem((members, sub, PAIR), bf16),
            vmem((members, sub, inner), bf16),
            vmem((members, sub, inner), bf16),
            vmem((rows_out, D), bf16),
            vmem((length, D), bf16),
            vmem((length, D), bf16),
            vmem((D, PAIR), bf16),
            vmem((STATE, length), bf16),
            vmem((members, shared, length), bf16),
            vmem((2, length, LANES), f32),
            vmem((2, chunks, STATE, LANES), bf16),
            vmem((length, inner), f32),
            vmem((length, inner), f32),
            vmem((length, inner), f32),
            vmem((2, D, LANES), bf16),
            vmem((D, inner), bf16),
            vmem((D // count, inner), bf16),
            vmem((2, LANES, D), bf16),
            vmem((2, D // 4, length), bf16),
            vmem((length, PAIR), f32),
            vmem((length, PAIR), f32),
            vmem((8, length), f32),
            vmem((3, 8, length), f32),
            vmem((2, 3, length, LANES), bf16),
            vmem((2, LANES, length), bf16),
            vmem((length + 8, LANES), f32),
            vmem((STATE, LANES), f32),
            vmem((PAIR, PAIR), f32),
            dma((6,)),
            dma((9,)),
            dma((9,)),
            dma((6,)),
            dma((6,)),
            RingGather.semaphores(4, count),
            RingGather.semaphores(4, count),
            dma((3,)),
            dma((3,)),
            dma((3,)),
            dma((3,)),
            dma((4,)),
            dma((8,)),
            dma((13 + 4 * groups,)),
        ],
        compiler_params=pltpu.CompilerParams(
            collective_id=0, has_side_effects=True, vmem_limit_bytes=VMEM_BYTES
        ),
        name="forward",
    )(
        tokens, cotangent, in_weight, out_weight, turn, vectors,
        jnp.broadcast_to(active.astype(f32), (8, PAIR)), block_mask(),
    )


def total_squares(value):
    return jnp.sum(jnp.sum(value * value, axis=0, keepdims=True), axis=1, keepdims=True)


def flipped(member, flip):
    return member + flip - 2 * flip * lax.rem(lax.div(member, flip), 2)


def shifted(value, by):
    length = value.shape[1]
    lane = lax.broadcasted_iota(jnp.int32, value.shape, 1)
    if by == 0:
        return value
    if by > 0:
        return jnp.where(lane >= by, pltpu.roll(value, by, 1), 0.0)
    return jnp.where(lane < length + by, pltpu.roll(value, length + by, 1), 0.0)


def backward_kernel(
    rows_ref, key_ref, query_ref, query_t_ref, block_ref, pick_ref, consts_ref, column_ref, heads_ref,
    head_pick_ref, shared_part_ref, shared_pre_ref, taps_ref, vectors_own_ref, gate_gain_ref,
    weight_small_ref,
    tokens_hbm, x_hbm, y_grad_hbm, states_hbm, columns_hbm, gated_hbm, gated_t_hbm, gate_grad_hbm, normed_t_hbm,
    cotangents_hbm, cotangent_hbm, weight_out_hbm, weight_gate_hbm, weight_x_hbm,
    layer_out_hbm, token_grad_hbm, gate_back, x_back, small_back,
    out_raw_ref, vectors_ref, gains_ref, total_ref,
    x_part, y_grad, states, columns, padded, following, state_back, inner_grad,
    x_grad, key_grad, query_grad, sums_ref, rest_ref, channel_ref,
    normed_t, gate_grad, gated_t, cotangent, wide,
    kept, near_out, near_in,
    shared_out, shared_in, raw, small_t, small_n,
    vector_sum, vector_in, gain_parts, gain_total, gate_out, x_out, small_out, scalar_out, scalar_in,
    first_held, first_arrived, gate_held, gate_arrived, small_held, small_arrived,
    load_sem, scan_sem, chunk_sem, store_sem, local_sem,
    near_send, near_recv, swap_send, swap_recv, vector_send, vector_recv, gain_send, gain_recv, return_send, return_recv,
    scalar_send, scalar_recv, ring_send, ring_recv, ring_free, near_free,
):
    ring = Ring()
    d, f, count, far = ring.me, lax.axis_index("fsdp"), ring.count, ring.far
    length, width = x_grad.shape
    groups, chunks = width // LANES, length // SPAN
    rows, rows_out, tokens = D // count, width // count, tokens_hbm.shape[0]
    sub, shared, heads = gate_back.shape[1], shared_part_ref.shape[0], HEADS // 4
    precise = partial(jnp.dot, precision=highest, preferred_element_type=f32)
    halves = [pl.ds(0, width // 2), pl.ds(width // 2, width // 2)]
    out_ring, gate_ring, small_ring, *x_rings = (
        RingScatter(ring, held, arrived, ring_send.at[i], ring_recv.at[i])
        for i, (held, arrived) in enumerate(
            [
                (first_held, first_arrived),
                (gate_held, gate_arrived),
                (small_held, small_arrived),
            ]
            + [(first_held.at[:, :, :, at], first_arrived.at[:, :, at]) for at in halves]
        )
    )

    def load(source, target, at):
        return pltpu.make_async_copy(source, target, load_sem.at[at])

    def lanes(group):
        return pl.ds(group * LANES, LANES)

    def scan_loads(group):
        slot = group % 2
        return [
            pltpu.make_async_copy(source, target, scan_sem.at[slot, i])
            for i, (source, target) in enumerate(
                [
                    (y_grad_hbm.at[:, lanes(group)], y_grad.at[slot]),
                    (states_hbm.at[:, :, lanes(group)], states.at[slot]),
                    (columns_hbm.at[:, pl.ds(group * PAIR, PAIR)], columns.at[slot]),
                ]
            )
        ]

    def x_load(group):
        return pltpu.make_async_copy(x_hbm.at[:, lanes(group)], x_part, scan_sem.at[2, 0])

    def chunk_load(owner, slot):
        return pltpu.make_async_copy(
            row_slice(gated_t_hbm, owner * rows_out, rows_out), gated_t.at[slot],
            chunk_sem.at[slot],
        )

    def hop_loads(hop):
        if hop == far:
            return [chunk_load(d, 2 * (hop % 2))]
        ways = (0,) if hop == 0 else (0, 1)
        return [chunk_load(out_ring.owner(way, hop), 2 * (hop % 2) + way) for way in ways]

    gated_blocks = [x_out, gate_out]

    def gated_load(i, flip):
        return load(
            row_slice(gated_hbm, partner(flip) * tokens, tokens), gated_blocks[i], 4 + i
        )

    cotangent_load = load(cotangents_hbm, cotangent, 0)
    normed_load = load(normed_t_hbm, normed_t, 1)
    gate_grad_load = load(gate_grad_hbm, gate_grad, 2)
    out_load = load(weight_out_hbm, wide, 3)
    for copy in hop_loads(0) + [cotangent_load]:
        copy.start()
    greet(
        [{"fsdp": partner(k)} for k in (1, 2, 3)]
        + [{"dp": lax.rem(d + k, count)} for k in range(1, count)]
    )

    def rows_of(owner):
        return pl.ds(pl.multiple_of(owner * rows, rows), rows)

    def out_term(hop):
        def term(owner, way):
            value = dot_rows(gated_t[2 * (hop % 2) + way], cotangent[...])
            return jnp.concatenate([value[:, :width], value[:, width:]], axis=0)

        return term

    def out_hop(hop):
        for copy in hop_loads(hop):
            copy.wait()
        out_ring.start(hop, out_term(hop))
        for copy in hop_loads(hop + 1):
            copy.start()

    def gate_term(owner, way):
        return dot_rows(normed_t[rows_of(owner), :], gate_grad[...])

    def x_term(at):
        return lambda owner, way: dot_rows(normed_t[rows_of(owner), :], x_grad[:, at])

    def x_hop(hop):
        for x_ring, at in zip(x_rings, halves):
            x_ring.start(hop, x_term(at))

    def small_term(owner, way):
        return dot_lanes(normed_t[rows_of(owner), :], small_t[...])

    def to_partner(k, source, target, send, recv, at):
        return pltpu.make_async_remote_copy(
            source, target, send.at[at], recv.at[at],
            device_id={"fsdp": partner(k)}, device_id_type=MESH,
        )

    def near_copy(use, i):
        return to_partner(
            2 if i == 2 else 1, near_out.at[i], near_in.at[i], near_send, near_recv, 3 * use + i
        )

    def scan(group):
        slot = group % 2
        x_load(group).wait()
        for copy in scan_loads(group):
            copy.wait()
        if group + 1 < groups:
            for copy in scan_loads(group + 1):
                copy.start()
        here = lanes(group)
        scan_backward_group(
            x_part, consts_ref.at[:, here], columns.at[slot], rows_ref.at[pl.ds(group * 8, 8)],
            key_ref, query_ref, query_t_ref, block_ref, pick_ref.at[pl.ds(3 * group, 3)],
            y_grad.at[slot], states.at[slot],
            x_grad.at[:, here], key_grad, query_grad, sums_ref, rest_ref.at[:, :, here],
            channel_ref.at[:, here], padded, following, state_back, inner_grad,
        )
        if group + 1 < groups:
            x_load(group + 1).start()

    cotangent_load.wait()
    normed_load.start()
    gate_grad_load.start()
    out_hop(0)
    out_load.start()
    gated_load(0, 3).start()
    gated_load(1, 1).start()
    x_load(0).start()
    for copy in scan_loads(0):
        copy.start()
    scan_backward_start(key_grad, query_grad, sums_ref, inner_grad)
    normed_load.wait()
    gate_grad_load.wait()
    gate_ring.start(0, gate_term)

    def added_block(i):
        return dot_rows(gated_blocks[i][...], wide[...])

    out_load.wait()
    for i, flip in ((0, 3), (1, 1)):
        gated_load(i, flip).wait()
        near_out[1 - i] = added_block(i).astype(bf16)
        near_copy(0, 1 - i).start()
        gated_load(i, (2, 0)[i]).start()
    out_hop(1)
    scan(0)
    gate_ring.start(1, gate_term)
    gated_load(0, 2).wait()
    value = added_block(0)
    near_copy(0, 1).wait_recv()
    near_out[2] = (value + near_in[1].astype(f32)).astype(bf16)
    near_copy(0, 2).start()
    gated_load(1, 0).wait()
    kept[...] = added_block(1)
    half = D // 4

    def weight_tiles(source, target, at):
        return [
            load(
                source.at[pl.ds(i * half, half)],
                target.at[pl.ds(i // 2 * half, half), pl.ds(i % 2 * width, width)], at + i,
            )
            for i in range(4)
        ]

    gate_tiles = weight_tiles(weight_gate_hbm, wide, 6)
    for copy in gate_tiles:
        copy.start()
    out_hop(2)
    scan(1)
    gate_ring.start(2, gate_term)
    scan(2)

    near_copy(0, 0).wait_send()
    tokens_load = load(tokens_hbm, near_out.at[0], 15)
    tokens_load.start()
    near_copy(0, 0).wait_recv()
    near_copy(0, 2).wait_recv()
    tokens_load.wait()
    value = near_out[0].astype(f32) + (
        (kept[...] + near_in[0].astype(f32)) + near_in[2].astype(f32)
    )
    for k in (0, 1):
        pl.semaphore_signal(
            near_free.at[k], inc=1, device_id={"fsdp": partner(k + 1)}, device_id_type=MESH
        )
    for i in (1, 2):
        near_copy(0, i).wait_send()
    near_out[2] = value.astype(bf16)
    layer_store = pltpu.make_async_copy(near_out.at[2], layer_out_hbm, store_sem.at[0])
    layer_store.start()

    for hop in range(3, far):
        out_hop(hop)
    scan(3)
    scan_backward_finish(key_ref, query_ref, key_grad, query_grad, inner_grad)

    for i, ref in ((0, key_grad), (2, query_grad)):
        across = ref[...].T
        for j in (0, 1):
            shared_out[i + j] = across[j * shared : (j + 1) * shared].astype(bf16)

    def shared_copy(k):
        return to_partner(
            k, shared_out.at[partner(k)], shared_in.at[k - 1], swap_send, swap_recv, k - 1
        )

    for k in (2, 3, 1):
        shared_copy(k).start()
    for copy in hop_loads(far):
        copy.wait()
    value = out_ring.finish(out_term(far))
    out_raw_ref[...] = jnp.concatenate([value[:rows_out], value[rows_out:]], axis=1)
    squares = total_squares(value)
    for way in (0, 1):
        pl.semaphore_signal(
            ring_free.at[way], inc=1, device_id=ring.target(1 - way), device_id_type=MESH
        )
    x_tiles = weight_tiles(weight_x_hbm, cotangent, 10)
    for copy in x_tiles:
        copy.start()
    for way in (0, 1):
        pl.semaphore_wait(ring_free.at[way], 1)
    x_hop(0)

    for hop in range(3, far):
        gate_ring.start(hop, gate_term)

    at_row = lax.broadcasted_iota(jnp.int32, (SPAN, SPAN), 0)
    at_lane = lax.broadcasted_iota(jnp.int32, (SPAN, SPAN), 1)
    later = (at_lane >= at_row).astype(f32)
    earlier = (at_lane < at_row).astype(f32)
    rest = precise(
        jnp.concatenate([rest_ref[c] for c in range(chunks)], axis=0), head_pick_ref[...]
    )
    decay, head_mask = heads_ref[0:1, :], heads_ref[1:2, :]
    step_bias_grad = jnp.zeros((1, PAIR), f32)
    decay_grad = jnp.zeros((1, PAIR), f32)
    for c in range(chunks):
        here = slice(c * SPAN, (c + 1) * SPAN)
        sums = sums_ref[here, :]
        log_grad = (
            precise(later, sums)
            + pltpu.roll(precise(earlier, sums), PAIR - heads, 1)
            + rest[c : c + 1]
        )
        steps = pltpu.roll(column_ref[here, :], PAIR - heads, 1)
        logits = pltpu.roll(column_ref[here, :], PAIR - 2 * heads, 1)
        raw_grad = (decay * log_grad + pltpu.roll(sums, PAIR - 2 * heads, 1)) * jax.nn.sigmoid(
            logits
        )
        step_bias_grad = step_bias_grad + jnp.sum(raw_grad, axis=0, keepdims=True)
        decay_grad = decay_grad + jnp.sum(steps * log_grad, axis=0, keepdims=True)
        raw[here, :] = raw_grad * head_mask
    decay_grad = decay_grad * decay

    for k in (2, 3, 1):
        shared_copy(k).wait_recv()
    part, pre = shared_part_ref[...], shared_pre_ref[...]
    gate = jax.nn.sigmoid(pre)
    pre_grad = shared_out[f].astype(f32)
    for k in (1, 2, 3):
        pre_grad = pre_grad + shared_in[k - 1].astype(f32)
    pre_grad = pre_grad * (gate * (1.0 + pre * (1.0 - gate)))
    shared_grad = jnp.zeros_like(pre_grad)
    lane = lax.broadcasted_iota(jnp.int32, (shared, PAIR), 1)
    shared_sums = jnp.where(lane == CONV, jnp.sum(pre_grad, axis=1, keepdims=True), 0.0)
    for k in range(CONV):
        shift = CONV - 1 - k
        shared_grad = shared_grad + taps_ref[:, k : k + 1] * shifted(pre_grad, -shift)
        shared_sums = shared_sums + jnp.where(
            lane == k, jnp.sum(pre_grad * shifted(part, shift), axis=1, keepdims=True), 0.0
        )
    small_t[0:shared, :] = shared_grad.astype(bf16)
    small_t[shared:, :] = raw[...].T[0 : PAIR - shared].astype(bf16)
    small_n[...] = small_t[...].T
    small_ring.start(0, small_term)

    vector_sum[...] = jnp.zeros_like(vector_sum)
    vector_sum[0:1, :] = gate_gain_ref[0:1, :]
    vector_sum[1 : CONV + 3, :] = channel_ref[0 : CONV + 2, :]
    vector_sum[15:16, 0:PAIR] = step_bias_grad
    vector_sum[15:16, PAIR : 2 * PAIR] = decay_grad
    across = jnp.concatenate([shared_sums, jnp.zeros((PAIR - shared, PAIR), f32)], axis=0)
    vector_sum[16:24, 0:PAIR] = across.T[0:8]
    flips = []
    while 1 << len(flips) < count:
        flips.append(1 << len(flips))

    def vector_copy(step):
        return pltpu.make_async_remote_copy(
            vector_in.at[step, 0], vector_in.at[step, 1], vector_send.at[step],
            vector_recv.at[step],
            device_id={"dp": flipped(d, flips[step])}, device_id_type=MESH,
        )

    def vector_step(step):
        if step:
            vector_copy(step - 1).wait_recv()
            vector_sum[...] = vector_sum[...] + vector_in[step - 1, 1]
        if step < len(flips):
            vector_in[step, 0] = vector_sum[...]
            vector_copy(step).start()

    def vector_spread(k):
        return to_partner(
            k, vector_sum, vectors_ref.at[f], vector_send, vector_recv, len(flips) + k - 1
        )

    vector_step(0)

    for copy in gate_tiles + x_tiles:
        copy.wait()

    def back_block(flip, target, kind):
        here = pl.ds(pl.multiple_of(partner(flip) * tokens, tokens), tokens)
        for i in range(4):
            at = (slice(i // 2 * half, (i // 2 + 1) * half), slice(i % 2 * width, (i % 2 + 1) * width))
            value = (
                dot_lanes(gate_grad[here, :], wide[at])
                + dot_lanes(x_grad[here, :], cotangent[at])
                + dot_lanes(small_n[here, :], weight_small_ref[i * half : (i + 1) * half, :])
            )
            target[:, i * half : (i + 1) * half] = value.astype(kind)

    for k in (0, 1):
        pl.semaphore_wait(near_free.at[k], 1)
    back_block(3, near_out.at[1], bf16)
    near_copy(1, 1).start()
    back_block(2, kept, f32)
    near_copy(1, 1).wait_recv()
    layer_store.wait()
    near_out[2] = (kept[...] + near_in[1].astype(f32)).astype(bf16)
    near_copy(1, 2).start()
    small_ring.start(1, small_term)
    vector_step(1)
    back_block(1, near_out.at[0], bf16)
    near_copy(1, 0).start()
    x_hop(1)
    vector_step(2)
    back_block(0, kept, f32)
    near_copy(1, 1).wait_send()
    own_load = load(cotangent_hbm, near_out.at[1], 14)
    own_load.start()
    near_copy(1, 0).wait_send()
    tokens_load = load(tokens_hbm, near_out.at[0], 15)
    tokens_load.start()

    returned = [(gate_out, gate_back), (small_out, small_back)] + [
        (x_out.at[:, at], x_back.at[:, :, at]) for at in halves
    ]

    def return_copy(part, k):
        source, target = returned[part]
        return to_partner(
            k, row_slice(source, partner(k) * sub, sub), target.at[f],
            return_send, return_recv, part * 3 + k - 1,
        )

    def own_copy(part):
        source, target = returned[part]
        return pltpu.make_async_copy(
            row_slice(source, f * sub, sub), target.at[f], local_sem.at[part]
        )

    def give_back(part, value):
        returned[part][0][...] = value.astype(bf16)
        for k in (2, 3, 1):
            return_copy(part, k).start()
        own_copy(part).start()

    value = gate_ring.finish(gate_term)
    squares = squares + total_squares(value)
    give_back(0, value)
    small_ring.start(2, small_term)
    x_hop(2)
    vector_step(3)
    for k in (2, 3, 1):
        vector_spread(k).start()
    vectors_ref[f] = vector_sum[...]
    near_copy(1, 0).wait_recv()
    near_copy(1, 2).wait_recv()
    own_load.wait()
    tokens_load.wait()
    inputs = near_out[0].astype(f32)
    inverse = lax.rsqrt(jnp.sum(inputs * inputs, axis=1, keepdims=True) / D + norm_eps)
    normed_grad = (kept[...] + near_in[0].astype(f32)) + near_in[2].astype(f32)
    pulled = normed_grad * norm_gain_row(vectors_own_ref)
    scaled = inputs * inverse
    input_grad = inverse * (
        pulled - scaled * (jnp.sum(pulled * scaled, axis=1, keepdims=True) / D)
    )
    near_out[1] = (near_out[1].astype(f32) + input_grad).astype(bf16)
    token_store = pltpu.make_async_copy(near_out.at[1], token_grad_hbm, store_sem.at[1])
    token_store.start()
    gain_grad = jnp.sum(normed_grad * scaled, axis=0, keepdims=True)

    for i in range(8):
        gain_parts[0, i : i + 1, :] = gain_grad[:, i * (D // 8) : (i + 1) * (D // 8)]

    def over_dp(k, source, target, send, recv, at):
        member = d
        for bit in flips:
            if k & bit:
                member = flipped(member, bit)
        return pltpu.make_async_remote_copy(
            source, target, send.at[at], recv.at[at],
            device_id={"dp": member}, device_id_type=MESH,
        )

    def gain_copy(k):
        return over_dp(k, gain_parts.at[0], gain_parts.at[k], gain_send, gain_recv, k)

    def paired(parts):
        while len(parts) > 1:
            parts = [parts[i] + parts[i + 1] for i in range(0, len(parts), 2)]
        return parts[0]

    for k in range(count - 1, 0, -1):
        gain_copy(k).start()
    for hop in range(3, far):
        small_ring.start(hop, small_term)
        x_hop(hop)
    for k in range(1, count):
        gain_copy(k).wait_recv()
    gain_total[...] = paired([gain_parts[k] for k in range(count)])

    def gain_spread(k):
        return to_partner(
            k, gain_total, gains_ref.at[f], gain_send, gain_recv, count + k - 1
        )

    for k in (2, 3, 1):
        gain_spread(k).start()
    gains_ref[f] = gain_total[...]

    value = small_ring.finish(small_term)
    squares = squares + total_squares(value)
    give_back(1, value)
    for part, (x_ring, at) in enumerate(zip(x_rings, halves)):
        value = x_ring.finish(x_term(at))
        give_back(2 + part, value)
        squares = squares + total_squares(value)

    total = jnp.broadcast_to(squares, (8, PAIR))
    scalar_out[0] = total

    def near_scalar(k):
        return to_partner(
            k, scalar_out.at[0], scalar_in.at[k], scalar_send, scalar_recv, k
        )

    for k in (2, 3, 1):
        near_scalar(k).start()
    for k in (2, 3, 1):
        near_scalar(k).wait_recv()
    total = (total + scalar_in[1]) + (scalar_in[2] + scalar_in[3])
    scalar_out[1] = total

    def far_scalar(k):
        return over_dp(
            k, scalar_out.at[1], scalar_in.at[3 + k], scalar_send, scalar_recv, 3 + k
        )

    for k in range(count - 1, 0, -1):
        far_scalar(k).start()
    parts = [total]
    for k in range(1, count):
        far_scalar(k).wait_recv()
        parts.append(scalar_in[3 + k])
    total_ref[...] = paired(parts)

    for k in (1, 2, 3):
        vector_spread(k).wait_recv()
        vector_spread(k).wait_send()
        gain_spread(k).wait_recv()
        gain_spread(k).wait_send()
        shared_copy(k).wait_send()
        near_scalar(k).wait_send()
        for i in range(4):
            return_copy(i, k).wait_recv()
            return_copy(i, k).wait_send()
    for k in range(1, count):
        far_scalar(k).wait_send()
        gain_copy(k).wait_send()
    near_copy(1, 2).wait_send()
    for i in range(4):
        own_copy(i).wait()
    for step in range(len(flips)):
        vector_copy(step).wait_send()
    token_store.wait()


def backward(
    scan_inputs, queries_t, column, heads, shared_part, shared_pre, taps, vectors, gate_gain, tokens,
    weight_small, x, y_grad, states, gated, gated_t, gate_grad, normed_t, cotangents, cotangent,
    weight_out, weight_gate, weight_x,
):
    consts, columns, rows_t, keys, queries = scan_inputs
    length, width = x.shape
    chunks, groups = length // SPAN, width // LANES
    count, members = lax.axis_size("dp"), lax.axis_size("fsdp")
    rows, rows_out = D // count, width // count
    sub, own, shared = rows // members, tokens.shape[0], shared_part.shape[0]
    far = count // 2
    hops = max(count - 1, 1).bit_length()
    assert groups == 4 and count == 8 and members == 4 and 2 * rows_out == rows and 2 * width == D
    head_pick = jnp.asarray(
        (np.arange(width)[:, None] // HEAD_DIM == np.arange(PAIR)[None, :]).astype(np.float32)
    )
    dma, vmem, sd = pltpu.SemaphoreType.DMA, pltpu.VMEM, jax.ShapeDtypeStruct
    return pl.pallas_call(
        backward_kernel,
        in_specs=[whole_spec()] * 16 + any_specs(14),
        out_specs=any_specs(5) + [whole_spec()] * 4,
        out_shape=[
            sd((own, D), bf16),
            sd((own, D), bf16),
            sd((members, sub, width), bf16),
            sd((members, sub, width), bf16),
            sd((members, sub, PAIR), bf16),
            sd((rows_out, D), f32),
            sd((members, 24, width), f32),
            sd((members, 8, D // 8), f32),
            sd((8, PAIR), f32),
        ],
        scratch_shapes=[
            vmem((length, LANES), f32),
            vmem((2, length, LANES), bf16),
            vmem((2, chunks, STATE, LANES), bf16),
            vmem((2, length, PAIR), f32),
            vmem((length + 8, LANES), f32),
            vmem((8, LANES), f32),
            vmem((STATE, LANES), f32),
            vmem((chunks, SPAN, SPAN), f32),
            vmem((length, width), bf16),
            vmem((length, STATE), f32),
            vmem((length, STATE), f32),
            vmem((length, PAIR), f32),
            vmem((chunks, 1, width), f32),
            vmem((8, width), f32),
            vmem((D, length), bf16),
            vmem((length, width), bf16),
            vmem((4, rows_out, length), bf16),
            vmem((length, D), bf16),
            vmem((width, D), bf16),
            vmem((own, D), f32),
            vmem((3, own, D), bf16),
            vmem((3, own, D), bf16),
            vmem((members, shared, length), bf16),
            vmem((members - 1, shared, length), bf16),
            vmem((length, PAIR), f32),
            vmem((PAIR, length), bf16),
            vmem((length, PAIR), bf16),
            vmem((24, width), f32),
            vmem((hops, 2, 24, width), f32),
            vmem((count, 8, D // 8), f32),
            vmem((8, D // 8), f32),
            vmem((rows, width), bf16),
            vmem((rows, width), bf16),
            vmem((rows, PAIR), bf16),
            vmem((2, 8, PAIR), f32),
            vmem((3 + count, 8, PAIR), f32),
        ]
        + RingScatter.scratch(count, rows, width) * 2
        + RingScatter.scratch(count, rows, PAIR)
        + [
            dma((16,)),
            dma((3, 3)),
            dma((4,)),
            dma((2,)),
            dma((4,)),
            dma((6,)),
            dma((6,)),
            dma((3,)),
            dma((3,)),
            dma((hops + 3,)),
            dma((hops + 3,)),
            dma((count + 3,)),
            dma((count + 3,)),
            dma((12,)),
            dma((12,)),
            dma((3 + count,)),
            dma((3 + count,)),
            dma((5, 2 * far)),
            dma((5, 2 * far)),
            pltpu.SemaphoreType.REGULAR((2,)),
            pltpu.SemaphoreType.REGULAR((2,)),
        ],
        compiler_params=pltpu.CompilerParams(
            collective_id=1, has_side_effects=True, vmem_limit_bytes=VMEM_BYTES
        ),
        name="backward",
    )(
        rows_t, keys, queries, queries_t, block_mask(), pick_masks(groups), consts, column, heads,
        head_pick, shared_part, shared_pre, taps, vectors, gate_gain, weight_small,
        tokens, x, y_grad, states, columns, gated, gated_t, gate_grad, normed_t, cotangents, cotangent,
        weight_out, weight_gate, weight_x,
    )


OPTIMIZER_STEPS = 4


def optimizer_kernel(
    squares_ref, parts_ref, gains_ref, vector_ref, vector_first_ref, vector_second_ref, turn_ref,
    gate_ref, x_ref, small_ref, in_ref, in_first_ref, in_second_ref,
    out_raw_ref, out_ref, out_first_ref, out_second_ref, layer_ref, token_ref,
    norm_ref, vector_grad_ref, vector_moment_ref, vector_square_ref, vector_master_ref,
    in_grad_ref, in_moment_ref, in_square_ref, in_master_ref, in_rounded_ref,
    out_grad_ref, out_moment_ref, out_square_ref, out_master_ref, out_rounded_ref,
    layer_out_ref, token_out_ref,
    joined, factor_ref, in_raw,
):
    members = parts_ref.shape[0]
    pairs = INNER // PAIR
    shared, heads = 2 * STATE // members, HEADS // members
    layer_out_ref[...] = layer_ref[...]
    token_out_ref[...] = token_ref[...]

    @pl.when(pl.program_id(0) == 0)
    def _():
        joined[...] = jnp.zeros_like(joined)
        width = parts_ref.shape[2]
        for i in range(D // PAIR):
            row = i * PAIR // (D // 8)
            lanes = slice(i * PAIR % (D // 8), i * PAIR % (D // 8) + PAIR)
            value = gains_ref[0, row : row + 1, lanes]
            for member in range(1, members):
                value = value + gains_ref[member, row : row + 1, lanes]
            joined[i : i + 1, :] = value

        def put_channels(first_row, row):
            for pair in range(pairs):
                at = pair // members
                joined[first_row + pair : first_row + pair + 1, :] = parts_ref[
                    pair % members, row : row + 1, at * PAIR : (at + 1) * PAIR
                ]

        put_channels(D // PAIR, 0)
        each = PAIR // shared
        for k in range(CONV + 1):
            first_row = TAPS_ROW + k * (XBC // PAIR)
            put_channels(first_row, 1 + k)
            for i in range(members // each):
                joined[first_row + pairs + i : first_row + pairs + i + 1, :] = jnp.concatenate(
                    [
                        parts_ref[i * each + j, 16 + k : 17 + k, 0:shared]
                        for j in range(each)
                    ],
                    axis=1,
                )
        precise = partial(jnp.dot, precision=highest, preferred_element_type=f32)
        last, skips = jnp.zeros((1, PAIR), f32), jnp.zeros((1, PAIR), f32)
        local_at = lax.broadcasted_iota(jnp.int32, (PAIR, PAIR), 0)
        head_at = lax.broadcasted_iota(jnp.int32, (PAIR, PAIR), 1)
        channel_head = lax.broadcasted_iota(jnp.int32, (width, PAIR), 0) // HEAD_DIM
        wide_at = lax.broadcasted_iota(jnp.int32, (width, PAIR), 1)
        for member in range(members):
            home = local_at // 2 * 2 * members + 2 * member + local_at % 2
            known = local_at < heads
            biases = parts_ref[member, 15:16, 0:PAIR]
            decays = parts_ref[member, 15:16, PAIR : 2 * PAIR]
            last = last + precise(biases, ((head_at == home) & known).astype(f32))
            last = last + precise(decays, ((head_at == home + HEADS) & known).astype(f32))
            home = channel_head // 2 * 2 * members + 2 * member + channel_head % 2
            skips = skips + precise(
                parts_ref[member, CONV + 2 : CONV + 3, :], (wide_at == home).astype(f32)
            )
        joined[LAST_ROW : LAST_ROW + 1, :] = last
        joined[LAST_ROW + 1 : LAST_ROW + 2, :] = skips
        vector_raw = joined[...]
        norm = jnp.sqrt(squares_ref[...] + total_squares(vector_raw))
        norm_ref[0, 0] = norm[0, 0]
        factor = jnp.minimum(1.0, clip_norm / (norm + 1e-06))
        factor_ref[...] = factor
        grad = vector_raw * factor[0:1, 0:1]
        vector_grad_ref[...] = grad
        vector_moment_ref[...], vector_square_ref[...], vector_master_ref[...] = adamw(
            vector_ref[...], vector_first_ref[...], vector_second_ref[...], grad, rate_vectors
        )

    factor = factor_ref[0:1, 0:1]
    for pair in range(pairs):
        at = pair // members
        lanes, held = slice(pair * PAIR, (pair + 1) * PAIR), slice(at * PAIR, (at + 1) * PAIR)
        in_raw[:, lanes] = gate_ref[pair % members, :, held].astype(f32)
        in_raw[:, INNER + pair * PAIR : INNER + (pair + 1) * PAIR] = x_ref[
            pair % members, :, held
        ].astype(f32)
    small = jnp.concatenate([small_ref[i] for i in range(members)], axis=1)
    in_raw[:, 2 * INNER :] = dot_rows(small, turn_ref[...])
    grad = in_raw[...] * factor
    in_grad_ref[...] = grad
    in_moment_ref[...], in_square_ref[...], master = adamw(
        in_ref[...], in_first_ref[...], in_second_ref[...], grad, rate_in_proj
    )
    in_master_ref[...] = master
    in_rounded_ref[...] = master.astype(bf16)
    grad = out_raw_ref[...] * factor
    out_grad_ref[...] = grad
    out_moment_ref[...], out_square_ref[...], master = adamw(
        out_ref[...], out_first_ref[...], out_second_ref[...], grad, rate_out_proj
    )
    out_master_ref[...] = master
    out_rounded_ref[...] = master.astype(bf16)


def optimizer(squares, parts, gains, vectors, gate, x, small, in_state, out_raw, out_state, passed):
    members, rows, width = x.shape
    in_shape, out_shape = in_state[0].shape, out_state[0].shape
    steps = OPTIMIZER_STEPS
    step_rows = rows // steps
    piece = lambda lanes: pl.BlockSpec((members, step_rows, lanes), lambda i: (0, i, 0))
    in_flat = pl.BlockSpec((step_rows, in_shape[1]), lambda i: (i, 0))
    out_flat = pl.BlockSpec((out_shape[0] // steps, out_shape[1]), lambda i: (i, 0))
    row_flat = pl.BlockSpec((passed[0].shape[0] // steps, D), lambda i: (i, 0))
    sd = jax.ShapeDtypeStruct
    vector_shape = sd(vectors[0].shape, f32)
    return pl.pallas_call(
        optimizer_kernel,
        grid=(steps,),
        in_specs=[whole_spec()] * 7
        + [piece(width), piece(width), piece(PAIR)]
        + [in_flat] * 3
        + [out_flat] * 4
        + [row_flat] * 2,
        out_specs=[pl.BlockSpec(memory_space=pltpu.SMEM)]
        + [whole_spec()] * 4
        + [in_flat] * 5
        + [out_flat] * 5
        + [row_flat] * 2,
        out_shape=[sd((1, 1), f32)]
        + [vector_shape] * 4
        + [sd(in_shape, f32)] * 4
        + [sd(in_shape, bf16)]
        + [sd(out_shape, f32)] * 4
        + [sd(out_shape, bf16)]
        + [sd(v.shape, v.dtype) for v in passed],
        scratch_shapes=[
            pltpu.VMEM(vectors[0].shape, f32),
            pltpu.VMEM((8, PAIR), f32),
            pltpu.VMEM((step_rows, in_shape[1]), f32),
        ],
        compiler_params=pltpu.CompilerParams(vmem_limit_bytes=VMEM_BYTES),
        name="optimizer",
    )(
        squares, parts, gains, *vectors, last_columns(members), gate, x, small, *in_state, out_raw,
        *out_state, *passed,
    )


def unpack(vectors):
    offset = D + INNER
    taps_end = offset + CONV * XBC
    heads_start = taps_end + XBC
    norm_gain = vectors[:D]
    gate_gain = vectors[D:offset]
    filter_taps = vectors[offset:taps_end].reshape(CONV, XBC)
    filter_bias = vectors[taps_end:heads_start]
    step_bias = vectors[heads_start : heads_start + HEADS]
    decay_log = vectors[heads_start + HEADS : heads_start + 2 * HEADS]
    skip_gain = vectors[heads_start + 2 * HEADS : heads_start + 3 * HEADS]
    return (norm_gain, gate_gain, filter_taps, filter_bias, step_bias, decay_log, skip_gain)


def adamw(weight, moment, square, gradient, step_rate):
    moment_new = beta_first * moment + (1.0 - beta_first) * gradient
    square_new = beta_second * square + (1.0 - beta_second) * gradient * gradient
    moment_hat = moment_new / (1.0 - beta_first**STEP)
    square_hat = square_new / (1.0 - beta_second**STEP)
    weight_new = weight - step_rate * (
        moment_hat / (jnp.sqrt(square_hat) + adam_eps) + weight_decay * weight
    )
    return (moment_new, square_new, weight_new)


def on_device(
    tokens,
    widths,
    cotangent,
    in_weight,
    in_first,
    in_second,
    out_weight,
    out_first,
    out_second,
    vectors,
    vector_first,
    vector_second,
):
    fsdp = lax.axis_size("fsdp")
    me = lax.axis_index("fsdp")
    heads = HEADS // fsdp
    inner = INNER // fsdp
    shared = 2 * STATE // fsdp
    pairs = HEADS // 2 // fsdp
    rows_in, rows_out = in_weight.shape[0], out_weight.shape[0]
    length = tokens.shape[0] * fsdp
    chunks = length // SPAN
    in_kernels = uses_ring("dp") and rows_out == PAIR and rows_in % 16 == 0

    def own_channels(v):
        lead = v.shape[:-1]
        cut = v.reshape(lead + (pairs, fsdp, PAIR))
        return lax.dynamic_index_in_dim(cut, me, len(lead) + 1, False).reshape(lead + (inner,))

    def own_heads(v):
        return lax.dynamic_index_in_dim(v.reshape(pairs, fsdp, 2), me, 1, False).reshape(heads)

    def own_shared(v):
        return lax.dynamic_slice_in_dim(v, me * shared, shared, v.ndim - 1)

    norm_gain, gate_gain, filter_taps, filter_bias, step_bias, decay_log, skip_gain = unpack(
        vectors
    )
    gain_own = own_channels(gate_gain)[None]
    taps_own = own_channels(filter_taps[:, :INNER])
    bias_own = own_channels(filter_bias[:INNER])[None]
    taps_shared = own_shared(filter_taps[:, INNER:])
    bias_shared = own_shared(filter_bias[INNER:])
    step_bias_own, decay_own = own_heads(step_bias), -jnp.exp(own_heads(decay_log))
    skip_own = jnp.repeat(own_heads(skip_gain), HEAD_DIM)[None]

    width_index = widths[0]
    active = HEADS // 8 * jnp.left_shift(jnp.int32(1), width_index)
    head_mask = (jnp.arange(heads, dtype=jnp.int32) < active // fsdp).astype(f32)
    mask = jnp.repeat(head_mask, HEAD_DIM)[None]
    channel_count = (active * HEAD_DIM).astype(f32)

    inputs = tokens.astype(f32)
    inverse_in = lax.rsqrt(jnp.mean(inputs * inputs, axis=-1, keepdims=True) + norm_eps)

    if in_kernels:
        vector_state = [vector_tiles(v) for v in (vectors, vector_first, vector_second)]
        (
            weight_shared, weight_x, weight_gate, weight_out, cotangents, normed_t, x_part, states,
            gated_low, gated_t, y_grad, gate_grad, consts, head_consts, shared_taps, head_columns,
            head_rows, head_all, keys, queries, queries_t, shared_part, shared_pre, gain_grad,
        ) = forward(tokens, cotangent, in_weight, out_weight, vector_state[0], active)
        scan_inputs = (consts, head_columns, head_rows, keys, queries)
    else:
        in_low = in_weight.astype(bf16)
        shared_cut = jnp.concatenate(
            [
                in_low[:, 2 * INNER : 2 * INNER + 2 * STATE]
                .reshape(rows_in, fsdp, shared)
                .transpose(1, 0, 2),
                in_low[:, 2 * INNER + 2 * STATE :]
                .reshape(rows_in, pairs, fsdp, 2)
                .transpose(2, 0, 1, 3)
                .reshape(fsdp, rows_in, heads),
            ],
            axis=2,
        )

        def channel_cut(part):
            return (
                part.reshape(rows_in, pairs, fsdp, PAIR)
                .transpose(2, 0, 1, 3)
                .reshape(fsdp, rows_in, inner)
            )

        def gathered(cut):
            block = exchanged(cut, "fsdp")
            return gather_rows(block.reshape(fsdp * rows_in, cut.shape[2]), "dp")

        normed_own = (inputs * inverse_in * norm_gain[None, :]).astype(bf16)
        x_cut = channel_cut(in_low[:, INNER : 2 * INNER])
        gate_cut = channel_cut(in_low[:, :INNER])
        out_low = out_weight.astype(bf16)

        weight_shared = gathered(shared_cut)
        weight_x = gathered(x_cut)
        weight_gate = gathered(gate_cut)
        weight_out = lax.dynamic_index_in_dim(
            lax.all_gather(out_low, ("dp", "fsdp"), axis=0, tiled=True).reshape(
                pairs, fsdp, PAIR, D
            ),
            me,
            1,
            False,
        ).reshape(inner, D)
        normed = spread(normed_own, "fsdp").reshape(length, D)
        cotangents = spread(cotangent, "fsdp").reshape(length, D)

        small = lax.dot_general(
            weight_shared, normed, (((0,), (1,)), ((), ())), preferred_element_type=f32
        )
        shared_part = small[:shared]
        step_raw = small[shared : shared + heads] * head_mask[:, None]
        shared_padded = jnp.pad(shared_part, ((0, 0), (CONV - 1, 0)))
        shared_pre = bias_shared[:, None] + sum(
            taps_shared[k][:, None] * shared_padded[:, k : k + length] for k in range(CONV)
        )
        shared_gate = jax.nn.sigmoid(shared_pre)
        shared_all = spread_small((shared_pre * shared_gate).astype(bf16), "fsdp").reshape(
            2 * STATE, length
        )
        keys_t, queries_t = shared_all[:STATE], shared_all[STATE:]
        keys, queries = keys_t.T, queries_t.T
        step_logits = step_raw + step_bias_own[:, None]
        step_sizes = jax.nn.softplus(step_logits)
        upto = (jnp.arange(SPAN)[:, None] <= jnp.arange(SPAN)[None, :]).astype(f32)
        log_sums = jnp.dot(
            (step_sizes * decay_own[:, None]).reshape(heads, chunks, SPAN), upto, precision=highest
        ).reshape(heads, length)
        groups = heads // GROUP
        head_all = jnp.concatenate(
            [log_sums, step_sizes, step_logits, jnp.zeros((PAIR - 3 * heads, length), f32)]
        ).T
        head_columns = jnp.concatenate(
            [jnp.roll(head_all, -group * GROUP, axis=1) for group in range(groups)], axis=1
        )
        head_rows = jnp.pad(
            log_sums.reshape(groups, GROUP, length), ((0, 0), (0, 8 - GROUP), (0, 0))
        ).reshape(groups * 8, length)

        consts = jnp.concatenate([taps_own, bias_own, mask, skip_own, gain_own])
        scan_inputs = (consts, head_columns, head_rows, keys, queries)
        x_part = jnp.dot(normed, weight_x, preferred_element_type=f32)
        y, states = scan_forward(x_part, *scan_inputs, keys_t)
        gate_part, gated_grad, stats = gate_forward(
            normed, weight_gate, cotangents, weight_out, y, gain_own, mask
        )
        stats = summed(stats[:, :2].T, "fsdp")
        inverse_out = lax.rsqrt(stats[0] / channel_count + norm_eps)
        pull = inverse_out**3 / channel_count * stats[1]
        gated_low, y_grad, gate_grad, gain_grad = norm_back(
            y, gate_part, gated_grad, jnp.stack([inverse_out, pull], axis=1), gain_own, mask
        )

        def in_term(grad):
            return lax.dot_general(
                normed, grad, (((0,), (0,)), ((), ())), preferred_element_type=f32
            ).astype(bf16)

    if in_kernels:
        (
            layer_out, token_grad, gate_back, x_back, small_back, out_raw, vector_rows, gains,
            squares,
        ) = backward(
            scan_inputs, queries_t, head_all, head_consts, shared_part, shared_pre, shared_taps,
            vector_state[0], gain_grad, tokens, weight_shared, x_part, y_grad, states, gated_low,
            gated_t, gate_grad, normed_t, cotangents, cotangent, weight_out, weight_gate, weight_x,
        )
        norm, *rest = optimizer(
            squares, vector_rows, gains, vector_state, gate_back, x_back, small_back,
            (in_weight, in_first, in_second), out_raw, (out_weight, out_first, out_second),
            (layer_out, token_grad),
        )
        vector_out = [v.reshape(-1)[: vectors.shape[0]] for v in rest[:4]]
        in_grad, in_moment, in_square, in_master, in_rounded = rest[4:9]
        out_grad, out_moment, out_square, out_master, out_rounded = rest[9:14]
        layer_out, token_grad = rest[14:]
        return (
            layer_out,
            token_grad,
            in_grad,
            out_grad,
            vector_out[0],
            norm[0, 0],
            in_moment,
            in_square,
            in_master,
            in_rounded,
            out_moment,
            out_square,
            out_master,
            out_rounded,
            *vector_out[1:],
        )
    else:
        out_term = lax.dot_general(
            gated_low, cotangents, (((0,), (0,)), ((), ())), preferred_element_type=f32
        )
        whole_term = jnp.zeros((pairs, fsdp, PAIR, D), f32)
        whole_term = lax.dynamic_update_slice(
            whole_term, out_term.reshape(pairs, 1, PAIR, D), (0, me, 0, 0)
        )
        out_raw = lax.psum_scatter(
            whole_term.reshape(INNER, D), ("dp", "fsdp"), scatter_dimension=0, tiled=True
        )
        added = halved(
            jnp.dot(gated_low, weight_out, preferred_element_type=f32)
            .astype(bf16)
            .reshape(fsdp, tokens.shape[0], D),
            "fsdp",
        )
        layer_out = (inputs + added).astype(bf16)
        gate_raw = scatter_rows(in_term(gate_grad), "dp")
        x_grad, key_grad, query_grad, sums, rest, channel_grad = scan_backward(
            x_part, *scan_inputs, queries_t, y_grad, states
        )
        x_raw = scatter_rows(in_term(x_grad), "dp")

        shared_grads = jnp.concatenate([key_grad, query_grad], axis=1).T.astype(bf16)
        arrived = exchanged(shared_grads.reshape(fsdp, shared, length), "fsdp").astype(f32)
        activated_grad = jnp.sum(arrived, axis=0)
        shared_pre_grad = activated_grad * shared_gate * (1.0 + shared_pre * (1.0 - shared_gate))
        shared_ahead = jnp.pad(shared_pre_grad, ((0, 0), (0, CONV - 1)))
        shared_grad = sum(
            taps_shared[k][:, None] * shared_ahead[:, CONV - 1 - k : CONV - 1 - k + length]
            for k in range(CONV)
        )
        taps_shared_grad = jnp.stack(
            [
                jnp.sum(shared_pre_grad * shared_padded[:, k : k + length], axis=1)
                for k in range(CONV)
            ]
        )
        bias_shared_grad = jnp.sum(shared_pre_grad, axis=1)

        sums = sums.T[: 3 * heads].reshape(3, heads, chunks, SPAN)
        before = (jnp.arange(SPAN)[:, None] < jnp.arange(SPAN)[None, :]).astype(f32)
        rest = rest.reshape(chunks, heads, HEAD_DIM).sum(axis=2).T
        log_grad = (
            jnp.dot(sums[0], 1.0 - before, precision=highest)
            + jnp.dot(sums[1], before, precision=highest)
            + rest[:, :, None]
        ).reshape(heads, length)
        step_grad = decay_own[:, None] * log_grad + sums[2].reshape(heads, length)
        raw_grad = step_grad * jax.nn.sigmoid(step_logits)
        step_bias_grad = jnp.sum(raw_grad, axis=1)
        decay_grad = jnp.sum(step_sizes * log_grad, axis=1) * decay_own
        small_grad = jnp.concatenate([shared_grad, raw_grad * head_mask[:, None]], axis=0).astype(bf16)
        small_raw = scatter_rows(
            lax.dot_general(
                normed, small_grad, (((0,), (1,)), ((), ())), preferred_element_type=f32
            ).astype(bf16),
            "dp",
        )

        def in_back(grad, weight, grad_dim=1):
            return lax.dot_general(
                grad, weight, (((grad_dim,), (1,)), ((), ())), preferred_element_type=f32
            )

        normed_grad = halved(
            (
                in_back(gate_grad, weight_gate)
                + in_back(x_grad, weight_x)
                + in_back(small_grad, weight_shared, 0)
            )
            .astype(bf16)
            .reshape(fsdp, tokens.shape[0], D),
            "fsdp",
        )
        pulled = normed_grad * norm_gain[None, :]
        input_grad = inverse_in * pulled - inputs * (
            inverse_in**3 * jnp.mean(pulled * inputs, axis=-1, keepdims=True)
        )
        token_grad = (cotangent.astype(f32) + input_grad).astype(bf16)
        norm_gain_grad = jnp.sum(normed_grad * inputs * inverse_in, axis=0)

        head_row = jnp.concatenate(
            [jnp.pad(step_bias_grad, (0, PAIR - heads)), jnp.pad(decay_grad, (0, PAIR - heads))]
        )
        shared_rows = jnp.concatenate([taps_shared_grad, bias_shared_grad[None]])
        vector_rows = jnp.concatenate(
            [
                gain_grad[0:1],
                channel_grad[: CONV + 2],
                norm_gain_grad.reshape(-1, inner),
                jnp.zeros((15 - CONV - 3 - D // inner, inner), f32),
                jnp.pad(head_row, (0, inner - 2 * PAIR))[None],
                jnp.pad(shared_rows, ((0, 7 - CONV), (0, inner - shared))),
            ]
        )
        vector_rows = spread_small(summed_in_steps(vector_rows, "dp"), "fsdp")
        squares = (
            jnp.sum(gate_raw * gate_raw)
            + jnp.sum(x_raw * x_raw)
            + jnp.sum(small_raw * small_raw)
            + jnp.sum(out_raw * out_raw)
        )
        squares = summed(summed(jnp.broadcast_to(squares, (8, 128)), "fsdp"), "dp")[0, 0]

    def joined_channels(v):
        return v.reshape(fsdp, pairs, PAIR).transpose(1, 0, 2).reshape(INNER)

    def joined_heads(v):
        return v.reshape(fsdp, pairs, 2).transpose(1, 0, 2).reshape(HEADS)

    shared_all = vector_rows[:, 16 : 17 + CONV, :shared]
    bias_shared_all = shared_all[:, CONV].reshape(-1)
    taps_all = [
        jnp.concatenate([joined_channels(vector_rows[:, 1 + k]), shared_all[:, k].reshape(-1)])
        for k in range(CONV)
    ]
    bias_all = jnp.concatenate([joined_channels(vector_rows[:, CONV + 1]), bias_shared_all])
    norm_rows = vector_rows[:, CONV + 3 : CONV + 3 + D // inner].reshape(fsdp, D)
    norm_all = norm_rows[0]
    for member in range(1, fsdp):
        norm_all = norm_all + norm_rows[member]
    skip_all = vector_rows[:, CONV + 2].reshape(fsdp * heads, HEAD_DIM).sum(axis=1)
    vector_raw = jnp.concatenate(
        [norm_all, joined_channels(vector_rows[:, 0])]
        + taps_all
        + [
            bias_all,
            joined_heads(vector_rows[:, 15, :heads]),
            joined_heads(vector_rows[:, 15, PAIR : PAIR + heads]),
            joined_heads(skip_all),
        ]
    )

    grad_norm = jnp.sqrt(squares + jnp.sum(vector_raw * vector_raw))
    factor = jnp.minimum(1.0, clip_norm / (grad_norm + 1e-06))
    def returned(raw):
        return exchanged(raw.astype(bf16).reshape(fsdp, rows_in, raw.shape[1]), "fsdp")

    def joined_columns(part):
        return (
            part.reshape(fsdp, rows_in, pairs, PAIR)
            .transpose(1, 2, 0, 3)
            .reshape(rows_in, INNER)
        )

    small_back = returned(small_raw)
    in_raw = jnp.concatenate(
        [
            joined_columns(returned(gate_raw)),
            joined_columns(returned(x_raw)),
            small_back[:, :, :shared].transpose(1, 0, 2).reshape(rows_in, 2 * STATE),
            small_back[:, :, shared:]
            .reshape(fsdp, rows_in, pairs, 2)
            .transpose(1, 2, 0, 3)
            .reshape(rows_in, HEADS),
        ],
        axis=1,
    ).astype(f32)
    in_grad = in_raw * factor
    in_moment, in_square, in_master = adamw(
        in_weight, in_first, in_second, in_grad, rate_in_proj
    )
    in_rounded = in_master.astype(bf16)
    out_grad = out_raw * factor
    vector_grad = vector_raw * factor
    out_moment, out_square, out_master = adamw(
        out_weight, out_first, out_second, out_grad, rate_out_proj
    )
    vector_moment, vector_square, vector_master = adamw(
        vectors, vector_first, vector_second, vector_grad, rate_vectors
    )
    return (
        layer_out,
        token_grad,
        in_grad,
        out_grad,
        vector_grad,
        grad_norm,
        in_moment,
        in_square,
        in_master,
        in_rounded,
        out_moment,
        out_square,
        out_master,
        out_master.astype(bf16),
        vector_moment,
        vector_square,
        vector_master,
    )


def solution(mesh):
    rows = P(("dp", "fsdp"), None)
    return jax.shard_map(
        on_device,
        mesh=mesh,
        in_specs=(rows, P("dp")) + (rows,) * 7 + (P(),) * 3,
        out_specs=(rows,) * 4 + (P(),) * 2 + (rows,) * 8 + (P(),) * 3,
        check_vma=False,
    )
```
